32 devices in a mesh: item: 4 (over x, core), seq: 2 (over y), mp: 4 (over z).
Axes of the slice: x: 2, y: 2, z: 4, core: 2. Of those that a mesh axis runs over, the one named last changes fastest.
Arguments:
- hidden_in: bfloat16 [4, 2560, 2048], P('item', 'seq'), may hold values from -6 to 6
- cotangent: bfloat16 [4, 2560, 2048], P('item', 'seq'), may hold values from -6 to 6
- seg_lengths: int32 [4, 2], P('item'), may hold values from 640 to 1230, as said below
- pre_gain: float32 [2048], replicated, may hold values from 0.1 to 1.9
- pre_shift: float32 [2048], replicated, may hold values from -2 to 2
- qkv_weight: bfloat16 [2048, 3, 2048], P(('item', 'seq'), None, 'mp'), may hold values from -0.125 to 0.125
- qv_bias: float32 [2, 2048], P(None, 'mp'), may hold values from -2 to 2
- out_weight: bfloat16 [2048, 2048], P('mp', ('item', 'seq')), may hold values from -0.5 to 0.5
- out_bias: float32 [2048], replicated, may hold values from -2 to 2
- mid_gain: float32 [2048], replicated, may hold values from 0.1 to 1.9
- mid_shift: float32 [2048], replicated, may hold values from -2 to 2
- up_weight: bfloat16 [2048, 8192], P(('item', 'seq'), 'mp'), may hold values from -0.125 to 0.125
- up_bias: float32 [8192], P('mp'), may hold values from -3 to 3
- down_weight: bfloat16 [8192, 2048], P('mp', ('item', 'seq')), may hold values from -0.0625 to 0.0625
- down_bias: float32 [2048], replicated, may hold values from -2 to 2
Outputs:
- hidden_out: bfloat16 [4, 2560, 2048], P('item', 'seq')
- input_grad: float32 [4, 2560, 2048], P('item', 'seq')
- pre_gain_grad: float32 [2048], replicated
- pre_shift_grad: float32 [2048], replicated
- qkv_grad: float32 [2048, 3, 2048], P(('item', 'seq'), None, 'mp')
- qv_bias_grad: float32 [2, 2048], P(None, 'mp')
- out_grad: float32 [2048, 2048], P('mp', ('item', 'seq'))
- out_bias_grad: float32 [2048], replicated
- mid_gain_grad: float32 [2048], replicated
- mid_shift_grad: float32 [2048], replicated
- up_grad: float32 [2048, 8192], P(('item', 'seq'), 'mp')
- up_bias_grad: float32 [8192], P('mp')
- down_grad: float32 [8192, 2048], P('mp', ('item', 'seq'))
- down_bias_grad: float32 [2048], replicated
The draws below stay inside these ranges and needn't reach their ends.
Inputs may be any that keep to these rules, and one draw needn't show every extreme that they name: `seg_lengths`: in every item at least one segment has 1230 content tokens.
All inputs are finite; a program needn't handle non-finite values.
Results may differ from the reference program's by a relative error of at most 0.012.
Values may be sent and summed in bfloat16 or wider, within the bound.
A program may use at most 320 MiB of HBM per device.

```python
import math
import jax
import jax.numpy as jnp
from jax import lax

D = 2048
HDIM = 64
FF = 8192
SLOT = 1280
SEGS = 2
SUMM = 50
TOKENS = 2560
ITEMS = 4


def draw_seg_lengths(key, part):
    key = jax.random.fold_in(key, 7)
    pick_key, length_key = jax.random.split(key)
    base = jax.random.randint(length_key, (ITEMS, SEGS), SLOT // 2, SLOT - SUMM + 1)
    chosen = jax.random.randint(pick_key, (ITEMS, 1), 0, SEGS)
    longest = jnp.arange(SEGS, dtype=jnp.int32)[None, :] == chosen
    return jnp.where(longest, SLOT - SUMM, base).astype(jnp.int32)


def level_of(key, shape, cuts, least, largest):
    loudness, own = 1.0, jax.random.fold_in(key, 6)
    for axis_at, shards_of in cuts:
        steps = jnp.exp(jax.random.uniform(jax.random.fold_in(own, axis_at), (shards_of,), jnp.float32, least / len(cuts), largest / len(cuts)))
        loudness = loudness * jnp.repeat(steps, shape[axis_at] // shards_of).reshape([-1 if axis == axis_at else 1 for axis in range(len(shape))])
    return loudness


def scatter_about(rng, shape, width, reach, cuts=(), kind=jnp.bfloat16):
    array = jax.random.normal(rng, shape, jnp.float32) * width
    if len(cuts) > 0:
        array = level_of(rng, shape, cuts, -0.22, 0.18) * array
    return jnp.clip(array, min=-reach, max=reach).astype(kind)


def setup_inputs(seed: int = 0) -> dict:
    key_list = jax.random.split(jax.random.key(seed), 16)
    hidden_in = scatter_about(key_list[0], (ITEMS, TOKENS, D), 1.0, 6.0, ((0, 4), (1, 2)))
    cotangent = scatter_about(key_list[1], (ITEMS, TOKENS, D), 1.0, 6.0, ((0, 4), (1, 2)))
    seg_lengths = draw_seg_lengths(jax.random.fold_in(key_list[15], 71), 0)
    pre_gain = jnp.clip(1.0 + 0.18 * jax.random.normal(key_list[3], (D,), jnp.float32), 0.1, 1.9)
    pre_shift = scatter_about(key_list[4], (D,), 0.3, 2.0, (), jnp.float32)
    qkv_weight = scatter_about(key_list[5], (D, 3, D), D ** -0.5, 0.125, ((0, 8), (2, 4)))
    qv_bias = scatter_about(key_list[6], (2, D), 0.3, 2.0, ((1, 4),), jnp.float32)
    out_weight = scatter_about(key_list[7], (D, D), (D // 16) ** -0.5, 0.5, ((0, 4), (1, 8)))
    out_bias = scatter_about(key_list[8], (D,), 0.3, 2.0, (), jnp.float32)
    mid_gain = jnp.clip(1.0 + 0.18 * jax.random.normal(key_list[9], (D,), jnp.float32), 0.1, 1.9)
    mid_shift = scatter_about(key_list[10], (D,), 0.3, 2.0, (), jnp.float32)
    up_weight = scatter_about(key_list[11], (D, FF), D ** -0.5, 0.125, ((0, 8), (1, 4)))
    up_bias = scatter_about(key_list[12], (FF,), 0.5, 3.0, ((0, 4),), jnp.float32)
    down_weight = scatter_about(key_list[13], (FF, D), FF ** -0.5, 0.0625, ((0, 4), (1, 8)))
    down_bias = scatter_about(key_list[14], (D,), 0.3, 2.0, (), jnp.float32)
    return dict(hidden_in=hidden_in, cotangent=cotangent, seg_lengths=seg_lengths, pre_gain=pre_gain, pre_shift=pre_shift, qkv_weight=qkv_weight, qv_bias=qv_bias, out_weight=out_weight, out_bias=out_bias, mid_gain=mid_gain, mid_shift=mid_shift, up_weight=up_weight, up_bias=up_bias, down_weight=down_weight, down_bias=down_bias)


@jax.custom_vjp
def low(v):
    return lax.optimization_barrier(v.astype(jnp.bfloat16)).astype(jnp.float32)

@jax.custom_vjp
def low_back(v):
    return v

def low_keep(v):
    return (low(v), None)

def low_pass(kept, grad):
    return (grad,)

def back_keep(v):
    return (v, None)

def back_low(kept, grad):
    return (low(grad),)
low.defvjp(low_keep, low_pass)
low_back.defvjp(back_keep, back_low)
eps = 1e-05

def rounded(value):
    return low(low_back(value))

def matmul(left_side, right_side):
    return jnp.dot(left_side, right_side, precision=lax.Precision.HIGHEST)

def layer_norm(values, gain, shift):
    center = lax.optimization_barrier(jnp.mean(values, axis=-1, keepdims=True))
    centered = values - center
    spread = lax.optimization_barrier(jnp.mean(centered * centered, axis=-1, keepdims=True))
    return centered * lax.rsqrt(spread + eps) * gain + shift

def row_layout(row_index, lengths):
    segment = row_index // SLOT
    offset = row_index % SLOT
    picked = segment[:, None] == jnp.arange(SEGS, dtype=jnp.int32)[None, :]
    content = lax.optimization_barrier(jnp.sum(jnp.where(picked, lengths[None, :], 0), axis=1))
    is_live = offset < content + SUMM
    is_summary = is_live & (offset >= content)
    return (segment, offset, is_live, is_summary)

def allowed(query_layout, key_layout):
    query_segment, query_offset, query_live, query_summary = query_layout
    key_segment, key_offset, key_live, key_summary = key_layout
    same = (query_segment[:, None] == key_segment[None, :]) & (key_offset[None, :] <= query_offset[:, None])
    earlier = key_summary[None, :] & (key_segment[None, :] < query_segment[:, None])
    return key_live[None, :] & (same | earlier)

def forward_layer(hidden, pre_gain, pre_shift, qkv_weight, qv_bias, out_weight, out_bias, mid_gain, mid_shift, up_weight, up_bias, down_weight, down_bias, lengths):
    normed = low(layer_norm(hidden, pre_gain, pre_shift))
    queries = rounded(matmul(normed, qkv_weight[:, 0, :]) + qv_bias[0])
    keys_all = rounded(matmul(normed, qkv_weight[:, 1, :]))
    values_all = rounded(matmul(normed, qkv_weight[:, 2, :]) + qv_bias[1])
    head_count = D // HDIM
    key_heads = keys_all.reshape(TOKENS, head_count, HDIM)
    value_heads = values_all.reshape(TOKENS, head_count, HDIM)
    all_rows = jnp.arange(TOKENS, dtype=jnp.int32)
    key_layout = row_layout(all_rows, lengths)
    block_rows = math.gcd(TOKENS, 512)
    block_count = TOKENS // block_rows
    scale = 1.0 / math.sqrt(HDIM)

    def attend(pieces):
        query_block, block_start = pieces
        query_rows = block_start + jnp.arange(block_rows, dtype=jnp.int32)
        permitted = allowed(row_layout(query_rows, lengths), key_layout)
        raw_scores = jnp.einsum('qhd,khd->hqk', query_block, key_heads, precision=lax.Precision.HIGHEST)
        scores = low_back(raw_scores) * scale
        scores = jnp.where(permitted[None], scores, -1e+30)
        attn_probs = jax.nn.softmax(scores, axis=-1)
        mixed_rows = jnp.einsum('hqk,khd->qhd', low(attn_probs), value_heads, precision=lax.Precision.HIGHEST)
        return mixed_rows.reshape(block_rows, D)
    starts = jnp.arange(block_count, dtype=jnp.int32) * block_rows
    mixed_all = lax.map(jax.checkpoint(attend), (queries.reshape(block_count, block_rows, head_count, HDIM), starts))
    attended = rounded(mixed_all.reshape(TOKENS, D))
    residual = hidden + low_back(matmul(attended, out_weight)) + out_bias
    mid_normed = low(layer_norm(residual, mid_gain, mid_shift))
    activated = low(jax.nn.gelu(low_back(matmul(mid_normed, up_weight) + up_bias), approximate=True))
    return residual + low_back(matmul(activated, down_weight)) + down_bias

def reference(hidden_in, cotangent, seg_lengths, pre_gain, pre_shift, qkv_weight, qv_bias, out_weight, out_bias, mid_gain, mid_shift, up_weight, up_bias, down_weight, down_bias):
    parameters = (pre_gain, pre_shift, qkv_weight.astype(jnp.float32), qv_bias, out_weight.astype(jnp.float32), out_bias, mid_gain, mid_shift, up_weight.astype(jnp.float32), up_bias, down_weight.astype(jnp.float32), down_bias)
    outputs = []
    input_grads = []
    totals = None
    for member in range(ITEMS):
        lengths = seg_lengths[member]

        def applied(hidden, *weights):
            return forward_layer(hidden, *weights, lengths)
        result, pullback = jax.vjp(applied, hidden_in[member].astype(jnp.float32), *parameters)
        gradients = pullback(cotangent[member].astype(jnp.float32))
        outputs.append(result.astype(jnp.bfloat16))
        input_grads.append(gradients[0])
        if totals is None:
            totals = tuple(gradients[1:])
        else:
            totals = tuple(jax.tree.map(jnp.add, totals, tuple(gradients[1:])))
    return (jnp.stack(outputs), jnp.stack(input_grads), totals[0], totals[1], totals[2], totals[3], totals[4], totals[5], totals[6], totals[7], totals[8], totals[9], totals[10], totals[11])
```

```python
import functools
import math

import jax
import jax.numpy as jnp
from jax import lax
from jax.experimental import pallas as pl
from jax.experimental.pallas import tpu as pltpu
from jax.sharding import PartitionSpec as P

HDIM = 64
SLOT = 1280
SEGS = 2
SUMM = 50
SUMM_ROWS = 64
TOKENS = 2560
PAIR = 2 * HDIM
PIECE = 32
MIB = 1 << 20
MESH = pl.DeviceIdType.MESH
MASKED = -1e30


eps = 1e-05

NN = (((1,), (0,)), ((), ()))
NT = (((1,), (1,)), ((), ()))


def mm(left, right, dims=NN):
    return lax.dot_general(left, right, dims, preferred_element_type=jnp.float32)


def norm_stats(values):
    center = jnp.mean(values, axis=-1, keepdims=True)
    centered = values - center
    inverse = lax.rsqrt(jnp.mean(centered * centered, axis=-1, keepdims=True) + eps)
    return centered * inverse, inverse


def norm_back(grad_out, normed, inverse, gain):
    scaled = grad_out * gain
    centered = scaled - jnp.mean(scaled, axis=-1, keepdims=True)
    return inverse * (centered - normed * jnp.mean(scaled * normed, axis=-1, keepdims=True))


def gelu_parts(values):
    c = math.sqrt(2 / math.pi)
    squared = values * values
    t = jnp.tanh(c * values * (1 + 0.044715 * squared))
    half = 0.5 * (1 + t)
    slope = half + 0.5 * values * (1 - t * t) * (c * (1 + 3 * 0.044715 * squared))
    return values * half, slope


def key_masks(facts_ref, block, rows, bq, nk):
    first = facts_ref[0] + block * bq
    limit = jnp.minimum(
        first + 1 + lax.broadcasted_iota(jnp.int32, (1, bq), 1), facts_ref[1]
    )
    own = lax.broadcasted_iota(jnp.int32, (nk, bq), 0) < limit
    earlier = lax.broadcasted_iota(jnp.int32, (SUMM_ROWS, bq), 0) < facts_ref[2]
    return own, earlier


def head_lanes(head):
    lane = lax.broadcasted_iota(jnp.int32, (1, PAIR), 1)
    return (lane >= head * HDIM) & (lane < (head + 1) * HDIM)


def attend_kernel(bq, causal, facts_ref, q_ref, k_ref, v_ref, ks_ref, vs_ref, o_ref, lse_ref):
    rows, seg = q_ref.shape[0], k_ref.shape[0]
    v_t = v_ref[...].T
    vs_t = vs_ref[...].T
    ks = ks_ref[...]
    low_half = lax.broadcasted_iota(jnp.int32, (PAIR, 1), 0) < HDIM
    for block in range(rows // bq):
        nk = (block + 1) * bq if causal else seg
        own, earlier = key_masks(facts_ref, block, rows, bq, nk)
        q = q_ref[block * bq : (block + 1) * bq, :] * jnp.bfloat16(HDIM**-0.5)
        mixed = []
        for head in range(2):
            qh = jnp.where(head_lanes(head), q, jnp.zeros_like(q))
            s = jnp.where(own, mm(k_ref[:nk, :], qh, NT), MASKED)
            s2 = jnp.where(earlier, mm(ks, qh, NT), MASKED)
            top = jnp.maximum(jnp.max(s, axis=0, keepdims=True), jnp.max(s2, axis=0, keepdims=True))
            p = jnp.exp(s - top)
            p2 = jnp.exp(s2 - top)
            total = jnp.sum(p, axis=0, keepdims=True) + jnp.sum(p2, axis=0, keepdims=True)
            out = mm(v_t[:, :nk], p.astype(jnp.bfloat16)) + mm(vs_t, p2.astype(jnp.bfloat16))
            mixed.append(out / total)
            lse_ref[0, head : head + 1, block * bq : (block + 1) * bq] = top + jnp.log(total)
        joined = jnp.where(low_half, mixed[0], mixed[1])
        o_ref[block * bq : (block + 1) * bq, :] = joined.T.astype(jnp.bfloat16)


def attend_back_kernel(
    bq,
    causal,
    facts_ref,
    q_ref,
    k_ref,
    v_ref,
    ks_ref,
    vs_ref,
    do_ref,
    lse_ref,
    dq_ref,
    dk_ref,
    dv_ref,
    dks_ref,
    dvs_ref,
    dk_acc,
    dv_acc,
):
    rows, seg = q_ref.shape[0], k_ref.shape[0]
    scale = jnp.bfloat16(HDIM**-0.5)
    k_t = (k_ref[...] * scale).T
    ks_t = (ks_ref[...] * scale).T
    ks = ks_ref[...]
    vs = vs_ref[...]
    low_half = lax.broadcasted_iota(jnp.int32, (PAIR, 1), 0) < HDIM
    dk_acc[...] = jnp.zeros_like(dk_acc)
    dv_acc[...] = jnp.zeros_like(dv_acc)
    dks = jnp.zeros((SUMM_ROWS, PAIR), jnp.float32)
    dvs = jnp.zeros((SUMM_ROWS, PAIR), jnp.float32)
    for block in range(rows // bq):
        nk = (block + 1) * bq if causal else seg
        own, earlier = key_masks(facts_ref, block, rows, bq, nk)
        q = q_ref[block * bq : (block + 1) * bq, :] * scale
        do = do_ref[block * bq : (block + 1) * bq, :]
        grads = []
        for head in range(2):
            qh = jnp.where(head_lanes(head), q, jnp.zeros_like(q))
            doh = jnp.where(head_lanes(head), do, jnp.zeros_like(do))
            lse = lse_ref[0, head : head + 1, block * bq : (block + 1) * bq]
            p = jnp.exp(jnp.where(own, mm(k_ref[:nk, :], qh, NT), MASKED) - lse)
            p2 = jnp.exp(jnp.where(earlier, mm(ks, qh, NT), MASKED) - lse)
            dp = mm(v_ref[:nk, :], doh, NT)
            dp2 = mm(vs, doh, NT)
            delta = jnp.sum(p * dp, axis=0, keepdims=True) + jnp.sum(p2 * dp2, axis=0, keepdims=True)
            ds = (p * (dp - delta)).astype(jnp.bfloat16)
            ds2 = (p2 * (dp2 - delta)).astype(jnp.bfloat16)
            dv_acc[:nk, :] += mm(p.astype(jnp.bfloat16), doh)
            dk_acc[:nk, :] += mm(ds, qh)
            dvs = dvs + mm(p2.astype(jnp.bfloat16), doh)
            dks = dks + mm(ds2, qh)
            grads.append(mm(k_t[:, :nk], ds) + mm(ks_t, ds2))
        joined = jnp.where(low_half, grads[0], grads[1])
        dq_ref[block * bq : (block + 1) * bq, :] = joined.T.astype(jnp.bfloat16)
    dk_ref[...] = dk_acc[...].astype(jnp.bfloat16)
    dv_ref[...] = dv_acc[...].astype(jnp.bfloat16)
    dks_ref[...] = dks
    dvs_ref[...] = dvs


def query_block(rows):
    return 256 if rows % 256 == 0 else math.gcd(rows, 160)


def attend(facts, q, k, v, ks, vs):
    rows, width = q.shape
    seg = k.shape[0]
    pairs = width // PAIR
    column = lambda n: pl.BlockSpec((n, PAIR), lambda i: (0, i))
    return pl.pallas_call(
        functools.partial(attend_kernel, query_block(rows), rows == seg),
        grid=(pairs,),
        in_specs=[pl.BlockSpec(memory_space=pltpu.SMEM)]
        + [column(n) for n in (rows, seg, seg, SUMM_ROWS, SUMM_ROWS)],
        out_specs=[column(rows), pl.BlockSpec((1, 2, rows), lambda i: (i, 0, 0))],
        out_shape=[
            jax.ShapeDtypeStruct((rows, width), jnp.bfloat16),
            jax.ShapeDtypeStruct((pairs, 2, rows), jnp.float32),
        ],
        compiler_params=pltpu.CompilerParams(vmem_limit_bytes=48 * MIB),
        cost_estimate=pl.CostEstimate(
            flops=4 * rows * seg * width, bytes_accessed=8 * rows * width, transcendentals=0
        ),
        name="attend",
    )(facts, q, k, v, ks, vs)


def attend_back(facts, q, k, v, ks, vs, do, lse):
    rows, width = q.shape
    seg = k.shape[0]
    pairs = width // PAIR
    column = lambda n: pl.BlockSpec((n, PAIR), lambda i: (0, i))
    low = lambda n: jax.ShapeDtypeStruct((n, width), jnp.bfloat16)
    wide = lambda n: jax.ShapeDtypeStruct((n, width), jnp.float32)
    return pl.pallas_call(
        functools.partial(attend_back_kernel, query_block(rows), rows == seg),
        grid=(pairs,),
        in_specs=[pl.BlockSpec(memory_space=pltpu.SMEM)]
        + [column(n) for n in (rows, seg, seg, SUMM_ROWS, SUMM_ROWS, rows)]
        + [pl.BlockSpec((1, 2, rows), lambda i: (i, 0, 0))],
        out_specs=[column(n) for n in (rows, seg, seg, SUMM_ROWS, SUMM_ROWS)],
        out_shape=[low(rows), low(seg), low(seg), wide(SUMM_ROWS), wide(SUMM_ROWS)],
        scratch_shapes=[pltpu.VMEM((seg, PAIR), jnp.float32)] * 2,
        compiler_params=pltpu.CompilerParams(vmem_limit_bytes=48 * MIB),
        cost_estimate=pl.CostEstimate(
            flops=10 * rows * seg * width, bytes_accessed=16 * rows * width, transcendentals=0
        ),
        name="attend_back",
    )(facts, q, k, v, ks, vs, do, lse)


def keys_for(local, lengths, seq_count):
    rows, width = local.shape[-2:]
    pad = ((0, 0), (0, SUMM_ROWS - SUMM), (0, 0))
    if rows == SLOT:
        here = lengths[lax.axis_index("seq")]
        summary = jnp.pad(lax.dynamic_slice(local, (0, here, 0), (2, SUMM, width)), pad)
        moves = [(i, i + 1) for i in range(seq_count - 1)]
        return local, lax.ppermute(summary, "seq", moves)
    everything = lax.all_gather(local, "seq", axis=1, tiled=True)
    segment = lax.axis_index("seq") * rows // SLOT
    own = lax.dynamic_slice(everything, (0, segment * SLOT, 0), (2, SLOT, width))
    summary = lax.dynamic_slice(everything, (0, lengths[0], 0), (2, SUMM, width))
    return own, jnp.pad(summary, pad)


def keys_back(own, summary, rows, lengths, seq_count):
    width = own.shape[-1]
    summary = summary[:, :SUMM]
    if rows == SLOT:
        moves = [(i + 1, i) for i in range(seq_count - 1)]
        arrived = lax.ppermute(summary, "seq", moves)
        here = lengths[lax.axis_index("seq")]
        old = lax.dynamic_slice(own, (0, here, 0), (2, SUMM, width))
        new = (old.astype(jnp.float32) + arrived).astype(jnp.bfloat16)
        return lax.dynamic_update_slice(own, new, (0, here, 0))
    segment = lax.axis_index("seq") * rows // SLOT
    everything = jnp.zeros((2, TOKENS, width), jnp.float32)
    everything = lax.dynamic_update_slice(
        everything, own.astype(jnp.float32), (0, segment * SLOT, 0)
    )
    old = lax.dynamic_slice(everything, (0, lengths[0], 0), (2, SUMM, width))
    added = jnp.where(segment > 0, summary, 0.0)
    everything = lax.dynamic_update_slice(everything, old + added, (0, lengths[0], 0))
    return lax.psum_scatter(
        everything.astype(jnp.bfloat16), "seq", scatter_dimension=1, tiled=True
    )


def body(
    seq_count,
    mp_count,
    hidden_in,
    cotangent,
    seg_lengths,
    pre_gain,
    pre_shift,
    qkv_weight,
    qv_bias,
    out_weight,
    out_bias,
    mid_gain,
    mid_shift,
    up_weight,
    up_bias,
    down_weight,
    down_bias,
):
    group = ("item", "seq")
    width = qkv_weight.shape[2]
    gathered = lambda weight, axis: lax.all_gather(weight, group, axis=axis, tiled=True)
    qkv_full = gathered(qkv_weight.reshape(-1, 3 * width), 0)
    out_full = gathered(out_weight, 1)
    up_full = gathered(up_weight, 0)
    down_full = gathered(down_weight, 1)
    hidden = hidden_in[0].astype(jnp.float32)
    lengths = seg_lengths[0]
    rows = hidden.shape[0]
    first_row = lax.axis_index("seq") * rows
    segment = first_row // SLOT
    facts = jnp.stack(
        [
            first_row % SLOT,
            lengths[segment] + SUMM,
            jnp.where(segment > 0, SUMM, 0),
        ]
    ).astype(jnp.int32)

    pre_normed, pre_inverse = norm_stats(hidden)
    normed = (pre_normed * pre_gain + pre_shift).astype(jnp.bfloat16)
    q = (mm(normed, qkv_full[:, :width]) + qv_bias[0]).astype(jnp.bfloat16)
    k = mm(normed, qkv_full[:, width : 2 * width]).astype(jnp.bfloat16)
    v = (mm(normed, qkv_full[:, 2 * width :]) + qv_bias[1]).astype(jnp.bfloat16)
    own, summary = keys_for(jnp.stack([k, v]), lengths, seq_count)
    tables = (own[0], own[1], summary[0], summary[1])
    attended, log_total = attend(facts, q, *tables)

    branch = lax.psum(mm(attended, out_full).astype(jnp.bfloat16), "mp").astype(jnp.float32)
    residual = hidden + branch + out_bias
    mid_normed, mid_inverse = norm_stats(residual)
    mid_low = (mid_normed * mid_gain + mid_shift).astype(jnp.bfloat16)
    activated, slope = gelu_parts(mm(mid_low, up_full) + up_bias)
    act_low = activated.astype(jnp.bfloat16)
    feed = lax.psum(mm(act_low, down_full).astype(jnp.bfloat16), "mp").astype(jnp.float32)
    hidden_out = (residual + feed + down_bias).astype(jnp.bfloat16)

    grad_down = cotangent[0]
    grad_out = grad_down.astype(jnp.float32)
    grad_pre = (slope * mm(grad_down, down_full, NT)).astype(jnp.bfloat16)
    over_rows = lambda left, right: mm(left, right, (((0,), (0,)), ((), ())))
    spread = lambda grad, axis: lax.psum_scatter(
        grad.astype(jnp.bfloat16), group, scatter_dimension=axis, tiled=True
    ).astype(jnp.float32)
    down_grad = spread(over_rows(act_low, grad_down), 1)
    up_grad = spread(over_rows(mid_low, grad_pre), 0)
    grad_mid = lax.psum(mm(grad_pre, up_full, NT).astype(jnp.bfloat16), "mp").astype(jnp.float32)
    grad_residual = grad_out + norm_back(grad_mid, mid_normed, mid_inverse, mid_gain)
    grad_branch = grad_residual.astype(jnp.bfloat16)
    out_grad = spread(over_rows(attended, grad_branch), 1)
    grad_attended = mm(grad_branch, out_full, NT).astype(jnp.bfloat16)

    dq, dk, dv, dks, dvs = attend_back(facts, q, *tables, grad_attended, log_total)
    dk, dv = keys_back(jnp.stack([dk, dv]), jnp.stack([dks, dvs]), rows, lengths, seq_count)
    grad_projected = jnp.concatenate([dq, dk, dv], axis=1)
    qkv_grad = spread(over_rows(normed, grad_projected), 0)
    grad_normed = lax.psum(mm(grad_projected, qkv_full, NT).astype(jnp.bfloat16), "mp").astype(
        jnp.float32
    )
    grad_input = grad_residual + norm_back(grad_normed, pre_normed, pre_inverse, pre_gain)
    total = lambda value: jnp.sum(value.astype(jnp.float32), axis=0)
    small = lax.psum(
        (
            total(grad_normed * pre_normed),
            total(grad_normed),
            jnp.stack([total(dq), total(dv)]),
            total(grad_residual),
            total(grad_mid * mid_normed),
            total(grad_mid),
            total(grad_pre),
            total(grad_out),
        ),
        group,
    )
    return (
        hidden_out[None],
        grad_input[None],
        small[0],
        small[1],
        qkv_grad.reshape(-1, 3, width),
        small[2],
        out_grad,
        small[3],
        small[4],
        small[5],
        up_grad,
        small[6],
        down_grad,
        small[7],
    )


def solution(mesh):
    rows = P("item", "seq", None)
    qkv = P(("item", "seq"), None, "mp")
    first = P(("item", "seq"), "mp")
    second = P("mp", ("item", "seq"))
    bias = P(None, "mp")
    return jax.shard_map(
        functools.partial(body, mesh.shape["seq"], mesh.shape["mp"]),
        mesh=mesh,
        in_specs=(
            rows,
            rows,
            P("item", None),
            P(),
            P(),
            qkv,
            bias,
            second,
            P(),
            P(),
            P(),
            first,
            P("mp"),
            second,
            P(),
        ),
        out_specs=(
            rows,
            rows,
            P(),
            P(),
            qkv,
            bias,
            second,
            P(),
            P(),
            P(),
            first,
            P("mp"),
            second,
            P(),
        ),
        check_vma=False,
    )
```

```python
import functools
import math

import jax
import jax.numpy as jnp
from jax import lax
from jax.experimental import pallas as pl
from jax.experimental.pallas import tpu as pltpu
from jax.sharding import PartitionSpec as P

HDIM = 64
SLOT = 1280
SEGS = 2
SUMM = 50
SUMM_ROWS = 64
TOKENS = 2560
PAIR = 2 * HDIM
PIECE = 32
SKEW = 2
MIB = 1 << 20
MESH = pl.DeviceIdType.MESH
MASKED = -1e30


eps = 1e-05

NN = (((1,), (0,)), ((), ()))
NT = (((1,), (1,)), ((), ()))


def mm(left, right, dims=NN):
    return lax.dot_general(left, right, dims, preferred_element_type=jnp.float32)


def norm_stats(values):
    center = jnp.mean(values, axis=-1, keepdims=True)
    centered = values - center
    inverse = lax.rsqrt(jnp.mean(centered * centered, axis=-1, keepdims=True) + eps)
    return centered * inverse, inverse


def norm_back(grad_out, normed, inverse, gain):
    scaled = grad_out * gain
    centered = scaled - jnp.mean(scaled, axis=-1, keepdims=True)
    return inverse * (centered - normed * jnp.mean(scaled * normed, axis=-1, keepdims=True))


def gelu_parts(values):
    c = math.sqrt(2 / math.pi)
    squared = values * values
    t = jnp.tanh(c * values * (1 + 0.044715 * squared))
    half = 0.5 * (1 + t)
    slope = half + 0.5 * values * (1 - t * t) * (c * (1 + 3 * 0.044715 * squared))
    return values * half, slope


def key_masks(facts_ref, block, rows, bq, nk):
    first = facts_ref[0] + block * bq
    limit = jnp.minimum(
        first + 1 + lax.broadcasted_iota(jnp.int32, (1, bq), 1), facts_ref[1]
    )
    own = lax.broadcasted_iota(jnp.int32, (nk, bq), 0) < limit
    earlier = lax.broadcasted_iota(jnp.int32, (SUMM_ROWS, bq), 0) < facts_ref[2]
    return own, earlier


def head_lanes(head):
    lane = lax.broadcasted_iota(jnp.int32, (1, PAIR), 1)
    return (lane >= head * HDIM) & (lane < (head + 1) * HDIM)


def attend_kernel(bq, causal, facts_ref, q_ref, k_ref, v_ref, ks_ref, vs_ref, o_ref, lse_ref):
    rows, seg = q_ref.shape[0], k_ref.shape[0]
    v_t = v_ref[...].T
    vs_t = vs_ref[...].T
    ks = ks_ref[...]
    low_half = lax.broadcasted_iota(jnp.int32, (PAIR, 1), 0) < HDIM
    for block in range(rows // bq):
        nk = (block + 1) * bq if causal else seg
        own, earlier = key_masks(facts_ref, block, rows, bq, nk)
        q = q_ref[block * bq : (block + 1) * bq, :] * jnp.bfloat16(HDIM**-0.5)
        mixed = []
        for head in range(2):
            qh = jnp.where(head_lanes(head), q, jnp.zeros_like(q))
            s = jnp.where(own, mm(k_ref[:nk, :], qh, NT), MASKED)
            s2 = jnp.where(earlier, mm(ks, qh, NT), MASKED)
            top = jnp.maximum(jnp.max(s, axis=0, keepdims=True), jnp.max(s2, axis=0, keepdims=True))
            p = jnp.exp(s - top)
            p2 = jnp.exp(s2 - top)
            total = jnp.sum(p, axis=0, keepdims=True) + jnp.sum(p2, axis=0, keepdims=True)
            out = mm(v_t[:, :nk], p.astype(jnp.bfloat16)) + mm(vs_t, p2.astype(jnp.bfloat16))
            mixed.append(out / total)
            lse_ref[0, head : head + 1, block * bq : (block + 1) * bq] = top + jnp.log(total)
        joined = jnp.where(low_half, mixed[0], mixed[1])
        o_ref[block * bq : (block + 1) * bq, :] = joined.T.astype(jnp.bfloat16)


def attend_back_kernel(
    bq,
    causal,
    facts_ref,
    q_ref,
    k_ref,
    v_ref,
    ks_ref,
    vs_ref,
    do_ref,
    lse_ref,
    dq_ref,
    dk_ref,
    dv_ref,
    dks_ref,
    dvs_ref,
    dk_acc,
    dv_acc,
):
    rows, seg = q_ref.shape[0], k_ref.shape[0]
    scale = jnp.bfloat16(HDIM**-0.5)
    k_t = (k_ref[...] * scale).T
    ks_t = (ks_ref[...] * scale).T
    ks = ks_ref[...]
    vs = vs_ref[...]
    low_half = lax.broadcasted_iota(jnp.int32, (PAIR, 1), 0) < HDIM
    dk_acc[...] = jnp.zeros_like(dk_acc)
    dv_acc[...] = jnp.zeros_like(dv_acc)
    dks = jnp.zeros((SUMM_ROWS, PAIR), jnp.float32)
    dvs = jnp.zeros((SUMM_ROWS, PAIR), jnp.float32)
    for block in range(rows // bq):
        nk = (block + 1) * bq if causal else seg
        own, earlier = key_masks(facts_ref, block, rows, bq, nk)
        q = q_ref[block * bq : (block + 1) * bq, :] * scale
        do = do_ref[block * bq : (block + 1) * bq, :]
        grads = []
        for head in range(2):
            qh = jnp.where(head_lanes(head), q, jnp.zeros_like(q))
            doh = jnp.where(head_lanes(head), do, jnp.zeros_like(do))
            lse = lse_ref[0, head : head + 1, block * bq : (block + 1) * bq]
            p = jnp.exp(jnp.where(own, mm(k_ref[:nk, :], qh, NT), MASKED) - lse)
            p2 = jnp.exp(jnp.where(earlier, mm(ks, qh, NT), MASKED) - lse)
            dp = mm(v_ref[:nk, :], doh, NT)
            dp2 = mm(vs, doh, NT)
            delta = jnp.sum(p * dp, axis=0, keepdims=True) + jnp.sum(p2 * dp2, axis=0, keepdims=True)
            ds = (p * (dp - delta)).astype(jnp.bfloat16)
            ds2 = (p2 * (dp2 - delta)).astype(jnp.bfloat16)
            dv_acc[:nk, :] += mm(p.astype(jnp.bfloat16), doh)
            dk_acc[:nk, :] += mm(ds, qh)
            dvs = dvs + mm(p2.astype(jnp.bfloat16), doh)
            dks = dks + mm(ds2, qh)
            grads.append(mm(k_t[:, :nk], ds) + mm(ks_t, ds2))
        joined = jnp.where(low_half, grads[0], grads[1])
        dq_ref[block * bq : (block + 1) * bq, :] = joined.T.astype(jnp.bfloat16)
    dk_ref[...] = dk_acc[...].astype(jnp.bfloat16)
    dv_ref[...] = dv_acc[...].astype(jnp.bfloat16)
    dks_ref[...] = dks
    dvs_ref[...] = dvs


def query_block(rows):
    return 256 if rows % 256 == 0 else math.gcd(rows, 160)


def attend(facts, q, k, v, ks, vs):
    rows, width = q.shape
    seg = k.shape[0]
    pairs = width // PAIR
    column = lambda n: pl.BlockSpec((n, PAIR), lambda i: (0, i))
    return pl.pallas_call(
        functools.partial(attend_kernel, query_block(rows), rows == seg),
        grid=(pairs,),
        in_specs=[pl.BlockSpec(memory_space=pltpu.SMEM)]
        + [column(n) for n in (rows, seg, seg, SUMM_ROWS, SUMM_ROWS)],
        out_specs=[column(rows), pl.BlockSpec((1, 2, rows), lambda i: (i, 0, 0))],
        out_shape=[
            jax.ShapeDtypeStruct((rows, width), jnp.bfloat16),
            jax.ShapeDtypeStruct((pairs, 2, rows), jnp.float32),
        ],
        compiler_params=pltpu.CompilerParams(vmem_limit_bytes=48 * MIB),
        cost_estimate=pl.CostEstimate(
            flops=4 * rows * seg * width, bytes_accessed=8 * rows * width, transcendentals=0
        ),
        name="attend",
    )(facts, q, k, v, ks, vs)


def attend_back(facts, q, k, v, ks, vs, do, lse):
    rows, width = q.shape
    seg = k.shape[0]
    pairs = width // PAIR
    column = lambda n: pl.BlockSpec((n, PAIR), lambda i: (0, i))
    low = lambda n: jax.ShapeDtypeStruct((n, width), jnp.bfloat16)
    wide = lambda n: jax.ShapeDtypeStruct((n, width), jnp.float32)
    return pl.pallas_call(
        functools.partial(attend_back_kernel, query_block(rows), rows == seg),
        grid=(pairs,),
        in_specs=[pl.BlockSpec(memory_space=pltpu.SMEM)]
        + [column(n) for n in (rows, seg, seg, SUMM_ROWS, SUMM_ROWS, rows)]
        + [pl.BlockSpec((1, 2, rows), lambda i: (i, 0, 0))],
        out_specs=[column(n) for n in (rows, seg, seg, SUMM_ROWS, SUMM_ROWS)],
        out_shape=[low(rows), low(seg), low(seg), wide(SUMM_ROWS), wide(SUMM_ROWS)],
        scratch_shapes=[pltpu.VMEM((seg, PAIR), jnp.float32)] * 2,
        compiler_params=pltpu.CompilerParams(vmem_limit_bytes=48 * MIB),
        cost_estimate=pl.CostEstimate(
            flops=10 * rows * seg * width, bytes_accessed=16 * rows * width, transcendentals=0
        ),
        name="attend_back",
    )(facts, q, k, v, ks, vs, do, lse)


def keys_for(local, lengths, seq_count):
    rows, width = local.shape[-2:]
    pad = ((0, 0), (0, SUMM_ROWS - SUMM), (0, 0))
    if rows == SLOT:
        here = lengths[lax.axis_index("seq")]
        summary = jnp.pad(lax.dynamic_slice(local, (0, here, 0), (2, SUMM, width)), pad)
        moves = [(i, i + 1) for i in range(seq_count - 1)]
        return local, lax.ppermute(summary, "seq", moves)
    everything = lax.all_gather(local, "seq", axis=1, tiled=True)
    segment = lax.axis_index("seq") * rows // SLOT
    own = lax.dynamic_slice(everything, (0, segment * SLOT, 0), (2, SLOT, width))
    summary = lax.dynamic_slice(everything, (0, lengths[0], 0), (2, SUMM, width))
    return own, jnp.pad(summary, pad)


def keys_back(own, summary, rows, lengths, seq_count):
    width = own.shape[-1]
    summary = summary[:, :SUMM]
    if rows == SLOT:
        moves = [(i + 1, i) for i in range(seq_count - 1)]
        arrived = lax.ppermute(summary, "seq", moves)
        here = lengths[lax.axis_index("seq")]
        old = lax.dynamic_slice(own, (0, here, 0), (2, SUMM, width))
        new = (old.astype(jnp.float32) + arrived).astype(jnp.bfloat16)
        return lax.dynamic_update_slice(own, new, (0, here, 0))
    segment = lax.axis_index("seq") * rows // SLOT
    everything = jnp.zeros((2, TOKENS, width), jnp.float32)
    everything = lax.dynamic_update_slice(
        everything, own.astype(jnp.float32), (0, segment * SLOT, 0)
    )
    old = lax.dynamic_slice(everything, (0, lengths[0], 0), (2, SUMM, width))
    added = jnp.where(segment > 0, summary, 0.0)
    everything = lax.dynamic_update_slice(everything, old + added, (0, lengths[0], 0))
    return lax.psum_scatter(
        everything.astype(jnp.bfloat16), "seq", scatter_dimension=1, tiled=True
    )


def line_kernel(count, half, group, dims, n_left, n_extra, n_owned, n_acc, finish, *refs):
    refs = list(refs)
    take = lambda n: [refs.pop(0) for _ in range(n)]
    lefts, (right,), extras = take(n_left), take(1), take(n_extra)
    (out,), owned, accs = take(1), take(n_owned), take(1 if n_acc else 0)
    part, arrived, staged, up_sent, up_got, down_sent, down_got, local = refs
    me = lax.axis_index("mp")
    pieces = half // PIECE
    per_group = group // PIECE
    barrier = pltpu.get_barrier_semaphore()

    @pl.when(me > 0)
    def _():
        pl.semaphore_signal(barrier, inc=1, device_id={"mp": me - 1}, device_id_type=MESH)

    @pl.when(me < count - 1)
    def _():
        pl.semaphore_signal(barrier, inc=1, device_id={"mp": me + 1}, device_id_type=MESH)

    if n_acc:
        accs[0][...] = jnp.zeros_like(accs[0])

    def multiply(flow, g):
        rows = pl.ds(pl.multiple_of(flow * half + g * group, 16), group)
        at = 0
        for number, left in enumerate(lefts):
            depth = left.shape[1]
            cut = right.at[:, at : at + depth] if dims == NT else right.at[at : at + depth, :]
            product = mm(left[rows, :], cut[...], dims)
            if number == 0:
                part[flow, g % 2] = product
            else:
                part[flow, g % 2] += product
            at += depth

    for flow in range(2):
        multiply(flow, 0)

    ends = (me == 0) | (me == count - 1)

    @pl.when(ends)
    def _():
        pl.semaphore_wait(barrier, 1)

    @pl.when(jnp.logical_not(ends))
    def _():
        pl.semaphore_wait(barrier, 2)

    def onward(flow, k, place):
        to = me - 1 if flow == 0 else me + 1
        return pltpu.make_async_remote_copy(
            src_ref=staged.at[flow, pl.ds(k * PIECE, PIECE)],
            dst_ref=arrived.at[flow, pl.ds(k * PIECE, PIECE)],
            send_sem=up_sent.at[flow, k],
            recv_sem=up_got.at[flow, k],
            device_id={"mp": to},
            device_id_type=MESH,
        )

    def back(flow, k, owner):
        to = me + 1 if flow == 0 else me - 1
        rows = pl.ds(flow * half + k * PIECE, PIECE)
        return pltpu.make_async_remote_copy(
            src_ref=staged.at[flow, pl.ds(k * PIECE, PIECE)] if owner else out.at[rows],
            dst_ref=out.at[rows],
            send_sem=down_sent.at[flow, k],
            recv_sem=down_got.at[flow, k],
            device_id={"mp": to},
            device_id_type=MESH,
        )

    def keep(flow, k):
        return pltpu.make_async_copy(
            staged.at[flow, pl.ds(k * PIECE, PIECE)],
            out.at[pl.ds(flow * half + k * PIECE, PIECE)],
            local.at[k],
        )

    def step(t, carry):
        for flow in range(2):
            place = count - 1 - me if flow == 0 else me
            k = t - SKEW * place
            here = pl.ds(pl.multiple_of(k * PIECE, PIECE), PIECE)
            busy = (k >= 0) & (k < pieces)

            def mine():
                slot = (k // per_group) % 2
                inner = pl.ds(pl.multiple_of((k % per_group) * PIECE, PIECE), PIECE)
                return part[flow, slot, inner, :]

            @pl.when(busy & (place == 0))
            def _():
                staged[flow, here, :] = mine().astype(jnp.bfloat16)
                onward(flow, k, place).start()

            @pl.when(busy & (place > 0) & (place < count - 1))
            def _():
                onward(flow, k, place).wait_recv()
                total = mine() + arrived[flow, here, :].astype(jnp.float32)
                staged[flow, here, :] = total.astype(jnp.bfloat16)
                onward(flow, k, place).start()

            @pl.when(busy & (place == count - 1))
            def _():
                onward(flow, k, place).wait_recv()
                total = mine() + arrived[flow, here, :].astype(jnp.float32)
                staged[flow, here, :] = finish(flow, k, total, extras, owned, accs).astype(
                    jnp.bfloat16
                )
                back(flow, k, True).start()
                keep(flow, k).start()

        for flow in range(2):
            place = count - 1 - me if flow == 0 else me
            j = t - SKEW * (2 * (count - 1) - place)

            @pl.when((j >= 0) & (j < pieces) & (place < count - 1))
            def _():
                back(flow, j, False).wait_recv()

                @pl.when(place > 0)
                def _():
                    back(flow, j, False).start()

        for flow in range(2):
            place = count - 1 - me if flow == 0 else me
            k = t - SKEW * place
            g = k // per_group + 1

            @pl.when((k >= 0) & (k % per_group == 0) & (g < pieces // per_group))
            def _():
                multiply(flow, g)

        return carry

    lax.fori_loop(0, pieces + 2 * SKEW * (count - 1), step, 0)

    def settle(k, carry):
        for flow in range(2):
            place = count - 1 - me if flow == 0 else me

            @pl.when(place < count - 1)
            def _():
                onward(flow, k, place).wait_send()

                @pl.when(place > 0)
                def _():
                    back(flow, k, False).wait_send()

            @pl.when(place == count - 1)
            def _():
                back(flow, k, True).wait_send()
                keep(flow, k).wait()

        return carry

    lax.fori_loop(0, pieces, settle, 0)


def line_sum(number, count, lefts, right, dims, extras, n_owned, n_acc, finish, name):
    rows = lefts[0].shape[0]
    features = right.shape[1 if dims == NN else 0]
    half = rows // 2
    pieces = half // PIECE
    group = 5 * PIECE if pieces % 5 == 0 else PIECE
    vmem = pl.BlockSpec(memory_space=pltpu.VMEM)
    anywhere = pl.BlockSpec(memory_space=pl.ANY)
    acc = [jax.ShapeDtypeStruct((n_acc, 8, features), jnp.float32)] if n_acc else []
    dma = lambda *shape: pltpu.SemaphoreType.DMA(shape)
    return pl.pallas_call(
        functools.partial(
            line_kernel, count, half, group, dims, len(lefts), len(extras), n_owned, n_acc, finish
        ),
        in_specs=[vmem] * (len(lefts) + 1 + len(extras)),
        out_specs=[anywhere] + [vmem] * (n_owned + len(acc)),
        out_shape=[jax.ShapeDtypeStruct((rows, features), jnp.bfloat16)]
        + [jax.ShapeDtypeStruct((half, features), jnp.float32)] * n_owned
        + acc,
        scratch_shapes=[
            pltpu.VMEM((2, 2, group, features), jnp.float32),
            pltpu.VMEM((2, half, features), jnp.bfloat16),
            pltpu.VMEM((2, half, features), jnp.bfloat16),
            dma(2, pieces),
            dma(2, pieces),
            dma(2, pieces),
            dma(2, pieces),
            dma(pieces),
        ],
        compiler_params=pltpu.CompilerParams(
            collective_id=number, has_side_effects=True, vmem_limit_bytes=60 * MIB
        ),
        cost_estimate=pl.CostEstimate(
            flops=2 * rows * features * sum(left.shape[1] for left in lefts),
            bytes_accessed=4 * rows * features,
            transcendentals=0,
        ),
        name=name,
    )(*lefts, right, *extras)


def piece_rows(flow, k, half):
    return pl.ds(pl.multiple_of(flow * half + k * PIECE, PIECE), PIECE)


def fold(values):
    return jnp.sum(values.reshape(-1, 8, values.shape[-1]), axis=0)


def finish_mid(flow, k, total, extras, owned, accs):
    hidden, bias, gain, shift = extras
    (residual_ref,) = owned
    half = residual_ref.shape[0]
    residual = hidden[piece_rows(flow, k, half), :].astype(jnp.float32) + total + bias[...]
    residual_ref[piece_rows(0, k, half), :] = residual
    return norm_stats(residual)[0] * gain[...] + shift[...]


def finish_branch(flow, k, total, extras, owned, accs):
    residual, cotangent, gain = extras
    (grad_ref,) = owned
    (acc,) = accs
    half = grad_ref.shape[0]
    normed, inverse = norm_stats(residual[piece_rows(0, k, half), :])
    grad = cotangent[piece_rows(flow, k, half), :].astype(jnp.float32)
    grad = grad + norm_back(total, normed, inverse, gain[...])
    grad_ref[piece_rows(0, k, half), :] = grad
    acc[0] += fold(total * normed)
    acc[1] += fold(total)
    acc[2] += fold(grad)
    return grad


def finish_input(flow, k, total, extras, owned, accs):
    hidden, grad, gain = extras
    (acc,) = accs
    half = grad.shape[0]
    normed, inverse = norm_stats(hidden[piece_rows(flow, k, half), :].astype(jnp.float32))
    acc[0] += fold(total * normed)
    acc[1] += fold(total)
    return grad[piece_rows(0, k, half), :] + norm_back(total, normed, inverse, gain[...])


def finish_out(flow, k, total, extras, owned, accs):
    residual, bias = extras
    half = residual.shape[0]
    return residual[piece_rows(0, k, half), :] + total + bias[...]


def small_kernel(stages, shared, own_ref, out_ref, sent, got, send_sem, recv_sem):
    barrier = pltpu.get_barrier_semaphore()

    def partner(axis, bit):
        index = lax.axis_index(axis)
        return {axis: index + bit - 2 * bit * ((index // bit) % 2)}

    for axis, bit in stages:
        pl.semaphore_signal(barrier, inc=1, device_id=partner(axis, bit), device_id_type=MESH)
    pl.semaphore_wait(barrier, len(stages))
    sent[0] = own_ref[...]
    row = lax.broadcasted_iota(jnp.int32, own_ref.shape, 0)
    for number, (axis, bit) in enumerate(stages):
        copy = pltpu.make_async_remote_copy(
            src_ref=sent.at[number],
            dst_ref=got.at[number],
            send_sem=send_sem.at[number],
            recv_sem=recv_sem.at[number],
            device_id=partner(axis, bit),
            device_id_type=MESH,
        )
        copy.start()
        copy.wait()
        total = sent[number] + got[number]
        if axis == "mp":
            total = jnp.where(row < shared, total, sent[number])
        if number + 1 < len(stages):
            sent[number + 1] = total
        else:
            out_ref[...] = total


def small_sum(number, sizes, shared, values):
    stages = tuple(
        (axis, 1 << bit) for axis, size in sizes for bit in range(size.bit_length() - 1)
    )
    steps = len(stages)
    vmem = pl.BlockSpec(memory_space=pltpu.VMEM)
    return pl.pallas_call(
        functools.partial(small_kernel, stages, shared),
        in_specs=[vmem],
        out_specs=vmem,
        out_shape=jax.ShapeDtypeStruct(values.shape, jnp.float32),
        scratch_shapes=[
            pltpu.VMEM((steps, *values.shape), jnp.float32),
            pltpu.VMEM((steps, *values.shape), jnp.float32),
            pltpu.SemaphoreType.DMA((steps,)),
            pltpu.SemaphoreType.DMA((steps,)),
        ],
        compiler_params=pltpu.CompilerParams(collective_id=number, has_side_effects=True),
        name="small_sum",
    )(values)


def body(
    item_count,
    seq_count,
    mp_count,
    hidden_in,
    cotangent,
    seg_lengths,
    pre_gain,
    pre_shift,
    qkv_weight,
    qv_bias,
    out_weight,
    out_bias,
    mid_gain,
    mid_shift,
    up_weight,
    up_bias,
    down_weight,
    down_bias,
):
    group = ("item", "seq")
    width = qkv_weight.shape[2]
    gathered = lambda weight, axis: lax.all_gather(weight, group, axis=axis, tiled=True)
    qkv_full = gathered(qkv_weight.reshape(-1, 3 * width), 0)
    out_full = gathered(out_weight, 1)
    up_full = gathered(up_weight, 0)
    down_full = gathered(down_weight, 1)
    hidden = hidden_in[0].astype(jnp.float32)
    lengths = seg_lengths[0]
    rows = hidden.shape[0]
    first_row = lax.axis_index("seq") * rows
    segment = first_row // SLOT
    facts = jnp.stack(
        [
            first_row % SLOT,
            lengths[segment] + SUMM,
            jnp.where(segment > 0, SUMM, 0),
        ]
    ).astype(jnp.int32)

    normed = (norm_stats(hidden)[0] * pre_gain + pre_shift).astype(jnp.bfloat16)
    q = (mm(normed, qkv_full[:, :width]) + qv_bias[0]).astype(jnp.bfloat16)
    k = mm(normed, qkv_full[:, width : 2 * width]).astype(jnp.bfloat16)
    v = (mm(normed, qkv_full[:, 2 * width :]) + qv_bias[1]).astype(jnp.bfloat16)
    own, summary = keys_for(jnp.stack([k, v]), lengths, seq_count)
    tables = (own[0], own[1], summary[0], summary[1])
    attended, log_total = attend(facts, q, *tables)

    row = lambda vector: vector[None, :]
    mid_low, residual = line_sum(
        1,
        mp_count,
        [attended],
        out_full,
        NN,
        [hidden_in[0], row(out_bias), row(mid_gain), row(mid_shift)],
        1,
        0,
        finish_mid,
        "out_sum",
    )
    activated, slope = gelu_parts(mm(mid_low, up_full) + up_bias)
    act_low = activated.astype(jnp.bfloat16)
    grad_down = cotangent[0]
    grad_pre = (slope * mm(grad_down, down_full, NT)).astype(jnp.bfloat16)
    grad_branch, grad_residual, mid_sums = line_sum(
        2,
        mp_count,
        [grad_pre],
        up_full,
        NT,
        [residual, grad_down, row(mid_gain)],
        1,
        3,
        finish_branch,
        "mid_sum",
    )
    over_rows = lambda left, right: mm(left, right, (((0,), (0,)), ((), ())))
    spread = lambda grad, axis: lax.psum_scatter(
        grad.astype(jnp.bfloat16), group, scatter_dimension=axis, tiled=True
    ).astype(jnp.float32)
    down_grad = spread(over_rows(act_low, grad_down), 1)
    up_grad = spread(over_rows(mid_low, grad_pre), 0)
    out_grad = spread(over_rows(attended, grad_branch), 1)
    grad_attended = mm(grad_branch, out_full, NT).astype(jnp.bfloat16)
    (hidden_out,) = line_sum(
        3,
        mp_count,
        [act_low],
        down_full,
        NN,
        [residual, row(down_bias)],
        0,
        0,
        finish_out,
        "down_sum",
    )

    dq, dk, dv, dks, dvs = attend_back(facts, q, *tables, grad_attended, log_total)
    dk, dv = keys_back(jnp.stack([dk, dv]), jnp.stack([dks, dvs]), rows, lengths, seq_count)
    grad_input, pre_sums = line_sum(
        4,
        mp_count,
        [dq, dk, dv],
        qkv_full,
        NT,
        [hidden_in[0], grad_residual, row(pre_gain)],
        0,
        2,
        finish_input,
        "input_sum",
    )
    qkv_grad = spread(over_rows(normed, jnp.concatenate([dq, dk, dv], axis=1)), 0)
    total = lambda value: jnp.sum(value.astype(jnp.float32), axis=0)
    features = hidden.shape[1]
    qv_sums = jnp.concatenate([total(dq), total(dv)])
    sums = small_sum(
        5,
        [("item", item_count), ("seq", seq_count), ("mp", mp_count)],
        6,
        jnp.concatenate(
            [
                jnp.sum(mid_sums, axis=1),
                jnp.sum(pre_sums, axis=1),
                row(jnp.where(lax.axis_index("mp") == 0, total(grad_down), 0.0)),
                total(grad_pre).reshape(-1, features),
                jnp.pad(qv_sums, (0, -qv_sums.shape[0] % features)).reshape(-1, features),
            ]
        ),
    )
    ff_rows = up_weight.shape[1] // features
    up_bias_grad = sums[6 : 6 + ff_rows].reshape(-1)
    qv_bias_grad = sums[6 + ff_rows :].reshape(-1)[: 2 * width].reshape(2, width)
    return (
        hidden_out[None],
        grad_input.astype(jnp.float32)[None],
        sums[3],
        sums[4],
        qkv_grad.reshape(-1, 3, width),
        qv_bias_grad,
        out_grad,
        sums[2],
        sums[0],
        sums[1],
        up_grad,
        up_bias_grad,
        down_grad,
        sums[5],
    )


def solution(mesh):
    rows = P("item", "seq", None)
    qkv = P(("item", "seq"), None, "mp")
    first = P(("item", "seq"), "mp")
    second = P("mp", ("item", "seq"))
    bias = P(None, "mp")
    return jax.shard_map(
        functools.partial(body, mesh.shape["item"], mesh.shape["seq"], mesh.shape["mp"]),
        mesh=mesh,
        in_specs=(
            rows,
            rows,
            P("item", None),
            P(),
            P(),
            qkv,
            bias,
            second,
            P(),
            P(),
            P(),
            first,
            P("mp"),
            second,
            P(),
        ),
        out_specs=(
            rows,
            rows,
            P(),
            P(),
            qkv,
            bias,
            second,
            P(),
            P(),
            P(),
            first,
            P("mp"),
            second,
            P(),
        ),
        check_vma=False,
    )
```

```python
import functools
import math

import jax
import jax.numpy as jnp
from jax import lax
from jax.experimental import pallas as pl
from jax.experimental.pallas import tpu as pltpu
from jax.sharding import PartitionSpec as P

HDIM = 64
SLOT = 1280
SEGS = 2
SUMM = 50
SUMM_ROWS = 64
TOKENS = 2560
PAIR = 2 * HDIM
PIECE = 32
SKEW = 2
MIB = 1 << 20
MESH = pl.DeviceIdType.MESH
MASKED = -1e30


eps = 1e-05

NN = (((1,), (0,)), ((), ()))
NT = (((1,), (1,)), ((), ()))


def mm(left, right, dims=NN):
    return lax.dot_general(left, right, dims, preferred_element_type=jnp.float32)


def norm_stats(values):
    center = jnp.mean(values, axis=-1, keepdims=True)
    centered = values - center
    inverse = lax.rsqrt(jnp.mean(centered * centered, axis=-1, keepdims=True) + eps)
    return centered * inverse, inverse


def norm_back(grad_out, normed, inverse, gain):
    scaled = grad_out * gain
    centered = scaled - jnp.mean(scaled, axis=-1, keepdims=True)
    return inverse * (centered - normed * jnp.mean(scaled * normed, axis=-1, keepdims=True))


def gelu_parts(values):
    c = math.sqrt(2 / math.pi)
    squared = values * values
    t = jnp.tanh(c * values * (1 + 0.044715 * squared))
    half = 0.5 * (1 + t)
    slope = half + 0.5 * values * (1 - t * t) * (c * (1 + 3 * 0.044715 * squared))
    return values * half, slope


def key_masks(facts_ref, block, rows, bq, nk):
    first = facts_ref[0] + block * bq
    limit = jnp.minimum(
        first + 1 + lax.broadcasted_iota(jnp.int32, (1, bq), 1), facts_ref[1]
    )
    own = lax.broadcasted_iota(jnp.int32, (nk, bq), 0) < limit
    earlier = lax.broadcasted_iota(jnp.int32, (SUMM_ROWS, bq), 0) < facts_ref[2]
    return own, earlier


def head_lanes(head):
    lane = lax.broadcasted_iota(jnp.int32, (1, PAIR), 1)
    return (lane >= head * HDIM) & (lane < (head + 1) * HDIM)


def attend_kernel(bq, causal, facts_ref, q_ref, k_ref, v_ref, ks_ref, vs_ref, o_ref, lse_ref):
    rows, seg = q_ref.shape[0], k_ref.shape[0]
    v_t = v_ref[...].T
    vs_t = vs_ref[...].T
    ks = ks_ref[...]
    low_half = lax.broadcasted_iota(jnp.int32, (PAIR, 1), 0) < HDIM
    for block in range(rows // bq):
        nk = (block + 1) * bq if causal else seg
        own, earlier = key_masks(facts_ref, block, rows, bq, nk)
        q = q_ref[block * bq : (block + 1) * bq, :] * jnp.bfloat16(HDIM**-0.5)
        mixed = []
        for head in range(2):
            qh = jnp.where(head_lanes(head), q, jnp.zeros_like(q))
            s = jnp.where(own, mm(k_ref[:nk, :], qh, NT), MASKED)
            s2 = jnp.where(earlier, mm(ks, qh, NT), MASKED)
            top = jnp.maximum(jnp.max(s, axis=0, keepdims=True), jnp.max(s2, axis=0, keepdims=True))
            p = jnp.exp(s - top)
            p2 = jnp.exp(s2 - top)
            total = jnp.sum(p, axis=0, keepdims=True) + jnp.sum(p2, axis=0, keepdims=True)
            out = mm(v_t[:, :nk], p.astype(jnp.bfloat16)) + mm(vs_t, p2.astype(jnp.bfloat16))
            mixed.append(out / total)
            lse_ref[0, head : head + 1, block * bq : (block + 1) * bq] = top + jnp.log(total)
        joined = jnp.where(low_half, mixed[0], mixed[1])
        o_ref[block * bq : (block + 1) * bq, :] = joined.T.astype(jnp.bfloat16)


def query_block(rows):
    return 256 if rows % 256 == 0 else math.gcd(rows, 160)


def attend(facts, q, k, v, ks, vs):
    rows, width = q.shape
    seg = k.shape[0]
    pairs = width // PAIR
    column = lambda n: pl.BlockSpec((n, PAIR), lambda i: (0, i))
    return pl.pallas_call(
        functools.partial(attend_kernel, query_block(rows), rows == seg),
        grid=(pairs,),
        in_specs=[pl.BlockSpec(memory_space=pltpu.SMEM)]
        + [column(n) for n in (rows, seg, seg, SUMM_ROWS, SUMM_ROWS)],
        out_specs=[column(rows), pl.BlockSpec((1, 2, rows), lambda i: (i, 0, 0))],
        out_shape=[
            jax.ShapeDtypeStruct((rows, width), jnp.bfloat16),
            jax.ShapeDtypeStruct((pairs, 2, rows), jnp.float32),
        ],
        compiler_params=pltpu.CompilerParams(vmem_limit_bytes=48 * MIB),
        cost_estimate=pl.CostEstimate(
            flops=4 * rows * seg * width, bytes_accessed=8 * rows * width, transcendentals=0
        ),
        name="attend",
    )(facts, q, k, v, ks, vs)


def keys_for(local, lengths, seq_count):
    rows, width = local.shape[-2:]
    pad = ((0, 0), (0, SUMM_ROWS - SUMM), (0, 0))
    if rows == SLOT:
        here = lengths[lax.axis_index("seq")]
        summary = jnp.pad(lax.dynamic_slice(local, (0, here, 0), (2, SUMM, width)), pad)
        moves = [(i, i + 1) for i in range(seq_count - 1)]
        return local, lax.ppermute(summary, "seq", moves)
    everything = lax.all_gather(local, "seq", axis=1, tiled=True)
    segment = lax.axis_index("seq") * rows // SLOT
    own = lax.dynamic_slice(everything, (0, segment * SLOT, 0), (2, SLOT, width))
    summary = lax.dynamic_slice(everything, (0, lengths[0], 0), (2, SUMM, width))
    return own, jnp.pad(summary, pad)


def keys_back(own, summary, rows, lengths, seq_count):
    width = own.shape[-1]
    summary = summary[:, :SUMM]
    if rows == SLOT:
        moves = [(i + 1, i) for i in range(seq_count - 1)]
        arrived = lax.ppermute(summary, "seq", moves)
        here = lengths[lax.axis_index("seq")]
        old = lax.dynamic_slice(own, (0, here, 0), (2, SUMM, width))
        new = (old.astype(jnp.float32) + arrived).astype(jnp.bfloat16)
        return lax.dynamic_update_slice(own, new, (0, here, 0))
    segment = lax.axis_index("seq") * rows // SLOT
    everything = jnp.zeros((2, TOKENS, width), jnp.float32)
    everything = lax.dynamic_update_slice(
        everything, own.astype(jnp.float32), (0, segment * SLOT, 0)
    )
    old = lax.dynamic_slice(everything, (0, lengths[0], 0), (2, SUMM, width))
    added = jnp.where(segment > 0, summary, 0.0)
    everything = lax.dynamic_update_slice(everything, old + added, (0, lengths[0], 0))
    return lax.psum_scatter(
        everything.astype(jnp.bfloat16), "seq", scatter_dimension=1, tiled=True
    )


class Line:
    def __init__(self, count, half, multiply, finish, out, part, moving, sems):
        self.count, self.half, self.multiply, self.finish = count, half, multiply, finish
        self.out, self.part, self.moving = out, part, moving
        self.up_sent, self.up_got, self.down_sent, self.down_got, self.local = sems
        self.me = lax.axis_index("mp")
        self.pieces = half // PIECE
        self.per_group = part.shape[2] // PIECE
        self.steps = self.pieces + 2 * SKEW * (count - 1)

    @staticmethod
    def scratch(half, features):
        pieces = half // PIECE
        group = 5 * PIECE if pieces % 5 == 0 else PIECE
        dma = lambda *shape: pltpu.SemaphoreType.DMA(shape)
        return [
            pltpu.VMEM((2, 2, group, features), jnp.float32),
            pltpu.VMEM((2, half, features), jnp.bfloat16),
            dma(2, pieces),
            dma(2, pieces),
            dma(2, pieces),
            dma(2, pieces),
            dma(pieces),
        ]

    def place(self, flow):
        return self.count - 1 - self.me if flow == 0 else self.me

    def greet(self, barrier):
        me = self.me

        @pl.when(me > 0)
        def _():
            pl.semaphore_signal(barrier, inc=1, device_id={"mp": me - 1}, device_id_type=MESH)

        @pl.when(me < self.count - 1)
        def _():
            pl.semaphore_signal(barrier, inc=1, device_id={"mp": me + 1}, device_id_type=MESH)

    def meet(self, barrier, others=0):
        ends = (self.me == 0) | (self.me == self.count - 1)

        @pl.when(ends)
        def _():
            pl.semaphore_wait(barrier, 1 + others)

        @pl.when(jnp.logical_not(ends))
        def _():
            pl.semaphore_wait(barrier, 2 + others)

    def first(self):
        for flow in range(2):
            self.part[flow, 0] = self.multiply(flow, 0)

    def onward(self, flow, k):
        here = self.moving.at[flow, pl.ds(k * PIECE, PIECE)]
        return pltpu.make_async_remote_copy(
            src_ref=here,
            dst_ref=here,
            send_sem=self.up_sent.at[flow, k],
            recv_sem=self.up_got.at[flow, k],
            device_id={"mp": self.me - 1 if flow == 0 else self.me + 1},
            device_id_type=MESH,
        )

    def back(self, flow, k, owner):
        rows = self.out.at[pl.ds(flow * self.half + k * PIECE, PIECE)]
        return pltpu.make_async_remote_copy(
            src_ref=self.moving.at[flow, pl.ds(k * PIECE, PIECE)] if owner else rows,
            dst_ref=rows,
            send_sem=self.down_sent.at[flow, k],
            recv_sem=self.down_got.at[flow, k],
            device_id={"mp": self.me + 1 if flow == 0 else self.me - 1},
            device_id_type=MESH,
        )

    def keep(self, flow, k):
        return pltpu.make_async_copy(
            self.moving.at[flow, pl.ds(k * PIECE, PIECE)],
            self.out.at[pl.ds(flow * self.half + k * PIECE, PIECE)],
            self.local.at[k],
        )

    def step(self, t):
        last = self.count - 1
        for flow in range(2):
            place = self.place(flow)
            k = t - SKEW * place
            here = pl.ds(pl.multiple_of(k * PIECE, PIECE), PIECE)
            busy = (k >= 0) & (k < self.pieces)

            def mine():
                slot = (k // self.per_group) % 2
                inner = pl.ds(pl.multiple_of((k % self.per_group) * PIECE, PIECE), PIECE)
                return self.part[flow, slot, inner, :]

            @pl.when(busy & (place == 0))
            def _():
                self.moving[flow, here, :] = mine().astype(jnp.bfloat16)
                self.onward(flow, k).start()

            @pl.when(busy & (place > 0) & (place < last))
            def _():
                self.onward(flow, k).wait_recv()
                total = mine() + self.moving[flow, here, :].astype(jnp.float32)
                self.moving[flow, here, :] = total.astype(jnp.bfloat16)
                self.onward(flow, k).start()

            @pl.when(busy & (place == last))
            def _():
                self.onward(flow, k).wait_recv()
                total = mine() + self.moving[flow, here, :].astype(jnp.float32)
                self.moving[flow, here, :] = self.finish(flow, k, total).astype(jnp.bfloat16)
                self.back(flow, k, True).start()
                self.keep(flow, k).start()

        for flow in range(2):
            place = self.place(flow)
            j = t - SKEW * (2 * last - place)

            @pl.when((j >= 0) & (j < self.pieces) & (place < last))
            def _():
                self.back(flow, j, False).wait_recv()

                @pl.when(place > 0)
                def _():
                    self.back(flow, j, False).start()

        for flow in range(2):
            k = t - SKEW * self.place(flow)
            g = k // self.per_group + 1

            @pl.when((k >= 0) & (k % self.per_group == 0) & (g < self.pieces // self.per_group))
            def _():
                self.part[flow, g % 2] = self.multiply(flow, g)

    def settle(self):
        def one(k, carry):
            for flow in range(2):
                place = self.place(flow)

                @pl.when(place < self.count - 1)
                def _():
                    self.onward(flow, k).wait_send()

                    @pl.when(place > 0)
                    def _():
                        self.back(flow, k, False).wait_send()

                @pl.when(place == self.count - 1)
                def _():
                    self.back(flow, k, True).wait_send()
                    self.keep(flow, k).wait()

            return carry

        lax.fori_loop(0, self.pieces, one, 0)


def group_product(lefts, right, dims, half, group):
    def multiply(flow, g):
        rows = pl.ds(pl.multiple_of(flow * half + g * group, 16), group)
        at, total = 0, None
        for left in lefts:
            depth = left.shape[1]
            cut = right[:, at : at + depth] if dims == NT else right[at : at + depth, :]
            product = mm(left[rows, :], cut, dims)
            total = product if total is None else total + product
            at += depth
        return total

    return multiply


def line_kernel(count, half, dims, n_left, n_extra, n_owned, n_acc, finish, side, *refs):
    refs = list(refs)
    take = lambda n: [refs.pop(0) for _ in range(n)]
    lefts, (right,), extras, side_in = take(n_left), take(1), take(n_extra), take(side.n_in)
    (out,), owned, accs = take(1), take(n_owned), take(1 if n_acc else 0)
    side_out = take(side.n_out)
    part, moving, sems, side_scratch = *take(2), take(5), refs
    multiply = group_product(lefts, right, dims, half, part.shape[2])
    ending = lambda flow, k, total: finish(flow, k, total, extras, owned, accs)
    line = Line(count, half, multiply, ending, out, part, moving, sems)
    job = side(side_in, side_out, side_scratch)
    barrier = pltpu.get_barrier_semaphore()
    line.greet(barrier)
    job.greet(barrier)
    if n_acc:
        accs[0][...] = jnp.zeros_like(accs[0])
    job.first()
    line.first()
    line.meet(barrier, job.others)

    def step(t, carry):
        line.step(t)
        job.step(t)
        return carry

    lax.fori_loop(0, max(line.steps, job.steps), step, 0)
    line.settle()
    job.settle()


class Nothing:
    n_in = n_out = others = steps = 0
    operands, in_specs, out_shape, out_specs, scratch_shapes = (), (), (), (), ()

    def __call__(self, ins, outs, scratch):
        return self

    def greet(self, barrier):
        pass

    def first(self):
        pass

    def step(self, t):
        pass

    def settle(self):
        pass


VMEM = pl.BlockSpec(memory_space=pltpu.VMEM)
ANY = pl.BlockSpec(memory_space=pl.ANY)
SMEM = pl.BlockSpec(memory_space=pltpu.SMEM)


def line_sum(number, count, lefts, right, dims, extras, n_owned, n_acc, finish, name, side=Nothing()):
    rows = lefts[0].shape[0]
    features = right.shape[1 if dims == NN else 0]
    half = rows // 2
    acc = [jax.ShapeDtypeStruct((n_acc, 8, features), jnp.float32)] if n_acc else []
    return pl.pallas_call(
        functools.partial(
            line_kernel,
            count,
            half,
            dims,
            len(lefts),
            len(extras),
            n_owned,
            n_acc,
            finish,
            side,
        ),
        in_specs=[VMEM] * (len(lefts) + 1 + len(extras)) + list(side.in_specs),
        out_specs=[ANY] + [VMEM] * (n_owned + len(acc)) + list(side.out_specs),
        out_shape=[jax.ShapeDtypeStruct((rows, features), jnp.bfloat16)]
        + [jax.ShapeDtypeStruct((half, features), jnp.float32)] * n_owned
        + acc
        + list(side.out_shape),
        scratch_shapes=Line.scratch(half, features) + list(side.scratch_shapes),
        compiler_params=pltpu.CompilerParams(
            collective_id=number, has_side_effects=True, vmem_limit_bytes=62 * MIB
        ),
        cost_estimate=pl.CostEstimate(
            flops=2 * rows * features * sum(left.shape[1] for left in lefts),
            bytes_accessed=4 * rows * features,
            transcendentals=0,
        ),
        name=name,
    )(*lefts, right, *extras, *side.operands)


def piece_rows(flow, k, half):
    return pl.ds(pl.multiple_of(flow * half + k * PIECE, PIECE), PIECE)


def fold(values):
    return jnp.sum(values.reshape(-1, 8, values.shape[-1]), axis=0)


def finish_mid(flow, k, total, extras, owned, accs):
    hidden, bias, gain, shift = extras
    (residual_ref,) = owned
    half = residual_ref.shape[0]
    residual = hidden[piece_rows(flow, k, half), :].astype(jnp.float32) + total + bias[...]
    residual_ref[piece_rows(0, k, half), :] = residual
    return norm_stats(residual)[0] * gain[...] + shift[...]


def finish_branch(flow, k, total, extras, owned, accs):
    residual, cotangent, gain = extras
    (grad_ref,) = owned
    (acc,) = accs
    half = grad_ref.shape[0]
    normed, inverse = norm_stats(residual[piece_rows(0, k, half), :])
    grad = cotangent[piece_rows(flow, k, half), :].astype(jnp.float32)
    grad = grad + norm_back(total, normed, inverse, gain[...])
    grad_ref[piece_rows(0, k, half), :] = grad
    acc[0] += fold(total * normed)
    acc[1] += fold(total)
    acc[2] += fold(grad)
    return grad


def finish_input(flow, k, total, extras, owned, accs):
    hidden, grad, gain = extras
    (acc,) = accs
    half = grad.shape[0]
    normed, inverse = norm_stats(hidden[piece_rows(flow, k, half), :].astype(jnp.float32))
    acc[0] += fold(total * normed)
    acc[1] += fold(total)
    return grad[piece_rows(0, k, half), :] + norm_back(total, normed, inverse, gain[...])


def finish_out(flow, k, total, extras, owned, accs):
    residual, bias = extras
    half = residual.shape[0]
    return residual[piece_rows(0, k, half), :] + total + bias[...]


class AttendBack(Nothing):
    n_in, n_out = 8, 5

    def __init__(self, facts, q, k, v, ks, vs, do, lse):
        rows, width = q.shape
        seg = k.shape[0]
        self.operands = (facts, q, k, v, ks, vs, do, lse)
        self.in_specs = (SMEM,) + (VMEM,) * 7
        low = lambda n: jax.ShapeDtypeStruct((n, width), jnp.bfloat16)
        wide = lambda n: jax.ShapeDtypeStruct((n, width), jnp.float32)
        self.out_shape = (low(rows), low(seg), low(seg), wide(SUMM_ROWS), wide(SUMM_ROWS))
        self.out_specs = (VMEM,) * 5
        self.scratch_shapes = (
            pltpu.VMEM((seg, PAIR), jnp.float32),
            pltpu.VMEM((seg, PAIR), jnp.float32),
            pltpu.VMEM((PAIR, seg), jnp.bfloat16),
        )
        self.bq = query_block(rows)
        self.blocks = rows // self.bq
        self.pairs = width // PAIR
        self.steps = self.pairs * self.blocks
        self.causal = rows == seg

    def __call__(self, ins, outs, scratch):
        self.ins, self.outs, self.scratch = ins, outs, scratch
        return self

    def step(self, t):
        pair = t // self.blocks
        for block in range(self.blocks):

            @pl.when((t < self.steps) & (t % self.blocks == block))
            def _():
                self.unit(pair, block)

    def unit(self, pair, block):
        facts, q_ref, k_ref, v_ref, ks_ref, vs_ref, do_ref, lse_ref = self.ins
        dq_ref, dk_ref, dv_ref, dks_ref, dvs_ref = self.outs
        dk_acc, dv_acc, k_t = self.scratch
        seg, bq = k_ref.shape[0], self.bq
        cols = pl.ds(pl.multiple_of(pair * PAIR, PAIR), PAIR)
        scale = jnp.bfloat16(HDIM**-0.5)
        low_half = lax.broadcasted_iota(jnp.int32, (PAIR, 1), 0) < HDIM
        if block == 0:
            k_t[...] = (k_ref[:, cols] * scale).T
            dk_acc[...] = jnp.zeros_like(dk_acc)
            dv_acc[...] = jnp.zeros_like(dv_acc)
            dks_ref[:, cols] = jnp.zeros((SUMM_ROWS, PAIR), jnp.float32)
            dvs_ref[:, cols] = jnp.zeros((SUMM_ROWS, PAIR), jnp.float32)
        ks, vs = ks_ref[:, cols], vs_ref[:, cols]
        ks_t = (ks * scale).T
        nk = (block + 1) * bq if self.causal else seg
        here = slice(block * bq, (block + 1) * bq)
        own, earlier = key_masks(facts, block, self.blocks * bq, bq, nk)
        q = q_ref[here, cols] * scale
        do = do_ref[here, cols]
        k, v = k_ref[:nk, cols], v_ref[:nk, cols]
        grads = []
        for head in range(2):
            qh = jnp.where(head_lanes(head), q, jnp.zeros_like(q))
            doh = jnp.where(head_lanes(head), do, jnp.zeros_like(do))
            lse = lse_ref[pair, head : head + 1, here]
            p = jnp.exp(jnp.where(own, mm(k, qh, NT), MASKED) - lse)
            p2 = jnp.exp(jnp.where(earlier, mm(ks, qh, NT), MASKED) - lse)
            dp = mm(v, doh, NT)
            dp2 = mm(vs, doh, NT)
            delta = jnp.sum(p * dp, axis=0, keepdims=True) + jnp.sum(p2 * dp2, axis=0, keepdims=True)
            ds = (p * (dp - delta)).astype(jnp.bfloat16)
            ds2 = (p2 * (dp2 - delta)).astype(jnp.bfloat16)
            dv_acc[:nk, :] += mm(p.astype(jnp.bfloat16), doh)
            dk_acc[:nk, :] += mm(ds, qh)
            dvs_ref[:, cols] += mm(p2.astype(jnp.bfloat16), doh)
            dks_ref[:, cols] += mm(ds2, qh)
            grads.append(mm(k_t[:, :nk], ds) + mm(ks_t, ds2))
        joined = jnp.where(low_half, grads[0], grads[1])
        dq_ref[here, cols] = joined.T.astype(jnp.bfloat16)
        if block == self.blocks - 1:
            dk_ref[:, cols] = dk_acc[...].astype(jnp.bfloat16)
            dv_ref[:, cols] = dv_acc[...].astype(jnp.bfloat16)


class Spread(Nothing):
    others = 3
    n_in, n_out = 10, 4
    block = 256
    lag = (2, 5, 8)

    def __init__(self, factors, columns):
        rows, features = factors[0].shape
        block, half = self.block, self.block // 2
        assert features == 8 * block
        self.rows = rows
        self.operands = tuple(factors) + tuple(right for _, right, _, _ in columns)
        self.in_specs = (ANY,) * self.n_in
        self.table, self.phases = [], {}
        at, widths = 0, [0] * 4
        for number, (left, right, result, place) in enumerate(columns):
            self.phases.setdefault(left, at)
            self.table.append((number, at, at + right.shape[1] // block, result, place))
            at += right.shape[1] // block
            widths[result] += right.shape[1]
        self.chunks = at
        self.steps = at + self.lag[2]
        self.across = (True, False, False, True)
        self.out_shape = tuple(
            jax.ShapeDtypeStruct((block, n) if across else (n, block), jnp.float32)
            for n, across in zip(widths, self.across)
        )
        self.out_specs = (ANY,) * 4
        low = lambda *shape: pltpu.VMEM(shape, jnp.bfloat16)
        wide = lambda *shape: pltpu.VMEM(shape, jnp.float32)
        dma = lambda n: pltpu.SemaphoreType.DMA((n,))
        self.scratch_shapes = (
            low(2, rows, features),
            low(2, rows, block),
            low(3, 2, block, 2 * block),
            wide(3, 2, block, 2 * block),
            low(4, 2, block, 2 * block),
            low(3, half, 2 * block),
            low(3, 2, half, block),
            wide(3, half, 2 * block),
            wide(3, 2, half, block),
            low(6, half, 2 * block),
            low(6, 2, half, block),
            low(3, 2, half, block),
            wide(3, 2, half, block),
            low(6, 2, half, block),
            wide(3, block, block),
            dma(2),
            dma(2),
            dma(3),
            dma(4),
            dma(3),
            dma(6),
            dma(3),
            dma(6),
            dma(3),
            dma(6),
            dma(3),
            dma(6),
            dma(3),
        )

    def __call__(self, ins, outs, scratch):
        self.lefts, self.rights, self.outs = ins[:4], ins[4:], outs
        (
            self.x_buf,
            self.y_buf,
            self.s1,
            self.own,
            self.r1,
            self.s2x,
            self.s2y,
            self.top,
            self.low,
            self.r2x,
            self.r2y,
            self.s3,
            self.kept,
            self.r3,
            self.tile,
            self.x_sem,
            self.y_sem,
            self.s1_sem,
            self.r1_sem,
            self.s2x_sem,
            self.r2x_sem,
            self.s2y_sem,
            self.r2y_sem,
            self.s3y_sem,
            self.r3y_sem,
            self.s3x_sem,
            self.r3x_sem,
            self.out_sem,
        ) = scratch
        item, seq = lax.axis_index("item"), lax.axis_index("seq")
        self.core, self.x, self.y = item % 2, item // 2, seq
        self.to_core = {"item": item + 1 - 2 * self.core}
        self.to_x = {"item": item + 2 - 4 * self.x}
        self.to_y = {"seq": 1 - seq}
        return self

    def greet(self, barrier):
        for to in (self.to_core, self.to_x, self.to_y):
            pl.semaphore_signal(barrier, inc=1, device_id=to, device_id_type=MESH)


    def left_copy(self, left):
        slot = list(self.phases).index(left) % 2
        return pltpu.make_async_copy(self.lefts[left], self.x_buf.at[slot], self.x_sem.at[slot])

    def right_copy(self, m, act):
        for number, start, stop, _, _ in self.table:

            @pl.when((m >= start) & (m < stop))
            def _():
                cols = pl.ds(pl.multiple_of((m - start) * self.block, self.block), self.block)
                act(
                    pltpu.make_async_copy(
                        self.rights[number].at[:, cols], self.y_buf.at[m % 2], self.y_sem.at[m % 2]
                    )
                )

    def out_copy(self, m, act):
        for _, start, stop, result, place in self.table:

            @pl.when((m >= start) & (m < stop))
            def _():
                cols = pl.ds(
                    pl.multiple_of(place + (m - start) * self.block, self.block), self.block
                )
                out = self.outs[result]
                out = out.at[:, cols] if self.across[result] else out.at[cols, :]
                act(pltpu.make_async_copy(self.tile.at[m % 3], out, self.out_sem.at[m % 3]))

    def remote(self, src, dst, send, recv, to):
        return pltpu.make_async_remote_copy(
            src_ref=src, dst_ref=dst, send_sem=send, recv_sem=recv, device_id=to, device_id_type=MESH
        )

    def first_copy(self, m):
        return self.remote(
            self.s1.at[m % 3],
            self.r1.at[m % 4],
            self.s1_sem.at[m % 3],
            self.r1_sem.at[m % 4],
            self.to_core,
        )

    def second_copies(self, m):
        return (
            self.remote(
                self.s2x.at[m % 3],
                self.r2x.at[m % 6],
                self.s2x_sem.at[m % 3],
                self.r2x_sem.at[m % 6],
                self.to_x,
            ),
            self.remote(
                self.s2y.at[m % 3],
                self.r2y.at[m % 6],
                self.s2y_sem.at[m % 3],
                self.r2y_sem.at[m % 6],
                self.to_y,
            ),
        )

    def third_copies(self, m):
        return (
            self.remote(
                self.s3.at[m % 3, 0],
                self.r3.at[m % 6, 0],
                self.s3y_sem.at[m % 3],
                self.r3y_sem.at[m % 6],
                self.to_y,
            ),
            self.remote(
                self.s3.at[m % 3, 1],
                self.r3.at[m % 6, 1],
                self.s3x_sem.at[m % 3],
                self.r3x_sem.at[m % 6],
                self.to_x,
            ),
        )

    def first(self):
        for left in list(self.phases)[:2]:
            self.left_copy(left).start()
        self.right_copy(0, lambda copy: copy.start())

    def step(self, t):
        for stage, lag in ((self.fourth, 8), (self.third, 5), (self.second, 2), (self.multiply, 0)):
            m = t - lag

            @pl.when((m >= 0) & (m < self.chunks))
            def _():
                stage(m)

    def multiply(self, m):
        order = list(self.phases)
        for number, left in enumerate(order):

            @pl.when(m == self.phases[left])
            def _():
                self.left_copy(left).wait()
                if 1 <= number < len(order) - 1:
                    self.left_copy(order[number + 1]).start()

        @pl.when(m + 1 < self.chunks)
        def _():
            self.right_copy(m + 1, lambda copy: copy.start())

        self.right_copy(m, lambda copy: copy.wait())

        @pl.when(m >= 3)
        def _():
            self.first_copy(m - 3).wait_send()

        phase = sum((m >= start).astype(jnp.int32) for start in self.phases.values()) - 1
        turned = self.y_buf[m % 2].T
        wide = 2 * self.block

        def product(x, core):
            cols = pl.ds(pl.multiple_of(x * 2 * wide + core * wide, wide), wide)
            return mm(turned, self.x_buf[phase % 2, :, cols])

        for x in range(2):
            self.s1[m % 3, x] = product(x, 1 - self.core).astype(jnp.bfloat16)
        self.first_copy(m).start()
        for x in range(2):
            self.own[m % 3, x] = product(x, self.core)

    def second(self, m):
        half = self.block // 2

        @pl.when(m >= 3)
        def _():
            for copy in self.second_copies(m - 3):
                copy.wait_send()

        self.first_copy(m).wait_recv()
        slot = m % 3
        here, there = self.x, 1 - self.x
        mine = pl.ds(pl.multiple_of(self.y * self.block, self.block), self.block)
        others = pl.ds(pl.multiple_of((1 - self.y) * self.block, self.block), self.block)
        added = lambda x, rows, cols: (
            self.own[slot, x, rows, cols] + self.r1[m % 4, x, rows, cols].astype(jnp.float32)
        )
        upper, lower, every = pl.ds(0, half), pl.ds(half, half), pl.ds(0, 2 * self.block)
        self.s2x[slot] = added(there, upper, every).astype(jnp.bfloat16)
        for x in range(2):
            self.s2y[slot, x] = added(x, lower, others).astype(jnp.bfloat16)
        for copy in self.second_copies(m):
            copy.start()
        self.top[slot] = added(here, upper, every)
        for x in range(2):
            self.low[slot, x] = added(x, lower, mine)

    def third(self, m):
        @pl.when(m >= 3)
        def _():
            for copy in self.third_copies(m - 3):
                copy.wait_send()

        for copy in self.second_copies(m):
            copy.wait_recv()
        slot, got = m % 3, m % 6
        mine = pl.ds(pl.multiple_of(self.y * self.block, self.block), self.block)
        others = pl.ds(pl.multiple_of((1 - self.y) * self.block, self.block), self.block)
        top = lambda cols: self.top[slot, :, cols] + self.r2x[got, :, cols].astype(jnp.float32)
        low = lambda x: self.low[slot, x] + self.r2y[got, x].astype(jnp.float32)
        self.s3[slot, 0] = top(others).astype(jnp.bfloat16)
        self.s3[slot, 1] = low(1 - self.x).astype(jnp.bfloat16)
        for copy in self.third_copies(m):
            copy.start()
        self.kept[slot, 0] = top(mine)
        self.kept[slot, 1] = low(self.x)

    def fourth(self, m):
        @pl.when(m >= 3)
        def _():
            self.out_copy(m - 3, lambda copy: copy.wait())

        for copy in self.third_copies(m):
            copy.wait_recv()
        slot, half = m % 3, self.block // 2
        total = self.kept[slot] + self.r3[m % 6].astype(jnp.float32)
        total = total.reshape(self.block, self.block)
        across = jnp.zeros((), jnp.bool_)
        for _, start, stop, result, _ in self.table:
            if self.across[result]:
                across = across | ((m >= start) & (m < stop))

        @pl.when(across)
        def _():
            self.tile[slot] = total.T

        @pl.when(jnp.logical_not(across))
        def _():
            self.tile[slot] = total

        self.out_copy(m, lambda copy: copy.start())

    def settle(self):
        for m in range(self.chunks - 3, self.chunks):
            self.first_copy(m).wait_send()
            for copy in self.second_copies(m) + self.third_copies(m):
                copy.wait_send()
            self.out_copy(jnp.int32(m), lambda copy: copy.wait())


def small_kernel(stages, shared, own_ref, out_ref, sent, got, send_sem, recv_sem):
    barrier = pltpu.get_barrier_semaphore()

    def partner(axis, bit):
        index = lax.axis_index(axis)
        return {axis: index + bit - 2 * bit * ((index // bit) % 2)}

    for axis, bit in stages:
        pl.semaphore_signal(barrier, inc=1, device_id=partner(axis, bit), device_id_type=MESH)
    pl.semaphore_wait(barrier, len(stages))
    sent[0] = own_ref[...]
    row = lax.broadcasted_iota(jnp.int32, own_ref.shape, 0)
    for number, (axis, bit) in enumerate(stages):
        copy = pltpu.make_async_remote_copy(
            src_ref=sent.at[number],
            dst_ref=got.at[number],
            send_sem=send_sem.at[number],
            recv_sem=recv_sem.at[number],
            device_id=partner(axis, bit),
            device_id_type=MESH,
        )
        copy.start()
        copy.wait()
        total = sent[number] + got[number]
        if axis == "mp":
            total = jnp.where(row < shared, total, sent[number])
        if number + 1 < len(stages):
            sent[number + 1] = total
        else:
            out_ref[...] = total


def small_sum(number, sizes, shared, values):
    stages = tuple(
        (axis, 1 << bit) for axis, size in sizes for bit in range(size.bit_length() - 1)
    )
    steps = len(stages)
    vmem = pl.BlockSpec(memory_space=pltpu.VMEM)
    return pl.pallas_call(
        functools.partial(small_kernel, stages, shared),
        in_specs=[vmem],
        out_specs=vmem,
        out_shape=jax.ShapeDtypeStruct(values.shape, jnp.float32),
        scratch_shapes=[
            pltpu.VMEM((steps, *values.shape), jnp.float32),
            pltpu.VMEM((steps, *values.shape), jnp.float32),
            pltpu.SemaphoreType.DMA((steps,)),
            pltpu.SemaphoreType.DMA((steps,)),
        ],
        compiler_params=pltpu.CompilerParams(collective_id=number, has_side_effects=True),
        name="small_sum",
    )(values)


def gradients_over(group, lefts, columns):
    over_rows = lambda left, right: mm(left, right, (((0,), (0,)), ((), ()))).astype(jnp.bfloat16)
    parts = [[] for _ in range(4)]
    for left, right, result, _ in columns:
        across = result in (0, 3)
        product = over_rows(lefts[left], right) if across else over_rows(right, lefts[left])
        parts[result].append(product)
    return [
        lax.psum_scatter(
            jnp.concatenate(part, axis=1),
            group,
            scatter_dimension=0 if result in (0, 3) else 1,
            tiled=True,
        ).astype(jnp.float32)
        for result, part in enumerate(parts)
    ]


def body(
    item_count,
    seq_count,
    mp_count,
    hidden_in,
    cotangent,
    seg_lengths,
    pre_gain,
    pre_shift,
    qkv_weight,
    qv_bias,
    out_weight,
    out_bias,
    mid_gain,
    mid_shift,
    up_weight,
    up_bias,
    down_weight,
    down_bias,
):
    group = ("item", "seq")
    width = qkv_weight.shape[2]
    gathered = lambda weight, axis: lax.all_gather(weight, group, axis=axis, tiled=True)
    qkv_full = gathered(qkv_weight.reshape(-1, 3 * width), 0)
    out_full = gathered(out_weight, 1)
    up_full = gathered(up_weight, 0)
    down_full = gathered(down_weight, 1)
    hidden = hidden_in[0].astype(jnp.float32)
    lengths = seg_lengths[0]
    rows = hidden.shape[0]
    first_row = lax.axis_index("seq") * rows
    segment = first_row // SLOT
    facts = jnp.stack(
        [
            first_row % SLOT,
            lengths[segment] + SUMM,
            jnp.where(segment > 0, SUMM, 0),
        ]
    ).astype(jnp.int32)

    normed = (norm_stats(hidden)[0] * pre_gain + pre_shift).astype(jnp.bfloat16)
    q = (mm(normed, qkv_full[:, :width]) + qv_bias[0]).astype(jnp.bfloat16)
    k = mm(normed, qkv_full[:, width : 2 * width]).astype(jnp.bfloat16)
    v = (mm(normed, qkv_full[:, 2 * width :]) + qv_bias[1]).astype(jnp.bfloat16)
    own, summary = keys_for(jnp.stack([k, v]), lengths, seq_count)
    tables = (own[0], own[1], summary[0], summary[1])
    attended, log_total = attend(facts, q, *tables)

    row = lambda vector: vector[None, :]
    mid_low, residual = line_sum(
        1,
        mp_count,
        [attended],
        out_full,
        NN,
        [hidden_in[0], row(out_bias), row(mid_gain), row(mid_shift)],
        1,
        0,
        finish_mid,
        "out_sum",
    )
    activated, slope = gelu_parts(mm(mid_low, up_full) + up_bias)
    act_low = activated.astype(jnp.bfloat16)
    grad_down = cotangent[0]
    grad_pre = (slope * mm(grad_down, down_full, NT)).astype(jnp.bfloat16)
    grad_branch, grad_residual, mid_sums = line_sum(
        2,
        mp_count,
        [grad_pre],
        up_full,
        NT,
        [residual, grad_down, row(mid_gain)],
        1,
        3,
        finish_branch,
        "mid_sum",
    )
    grad_attended = mm(grad_branch, out_full, NT).astype(jnp.bfloat16)
    hidden_out, dq, dk, dv, dks, dvs = line_sum(
        3,
        mp_count,
        [act_low],
        down_full,
        NN,
        [residual, row(down_bias)],
        0,
        0,
        finish_out,
        "down_sum",
        AttendBack(facts, q, *tables, grad_attended, log_total),
    )
    dk, dv = keys_back(jnp.stack([dk, dv]), jnp.stack([dks, dvs]), rows, lengths, seq_count)
    lefts = (mid_low, grad_down, grad_branch, normed)
    columns = (
        (0, grad_pre, 0, 0),
        (1, act_low, 1, 0),
        (2, attended, 2, 0),
        (3, dq, 3, 0),
        (3, dk, 3, width),
        (3, dv, 3, 2 * width),
    )
    spread = Nothing()
    if (item_count, seq_count) == (4, 2):
        spread = Spread(lefts, columns)
    grad_input, pre_sums, *weight_grads = line_sum(
        4,
        mp_count,
        [dq, dk, dv],
        qkv_full,
        NT,
        [hidden_in[0], grad_residual, row(pre_gain)],
        0,
        2,
        finish_input,
        "input_sum",
        spread,
    )
    if not weight_grads:
        weight_grads = gradients_over(group, lefts, columns)
    up_grad, down_grad, out_grad, qkv_grad = weight_grads
    total = lambda value: jnp.sum(value.astype(jnp.float32), axis=0)
    features = hidden.shape[1]
    qv_sums = jnp.concatenate([total(dq), total(dv)])
    sums = small_sum(
        5,
        [("item", item_count), ("seq", seq_count), ("mp", mp_count)],
        6,
        jnp.concatenate(
            [
                jnp.sum(mid_sums, axis=1),
                jnp.sum(pre_sums, axis=1),
                row(jnp.where(lax.axis_index("mp") == 0, total(grad_down), 0.0)),
                total(grad_pre).reshape(-1, features),
                jnp.pad(qv_sums, (0, -qv_sums.shape[0] % features)).reshape(-1, features),
            ]
        ),
    )
    ff_rows = up_weight.shape[1] // features
    up_bias_grad = sums[6 : 6 + ff_rows].reshape(-1)
    qv_bias_grad = sums[6 + ff_rows :].reshape(-1)[: 2 * width].reshape(2, width)
    return (
        hidden_out[None],
        grad_input.astype(jnp.float32)[None],
        sums[3],
        sums[4],
        qkv_grad.reshape(-1, 3, width),
        qv_bias_grad,
        out_grad,
        sums[2],
        sums[0],
        sums[1],
        up_grad,
        up_bias_grad,
        down_grad,
        sums[5],
    )


def solution(mesh):
    rows = P("item", "seq", None)
    qkv = P(("item", "seq"), None, "mp")
    first = P(("item", "seq"), "mp")
    second = P("mp", ("item", "seq"))
    bias = P(None, "mp")
    return jax.shard_map(
        functools.partial(body, mesh.shape["item"], mesh.shape["seq"], mesh.shape["mp"]),
        mesh=mesh,
        in_specs=(
            rows,
            rows,
            P("item", None),
            P(),
            P(),
            qkv,
            bias,
            second,
            P(),
            P(),
            P(),
            first,
            P("mp"),
            second,
            P(),
        ),
        out_specs=(
            rows,
            rows,
            P(),
            P(),
            qkv,
            bias,
            second,
            P(),
            P(),
            P(),
            first,
            P("mp"),
            second,
            P(),
        ),
        check_vma=False,
    )
```

```python
import functools
import math

import jax
import jax.numpy as jnp
from jax import lax
from jax.experimental import pallas as pl
from jax.experimental.pallas import tpu as pltpu
from jax.sharding import PartitionSpec as P

HDIM = 64
SLOT = 1280
SEGS = 2
SUMM = 50
SUMM_ROWS = 64
TOKENS = 2560
PAIR = 2 * HDIM
PIECE = 32
SKEW = 2
SECOND_STREAM = 19
WEIGHTS_READY = 16
MIB = 1 << 20
MESH = pl.DeviceIdType.MESH
MASKED = -1e30


eps = 1e-05

NN = (((1,), (0,)), ((), ()))
NT = (((1,), (1,)), ((), ()))


def mm(left, right, dims=NN):
    return lax.dot_general(left, right, dims, preferred_element_type=jnp.float32)


def norm_stats(values):
    center = jnp.mean(values, axis=-1, keepdims=True)
    centered = values - center
    inverse = lax.rsqrt(jnp.mean(centered * centered, axis=-1, keepdims=True) + eps)
    return centered * inverse, inverse


def norm_back(grad_out, normed, inverse, gain):
    scaled = grad_out * gain
    centered = scaled - jnp.mean(scaled, axis=-1, keepdims=True)
    return inverse * (centered - normed * jnp.mean(scaled * normed, axis=-1, keepdims=True))


def gelu_parts(values):
    c = math.sqrt(2 / math.pi)
    squared = values * values
    t = jnp.tanh(c * values * (1 + 0.044715 * squared))
    half = 0.5 * (1 + t)
    slope = half + 0.5 * values * (1 - t * t) * (c * (1 + 3 * 0.044715 * squared))
    return values * half, slope


def key_masks(facts_ref, block, rows, bq, nk):
    first = facts_ref[0] + block * bq
    limit = jnp.minimum(
        first + 1 + lax.broadcasted_iota(jnp.int32, (1, bq), 1), facts_ref[1]
    )
    own = lax.broadcasted_iota(jnp.int32, (nk, bq), 0) < limit
    earlier = lax.broadcasted_iota(jnp.int32, (SUMM_ROWS, bq), 0) < facts_ref[2]
    return own, earlier


def head_lanes(head):
    lane = lax.broadcasted_iota(jnp.int32, (1, PAIR), 1)
    return (lane >= head * HDIM) & (lane < (head + 1) * HDIM)


def attend_kernel(bq, causal, facts_ref, q_ref, k_ref, v_ref, ks_ref, vs_ref, o_ref, lse_ref):
    rows, seg = q_ref.shape[0], k_ref.shape[0]
    v_t = v_ref[...].T
    vs_t = vs_ref[...].T
    ks = ks_ref[...]
    low_half = lax.broadcasted_iota(jnp.int32, (PAIR, 1), 0) < HDIM
    for block in range(rows // bq):
        nk = (block + 1) * bq if causal else seg
        own, earlier = key_masks(facts_ref, block, rows, bq, nk)
        q = q_ref[block * bq : (block + 1) * bq, :] * jnp.bfloat16(HDIM**-0.5)
        mixed = []
        for head in range(2):
            qh = jnp.where(head_lanes(head), q, jnp.zeros_like(q))
            s = jnp.where(own, mm(k_ref[:nk, :], qh, NT), MASKED)
            s2 = jnp.where(earlier, mm(ks, qh, NT), MASKED)
            top = jnp.maximum(jnp.max(s, axis=0, keepdims=True), jnp.max(s2, axis=0, keepdims=True))
            p = jnp.exp(s - top)
            p2 = jnp.exp(s2 - top)
            total = jnp.sum(p, axis=0, keepdims=True) + jnp.sum(p2, axis=0, keepdims=True)
            out = mm(v_t[:, :nk], p.astype(jnp.bfloat16)) + mm(vs_t, p2.astype(jnp.bfloat16))
            mixed.append(out / total)
            lse_ref[0, head : head + 1, block * bq : (block + 1) * bq] = top + jnp.log(total)
        joined = jnp.where(low_half, mixed[0], mixed[1])
        o_ref[block * bq : (block + 1) * bq, :] = joined.T.astype(jnp.bfloat16)


def query_block(rows):
    return 256 if rows % 256 == 0 else math.gcd(rows, 160)


def attend(facts, q, k, v, ks, vs):
    rows, width = q.shape
    seg = k.shape[0]
    pairs = width // PAIR
    column = lambda n: pl.BlockSpec((n, PAIR), lambda i: (0, i))
    return pl.pallas_call(
        functools.partial(attend_kernel, query_block(rows), rows == seg),
        grid=(pairs,),
        in_specs=[pl.BlockSpec(memory_space=pltpu.SMEM)]
        + [column(n) for n in (rows, seg, seg, SUMM_ROWS, SUMM_ROWS)],
        out_specs=[column(rows), pl.BlockSpec((1, 2, rows), lambda i: (i, 0, 0))],
        out_shape=[
            jax.ShapeDtypeStruct((rows, width), jnp.bfloat16),
            jax.ShapeDtypeStruct((pairs, 2, rows), jnp.float32),
        ],
        compiler_params=pltpu.CompilerParams(vmem_limit_bytes=48 * MIB),
        cost_estimate=pl.CostEstimate(
            flops=4 * rows * seg * width, bytes_accessed=8 * rows * width, transcendentals=0
        ),
        name="attend",
    )(facts, q, k, v, ks, vs)


def keys_for(local, lengths, seq_count):
    rows, width = local.shape[-2:]
    pad = ((0, 0), (0, SUMM_ROWS - SUMM), (0, 0))
    if rows == SLOT:
        here = lengths[lax.axis_index("seq")]
        summary = jnp.pad(lax.dynamic_slice(local, (0, here, 0), (2, SUMM, width)), pad)
        moves = [(i, i + 1) for i in range(seq_count - 1)]
        return local, lax.ppermute(summary, "seq", moves)
    everything = lax.all_gather(local, "seq", axis=1, tiled=True)
    segment = lax.axis_index("seq") * rows // SLOT
    own = lax.dynamic_slice(everything, (0, segment * SLOT, 0), (2, SLOT, width))
    summary = lax.dynamic_slice(everything, (0, lengths[0], 0), (2, SUMM, width))
    return own, jnp.pad(summary, pad)


def keys_back(own, summary, rows, lengths, seq_count):
    width = own.shape[-1]
    summary = summary[:, :SUMM]
    if rows == SLOT:
        moves = [(i + 1, i) for i in range(seq_count - 1)]
        arrived = lax.ppermute(summary, "seq", moves)
        here = lengths[lax.axis_index("seq")]
        old = lax.dynamic_slice(own, (0, here, 0), (2, SUMM, width))
        new = (old.astype(jnp.float32) + arrived).astype(jnp.bfloat16)
        return lax.dynamic_update_slice(own, new, (0, here, 0))
    segment = lax.axis_index("seq") * rows // SLOT
    everything = jnp.zeros((2, TOKENS, width), jnp.float32)
    everything = lax.dynamic_update_slice(
        everything, own.astype(jnp.float32), (0, segment * SLOT, 0)
    )
    old = lax.dynamic_slice(everything, (0, lengths[0], 0), (2, SUMM, width))
    added = jnp.where(segment > 0, summary, 0.0)
    everything = lax.dynamic_update_slice(everything, old + added, (0, lengths[0], 0))
    return lax.psum_scatter(
        everything.astype(jnp.bfloat16), "seq", scatter_dimension=1, tiled=True
    )


class Line:
    def __init__(self, count, half, multiply, finish, out, part, moving, sems):
        self.count, self.half, self.multiply, self.finish = count, half, multiply, finish
        self.out, self.part, self.moving = out, part, moving
        self.up_sent, self.up_got, self.down_sent, self.down_got, self.local = sems
        self.me = lax.axis_index("mp")
        self.pieces = half // PIECE
        self.per_group = part.shape[2] // PIECE
        self.steps = self.pieces + 2 * SKEW * (count - 1)

    @staticmethod
    def scratch(half, features):
        pieces = half // PIECE
        group = 5 * PIECE if pieces % 5 == 0 else PIECE
        dma = lambda *shape: pltpu.SemaphoreType.DMA(shape)
        return [
            pltpu.VMEM((2, 2, group, features), jnp.float32),
            pltpu.VMEM((2, half, features), jnp.bfloat16),
            dma(2, pieces),
            dma(2, pieces),
            dma(2, pieces),
            dma(2, pieces),
            dma(pieces),
        ]

    def place(self, flow):
        return self.count - 1 - self.me if flow == 0 else self.me

    def greet(self, barrier):
        me = self.me

        @pl.when(me > 0)
        def _():
            pl.semaphore_signal(barrier, inc=1, device_id={"mp": me - 1}, device_id_type=MESH)

        @pl.when(me < self.count - 1)
        def _():
            pl.semaphore_signal(barrier, inc=1, device_id={"mp": me + 1}, device_id_type=MESH)

    def meet(self, barrier, others=0):
        ends = (self.me == 0) | (self.me == self.count - 1)

        @pl.when(ends)
        def _():
            pl.semaphore_wait(barrier, 1 + others)

        @pl.when(jnp.logical_not(ends))
        def _():
            pl.semaphore_wait(barrier, 2 + others)

    def first(self):
        for flow in range(2):
            self.part[flow, 0] = self.multiply(flow, 0)

    def onward(self, flow, k):
        here = self.moving.at[flow, pl.ds(k * PIECE, PIECE)]
        return pltpu.make_async_remote_copy(
            src_ref=here,
            dst_ref=here,
            send_sem=self.up_sent.at[flow, k],
            recv_sem=self.up_got.at[flow, k],
            device_id={"mp": self.me - 1 if flow == 0 else self.me + 1},
            device_id_type=MESH,
        )

    def back(self, flow, k, owner):
        rows = self.out.at[pl.ds(flow * self.half + k * PIECE, PIECE)]
        return pltpu.make_async_remote_copy(
            src_ref=self.moving.at[flow, pl.ds(k * PIECE, PIECE)] if owner else rows,
            dst_ref=rows,
            send_sem=self.down_sent.at[flow, k],
            recv_sem=self.down_got.at[flow, k],
            device_id={"mp": self.me + 1 if flow == 0 else self.me - 1},
            device_id_type=MESH,
        )

    def keep(self, flow, k):
        return pltpu.make_async_copy(
            self.moving.at[flow, pl.ds(k * PIECE, PIECE)],
            self.out.at[pl.ds(flow * self.half + k * PIECE, PIECE)],
            self.local.at[k],
        )

    def step(self, t):
        last = self.count - 1
        for flow in range(2):
            place = self.place(flow)
            k = t - SKEW * place
            here = pl.ds(pl.multiple_of(k * PIECE, PIECE), PIECE)
            busy = (k >= 0) & (k < self.pieces)

            def mine():
                slot = (k // self.per_group) % 2
                inner = pl.ds(pl.multiple_of((k % self.per_group) * PIECE, PIECE), PIECE)
                return self.part[flow, slot, inner, :]

            @pl.when(busy & (place == 0))
            def _():
                self.moving[flow, here, :] = mine().astype(jnp.bfloat16)
                self.onward(flow, k).start()

            @pl.when(busy & (place > 0) & (place < last))
            def _():
                self.onward(flow, k).wait_recv()
                total = mine() + self.moving[flow, here, :].astype(jnp.float32)
                self.moving[flow, here, :] = total.astype(jnp.bfloat16)
                self.onward(flow, k).start()

            @pl.when(busy & (place == last))
            def _():
                self.onward(flow, k).wait_recv()
                total = mine() + self.moving[flow, here, :].astype(jnp.float32)
                self.moving[flow, here, :] = self.finish(flow, k, total).astype(jnp.bfloat16)
                self.back(flow, k, True).start()
                self.keep(flow, k).start()

        for flow in range(2):
            place = self.place(flow)
            j = t - SKEW * (2 * last - place)

            @pl.when((j >= 0) & (j < self.pieces) & (place < last))
            def _():
                self.back(flow, j, False).wait_recv()

                @pl.when(place > 0)
                def _():
                    self.back(flow, j, False).start()

        for flow in range(2 if self.multiply else 0):
            k = t - SKEW * self.place(flow)
            g = k // self.per_group + 1

            @pl.when((k >= 0) & (k % self.per_group == 0) & (g < self.pieces // self.per_group))
            def _():
                self.part[flow, g % 2] = self.multiply(flow, g)

    def settle(self):
        def one(k, carry):
            for flow in range(2):
                place = self.place(flow)

                @pl.when(place < self.count - 1)
                def _():
                    self.onward(flow, k).wait_send()

                    @pl.when(place > 0)
                    def _():
                        self.back(flow, k, False).wait_send()

                @pl.when(place == self.count - 1)
                def _():
                    self.back(flow, k, True).wait_send()
                    self.keep(flow, k).wait()

            return carry

        lax.fori_loop(0, self.pieces, one, 0)


def group_product(lefts, right, dims, half, group):
    def multiply(flow, g):
        rows = pl.ds(pl.multiple_of(flow * half + g * group, 16), group)
        at, total = 0, None
        for left in lefts:
            depth = left.shape[1]
            cut = right[:, at : at + depth] if dims == NT else right[at : at + depth, :]
            product = mm(left[rows, :], cut, dims)
            total = product if total is None else total + product
            at += depth
        return total

    return multiply


def line_kernel(count, half, dims, n_left, n_extra, n_owned, n_acc, finish, side, *refs):
    refs = list(refs)
    take = lambda n: [refs.pop(0) for _ in range(n)]
    lefts, (right,), extras, side_in = take(n_left), take(1), take(n_extra), take(side.n_in)
    (out,), owned, accs = take(1), take(n_owned), take(1 if n_acc else 0)
    side_out = take(side.n_out)
    part, moving, sems, side_scratch = *take(2), take(5), refs
    multiply = group_product(lefts, right, dims, half, part.shape[2])
    ending = lambda flow, k, total: finish(flow, k, total, extras, owned, accs)
    line = Line(count, half, multiply, ending, out, part, moving, sems)
    job = side(side_in, side_out, side_scratch)
    barrier = pltpu.get_barrier_semaphore()
    line.greet(barrier)
    job.greet(barrier)
    if n_acc:
        accs[0][...] = jnp.zeros_like(accs[0])
    job.first()
    line.first()
    line.meet(barrier, job.others)

    def step(t, carry):
        line.step(t)
        job.step(t)
        return carry

    lax.fori_loop(0, max(line.steps, job.steps), step, 0)
    line.settle()
    job.settle()


class Nothing:
    n_in = n_out = others = steps = 0
    operands, in_specs, out_shape, out_specs, scratch_shapes = (), (), (), (), ()

    def __call__(self, ins, outs, scratch):
        return self

    def greet(self, barrier):
        pass

    def first(self):
        pass

    def step(self, t):
        pass

    def settle(self):
        pass


VMEM = pl.BlockSpec(memory_space=pltpu.VMEM)
ANY = pl.BlockSpec(memory_space=pl.ANY)
SMEM = pl.BlockSpec(memory_space=pltpu.SMEM)


def line_sum(number, count, lefts, right, dims, extras, n_owned, n_acc, finish, name, side=Nothing()):
    rows = lefts[0].shape[0]
    features = right.shape[1 if dims == NN else 0]
    half = rows // 2
    acc = [jax.ShapeDtypeStruct((n_acc, 8, features), jnp.float32)] if n_acc else []
    return pl.pallas_call(
        functools.partial(
            line_kernel,
            count,
            half,
            dims,
            len(lefts),
            len(extras),
            n_owned,
            n_acc,
            finish,
            side,
        ),
        in_specs=[VMEM] * (len(lefts) + 1 + len(extras)) + list(side.in_specs),
        out_specs=[ANY] + [VMEM] * (n_owned + len(acc)) + list(side.out_specs),
        out_shape=[jax.ShapeDtypeStruct((rows, features), jnp.bfloat16)]
        + [jax.ShapeDtypeStruct((half, features), jnp.float32)] * n_owned
        + acc
        + list(side.out_shape),
        scratch_shapes=Line.scratch(half, features) + list(side.scratch_shapes),
        compiler_params=pltpu.CompilerParams(
            collective_id=number, has_side_effects=True, vmem_limit_bytes=62 * MIB
        ),
        cost_estimate=pl.CostEstimate(
            flops=2 * rows * features * sum(left.shape[1] for left in lefts),
            bytes_accessed=4 * rows * features,
            transcendentals=0,
        ),
        name=name,
    )(*lefts, right, *extras, *side.operands)


def piece_rows(flow, k, half):
    return pl.ds(pl.multiple_of(flow * half + k * PIECE, PIECE), PIECE)


def fold(values):
    return jnp.sum(values.reshape(-1, 8, values.shape[-1]), axis=0)


def finish_input(flow, k, total, extras, owned, accs):
    hidden, grad, gain = extras
    (acc,) = accs
    half = grad.shape[0]
    normed, inverse = norm_stats(hidden[piece_rows(flow, k, half), :].astype(jnp.float32))
    acc[0] += fold(total * normed)
    acc[1] += fold(total)
    return grad[piece_rows(0, k, half), :] + norm_back(total, normed, inverse, gain[...])


def finish_out(flow, k, total, extras, owned, accs):
    residual, bias = extras
    half = residual.shape[0]
    return residual[piece_rows(0, k, half), :] + total + bias[...]


class AttendBack(Nothing):
    n_in, n_out = 8, 5

    def __init__(self, facts, q, k, v, ks, vs, do, lse):
        rows, width = q.shape
        seg = k.shape[0]
        self.operands = (facts, q, k, v, ks, vs, do, lse)
        self.in_specs = (SMEM,) + (VMEM,) * 7
        low = lambda n: jax.ShapeDtypeStruct((n, width), jnp.bfloat16)
        wide = lambda n: jax.ShapeDtypeStruct((n, width), jnp.float32)
        self.out_shape = (low(rows), low(seg), low(seg), wide(SUMM_ROWS), wide(SUMM_ROWS))
        self.out_specs = (VMEM,) * 5
        self.scratch_shapes = (
            pltpu.VMEM((seg, PAIR), jnp.float32),
            pltpu.VMEM((seg, PAIR), jnp.float32),
            pltpu.VMEM((PAIR, seg), jnp.bfloat16),
        )
        self.bq = query_block(rows)
        self.blocks = rows // self.bq
        self.pairs = width // PAIR
        self.steps = self.pairs * self.blocks
        self.causal = rows == seg

    def __call__(self, ins, outs, scratch):
        self.ins, self.outs, self.scratch = ins, outs, scratch
        return self

    def step(self, t):
        pair = t // self.blocks
        for block in range(self.blocks):

            @pl.when((t < self.steps) & (t % self.blocks == block))
            def _():
                self.unit(pair, block)

    def unit(self, pair, block):
        facts, q_ref, k_ref, v_ref, ks_ref, vs_ref, do_ref, lse_ref = self.ins
        dq_ref, dk_ref, dv_ref, dks_ref, dvs_ref = self.outs
        dk_acc, dv_acc, k_t = self.scratch
        seg, bq = k_ref.shape[0], self.bq
        cols = pl.ds(pl.multiple_of(pair * PAIR, PAIR), PAIR)
        scale = jnp.bfloat16(HDIM**-0.5)
        low_half = lax.broadcasted_iota(jnp.int32, (PAIR, 1), 0) < HDIM
        if block == 0:
            k_t[...] = (k_ref[:, cols] * scale).T
            dk_acc[...] = jnp.zeros_like(dk_acc)
            dv_acc[...] = jnp.zeros_like(dv_acc)
            dks_ref[:, cols] = jnp.zeros((SUMM_ROWS, PAIR), jnp.float32)
            dvs_ref[:, cols] = jnp.zeros((SUMM_ROWS, PAIR), jnp.float32)
        ks, vs = ks_ref[:, cols], vs_ref[:, cols]
        ks_t = (ks * scale).T
        nk = (block + 1) * bq if self.causal else seg
        here = slice(block * bq, (block + 1) * bq)
        own, earlier = key_masks(facts, block, self.blocks * bq, bq, nk)
        q = q_ref[here, cols] * scale
        do = do_ref[here, cols]
        k, v = k_ref[:nk, cols], v_ref[:nk, cols]
        grads = []
        for head in range(2):
            qh = jnp.where(head_lanes(head), q, jnp.zeros_like(q))
            doh = jnp.where(head_lanes(head), do, jnp.zeros_like(do))
            lse = lse_ref[pair, head : head + 1, here]
            p = jnp.exp(jnp.where(own, mm(k, qh, NT), MASKED) - lse)
            p2 = jnp.exp(jnp.where(earlier, mm(ks, qh, NT), MASKED) - lse)
            dp = mm(v, doh, NT)
            dp2 = mm(vs, doh, NT)
            delta = jnp.sum(p * dp, axis=0, keepdims=True) + jnp.sum(p2 * dp2, axis=0, keepdims=True)
            ds = (p * (dp - delta)).astype(jnp.bfloat16)
            ds2 = (p2 * (dp2 - delta)).astype(jnp.bfloat16)
            dv_acc[:nk, :] += mm(p.astype(jnp.bfloat16), doh)
            dk_acc[:nk, :] += mm(ds, qh)
            dvs_ref[:, cols] += mm(p2.astype(jnp.bfloat16), doh)
            dks_ref[:, cols] += mm(ds2, qh)
            grads.append(mm(k_t[:, :nk], ds) + mm(ks_t, ds2))
        joined = jnp.where(low_half, grads[0], grads[1])
        dq_ref[here, cols] = joined.T.astype(jnp.bfloat16)
        if block == self.blocks - 1:
            dk_ref[:, cols] = dk_acc[...].astype(jnp.bfloat16)
            dv_ref[:, cols] = dv_acc[...].astype(jnp.bfloat16)


class Spread(Nothing):
    others = 3
    n_in, n_out = 10, 4
    block = 256
    lag = (2, 5, 8)

    def __init__(self, factors, columns):
        rows, features = factors[0].shape
        block, half = self.block, self.block // 2
        assert features == 8 * block
        self.rows = rows
        self.operands = tuple(factors) + tuple(right for _, right, _, _ in columns)
        self.in_specs = (ANY,) * self.n_in
        self.table, self.phases = [], {}
        at, widths = 0, [0] * 4
        for number, (left, right, result, place) in enumerate(columns):
            self.phases.setdefault(left, at)
            self.table.append((number, at, at + right.shape[1] // block, result, place))
            at += right.shape[1] // block
            widths[result] += right.shape[1]
        self.chunks = at
        self.steps = at + self.lag[2]
        self.across = (True, False, False, True)
        self.out_shape = tuple(
            jax.ShapeDtypeStruct((block, n) if across else (n, block), jnp.float32)
            for n, across in zip(widths, self.across)
        )
        self.out_specs = (ANY,) * 4
        low = lambda *shape: pltpu.VMEM(shape, jnp.bfloat16)
        wide = lambda *shape: pltpu.VMEM(shape, jnp.float32)
        dma = lambda n: pltpu.SemaphoreType.DMA((n,))
        self.scratch_shapes = (
            low(2, rows, features),
            low(2, rows, block),
            low(3, 2, block, 2 * block),
            wide(3, 2, block, 2 * block),
            low(4, 2, block, 2 * block),
            low(3, half, 2 * block),
            low(3, 2, half, block),
            wide(3, half, 2 * block),
            wide(3, 2, half, block),
            low(6, half, 2 * block),
            low(6, 2, half, block),
            low(3, 2, half, block),
            wide(3, 2, half, block),
            low(6, 2, half, block),
            wide(3, block, block),
            dma(2),
            dma(2),
            dma(3),
            dma(4),
            dma(3),
            dma(6),
            dma(3),
            dma(6),
            dma(3),
            dma(6),
            dma(3),
            dma(6),
            dma(3),
        )

    def __call__(self, ins, outs, scratch):
        self.lefts, self.rights, self.outs = ins[:4], ins[4:], outs
        (
            self.x_buf,
            self.y_buf,
            self.s1,
            self.own,
            self.r1,
            self.s2x,
            self.s2y,
            self.top,
            self.low,
            self.r2x,
            self.r2y,
            self.s3,
            self.kept,
            self.r3,
            self.tile,
            self.x_sem,
            self.y_sem,
            self.s1_sem,
            self.r1_sem,
            self.s2x_sem,
            self.r2x_sem,
            self.s2y_sem,
            self.r2y_sem,
            self.s3y_sem,
            self.r3y_sem,
            self.s3x_sem,
            self.r3x_sem,
            self.out_sem,
        ) = scratch
        item, seq = lax.axis_index("item"), lax.axis_index("seq")
        self.core, self.x, self.y = item % 2, item // 2, seq
        self.to_core = {"item": item + 1 - 2 * self.core}
        self.to_x = {"item": item + 2 - 4 * self.x}
        self.to_y = {"seq": 1 - seq}
        return self

    def greet(self, barrier):
        for to in (self.to_core, self.to_x, self.to_y):
            pl.semaphore_signal(barrier, inc=1, device_id=to, device_id_type=MESH)


    def left_copy(self, left):
        slot = list(self.phases).index(left) % 2
        return pltpu.make_async_copy(self.lefts[left], self.x_buf.at[slot], self.x_sem.at[slot])

    def right_copy(self, m, act):
        for number, start, stop, _, _ in self.table:

            @pl.when((m >= start) & (m < stop))
            def _():
                cols = pl.ds(pl.multiple_of((m - start) * self.block, self.block), self.block)
                act(
                    pltpu.make_async_copy(
                        self.rights[number].at[:, cols], self.y_buf.at[m % 2], self.y_sem.at[m % 2]
                    )
                )

    def out_copy(self, m, act):
        for _, start, stop, result, place in self.table:

            @pl.when((m >= start) & (m < stop))
            def _():
                cols = pl.ds(
                    pl.multiple_of(place + (m - start) * self.block, self.block), self.block
                )
                out = self.outs[result]
                out = out.at[:, cols] if self.across[result] else out.at[cols, :]
                act(pltpu.make_async_copy(self.tile.at[m % 3], out, self.out_sem.at[m % 3]))

    def remote(self, src, dst, send, recv, to):
        return pltpu.make_async_remote_copy(
            src_ref=src, dst_ref=dst, send_sem=send, recv_sem=recv, device_id=to, device_id_type=MESH
        )

    def first_copy(self, m):
        return self.remote(
            self.s1.at[m % 3],
            self.r1.at[m % 4],
            self.s1_sem.at[m % 3],
            self.r1_sem.at[m % 4],
            self.to_core,
        )

    def second_copies(self, m):
        return (
            self.remote(
                self.s2x.at[m % 3],
                self.r2x.at[m % 6],
                self.s2x_sem.at[m % 3],
                self.r2x_sem.at[m % 6],
                self.to_x,
            ),
            self.remote(
                self.s2y.at[m % 3],
                self.r2y.at[m % 6],
                self.s2y_sem.at[m % 3],
                self.r2y_sem.at[m % 6],
                self.to_y,
            ),
        )

    def third_copies(self, m):
        return (
            self.remote(
                self.s3.at[m % 3, 0],
                self.r3.at[m % 6, 0],
                self.s3y_sem.at[m % 3],
                self.r3y_sem.at[m % 6],
                self.to_y,
            ),
            self.remote(
                self.s3.at[m % 3, 1],
                self.r3.at[m % 6, 1],
                self.s3x_sem.at[m % 3],
                self.r3x_sem.at[m % 6],
                self.to_x,
            ),
        )

    def first(self):
        for left in list(self.phases)[:2]:
            self.left_copy(left).start()
        self.right_copy(0, lambda copy: copy.start())

    def step(self, t):
        for stage, lag in ((self.fourth, 8), (self.third, 5), (self.second, 2), (self.multiply, 0)):
            m = t - lag

            @pl.when((m >= 0) & (m < self.chunks))
            def _():
                stage(m)

    def multiply(self, m):
        order = list(self.phases)
        for number, left in enumerate(order):

            @pl.when(m == self.phases[left])
            def _():
                self.left_copy(left).wait()
                if 1 <= number < len(order) - 1:
                    self.left_copy(order[number + 1]).start()

        @pl.when(m + 1 < self.chunks)
        def _():
            self.right_copy(m + 1, lambda copy: copy.start())

        self.right_copy(m, lambda copy: copy.wait())

        @pl.when(m >= 3)
        def _():
            self.first_copy(m - 3).wait_send()

        phase = sum((m >= start).astype(jnp.int32) for start in self.phases.values()) - 1
        turned = self.y_buf[m % 2].T
        wide = 2 * self.block

        def product(x, core):
            cols = pl.ds(pl.multiple_of(x * 2 * wide + core * wide, wide), wide)
            return mm(turned, self.x_buf[phase % 2, :, cols])

        for x in range(2):
            self.s1[m % 3, x] = product(x, 1 - self.core).astype(jnp.bfloat16)
        self.first_copy(m).start()
        for x in range(2):
            self.own[m % 3, x] = product(x, self.core)

    def second(self, m):
        half = self.block // 2

        @pl.when(m >= 3)
        def _():
            for copy in self.second_copies(m - 3):
                copy.wait_send()

        self.first_copy(m).wait_recv()
        slot = m % 3
        here, there = self.x, 1 - self.x
        mine = pl.ds(pl.multiple_of(self.y * self.block, self.block), self.block)
        others = pl.ds(pl.multiple_of((1 - self.y) * self.block, self.block), self.block)
        added = lambda x, rows, cols: (
            self.own[slot, x, rows, cols] + self.r1[m % 4, x, rows, cols].astype(jnp.float32)
        )
        upper, lower, every = pl.ds(0, half), pl.ds(half, half), pl.ds(0, 2 * self.block)
        self.s2x[slot] = added(there, upper, every).astype(jnp.bfloat16)
        for x in range(2):
            self.s2y[slot, x] = added(x, lower, others).astype(jnp.bfloat16)
        for copy in self.second_copies(m):
            copy.start()
        self.top[slot] = added(here, upper, every)
        for x in range(2):
            self.low[slot, x] = added(x, lower, mine)

    def third(self, m):
        @pl.when(m >= 3)
        def _():
            for copy in self.third_copies(m - 3):
                copy.wait_send()

        for copy in self.second_copies(m):
            copy.wait_recv()
        slot, got = m % 3, m % 6
        mine = pl.ds(pl.multiple_of(self.y * self.block, self.block), self.block)
        others = pl.ds(pl.multiple_of((1 - self.y) * self.block, self.block), self.block)
        top = lambda cols: self.top[slot, :, cols] + self.r2x[got, :, cols].astype(jnp.float32)
        low = lambda x: self.low[slot, x] + self.r2y[got, x].astype(jnp.float32)
        self.s3[slot, 0] = top(others).astype(jnp.bfloat16)
        self.s3[slot, 1] = low(1 - self.x).astype(jnp.bfloat16)
        for copy in self.third_copies(m):
            copy.start()
        self.kept[slot, 0] = top(mine)
        self.kept[slot, 1] = low(self.x)

    def fourth(self, m):
        @pl.when(m >= 3)
        def _():
            self.out_copy(m - 3, lambda copy: copy.wait())

        for copy in self.third_copies(m):
            copy.wait_recv()
        slot, half = m % 3, self.block // 2
        total = self.kept[slot] + self.r3[m % 6].astype(jnp.float32)
        total = total.reshape(self.block, self.block)
        across = jnp.zeros((), jnp.bool_)
        for _, start, stop, result, _ in self.table:
            if self.across[result]:
                across = across | ((m >= start) & (m < stop))

        @pl.when(across)
        def _():
            self.tile[slot] = total.T

        @pl.when(jnp.logical_not(across))
        def _():
            self.tile[slot] = total

        self.out_copy(m, lambda copy: copy.start())

    def settle(self):
        for m in range(self.chunks - 3, self.chunks):
            self.first_copy(m).wait_send()
            for copy in self.second_copies(m) + self.third_copies(m):
                copy.wait_send()
            self.out_copy(jnp.int32(m), lambda copy: copy.wait())


class Gather:
    others = 3

    def __init__(self, shards, fulls, sems):
        self.shards, self.fulls = shards, fulls
        self.sent, self.got, self.local = sems
        item, seq = lax.axis_index("item"), lax.axis_index("seq")
        self.core, self.x, self.y = item % 2, item // 2, seq
        self.to_core = {"item": item + 1 - 2 * self.core}
        self.to_x = {"item": item + 2 - 4 * self.x}
        self.to_y = {"seq": 1 - seq}

    @staticmethod
    def sems():
        dma = lambda *shape: pltpu.SemaphoreType.DMA(shape)
        return [dma(2, 9), dma(2, 9), dma(2)]

    def greet(self, barrier):
        for to in (self.to_core, self.to_x, self.to_y):
            pl.semaphore_signal(barrier, inc=1, device_id=to, device_id_type=MESH)

    def spot(self, w, x, core, y, part=None):
        size = self.shards[w].shape[w]
        at = pl.ds(pl.multiple_of(((2 * x + core) * 2 + y) * size, size), size)
        if w == 0:
            if part is not None:
                half = size // 2
                start = ((2 * x + core) * 2 + y) * size + part * half
                at = pl.ds(pl.multiple_of(start, half), half)
            return self.fulls[0].at[at, :]
        rows = self.fulls[1].shape[0]
        if part is not None:
            return self.fulls[1].at[pl.ds(part * (rows // 2), rows // 2), at]
        return self.fulls[1].at[:, at]

    def message(self, w, number, src, dst, to):
        return pltpu.make_async_remote_copy(
            src_ref=src,
            dst_ref=dst,
            send_sem=self.sent.at[w, number],
            recv_sem=self.got.at[w, number],
            device_id=to,
            device_id_type=MESH,
        )

    def messages(self, w):
        c, x, y = self.core, self.x, self.y
        own, spot = self.shards[w].at[...], functools.partial(self.spot, w)
        plan = (
            (own, spot(x, c, y), spot(x, 1 - c, y), self.to_core),
            (own, spot(x, c, y), spot(1 - x, c, y), self.to_x),
            (own, spot(x, c, y), spot(x, c, 1 - y), self.to_y),
            (None, spot(1 - x, c, y, 0), spot(1 - x, c, 1 - y, 0), self.to_y),
            (None, spot(x, c, 1 - y, 1), spot(1 - x, c, 1 - y, 1), self.to_x),
            (None, spot(1 - x, c, y), spot(1 - x, 1 - c, y), self.to_core),
            (None, spot(x, c, 1 - y), spot(x, 1 - c, 1 - y), self.to_core),
            (None, spot(1 - x, c, 1 - y, 0), spot(1 - x, 1 - c, 1 - y, 0), self.to_core),
            (None, spot(1 - x, c, 1 - y, 1), spot(1 - x, 1 - c, 1 - y, 1), self.to_core),
        )
        return [
            (
                self.message(w, number, out if src is None else src, out, to),
                self.message(w, number, landing, landing, to),
            )
            for number, (src, out, landing, to) in enumerate(plan)
        ]

    def send(self, w, numbers):
        messages = self.messages(w)
        for number in numbers:
            messages[number][0].start()

    def receive(self, w, numbers):
        messages = self.messages(w)
        for number in numbers:
            messages[number][1].wait_recv()

    def mine(self, w):
        return pltpu.make_async_copy(
            self.shards[w], self.spot(w, self.x, self.core, self.y), self.local.at[w]
        )

    def first(self):
        for w in range(2):
            self.mine(w).start()

    def begin(self):
        for w in range(2):
            self.send(w, (1, 2, 0))

    def step(self, t):
        for w, at in ((0, 5), (1, 9)):

            @pl.when(t == at)
            def _():
                self.receive(w, (1, 2))
                self.send(w, (3, 4, 5, 6))

        for w, at in ((0, 12), (1, 15)):

            @pl.when(t == at)
            def _():
                self.receive(w, (3, 4))
                self.send(w, (7, 8))

        @pl.when(t == WEIGHTS_READY)
        def _():
            for w in range(2):
                self.receive(w, (0, 5, 6, 7, 8))
                self.mine(w).wait()

    def settle(self):
        for w in range(2):
            for out, _ in self.messages(w):
                out.wait_send()


class Load:
    others = 0

    def __init__(self, shards, fulls, sems):
        self.copies = [
            pltpu.make_async_copy(shard, full, sems[2].at[w])
            for w, (shard, full) in enumerate(zip(shards, fulls))
        ]

    sems = Gather.sems

    def greet(self, barrier):
        pass

    def first(self):
        for copy in self.copies:
            copy.start()

    def begin(self):
        pass

    def step(self, t):
        @pl.when(t == WEIGHTS_READY)
        def _():
            for copy in self.copies:
                copy.wait()

    def settle(self):
        pass


def ffn_kernel(
    count,
    half,
    weights_job,
    attended,
    out_w,
    out_bias,
    mid_gain,
    mid_shift,
    up_bias,
    hidden,
    cotangent,
    up_shard,
    down_shard,
    mid,
    act,
    grad_pre,
    residual_out,
    branch,
    grad_out,
    down_out,
    acc,
    acc_up,
    part1,
    moving1,
    part2,
    moving2,
    rows_in,
    residual,
    up,
    down,
    mid_in,
    cot_in,
    act_out,
    pre_out,
    *sems,
):
    sems = list(sems)
    take = lambda n: [sems.pop(0) for _ in range(n)]
    sems1, sems2, weight_sems = take(5), take(5), take(3)
    in_sem, residual_sem, grad_sem, mid_sem, cot_sem, act_sem, pre_sem, down_sem = sems
    me = lax.axis_index("mp")
    group = part2.shape[2]
    per_group = group // PIECE
    pieces = half // PIECE
    last = count - 1
    weights = weights_job((up_shard, down_shard), (up, down), weight_sems)
    piece = lambda k: pl.ds(pl.multiple_of(k * PIECE, PIECE), PIECE)
    owner = (me == 0) | (me == last)
    my_flow = jnp.where(me == 0, 0, 1)

    def piece_in(source, k, flow):
        return pltpu.make_async_copy(
            source.at[pl.ds(flow * half + k * PIECE, PIECE)], rows_in.at[piece(k)], in_sem.at[k]
        )

    def residual_copy(k):
        return pltpu.make_async_copy(
            residual.at[piece(k)], residual_out.at[piece(k)], residual_sem.at[k]
        )

    def grad_copy(k):
        return pltpu.make_async_copy(residual.at[piece(k)], grad_out.at[piece(k)], grad_sem.at[k])

    def finish_first(flow, k, total):
        piece_in(hidden, k, flow).wait()
        value = rows_in[piece(k), :].astype(jnp.float32) + total + out_bias[...]
        residual[piece(k), :] = value
        residual_copy(k).start()
        piece_in(cotangent, k, flow).start()
        return norm_stats(value)[0] * mid_gain[...] + mid_shift[...]

    def finish_second(flow, k, total):
        piece_in(cotangent, k, flow).wait()
        residual_copy(k).wait()
        normed, inverse = norm_stats(residual[piece(k), :])
        grad = rows_in[piece(k), :].astype(jnp.float32)
        grad = grad + norm_back(total, normed, inverse, mid_gain[...])
        residual[piece(k), :] = grad
        grad_copy(k).start()
        acc[0] += fold(total * normed)
        acc[1] += fold(total)
        acc[2] += fold(grad)
        return grad

    multiply = group_product([attended], out_w, NN, half, part1.shape[2])
    line1 = Line(count, half, multiply, finish_first, mid, part1, moving1, sems1)
    line2 = Line(count, half, None, finish_second, branch, part2, moving2, sems2)

    def group_rows(flow, g):
        return pl.ds(pl.multiple_of(flow * half + g * group, 16), group)

    def mid_fetch(flow, g, here):
        rows = pl.ds(pl.multiple_of(g * group, 16), group)
        source = moving1.at[flow, rows] if here else mid.at[group_rows(flow, g)]
        return pltpu.make_async_copy(source, mid_in.at[flow], mid_sem.at[flow])

    def cot_fetch(flow, g):
        return pltpu.make_async_copy(
            cotangent.at[group_rows(flow, g)], cot_in.at[flow], cot_sem.at[flow]
        )

    def act_copy(flow, g):
        return pltpu.make_async_copy(
            act_out.at[flow], act.at[group_rows(flow, g)], act_sem.at[flow]
        )

    def pre_copy(flow, g):
        return pltpu.make_async_copy(
            pre_out.at[flow], grad_pre.at[group_rows(flow, g)], pre_sem.at[flow]
        )

    def products(flow, g):
        mid_fetch(flow, g, False).wait()
        cot_fetch(flow, g).wait()

        @pl.when(g > 0)
        def _():
            act_copy(flow, g - 1).wait()
            pre_copy(flow, g - 1).wait()

        block = 512
        for number in range(up.shape[1] // block):
            cols = slice(number * block, (number + 1) * block)
            value, slope = gelu_parts(mm(mid_in[flow], up[:, cols]) + up_bias[:, cols])
            act_out[flow, :, cols] = value.astype(jnp.bfloat16)
            pre = (slope * mm(cot_in[flow], down[cols, :], NT)).astype(jnp.bfloat16)
            pre_out[flow, :, cols] = pre
            acc_up[:, cols] += fold(pre.astype(jnp.float32))
            product = mm(pre, up[:, cols], NT)
            if number == 0:
                part2[flow, g % 2] = product
            else:
                part2[flow, g % 2] += product
        act_copy(flow, g).start()
        pre_copy(flow, g).start()

    barrier = pltpu.get_barrier_semaphore()
    line1.greet(barrier)
    weights.greet(barrier)
    acc[...] = jnp.zeros_like(acc)
    acc_up[...] = jnp.zeros_like(acc_up)
    weights.first()

    @pl.when(owner)
    def _():
        def one(k, carry):
            piece_in(hidden, k, my_flow).start()
            return carry

        lax.fori_loop(0, pieces, one, 0)

    line1.first()
    line1.meet(barrier, weights.others)
    weights.begin()

    def step(t, carry):
        line1.step(t)
        line2.step(t - SECOND_STREAM)
        weights.step(t)

        @pl.when(t == WEIGHTS_READY + 1)
        def _():
            pltpu.make_async_copy(down, down_out, down_sem.at[0]).start()

        for flow in range(2):
            place = line1.place(flow)
            u = t - SECOND_STREAM - SKEW * place
            fetch = u + 3
            compute = u + 2

            @pl.when((fetch >= 0) & (fetch % per_group == 0) & (fetch < pieces))
            def _():
                g = fetch // per_group
                cot_fetch(flow, g).start()

                @pl.when(place == last)
                def _():
                    mid_fetch(flow, g, True).start()

                @pl.when(place < last)
                def _():
                    mid_fetch(flow, g, False).start()

            @pl.when((compute >= 0) & (compute % per_group == 0) & (compute < pieces))
            def _():
                products(flow, compute // per_group)

        return carry

    lax.fori_loop(0, SECOND_STREAM + line2.steps, step, 0)
    line1.settle()
    line2.settle()
    weights.settle()
    pltpu.make_async_copy(down, down_out, down_sem.at[0]).wait()
    for flow in range(2):
        act_copy(flow, pieces // per_group - 1).wait()
        pre_copy(flow, pieces // per_group - 1).wait()

    @pl.when(owner)
    def _():
        def one(k, carry):
            grad_copy(k).wait()
            return carry

        lax.fori_loop(0, pieces, one, 0)


def ffn_sums(number, count, weights_job, attended, out_w, vectors, hidden, cotangent, up_w, down_w):
    rows, features = hidden.shape
    ff = up_w.shape[1]
    half = rows // 2
    pieces = half // PIECE
    low = lambda *shape: jax.ShapeDtypeStruct(shape, jnp.bfloat16)
    wide = lambda *shape: jax.ShapeDtypeStruct(shape, jnp.float32)
    first = Line.scratch(half, features)
    small = 2 * PIECE if pieces % 2 == 0 else PIECE
    first[0] = pltpu.VMEM((2, 2, small, features), jnp.float32)
    second = Line.scratch(half, features)
    group = second[0].shape[2]
    dma = lambda n: pltpu.SemaphoreType.DMA((n,))
    return pl.pallas_call(
        functools.partial(ffn_kernel, count, half, weights_job),
        in_specs=[VMEM] * 6 + [ANY] * 4,
        out_specs=[ANY] * 7 + [VMEM] * 2,
        out_shape=[
            low(rows, features),
            low(rows, ff),
            low(rows, ff),
            wide(half, features),
            low(rows, features),
            wide(half, features),
            low(ff, features),
            wide(3, 8, features),
            wide(8, ff),
        ],
        scratch_shapes=first[:2]
        + second[:2]
        + [
            pltpu.VMEM((half, features), jnp.bfloat16),
            pltpu.VMEM((half, features), jnp.float32),
            pltpu.VMEM((features, ff), jnp.bfloat16),
            pltpu.VMEM((ff, features), jnp.bfloat16),
            pltpu.VMEM((2, group, features), jnp.bfloat16),
            pltpu.VMEM((2, group, features), jnp.bfloat16),
            pltpu.VMEM((2, group, ff), jnp.bfloat16),
            pltpu.VMEM((2, group, ff), jnp.bfloat16),
        ]
        + first[2:]
        + second[2:]
        + Gather.sems()
        + [dma(pieces), dma(pieces), dma(pieces), dma(2), dma(2), dma(2), dma(2), dma(1)],
        compiler_params=pltpu.CompilerParams(
            collective_id=number, has_side_effects=True, vmem_limit_bytes=62 * MIB
        ),
        cost_estimate=pl.CostEstimate(
            flops=6 * rows * features * ff, bytes_accessed=30 * rows * features, transcendentals=0
        ),
        name="ffn_sums",
    )(attended, out_w, *vectors, hidden, cotangent, up_w, down_w)


def small_kernel(stages, shared, own_ref, out_ref, sent, got, send_sem, recv_sem):
    barrier = pltpu.get_barrier_semaphore()

    def partner(axis, bit):
        index = lax.axis_index(axis)
        return {axis: index + bit - 2 * bit * ((index // bit) % 2)}

    for axis, bit in stages:
        pl.semaphore_signal(barrier, inc=1, device_id=partner(axis, bit), device_id_type=MESH)
    pl.semaphore_wait(barrier, len(stages))
    sent[0] = own_ref[...]
    row = lax.broadcasted_iota(jnp.int32, own_ref.shape, 0)
    for number, (axis, bit) in enumerate(stages):
        copy = pltpu.make_async_remote_copy(
            src_ref=sent.at[number],
            dst_ref=got.at[number],
            send_sem=send_sem.at[number],
            recv_sem=recv_sem.at[number],
            device_id=partner(axis, bit),
            device_id_type=MESH,
        )
        copy.start()
        copy.wait()
        total = sent[number] + got[number]
        if axis == "mp":
            total = jnp.where(row < shared, total, sent[number])
        if number + 1 < len(stages):
            sent[number + 1] = total
        else:
            out_ref[...] = total


def small_sum(number, sizes, shared, values):
    stages = tuple(
        (axis, 1 << bit) for axis, size in sizes for bit in range(size.bit_length() - 1)
    )
    steps = len(stages)
    vmem = pl.BlockSpec(memory_space=pltpu.VMEM)
    return pl.pallas_call(
        functools.partial(small_kernel, stages, shared),
        in_specs=[vmem],
        out_specs=vmem,
        out_shape=jax.ShapeDtypeStruct(values.shape, jnp.float32),
        scratch_shapes=[
            pltpu.VMEM((steps, *values.shape), jnp.float32),
            pltpu.VMEM((steps, *values.shape), jnp.float32),
            pltpu.SemaphoreType.DMA((steps,)),
            pltpu.SemaphoreType.DMA((steps,)),
        ],
        compiler_params=pltpu.CompilerParams(collective_id=number, has_side_effects=True),
        name="small_sum",
    )(values)


def gradients_over(group, lefts, columns):
    over_rows = lambda left, right: mm(left, right, (((0,), (0,)), ((), ()))).astype(jnp.bfloat16)
    parts = [[] for _ in range(4)]
    for left, right, result, _ in columns:
        across = result in (0, 3)
        product = over_rows(lefts[left], right) if across else over_rows(right, lefts[left])
        parts[result].append(product)
    return [
        lax.psum_scatter(
            jnp.concatenate(part, axis=1),
            group,
            scatter_dimension=0 if result in (0, 3) else 1,
            tiled=True,
        ).astype(jnp.float32)
        for result, part in enumerate(parts)
    ]


def body(
    item_count,
    seq_count,
    mp_count,
    hidden_in,
    cotangent,
    seg_lengths,
    pre_gain,
    pre_shift,
    qkv_weight,
    qv_bias,
    out_weight,
    out_bias,
    mid_gain,
    mid_shift,
    up_weight,
    up_bias,
    down_weight,
    down_bias,
):
    group = ("item", "seq")
    width = qkv_weight.shape[2]
    gathered = lambda weight, axis: lax.all_gather(weight, group, axis=axis, tiled=True)
    qkv_full = gathered(qkv_weight.reshape(-1, 3 * width), 0)
    out_full = gathered(out_weight, 1)
    hidden = hidden_in[0].astype(jnp.float32)
    lengths = seg_lengths[0]
    rows = hidden.shape[0]
    first_row = lax.axis_index("seq") * rows
    segment = first_row // SLOT
    facts = jnp.stack(
        [
            first_row % SLOT,
            lengths[segment] + SUMM,
            jnp.where(segment > 0, SUMM, 0),
        ]
    ).astype(jnp.int32)

    normed = (norm_stats(hidden)[0] * pre_gain + pre_shift).astype(jnp.bfloat16)
    q = (mm(normed, qkv_full[:, :width]) + qv_bias[0]).astype(jnp.bfloat16)
    k = mm(normed, qkv_full[:, width : 2 * width]).astype(jnp.bfloat16)
    v = (mm(normed, qkv_full[:, 2 * width :]) + qv_bias[1]).astype(jnp.bfloat16)
    own, summary = keys_for(jnp.stack([k, v]), lengths, seq_count)
    tables = (own[0], own[1], summary[0], summary[1])
    attended, log_total = attend(facts, q, *tables)

    row = lambda vector: vector[None, :]
    ours = (item_count, seq_count) == (4, 2)
    grad_down = cotangent[0]
    (
        mid_low,
        act_low,
        grad_pre,
        residual,
        grad_branch,
        grad_residual,
        down_full,
        mid_sums,
        up_sums,
    ) = ffn_sums(
        1,
        mp_count,
        Gather if ours else Load,
        attended,
        out_full,
        (row(out_bias), row(mid_gain), row(mid_shift), row(up_bias)),
        hidden_in[0],
        grad_down,
        up_weight if ours else gathered(up_weight, 0),
        down_weight if ours else gathered(down_weight, 1),
    )
    grad_attended = mm(grad_branch, out_full, NT).astype(jnp.bfloat16)
    hidden_out, dq, dk, dv, dks, dvs = line_sum(
        3,
        mp_count,
        [act_low],
        down_full,
        NN,
        [residual, row(down_bias)],
        0,
        0,
        finish_out,
        "down_sum",
        AttendBack(facts, q, *tables, grad_attended, log_total),
    )
    dk, dv = keys_back(jnp.stack([dk, dv]), jnp.stack([dks, dvs]), rows, lengths, seq_count)
    lefts = (mid_low, grad_down, grad_branch, normed)
    columns = (
        (0, grad_pre, 0, 0),
        (1, act_low, 1, 0),
        (2, attended, 2, 0),
        (3, dq, 3, 0),
        (3, dk, 3, width),
        (3, dv, 3, 2 * width),
    )
    spread = Nothing()
    if ours:
        spread = Spread(lefts, columns)
    grad_input, pre_sums, *weight_grads = line_sum(
        4,
        mp_count,
        [dq, dk, dv],
        qkv_full,
        NT,
        [hidden_in[0], grad_residual, row(pre_gain)],
        0,
        2,
        finish_input,
        "input_sum",
        spread,
    )
    if not weight_grads:
        weight_grads = gradients_over(group, lefts, columns)
    up_grad, down_grad, out_grad, qkv_grad = weight_grads
    total = lambda value: jnp.sum(value.astype(jnp.float32), axis=0)
    features = hidden.shape[1]
    qv_sums = jnp.concatenate([total(dq), total(dv)])
    sums = small_sum(
        5,
        [("item", item_count), ("seq", seq_count), ("mp", mp_count)],
        6,
        jnp.concatenate(
            [
                jnp.sum(mid_sums, axis=1),
                jnp.sum(pre_sums, axis=1),
                row(jnp.where(lax.axis_index("mp") == 0, total(grad_down), 0.0)),
                total(up_sums).reshape(-1, features),
                jnp.pad(qv_sums, (0, -qv_sums.shape[0] % features)).reshape(-1, features),
            ]
        ),
    )
    ff_rows = up_weight.shape[1] // features
    up_bias_grad = sums[6 : 6 + ff_rows].reshape(-1)
    qv_bias_grad = sums[6 + ff_rows :].reshape(-1)[: 2 * width].reshape(2, width)
    return (
        hidden_out[None],
        grad_input.astype(jnp.float32)[None],
        sums[3],
        sums[4],
        qkv_grad.reshape(-1, 3, width),
        qv_bias_grad,
        out_grad,
        sums[2],
        sums[0],
        sums[1],
        up_grad,
        up_bias_grad,
        down_grad,
        sums[5],
    )


def solution(mesh):
    rows = P("item", "seq", None)
    qkv = P(("item", "seq"), None, "mp")
    first = P(("item", "seq"), "mp")
    second = P("mp", ("item", "seq"))
    bias = P(None, "mp")
    return jax.shard_map(
        functools.partial(body, mesh.shape["item"], mesh.shape["seq"], mesh.shape["mp"]),
        mesh=mesh,
        in_specs=(
            rows,
            rows,
            P("item", None),
            P(),
            P(),
            qkv,
            bias,
            second,
            P(),
            P(),
            P(),
            first,
            P("mp"),
            second,
            P(),
        ),
        out_specs=(
            rows,
            rows,
            P(),
            P(),
            qkv,
            bias,
            second,
            P(),
            P(),
            P(),
            first,
            P("mp"),
            second,
            P(),
        ),
        check_vma=False,
    )
```

```python
import functools
import math

import jax
import jax.numpy as jnp
from jax import lax
from jax.experimental import pallas as pl
from jax.experimental.pallas import tpu as pltpu
from jax.sharding import PartitionSpec as P

HDIM = 64
SLOT = 1280
SEGS = 2
SUMM = 50
SUMM_ROWS = 64
TOKENS = 2560
PAIR = 2 * HDIM
PIECE = 32
SKEW = 2
MIB = 1 << 20
MESH = pl.DeviceIdType.MESH
MASKED = -1e30


eps = 1e-05

NN = (((1,), (0,)), ((), ()))
NT = (((1,), (1,)), ((), ()))


def mm(left, right, dims=NN):
    return lax.dot_general(left, right, dims, preferred_element_type=jnp.float32)


def norm_stats(values):
    center = jnp.mean(values, axis=-1, keepdims=True)
    centered = values - center
    inverse = lax.rsqrt(jnp.mean(centered * centered, axis=-1, keepdims=True) + eps)
    return centered * inverse, inverse


def norm_back(grad_out, normed, inverse, gain):
    scaled = grad_out * gain
    centered = scaled - jnp.mean(scaled, axis=-1, keepdims=True)
    return inverse * (centered - normed * jnp.mean(scaled * normed, axis=-1, keepdims=True))


def gelu_parts(values):
    c = math.sqrt(2 / math.pi)
    squared = values * values
    t = jnp.tanh(c * values * (1 + 0.044715 * squared))
    half = 0.5 * (1 + t)
    slope = half + 0.5 * values * (1 - t * t) * (c * (1 + 3 * 0.044715 * squared))
    return values * half, slope


def key_masks(facts_ref, block, rows, bq, nk):
    first = facts_ref[0] + block * bq
    limit = jnp.minimum(
        first + 1 + lax.broadcasted_iota(jnp.int32, (1, bq), 1), facts_ref[1]
    )
    own = lax.broadcasted_iota(jnp.int32, (nk, bq), 0) < limit
    earlier = lax.broadcasted_iota(jnp.int32, (SUMM_ROWS, bq), 0) < facts_ref[2]
    return own, earlier


def head_lanes(head):
    lane = lax.broadcasted_iota(jnp.int32, (1, PAIR), 1)
    return (lane >= head * HDIM) & (lane < (head + 1) * HDIM)


def attend_kernel(bq, causal, facts_ref, q_ref, k_ref, v_ref, ks_ref, vs_ref, o_ref, lse_ref):
    rows, seg = q_ref.shape[0], k_ref.shape[0]
    v_t = v_ref[...].T
    vs_t = vs_ref[...].T
    ks = ks_ref[...]
    low_half = lax.broadcasted_iota(jnp.int32, (PAIR, 1), 0) < HDIM
    for block in range(rows // bq):
        nk = (block + 1) * bq if causal else seg
        own, earlier = key_masks(facts_ref, block, rows, bq, nk)
        q = q_ref[block * bq : (block + 1) * bq, :] * jnp.bfloat16(HDIM**-0.5)
        mixed = []
        for head in range(2):
            qh = jnp.where(head_lanes(head), q, jnp.zeros_like(q))
            s = jnp.where(own, mm(k_ref[:nk, :], qh, NT), MASKED)
            s2 = jnp.where(earlier, mm(ks, qh, NT), MASKED)
            top = jnp.maximum(jnp.max(s, axis=0, keepdims=True), jnp.max(s2, axis=0, keepdims=True))
            p = jnp.exp(s - top)
            p2 = jnp.exp(s2 - top)
            total = jnp.sum(p, axis=0, keepdims=True) + jnp.sum(p2, axis=0, keepdims=True)
            out = mm(v_t[:, :nk], p.astype(jnp.bfloat16)) + mm(vs_t, p2.astype(jnp.bfloat16))
            mixed.append(out / total)
            lse_ref[0, head : head + 1, block * bq : (block + 1) * bq] = top + jnp.log(total)
        joined = jnp.where(low_half, mixed[0], mixed[1])
        o_ref[block * bq : (block + 1) * bq, :] = joined.T.astype(jnp.bfloat16)


def query_block(rows):
    return 256 if rows % 256 == 0 else math.gcd(rows, 160)


def attend(facts, q, k, v, ks, vs):
    rows, width = q.shape
    seg = k.shape[0]
    pairs = width // PAIR
    column = lambda n: pl.BlockSpec((n, PAIR), lambda i: (0, i))
    return pl.pallas_call(
        functools.partial(attend_kernel, query_block(rows), rows == seg),
        grid=(pairs,),
        in_specs=[pl.BlockSpec(memory_space=pltpu.SMEM)]
        + [column(n) for n in (rows, seg, seg, SUMM_ROWS, SUMM_ROWS)],
        out_specs=[column(rows), pl.BlockSpec((1, 2, rows), lambda i: (i, 0, 0))],
        out_shape=[
            jax.ShapeDtypeStruct((rows, width), jnp.bfloat16),
            jax.ShapeDtypeStruct((pairs, 2, rows), jnp.float32),
        ],
        compiler_params=pltpu.CompilerParams(vmem_limit_bytes=48 * MIB),
        cost_estimate=pl.CostEstimate(
            flops=4 * rows * seg * width, bytes_accessed=8 * rows * width, transcendentals=0
        ),
        name="attend",
    )(facts, q, k, v, ks, vs)


def keys_for(local, lengths, seq_count):
    rows, width = local.shape[-2:]
    pad = ((0, 0), (0, SUMM_ROWS - SUMM), (0, 0))
    if rows == SLOT:
        here = lengths[lax.axis_index("seq")]
        summary = jnp.pad(lax.dynamic_slice(local, (0, here, 0), (2, SUMM, width)), pad)
        moves = [(i, i + 1) for i in range(seq_count - 1)]
        return local, lax.ppermute(summary, "seq", moves)
    everything = lax.all_gather(local, "seq", axis=1, tiled=True)
    segment = lax.axis_index("seq") * rows // SLOT
    own = lax.dynamic_slice(everything, (0, segment * SLOT, 0), (2, SLOT, width))
    summary = lax.dynamic_slice(everything, (0, lengths[0], 0), (2, SUMM, width))
    return own, jnp.pad(summary, pad)


def keys_back(own, summary, rows, lengths, seq_count):
    width = own.shape[-1]
    summary = summary[:, :SUMM]
    if rows == SLOT:
        moves = [(i + 1, i) for i in range(seq_count - 1)]
        arrived = lax.ppermute(summary, "seq", moves)
        here = lengths[lax.axis_index("seq")]
        old = lax.dynamic_slice(own, (0, here, 0), (2, SUMM, width))
        new = (old.astype(jnp.float32) + arrived).astype(jnp.bfloat16)
        return lax.dynamic_update_slice(own, new, (0, here, 0))
    segment = lax.axis_index("seq") * rows // SLOT
    everything = jnp.zeros((2, TOKENS, width), jnp.float32)
    everything = lax.dynamic_update_slice(
        everything, own.astype(jnp.float32), (0, segment * SLOT, 0)
    )
    old = lax.dynamic_slice(everything, (0, lengths[0], 0), (2, SUMM, width))
    added = jnp.where(segment > 0, summary, 0.0)
    everything = lax.dynamic_update_slice(everything, old + added, (0, lengths[0], 0))
    return lax.psum_scatter(
        everything.astype(jnp.bfloat16), "seq", scatter_dimension=1, tiled=True
    )


class Line:
    def __init__(self, count, half, multiply, finish, out, part, moving, sems):
        self.count, self.half, self.multiply, self.finish = count, half, multiply, finish
        self.out, self.part, self.moving = out, part, moving
        self.up_sent, self.up_got, self.down_sent, self.down_got, self.local = sems
        self.me = lax.axis_index("mp")
        self.pieces = half // PIECE
        self.per_group = part.shape[2] // PIECE
        self.steps = self.pieces + 2 * SKEW * (count - 1)

    @staticmethod
    def scratch(half, features):
        pieces = half // PIECE
        group = 160 if half % 160 == 0 else PIECE
        dma = lambda *shape: pltpu.SemaphoreType.DMA(shape)
        return [
            pltpu.VMEM((2, 2, group, features), jnp.float32),
            pltpu.VMEM((2, half, features), jnp.bfloat16),
            dma(2, pieces),
            dma(2, pieces),
            dma(2, pieces),
            dma(2, pieces),
            dma(pieces),
        ]

    def place(self, flow):
        return self.count - 1 - self.me if flow == 0 else self.me

    def greet(self, barrier):
        me = self.me

        @pl.when(me > 0)
        def _():
            pl.semaphore_signal(barrier, inc=1, device_id={"mp": me - 1}, device_id_type=MESH)

        @pl.when(me < self.count - 1)
        def _():
            pl.semaphore_signal(barrier, inc=1, device_id={"mp": me + 1}, device_id_type=MESH)

    def meet(self, barrier, others=0):
        ends = (self.me == 0) | (self.me == self.count - 1)

        @pl.when(ends)
        def _():
            pl.semaphore_wait(barrier, 1 + others)

        @pl.when(jnp.logical_not(ends))
        def _():
            pl.semaphore_wait(barrier, 2 + others)

    def first(self):
        for flow in range(2):
            self.part[flow, 0] = self.multiply(flow, 0)

    def onward(self, flow, k):
        here = self.moving.at[flow, pl.ds(k * PIECE, PIECE)]
        return pltpu.make_async_remote_copy(
            src_ref=here,
            dst_ref=here,
            send_sem=self.up_sent.at[flow, k],
            recv_sem=self.up_got.at[flow, k],
            device_id={"mp": self.me - 1 if flow == 0 else self.me + 1},
            device_id_type=MESH,
        )

    def back(self, flow, k, owner):
        rows = self.out.at[pl.ds(flow * self.half + k * PIECE, PIECE)]
        return pltpu.make_async_remote_copy(
            src_ref=self.moving.at[flow, pl.ds(k * PIECE, PIECE)] if owner else rows,
            dst_ref=rows,
            send_sem=self.down_sent.at[flow, k],
            recv_sem=self.down_got.at[flow, k],
            device_id={"mp": self.me + 1 if flow == 0 else self.me - 1},
            device_id_type=MESH,
        )

    def keep(self, flow, k):
        return pltpu.make_async_copy(
            self.moving.at[flow, pl.ds(k * PIECE, PIECE)],
            self.out.at[pl.ds(flow * self.half + k * PIECE, PIECE)],
            self.local.at[k],
        )

    def step(self, t):
        last = self.count - 1
        for flow in range(2):
            place = self.place(flow)
            k = t - SKEW * place
            here = pl.ds(pl.multiple_of(k * PIECE, PIECE), PIECE)
            busy = (k >= 0) & (k < self.pieces)

            def mine():
                slot = (k // self.per_group) % 2
                inner = pl.ds(pl.multiple_of((k % self.per_group) * PIECE, PIECE), PIECE)
                return self.part[flow, slot, inner, :]

            @pl.when(busy & (place == 0))
            def _():
                self.moving[flow, here, :] = mine().astype(jnp.bfloat16)
                self.onward(flow, k).start()

            @pl.when(busy & (place > 0) & (place < last))
            def _():
                self.onward(flow, k).wait_recv()
                total = mine() + self.moving[flow, here, :].astype(jnp.float32)
                self.moving[flow, here, :] = total.astype(jnp.bfloat16)
                self.onward(flow, k).start()

            @pl.when(busy & (place == last))
            def _():
                self.onward(flow, k).wait_recv()
                total = mine() + self.moving[flow, here, :].astype(jnp.float32)
                self.moving[flow, here, :] = self.finish(flow, k, total).astype(jnp.bfloat16)
                self.back(flow, k, True).start()
                self.keep(flow, k).start()

        for flow in range(2):
            place = self.place(flow)
            j = t - SKEW * (2 * last - place)

            @pl.when((j >= 0) & (j < self.pieces) & (place < last))
            def _():
                self.back(flow, j, False).wait_recv()

                @pl.when(place > 0)
                def _():
                    self.back(flow, j, False).start()

        for flow in range(2 if self.multiply else 0):
            k = t - SKEW * self.place(flow)
            g = k // self.per_group + 1

            @pl.when((k >= 0) & (k % self.per_group == 0) & (g < self.pieces // self.per_group))
            def _():
                self.part[flow, g % 2] = self.multiply(flow, g)

    def settle(self):
        def one(k, carry):
            for flow in range(2):
                place = self.place(flow)

                @pl.when(place < self.count - 1)
                def _():
                    self.onward(flow, k).wait_send()

                    @pl.when(place > 0)
                    def _():
                        self.back(flow, k, False).wait_send()

                @pl.when(place == self.count - 1)
                def _():
                    self.back(flow, k, True).wait_send()
                    self.keep(flow, k).wait()

            return carry

        lax.fori_loop(0, self.pieces, one, 0)


def group_product(lefts, right, dims, half, group):
    def multiply(flow, g):
        rows = pl.ds(pl.multiple_of(flow * half + g * group, 16), group)
        at, total = 0, None
        for left in lefts:
            depth = left.shape[1]
            cut = right[:, at : at + depth] if dims == NT else right[at : at + depth, :]
            product = mm(left[rows, :], cut, dims)
            total = product if total is None else total + product
            at += depth
        return total

    return multiply


def line_kernel(count, half, dims, n_left, n_extra, n_owned, n_acc, finish, sides, *refs):
    refs = list(refs)
    take = lambda n: [refs.pop(0) for _ in range(n)]
    lefts, (right,), extras = take(n_left), take(1), take(n_extra)
    side_in = [take(side.n_in) for side in sides]
    (out,), owned, accs = take(1), take(n_owned), take(1 if n_acc else 0)
    side_out = [take(side.n_out) for side in sides]
    part, moving, sems = *take(2), take(5)
    multiply = group_product(lefts, right, dims, half, part.shape[2])
    ending = lambda flow, k, total: finish(flow, k, total, extras, owned, accs)
    line = Line(count, half, multiply, ending, out, part, moving, sems)
    jobs = [
        side(ins, outs, take(len(side.scratch_shapes)), accs)
        for side, ins, outs in zip(sides, side_in, side_out)
    ]
    barrier = pltpu.get_barrier_semaphore()
    line.greet(barrier)
    for job in jobs:
        job.greet(barrier)
    if n_acc:
        accs[0][...] = jnp.zeros_like(accs[0])
    for job in jobs:
        job.first()
    line.first()
    line.meet(barrier, sum(job.others for job in jobs))

    def step(t, carry):
        line.step(t)
        for job in jobs:
            job.step(t)
        return carry

    lax.fori_loop(0, max([line.steps] + [job.steps for job in jobs]), step, 0)
    line.settle()
    for job in jobs:
        job.settle()


class Nothing:
    n_in = n_out = others = steps = 0
    operands, in_specs, out_shape, out_specs, scratch_shapes = (), (), (), (), ()

    def __call__(self, ins, outs, scratch, accs):
        return self

    def greet(self, barrier):
        pass

    def first(self):
        pass

    def step(self, t):
        pass

    def settle(self):
        pass


VMEM = pl.BlockSpec(memory_space=pltpu.VMEM)
ANY = pl.BlockSpec(memory_space=pl.ANY)
SMEM = pl.BlockSpec(memory_space=pltpu.SMEM)


def line_sum(number, count, lefts, right, dims, extras, n_owned, n_acc, finish, name, sides):
    rows = lefts[0].shape[0]
    features = right.shape[1 if dims == NN else 0]
    half = rows // 2
    acc = [jax.ShapeDtypeStruct((n_acc, 8, features), jnp.float32)] if n_acc else []
    return pl.pallas_call(
        functools.partial(
            line_kernel,
            count,
            half,
            dims,
            len(lefts),
            len(extras),
            n_owned,
            n_acc,
            finish,
            sides,
        ),
        in_specs=[VMEM] * (len(lefts) + 1 + len(extras)) + [s for side in sides for s in side.in_specs],
        out_specs=[ANY] + [VMEM] * (n_owned + len(acc)) + [s for side in sides for s in side.out_specs],
        out_shape=[jax.ShapeDtypeStruct((rows, features), jnp.bfloat16)]
        + [jax.ShapeDtypeStruct((half, features), jnp.float32)] * n_owned
        + acc
        + [s for side in sides for s in side.out_shape],
        scratch_shapes=Line.scratch(half, features) + [s for side in sides for s in side.scratch_shapes],
        compiler_params=pltpu.CompilerParams(
            collective_id=number, has_side_effects=True, vmem_limit_bytes=62 * MIB
        ),
        cost_estimate=pl.CostEstimate(
            flops=2 * rows * features * sum(left.shape[1] for left in lefts),
            bytes_accessed=4 * rows * features,
            transcendentals=0,
        ),
        name=name,
    )(*lefts, right, *extras, *[value for side in sides for value in side.operands])


def piece_rows(flow, k, half):
    return pl.ds(pl.multiple_of(flow * half + k * PIECE, PIECE), PIECE)


def fold(values):
    return jnp.sum(values.reshape(-1, 8, values.shape[-1]), axis=0)


def finish_input(flow, k, total, extras, owned, accs):
    hidden, grad, gain = extras
    (acc,) = accs
    half = grad.shape[0]
    normed, inverse = norm_stats(hidden[piece_rows(flow, k, half), :].astype(jnp.float32))
    acc[0] += fold(total * normed)
    acc[1] += fold(total)
    return grad[piece_rows(0, k, half), :] + norm_back(total, normed, inverse, gain[...])


def finish_out(flow, k, total, extras, owned, accs):
    residual, bias = extras
    half = residual.shape[0]
    return residual[piece_rows(0, k, half), :] + total + bias[...]


class AttendBack(Nothing):
    n_in, n_out = 8, 5

    def __init__(self, facts, q, k, v, ks, vs, do, lse):
        rows, width = q.shape
        seg = k.shape[0]
        self.operands = (facts, q, k, v, ks, vs, do, lse)
        self.in_specs = (SMEM,) + (VMEM,) * 7
        low = lambda n: jax.ShapeDtypeStruct((n, width), jnp.bfloat16)
        wide = lambda n: jax.ShapeDtypeStruct((n, width), jnp.float32)
        self.out_shape = (low(rows), low(seg), low(seg), wide(SUMM_ROWS), wide(SUMM_ROWS))
        self.out_specs = (VMEM,) * 5
        self.scratch_shapes = (
            pltpu.VMEM((seg, PAIR), jnp.float32),
            pltpu.VMEM((seg, PAIR), jnp.float32),
            pltpu.VMEM((PAIR, seg), jnp.bfloat16),
        )
        self.bq = query_block(rows)
        self.blocks = rows // self.bq
        self.pairs = width // PAIR
        self.steps = self.pairs * self.blocks
        self.causal = rows == seg

    def __call__(self, ins, outs, scratch, accs):
        self.ins, self.outs, self.scratch = ins, outs, scratch
        return self

    def step(self, t):
        pair = t // self.blocks
        for block in range(self.blocks):

            @pl.when((t < self.steps) & (t % self.blocks == block))
            def _():
                self.unit(pair, block)

    def unit(self, pair, block):
        facts, q_ref, k_ref, v_ref, ks_ref, vs_ref, do_ref, lse_ref = self.ins
        dq_ref, dk_ref, dv_ref, dks_ref, dvs_ref = self.outs
        dk_acc, dv_acc, k_t = self.scratch
        seg, bq = k_ref.shape[0], self.bq
        cols = pl.ds(pl.multiple_of(pair * PAIR, PAIR), PAIR)
        scale = jnp.bfloat16(HDIM**-0.5)
        low_half = lax.broadcasted_iota(jnp.int32, (PAIR, 1), 0) < HDIM
        if block == 0:
            k_t[...] = (k_ref[:, cols] * scale).T
            dk_acc[...] = jnp.zeros_like(dk_acc)
            dv_acc[...] = jnp.zeros_like(dv_acc)
            dks_ref[:, cols] = jnp.zeros((SUMM_ROWS, PAIR), jnp.float32)
            dvs_ref[:, cols] = jnp.zeros((SUMM_ROWS, PAIR), jnp.float32)
        ks, vs = ks_ref[:, cols], vs_ref[:, cols]
        ks_t = (ks * scale).T
        nk = (block + 1) * bq if self.causal else seg
        here = slice(block * bq, (block + 1) * bq)
        own, earlier = key_masks(facts, block, self.blocks * bq, bq, nk)
        q = q_ref[here, cols] * scale
        do = do_ref[here, cols]
        k, v = k_ref[:nk, cols], v_ref[:nk, cols]
        grads = []
        for head in range(2):
            qh = jnp.where(head_lanes(head), q, jnp.zeros_like(q))
            doh = jnp.where(head_lanes(head), do, jnp.zeros_like(do))
            lse = lse_ref[pair, head : head + 1, here]
            p = jnp.exp(jnp.where(own, mm(k, qh, NT), MASKED) - lse)
            p2 = jnp.exp(jnp.where(earlier, mm(ks, qh, NT), MASKED) - lse)
            dp = mm(v, doh, NT)
            dp2 = mm(vs, doh, NT)
            delta = jnp.sum(p * dp, axis=0, keepdims=True) + jnp.sum(p2 * dp2, axis=0, keepdims=True)
            ds = (p * (dp - delta)).astype(jnp.bfloat16)
            ds2 = (p2 * (dp2 - delta)).astype(jnp.bfloat16)
            dv_acc[:nk, :] += mm(p.astype(jnp.bfloat16), doh)
            dk_acc[:nk, :] += mm(ds, qh)
            dvs_ref[:, cols] += mm(p2.astype(jnp.bfloat16), doh)
            dks_ref[:, cols] += mm(ds2, qh)
            grads.append(mm(k_t[:, :nk], ds) + mm(ks_t, ds2))
        joined = jnp.where(low_half, grads[0], grads[1])
        dq_ref[here, cols] = joined.T.astype(jnp.bfloat16)
        if block == self.blocks - 1:
            dk_ref[:, cols] = dk_acc[...].astype(jnp.bfloat16)
            dv_ref[:, cols] = dv_acc[...].astype(jnp.bfloat16)


class Spread(Nothing):
    others = 3
    n_in, n_out = 10, 4
    block = 256
    lag = (2, 5, 8)

    def __init__(self, factors, columns):
        rows, features = factors[0].shape
        block, half = self.block, self.block // 2
        assert features == 8 * block
        self.rows = rows
        self.operands = tuple(factors) + tuple(right for _, right, _, _ in columns)
        self.in_specs = (ANY,) * self.n_in
        self.table, self.phases = [], {}
        at, widths = 0, [0] * 4
        for number, (left, right, result, place) in enumerate(columns):
            self.phases.setdefault(left, at)
            self.table.append((number, at, at + right.shape[1] // block, result, place))
            at += right.shape[1] // block
            widths[result] += right.shape[1]
        self.chunks = at
        self.steps = at + self.lag[2]
        self.across = (True, False, False, True)
        self.out_shape = tuple(
            jax.ShapeDtypeStruct((block, n) if across else (n, block), jnp.float32)
            for n, across in zip(widths, self.across)
        )
        self.out_specs = (ANY,) * 4
        low = lambda *shape: pltpu.VMEM(shape, jnp.bfloat16)
        wide = lambda *shape: pltpu.VMEM(shape, jnp.float32)
        dma = lambda n: pltpu.SemaphoreType.DMA((n,))
        self.scratch_shapes = (
            low(2, rows, features),
            low(2, rows, block),
            low(3, 2, block, 2 * block),
            wide(3, 2, block, 2 * block),
            low(4, 2, block, 2 * block),
            low(3, half, 2 * block),
            low(3, 2, half, block),
            wide(3, half, 2 * block),
            wide(3, 2, half, block),
            low(6, half, 2 * block),
            low(6, 2, half, block),
            low(3, 2, half, block),
            wide(3, 2, half, block),
            low(6, 2, half, block),
            wide(3, block, block),
            dma(2),
            dma(2),
            dma(3),
            dma(4),
            dma(3),
            dma(6),
            dma(3),
            dma(6),
            dma(3),
            dma(6),
            dma(3),
            dma(6),
            dma(3),
        )

    def __call__(self, ins, outs, scratch, accs):
        self.lefts, self.rights, self.outs = ins[:4], ins[4:], outs
        (
            self.x_buf,
            self.y_buf,
            self.s1,
            self.own,
            self.r1,
            self.s2x,
            self.s2y,
            self.top,
            self.low,
            self.r2x,
            self.r2y,
            self.s3,
            self.kept,
            self.r3,
            self.tile,
            self.x_sem,
            self.y_sem,
            self.s1_sem,
            self.r1_sem,
            self.s2x_sem,
            self.r2x_sem,
            self.s2y_sem,
            self.r2y_sem,
            self.s3y_sem,
            self.r3y_sem,
            self.s3x_sem,
            self.r3x_sem,
            self.out_sem,
        ) = scratch
        item, seq = lax.axis_index("item"), lax.axis_index("seq")
        self.core, self.x, self.y = item % 2, item // 2, seq
        self.to_core = {"item": item + 1 - 2 * self.core}
        self.to_x = {"item": item + 2 - 4 * self.x}
        self.to_y = {"seq": 1 - seq}
        return self

    def greet(self, barrier):
        for to in (self.to_core, self.to_x, self.to_y):
            pl.semaphore_signal(barrier, inc=1, device_id=to, device_id_type=MESH)


    def left_copy(self, left):
        slot = list(self.phases).index(left) % 2
        return pltpu.make_async_copy(self.lefts[left], self.x_buf.at[slot], self.x_sem.at[slot])

    def right_copy(self, m, act):
        for number, start, stop, _, _ in self.table:

            @pl.when((m >= start) & (m < stop))
            def _():
                cols = pl.ds(pl.multiple_of((m - start) * self.block, self.block), self.block)
                act(
                    pltpu.make_async_copy(
                        self.rights[number].at[:, cols], self.y_buf.at[m % 2], self.y_sem.at[m % 2]
                    )
                )

    def out_copy(self, m, act):
        for _, start, stop, result, place in self.table:

            @pl.when((m >= start) & (m < stop))
            def _():
                cols = pl.ds(
                    pl.multiple_of(place + (m - start) * self.block, self.block), self.block
                )
                out = self.outs[result]
                out = out.at[:, cols] if self.across[result] else out.at[cols, :]
                act(pltpu.make_async_copy(self.tile.at[m % 3], out, self.out_sem.at[m % 3]))

    def remote(self, src, dst, send, recv, to):
        return pltpu.make_async_remote_copy(
            src_ref=src, dst_ref=dst, send_sem=send, recv_sem=recv, device_id=to, device_id_type=MESH
        )

    def first_copy(self, m):
        return self.remote(
            self.s1.at[m % 3],
            self.r1.at[m % 4],
            self.s1_sem.at[m % 3],
            self.r1_sem.at[m % 4],
            self.to_core,
        )

    def second_copies(self, m):
        return (
            self.remote(
                self.s2x.at[m % 3],
                self.r2x.at[m % 6],
                self.s2x_sem.at[m % 3],
                self.r2x_sem.at[m % 6],
                self.to_x,
            ),
            self.remote(
                self.s2y.at[m % 3],
                self.r2y.at[m % 6],
                self.s2y_sem.at[m % 3],
                self.r2y_sem.at[m % 6],
                self.to_y,
            ),
        )

    def third_copies(self, m):
        return (
            self.remote(
                self.s3.at[m % 3, 0],
                self.r3.at[m % 6, 0],
                self.s3y_sem.at[m % 3],
                self.r3y_sem.at[m % 6],
                self.to_y,
            ),
            self.remote(
                self.s3.at[m % 3, 1],
                self.r3.at[m % 6, 1],
                self.s3x_sem.at[m % 3],
                self.r3x_sem.at[m % 6],
                self.to_x,
            ),
        )

    def first(self):
        for left in list(self.phases)[:2]:
            self.left_copy(left).start()
        self.right_copy(0, lambda copy: copy.start())

    def step(self, t):
        for stage, lag in ((self.fourth, 8), (self.third, 5), (self.second, 2), (self.multiply, 0)):
            m = t - lag

            @pl.when((m >= 0) & (m < self.chunks))
            def _():
                stage(m)

    def multiply(self, m):
        order = list(self.phases)
        for number, left in enumerate(order):

            @pl.when(m == self.phases[left])
            def _():
                self.left_copy(left).wait()
                if 1 <= number < len(order) - 1:
                    self.left_copy(order[number + 1]).start()

        @pl.when(m + 1 < self.chunks)
        def _():
            self.right_copy(m + 1, lambda copy: copy.start())

        self.right_copy(m, lambda copy: copy.wait())

        @pl.when(m >= 3)
        def _():
            self.first_copy(m - 3).wait_send()

        phase = sum((m >= start).astype(jnp.int32) for start in self.phases.values()) - 1
        turned = self.y_buf[m % 2].T
        wide = 2 * self.block

        def product(x, core):
            cols = pl.ds(pl.multiple_of(x * 2 * wide + core * wide, wide), wide)
            return mm(turned, self.x_buf[phase % 2, :, cols])

        for x in range(2):
            self.s1[m % 3, x] = product(x, 1 - self.core).astype(jnp.bfloat16)
        self.first_copy(m).start()
        for x in range(2):
            self.own[m % 3, x] = product(x, self.core)

    def second(self, m):
        half = self.block // 2

        @pl.when(m >= 3)
        def _():
            for copy in self.second_copies(m - 3):
                copy.wait_send()

        self.first_copy(m).wait_recv()
        slot = m % 3
        here, there = self.x, 1 - self.x
        mine = pl.ds(pl.multiple_of(self.y * self.block, self.block), self.block)
        others = pl.ds(pl.multiple_of((1 - self.y) * self.block, self.block), self.block)
        added = lambda x, rows, cols: (
            self.own[slot, x, rows, cols] + self.r1[m % 4, x, rows, cols].astype(jnp.float32)
        )
        upper, lower, every = pl.ds(0, half), pl.ds(half, half), pl.ds(0, 2 * self.block)
        self.s2x[slot] = added(there, upper, every).astype(jnp.bfloat16)
        for x in range(2):
            self.s2y[slot, x] = added(x, lower, others).astype(jnp.bfloat16)
        for copy in self.second_copies(m):
            copy.start()
        self.top[slot] = added(here, upper, every)
        for x in range(2):
            self.low[slot, x] = added(x, lower, mine)

    def third(self, m):
        @pl.when(m >= 3)
        def _():
            for copy in self.third_copies(m - 3):
                copy.wait_send()

        for copy in self.second_copies(m):
            copy.wait_recv()
        slot, got = m % 3, m % 6
        mine = pl.ds(pl.multiple_of(self.y * self.block, self.block), self.block)
        others = pl.ds(pl.multiple_of((1 - self.y) * self.block, self.block), self.block)
        top = lambda cols: self.top[slot, :, cols] + self.r2x[got, :, cols].astype(jnp.float32)
        low = lambda x: self.low[slot, x] + self.r2y[got, x].astype(jnp.float32)
        self.s3[slot, 0] = top(others).astype(jnp.bfloat16)
        self.s3[slot, 1] = low(1 - self.x).astype(jnp.bfloat16)
        for copy in self.third_copies(m):
            copy.start()
        self.kept[slot, 0] = top(mine)
        self.kept[slot, 1] = low(self.x)

    def fourth(self, m):
        @pl.when(m >= 3)
        def _():
            self.out_copy(m - 3, lambda copy: copy.wait())

        for copy in self.third_copies(m):
            copy.wait_recv()
        slot, half = m % 3, self.block // 2
        total = self.kept[slot] + self.r3[m % 6].astype(jnp.float32)
        total = total.reshape(self.block, self.block)
        across = jnp.zeros((), jnp.bool_)
        for _, start, stop, result, _ in self.table:
            if self.across[result]:
                across = across | ((m >= start) & (m < stop))

        @pl.when(across)
        def _():
            self.tile[slot] = total.T

        @pl.when(jnp.logical_not(across))
        def _():
            self.tile[slot] = total

        self.out_copy(m, lambda copy: copy.start())

    def settle(self):
        for m in range(self.chunks - 3, self.chunks):
            self.first_copy(m).wait_send()
            for copy in self.second_copies(m) + self.third_copies(m):
                copy.wait_send()
            self.out_copy(jnp.int32(m), lambda copy: copy.wait())


class Gather:
    others = 3

    def __init__(self, shards, fulls, sems, ready):
        self.shards, self.fulls, self.ready = shards, fulls, ready
        self.sent, self.got, self.local = sems
        item, seq = lax.axis_index("item"), lax.axis_index("seq")
        self.core, self.x, self.y = item % 2, item // 2, seq
        self.to_core = {"item": item + 1 - 2 * self.core}
        self.to_x = {"item": item + 2 - 4 * self.x}
        self.to_y = {"seq": 1 - seq}

    @staticmethod
    def sems(count=2):
        dma = lambda *shape: pltpu.SemaphoreType.DMA(shape)
        return [dma(count, 9), dma(count, 9), dma(count)]

    def greet(self, barrier):
        for to in (self.to_core, self.to_x, self.to_y):
            pl.semaphore_signal(barrier, inc=1, device_id=to, device_id_type=MESH)

    def spot(self, w, x, core, y, part=None):
        size = self.shards[w].shape[w]
        at = pl.ds(pl.multiple_of(((2 * x + core) * 2 + y) * size, size), size)
        if w == 0:
            if part is not None:
                half = size // 2
                start = ((2 * x + core) * 2 + y) * size + part * half
                at = pl.ds(pl.multiple_of(start, half), half)
            return self.fulls[0].at[at, :]
        rows = self.fulls[1].shape[0]
        if part is not None:
            return self.fulls[1].at[pl.ds(part * (rows // 2), rows // 2), at]
        return self.fulls[1].at[:, at]

    def message(self, w, number, src, dst, to):
        return pltpu.make_async_remote_copy(
            src_ref=src,
            dst_ref=dst,
            send_sem=self.sent.at[w, number],
            recv_sem=self.got.at[w, number],
            device_id=to,
            device_id_type=MESH,
        )

    def messages(self, w):
        c, x, y = self.core, self.x, self.y
        own, spot = self.shards[w].at[...], functools.partial(self.spot, w)
        plan = (
            (own, spot(x, c, y), spot(x, 1 - c, y), self.to_core),
            (own, spot(x, c, y), spot(1 - x, c, y), self.to_x),
            (own, spot(x, c, y), spot(x, c, 1 - y), self.to_y),
            (None, spot(1 - x, c, y, 0), spot(1 - x, c, 1 - y, 0), self.to_y),
            (None, spot(x, c, 1 - y, 1), spot(1 - x, c, 1 - y, 1), self.to_x),
            (None, spot(1 - x, c, y), spot(1 - x, 1 - c, y), self.to_core),
            (None, spot(x, c, 1 - y), spot(x, 1 - c, 1 - y), self.to_core),
            (None, spot(1 - x, c, 1 - y, 0), spot(1 - x, 1 - c, 1 - y, 0), self.to_core),
            (None, spot(1 - x, c, 1 - y, 1), spot(1 - x, 1 - c, 1 - y, 1), self.to_core),
        )
        return [
            (
                self.message(w, number, out if src is None else src, out, to),
                self.message(w, number, landing, landing, to),
            )
            for number, (src, out, landing, to) in enumerate(plan)
        ]

    def send(self, w, numbers):
        messages = self.messages(w)
        for number in numbers:
            messages[number][0].start()

    def receive(self, w, numbers):
        messages = self.messages(w)
        for number in numbers:
            messages[number][1].wait_recv()

    def mine(self, w):
        return pltpu.make_async_copy(
            self.shards[w], self.spot(w, self.x, self.core, self.y), self.local.at[w]
        )

    def first(self):
        for w in range(len(self.shards)):
            self.mine(w).start()

    def begin(self):
        for w in range(2):
            self.send(w, (1, 2, 0))

    def step(self, t):
        for w, at in ((0, self.ready * 5 // 16), (1, self.ready * 9 // 16)):

            @pl.when(t == at)
            def _():
                self.receive(w, (1, 2))
                self.send(w, (3, 4, 5, 6))

        for w, at in ((0, self.ready * 12 // 16), (1, self.ready * 15 // 16)):

            @pl.when(t == at)
            def _():
                self.receive(w, (3, 4))
                self.send(w, (7, 8))

        @pl.when(t == self.ready)
        def _():
            for w in range(2):
                self.receive(w, (0, 5, 6, 7, 8))
                self.mine(w).wait()

    def settle(self):
        for w in range(len(self.shards)):
            for out, _ in self.messages(w):
                out.wait_send()


class Load:
    others = 0

    def __init__(self, shards, fulls, sems, ready):
        self.ready = ready
        self.copies = [
            pltpu.make_async_copy(shard, full, sems[2].at[w])
            for w, (shard, full) in enumerate(zip(shards, fulls))
        ]

    sems = Gather.sems

    def greet(self, barrier):
        pass

    def first(self):
        for copy in self.copies:
            copy.start()

    def begin(self):
        pass

    def step(self, t):
        @pl.when(t == self.ready)
        def _():
            for copy in self.copies:
                copy.wait()

    def settle(self):
        pass


class Attend:
    bq = 128

    def __init__(self, half, facts, q, k, v, earlier, attended, lse):
        self.half, self.facts, self.q, self.k, self.v = half, facts, q, k, v
        self.earlier, self.attended, self.lse = earlier, attended, lse
        self.pairs = q.shape[1] // PAIR
        self.blocks = half // self.bq

    def first(self):
        def one(pair, carry):
            for flow in range(2):
                self.unit(pair, flow * self.blocks)
            return carry

        lax.fori_loop(0, self.pairs, one, 0)

    def step(self, t):
        def both(pair, block):
            for flow in range(2):
                self.unit(pair, flow * self.blocks + block)

        @pl.when(t < 2)
        def _():
            each = self.pairs // 2

            def one(i, carry):
                both((t % 2) * each + i, 1)
                return carry

            lax.fori_loop(0, each, one, 0)

        for block in range(2, self.blocks):
            start = self.pairs * (block - 2) + 2

            @pl.when((t >= start) & (t < start + self.pairs))
            def _():
                both(t - start, block)

    def unit(self, pair, block):
        bq, nk = self.bq, (block + 1) * self.bq
        cols = pl.ds(pl.multiple_of(pair * PAIR, PAIR), PAIR)
        here = slice(block * bq, nk)
        query = block * bq + lax.broadcasted_iota(jnp.int32, (1, 2 * bq), 1) % bq
        limit = jnp.minimum(query + 1, self.facts[1])
        own = lax.broadcasted_iota(jnp.int32, (nk, 2 * bq), 0) < limit
        earlier = lax.broadcasted_iota(jnp.int32, (SUMM_ROWS, 2 * bq), 0) < self.facts[2]
        q = self.q[here, cols] * jnp.bfloat16(HDIM**-0.5)
        q = jnp.concatenate([jnp.where(head_lanes(h), q, jnp.zeros_like(q)) for h in range(2)])
        s = jnp.where(own, mm(self.k[:nk, cols], q, NT), MASKED)
        s2 = jnp.where(earlier, mm(self.earlier[0, :, cols], q, NT), MASKED)
        top = jnp.maximum(jnp.max(s, axis=0, keepdims=True), jnp.max(s2, axis=0, keepdims=True))
        p = jnp.exp(s - top)
        p2 = jnp.exp(s2 - top)
        total = jnp.sum(p, axis=0, keepdims=True) + jnp.sum(p2, axis=0, keepdims=True)
        out = mm(self.v[:nk, cols].T, p.astype(jnp.bfloat16))
        out = (out + mm(self.earlier[1, :, cols].T, p2.astype(jnp.bfloat16))) / total
        lse = top + jnp.log(total)
        for head in range(2):
            self.lse[pair, head : head + 1, here] = lse[:, head * bq : (head + 1) * bq]
        low_half = lax.broadcasted_iota(jnp.int32, (PAIR, 1), 0) < HDIM
        joined = jnp.where(low_half, out[:, :bq], out[:, bq:])
        self.attended[here, cols] = joined.T.astype(jnp.bfloat16)


def ffn_kernel(count, half, weights_job, n_attend, *refs):
    if n_attend == 1:
        ffn_body(count, half, weights_job, None, *refs)
    else:
        facts, q, k, v, earlier, *rest = refs
        inputs, outputs, scratch = rest[:9], rest[9:20], rest[20:]
        *outputs, attended, lse = outputs
        job = Attend(half, facts, q, k, v, earlier, attended, lse)
        ffn_body(count, half, weights_job, job, attended, *inputs, *outputs, *scratch)


def ffn_body(
    count,
    half,
    weights_job,
    attention,
    attended,
    out_w,
    out_bias,
    mid_gain,
    mid_shift,
    up_bias,
    hidden,
    cotangent,
    up_shard,
    down_shard,
    mid,
    act,
    grad_pre,
    residual_out,
    branch,
    grad_out,
    down_out,
    acc,
    acc_up,
    part1,
    moving1,
    part2,
    moving2,
    rows_in,
    residual,
    up,
    down,
    mid_in,
    cot_in,
    act_out,
    pre_out,
    *sems,
):
    sems = list(sems)
    take = lambda n: [sems.pop(0) for _ in range(n)]
    sems1, sems2, weight_sems = take(5), take(5), take(3)
    in_sem, residual_sem, grad_sem, mid_sem, cot_sem, act_sem, pre_sem, down_sem = sems
    me = lax.axis_index("mp")
    group = part2.shape[2]
    blocks = 4
    block = up.shape[1] // blocks
    per_group = group // PIECE
    pieces = half // PIECE
    last = count - 1
    second = per_group + blocks + 2 * SKEW * (count - 1)
    weights = weights_job((up_shard, down_shard), (up, down), weight_sems, second - blocks - 1)
    piece = lambda k: pl.ds(pl.multiple_of(k * PIECE, PIECE), PIECE)
    owner = (me == 0) | (me == last)
    my_flow = jnp.where(me == 0, 0, 1)

    def piece_in(source, k, flow):
        return pltpu.make_async_copy(
            source.at[pl.ds(flow * half + k * PIECE, PIECE)], rows_in.at[piece(k)], in_sem.at[k]
        )

    def residual_copy(k):
        return pltpu.make_async_copy(
            residual.at[piece(k)], residual_out.at[piece(k)], residual_sem.at[k]
        )

    def grad_copy(k):
        return pltpu.make_async_copy(residual.at[piece(k)], grad_out.at[piece(k)], grad_sem.at[k])

    def finish_first(flow, k, total):
        piece_in(hidden, k, flow).wait()
        value = rows_in[piece(k), :].astype(jnp.float32) + total + out_bias[...]
        residual[piece(k), :] = value
        residual_copy(k).start()
        piece_in(cotangent, k, flow).start()
        return norm_stats(value)[0] * mid_gain[...] + mid_shift[...]

    def finish_second(flow, k, total):
        piece_in(cotangent, k, flow).wait()
        residual_copy(k).wait()
        normed, inverse = norm_stats(residual[piece(k), :])
        grad = rows_in[piece(k), :].astype(jnp.float32)
        grad = grad + norm_back(total, normed, inverse, mid_gain[...])
        residual[piece(k), :] = grad
        grad_copy(k).start()
        acc[0] += fold(total * normed)
        acc[1] += fold(total)
        acc[2] += fold(grad)
        return grad

    multiply = group_product([attended], out_w, NN, half, part1.shape[2])
    line1 = Line(count, half, multiply, finish_first, mid, part1, moving1, sems1)
    line2 = Line(count, half, None, finish_second, branch, part2, moving2, sems2)

    def group_rows(flow, g):
        return pl.ds(pl.multiple_of(flow * half + g * group, 16), group)

    def mid_fetch(flow, g, here):
        rows = pl.ds(pl.multiple_of(g * group, 16), group)
        source = moving1.at[flow, rows] if here else mid.at[group_rows(flow, g)]
        return pltpu.make_async_copy(source, mid_in.at[flow], mid_sem.at[flow])

    def cot_fetch(flow, g):
        return pltpu.make_async_copy(
            cotangent.at[group_rows(flow, g)], cot_in.at[flow], cot_sem.at[flow]
        )

    def act_copy(flow, g):
        return pltpu.make_async_copy(
            act_out.at[flow], act.at[group_rows(flow, g)], act_sem.at[flow]
        )

    def pre_copy(flow, g):
        return pltpu.make_async_copy(
            pre_out.at[flow], grad_pre.at[group_rows(flow, g)], pre_sem.at[flow]
        )

    def products(flow, g, number):
        @pl.when(number == 0)
        def _():
            mid_fetch(flow, g, False).wait()
            cot_fetch(flow, g).wait()

            @pl.when(g > 0)
            def _():
                act_copy(flow, g - 1).wait()
                pre_copy(flow, g - 1).wait()

        cols = pl.ds(pl.multiple_of(number * block, block), block)
        value, slope = gelu_parts(mm(mid_in[flow], up[:, cols]) + up_bias[:, cols])
        act_out[flow, :, cols] = value.astype(jnp.bfloat16)
        pre = (slope * mm(cot_in[flow], down[cols, :], NT)).astype(jnp.bfloat16)
        pre_out[flow, :, cols] = pre
        acc_up[:, cols] += fold(pre.astype(jnp.float32))
        product = mm(pre, up[:, cols], NT)

        @pl.when(number == 0)
        def _():
            part2[flow, g % 2] = product

        @pl.when(number > 0)
        def _():
            part2[flow, g % 2] += product

        @pl.when(number == blocks - 1)
        def _():
            act_copy(flow, g).start()
            pre_copy(flow, g).start()

    barrier = pltpu.get_barrier_semaphore()
    line1.greet(barrier)
    weights.greet(barrier)
    acc[...] = jnp.zeros_like(acc)
    acc_up[...] = jnp.zeros_like(acc_up)
    weights.first()

    @pl.when(owner)
    def _():
        def one(k, carry):
            piece_in(hidden, k, my_flow).start()
            return carry

        lax.fori_loop(0, pieces, one, 0)

    if attention is None:
        line1.first()
        line1.meet(barrier, weights.others)
        weights.begin()
    else:
        line1.meet(barrier, weights.others)
        weights.begin()
        attention.first()
        line1.first()

    def step(t, carry):
        if attention is not None:
            attention.step(t)
        line1.step(t)
        line2.step(t - second)
        weights.step(t)

        @pl.when(t == weights.ready + 1)
        def _():
            pltpu.make_async_copy(down, down_out, down_sem.at[0]).start()

        for flow in range(2):
            place = line1.place(flow)
            u = t - second - SKEW * place
            fetch = u + blocks + 1
            compute = u + blocks

            @pl.when((fetch >= 0) & (fetch % per_group == 0) & (fetch < pieces))
            def _():
                g = fetch // per_group
                cot_fetch(flow, g).start()

                @pl.when(place == last)
                def _():
                    mid_fetch(flow, g, True).start()

                @pl.when(place < last)
                def _():
                    mid_fetch(flow, g, False).start()

            @pl.when((compute >= 0) & (compute < pieces) & (compute % per_group < blocks))
            def _():
                products(flow, compute // per_group, compute % per_group)

        return carry

    lax.fori_loop(0, second + line2.steps, step, 0)
    line1.settle()
    line2.settle()
    weights.settle()
    pltpu.make_async_copy(down, down_out, down_sem.at[0]).wait()
    for flow in range(2):
        act_copy(flow, pieces // per_group - 1).wait()
        pre_copy(flow, pieces // per_group - 1).wait()

    @pl.when(owner)
    def _():
        def one(k, carry):
            grad_copy(k).wait()
            return carry

        lax.fori_loop(0, pieces, one, 0)


def ffn_sums(number, count, weights_job, attend_in, out_w, vectors, hidden, cotangent, up_w, down_w):
    rows, features = hidden.shape
    ff = up_w.shape[1]
    half = rows // 2
    pieces = half // PIECE
    low = lambda *shape: jax.ShapeDtypeStruct(shape, jnp.bfloat16)
    wide = lambda *shape: jax.ShapeDtypeStruct(shape, jnp.float32)
    attend_out = []
    if len(attend_in) > 1:
        width = attend_in[1].shape[1]
        attend_out = [low(rows, width), wide(width // PAIR, 2, rows)]
    first = Line.scratch(half, features)
    small = 64 if half % 64 == 0 else PIECE
    first[0] = pltpu.VMEM((2, 2, small, features), jnp.float32)
    second = Line.scratch(half, features)
    group = second[0].shape[2]
    dma = lambda n: pltpu.SemaphoreType.DMA((n,))
    return pl.pallas_call(
        functools.partial(ffn_kernel, count, half, weights_job, len(attend_in)),
        in_specs=[SMEM, VMEM, VMEM, VMEM, VMEM][-len(attend_in) :] + [VMEM] * 5 + [ANY] * 4,
        out_specs=[ANY] * 7 + [VMEM] * (2 + len(attend_out)),
        out_shape=[
            low(rows, features),
            low(rows, ff),
            low(rows, ff),
            wide(half, features),
            low(rows, features),
            wide(half, features),
            low(ff, features),
            wide(3, 8, features),
            wide(8, ff),
        ]
        + attend_out,
        scratch_shapes=first[:2]
        + second[:2]
        + [
            pltpu.VMEM((half, features), jnp.bfloat16),
            pltpu.VMEM((half, features), jnp.float32),
            pltpu.VMEM((features, ff), jnp.bfloat16),
            pltpu.VMEM((ff, features), jnp.bfloat16),
            pltpu.VMEM((2, group, features), jnp.bfloat16),
            pltpu.VMEM((2, group, features), jnp.bfloat16),
            pltpu.VMEM((2, group, ff), jnp.bfloat16),
            pltpu.VMEM((2, group, ff), jnp.bfloat16),
        ]
        + first[2:]
        + second[2:]
        + Gather.sems()
        + [dma(pieces), dma(pieces), dma(pieces), dma(2), dma(2), dma(2), dma(2), dma(1)],
        compiler_params=pltpu.CompilerParams(
            collective_id=number, has_side_effects=True, vmem_limit_bytes=62 * MIB
        ),
        cost_estimate=pl.CostEstimate(
            flops=6 * rows * features * ff, bytes_accessed=30 * rows * features, transcendentals=0
        ),
        name="ffn_sums",
    )(*attend_in, out_w, *vectors, hidden, cotangent, up_w, down_w)


def start_kernel(
    facts,
    hidden,
    gain,
    shift,
    bias,
    shard,
    out_shard,
    q_ref,
    k_ref,
    v_ref,
    earlier,
    normed_out,
    weight_out,
    out_whole,
    normed,
    weight,
    out_weight,
    total,
    summary,
    *sems,
):
    gather = Gather((shard, out_shard), (weight, out_weight), sems[:3], 0)
    summary_sent, summary_got, out_sems = sems[3:]
    rows = hidden.shape[0]
    width = q_ref.shape[1]
    size = shard.shape[0]
    chunk = 128
    barrier = pltpu.get_barrier_semaphore()
    gather.greet(barrier)
    gather.first()
    pl.semaphore_wait(barrier, gather.others)
    gather.send(0, (1, 2, 0))

    def norm(i, carry):
        here = pl.ds(pl.multiple_of(i * chunk, chunk), chunk)
        value = norm_stats(hidden[here, :].astype(jnp.float32))[0]
        normed[here, :] = (value * gain[...] + shift[...]).astype(jnp.bfloat16)
        return carry

    lax.fori_loop(0, rows // chunk, norm, 0)
    keep = pltpu.make_async_copy(normed, normed_out, out_sems.at[0])
    keep.start()
    c, x, y = gather.core, gather.x, gather.y

    def add(places, first=False, last=False):
        starts = [
            pl.multiple_of(((2 * px + pc) * 2 + py) * size, size) for px, pc, py in places
        ]

        def rows_of(i, carry):
            here = pl.ds(pl.multiple_of(i * chunk, chunk), chunk)
            for j, out in enumerate((q_ref, k_ref, v_ref)):
                cols = slice(j * width, (j + 1) * width)
                value = None if first else total[here, cols]
                for start in starts:
                    at = pl.ds(start, size)
                    product = mm(normed[here, at], weight[at, cols])
                    value = product if value is None else value + product
                if not last:
                    total[here, cols] = value
                elif j == 1:
                    out[here, :] = value.astype(jnp.bfloat16)
                else:
                    out[here, :] = (value + bias[j // 2 : j // 2 + 1, :]).astype(jnp.bfloat16)
            return carry

        lax.fori_loop(0, rows // chunk, rows_of, 0)

    gather.mine(0).wait()
    gather.receive(0, (0,))
    add(((x, c, y), (x, 1 - c, y)), first=True)
    gather.receive(0, (1, 2))
    gather.send(0, (3, 4, 5, 6))
    gather.send(1, (1, 2, 0))
    add(((1 - x, c, y), (x, c, 1 - y)))
    gather.receive(0, (5, 6))
    add(((1 - x, 1 - c, y), (x, 1 - c, 1 - y)))
    gather.receive(0, (3, 4))
    gather.send(0, (7, 8))
    add(((1 - x, c, 1 - y),))
    gather.receive(1, (1, 2))
    gather.send(1, (3, 4, 5, 6))
    gather.receive(0, (7, 8))
    store = pltpu.make_async_copy(weight, weight_out, out_sems.at[1])
    store.start()
    add(((1 - x, 1 - c, 1 - y),), last=True)

    shape = (SUMM_ROWS, rows)
    chosen = lax.broadcasted_iota(jnp.int32, shape, 1) == (
        facts[1] - SUMM + lax.broadcasted_iota(jnp.int32, shape, 0)
    )
    chosen = jnp.where(chosen, 1.0, 0.0).astype(jnp.bfloat16)
    summary[0] = mm(chosen, k_ref[...]).astype(jnp.bfloat16)
    summary[1] = mm(chosen, v_ref[...]).astype(jnp.bfloat16)
    swap = pltpu.make_async_remote_copy(
        src_ref=summary,
        dst_ref=earlier,
        send_sem=summary_sent.at[0],
        recv_sem=summary_got.at[0],
        device_id=gather.to_y,
        device_id_type=MESH,
    )
    swap.start()
    gather.receive(1, (3, 4))
    gather.send(1, (7, 8))
    gather.receive(1, (0, 5, 6, 7, 8))
    gather.mine(1).wait()
    store_out = pltpu.make_async_copy(out_weight, out_whole, out_sems.at[2])
    store_out.start()
    gather.settle()
    keep.wait()
    store.wait()
    swap.wait()
    store_out.wait()


def start(number, facts, hidden, gain, shift, bias, shard, out_shard):
    rows, features = hidden.shape
    width = bias.shape[1]
    low = lambda *shape: jax.ShapeDtypeStruct(shape, jnp.bfloat16)
    dma = lambda n: pltpu.SemaphoreType.DMA((n,))
    return pl.pallas_call(
        start_kernel,
        in_specs=[SMEM] + [VMEM] * 4 + [ANY] * 2,
        out_specs=[VMEM] * 3 + [ANY] * 4,
        out_shape=[low(rows, width)] * 3
        + [low(2, SUMM_ROWS, width), low(rows, features), low(features, 3 * width)]
        + [low(width, features)],
        scratch_shapes=[
            pltpu.VMEM((rows, features), jnp.bfloat16),
            pltpu.VMEM((features, 3 * width), jnp.bfloat16),
            pltpu.VMEM((width, features), jnp.bfloat16),
            pltpu.VMEM((rows, 3 * width), jnp.float32),
            pltpu.VMEM((2, SUMM_ROWS, width), jnp.bfloat16),
        ]
        + Gather.sems()
        + [dma(1), dma(1), dma(3)],
        compiler_params=pltpu.CompilerParams(
            collective_id=number, has_side_effects=True, vmem_limit_bytes=60 * MIB
        ),
        cost_estimate=pl.CostEstimate(
            flops=6 * rows * features * width, bytes_accessed=16 * rows * features, transcendentals=0
        ),
        name="start",
    )(facts, hidden, gain, shift, bias, shard, out_shard)


class SmallSums(Nothing):
    n_in = n_out = 1

    def __init__(self, sizes, shared, start, values):
        self.stages = tuple(
            (axis, 1 << bit) for axis, size in sizes for bit in range(size.bit_length() - 1)
        )
        self.shared, self.start = shared, start
        self.others = len(self.stages)
        self.steps = start + self.others + 1
        self.operands = (values,)
        self.in_specs = self.out_specs = (VMEM,)
        self.out_shape = (jax.ShapeDtypeStruct(values.shape, jnp.float32),)
        buffers = pltpu.VMEM((self.others, *values.shape), jnp.float32)
        sems = pltpu.SemaphoreType.DMA((self.others,))
        self.scratch_shapes = (buffers, buffers, sems, sems)

    def __call__(self, ins, outs, scratch, accs):
        (self.own,), (self.out,), (self.acc,) = ins, outs, accs
        self.sent, self.got, self.send_sem, self.recv_sem = scratch
        return self

    def partner(self, axis, bit):
        index = lax.axis_index(axis)
        return {axis: index + bit - 2 * bit * ((index // bit) % 2)}

    def greet(self, barrier):
        for axis, bit in self.stages:
            pl.semaphore_signal(
                barrier, inc=1, device_id=self.partner(axis, bit), device_id_type=MESH
            )

    def copy(self, number):
        return pltpu.make_async_remote_copy(
            src_ref=self.sent.at[number],
            dst_ref=self.got.at[number],
            send_sem=self.send_sem.at[number],
            recv_sem=self.recv_sem.at[number],
            device_id=self.partner(*self.stages[number]),
            device_id_type=MESH,
        )

    def step(self, t):
        @pl.when(t == self.start)
        def _():
            self.sent[0] = self.own[...]
            for number in range(self.acc.shape[0]):
                self.sent[0, 3 + number : 4 + number, :] = jnp.sum(
                    self.acc[number], axis=0, keepdims=True
                )
            self.copy(0).start()

        row = lax.broadcasted_iota(jnp.int32, self.own.shape, 0)
        for number, (axis, _) in enumerate(self.stages):

            @pl.when(t == self.start + 1 + number)
            def _():
                self.copy(number).wait()
                total = self.sent[number] + self.got[number]
                if axis == "mp":
                    total = jnp.where(row < self.shared, total, self.sent[number])
                if number + 1 < len(self.stages):
                    self.sent[number + 1] = total
                    self.copy(number + 1).start()
                else:
                    self.out[...] = total


def gradients_over(group, lefts, columns):
    over_rows = lambda left, right: mm(left, right, (((0,), (0,)), ((), ()))).astype(jnp.bfloat16)
    parts = [[] for _ in range(4)]
    for left, right, result, _ in columns:
        across = result in (0, 3)
        product = over_rows(lefts[left], right) if across else over_rows(right, lefts[left])
        parts[result].append(product)
    return [
        lax.psum_scatter(
            jnp.concatenate(part, axis=1),
            group,
            scatter_dimension=0 if result in (0, 3) else 1,
            tiled=True,
        ).astype(jnp.float32)
        for result, part in enumerate(parts)
    ]


def body(
    item_count,
    seq_count,
    mp_count,
    hidden_in,
    cotangent,
    seg_lengths,
    pre_gain,
    pre_shift,
    qkv_weight,
    qv_bias,
    out_weight,
    out_bias,
    mid_gain,
    mid_shift,
    up_weight,
    up_bias,
    down_weight,
    down_bias,
):
    group = ("item", "seq")
    width = qkv_weight.shape[2]
    gathered = lambda weight, axis: lax.all_gather(weight, group, axis=axis, tiled=True)
    hidden = hidden_in[0].astype(jnp.float32)
    lengths = seg_lengths[0]
    rows = hidden.shape[0]
    first_row = lax.axis_index("seq") * rows
    segment = first_row // SLOT
    facts = jnp.stack(
        [
            first_row % SLOT,
            lengths[segment] + SUMM,
            jnp.where(segment > 0, SUMM, 0),
        ]
    ).astype(jnp.int32)

    ours = (item_count, seq_count) == (4, 2) and rows == SLOT
    row = lambda vector: vector[None, :]
    shard = qkv_weight.reshape(-1, 3 * width)
    if ours:
        q, k, v, summary, normed, qkv_full, out_full = start(
            5, facts, hidden_in[0], row(pre_gain), row(pre_shift), qv_bias, shard, out_weight
        )
        attend_in = (facts, q, k, v, summary)
        tables = (k, v, summary[0], summary[1])
    else:
        qkv_full = gathered(shard, 0)
        out_full = gathered(out_weight, 1)
        normed = (norm_stats(hidden)[0] * pre_gain + pre_shift).astype(jnp.bfloat16)
        q = (mm(normed, qkv_full[:, :width]) + qv_bias[0]).astype(jnp.bfloat16)
        k = mm(normed, qkv_full[:, width : 2 * width]).astype(jnp.bfloat16)
        v = (mm(normed, qkv_full[:, 2 * width :]) + qv_bias[1]).astype(jnp.bfloat16)
        own, summary = keys_for(jnp.stack([k, v]), lengths, seq_count)
        tables = (own[0], own[1], summary[0], summary[1])
        attended, log_total = attend(facts, q, *tables)
        attend_in = (attended,)

    grad_down = cotangent[0]
    (
        mid_low,
        act_low,
        grad_pre,
        residual,
        grad_branch,
        grad_residual,
        down_full,
        mid_sums,
        up_sums,
        *attend_out,
    ) = ffn_sums(
        1,
        mp_count,
        Gather if ours else Load,
        attend_in,
        out_full,
        (row(out_bias), row(mid_gain), row(mid_shift), row(up_bias)),
        hidden_in[0],
        grad_down,
        up_weight if ours else gathered(up_weight, 0),
        down_weight if ours else gathered(down_weight, 1),
    )
    if ours:
        attended, log_total = attend_out
    grad_attended = mm(grad_branch, out_full, NT).astype(jnp.bfloat16)
    hidden_out, dq, dk, dv, dks, dvs = line_sum(
        3,
        mp_count,
        [act_low],
        down_full,
        NN,
        [residual, row(down_bias)],
        0,
        0,
        finish_out,
        "down_sum",
        (AttendBack(facts, q, *tables, grad_attended, log_total),),
    )
    dk, dv = keys_back(jnp.stack([dk, dv]), jnp.stack([dks, dvs]), rows, lengths, seq_count)
    lefts = (mid_low, grad_down, grad_branch, normed)
    columns = (
        (0, grad_pre, 0, 0),
        (1, act_low, 1, 0),
        (2, attended, 2, 0),
        (3, dq, 3, 0),
        (3, dk, 3, width),
        (3, dv, 3, 2 * width),
    )
    total = lambda value: jnp.sum(value.astype(jnp.float32), axis=0)
    features = hidden.shape[1]
    qv_sums = jnp.concatenate([total(dq), total(dv)])
    small = SmallSums(
        [("item", item_count), ("seq", seq_count), ("mp", mp_count)],
        6,
        rows // 2 // PIECE + SKEW * (mp_count - 1),
        jnp.concatenate(
            [
                jnp.sum(mid_sums, axis=1),
                jnp.zeros((2, features), jnp.float32),
                row(jnp.where(lax.axis_index("mp") == 0, total(grad_down), 0.0)),
                total(up_sums).reshape(-1, features),
                jnp.pad(qv_sums, (0, -qv_sums.shape[0] % features)).reshape(-1, features),
            ]
        ),
    )
    grad_input, _, *weight_grads, sums = line_sum(
        4,
        mp_count,
        [dq, dk, dv],
        qkv_full,
        NT,
        [hidden_in[0], grad_residual, row(pre_gain)],
        0,
        2,
        finish_input,
        "input_sum",
        ((Spread(lefts, columns),) if ours else ()) + (small,),
    )
    if not weight_grads:
        weight_grads = gradients_over(group, lefts, columns)
    up_grad, down_grad, out_grad, qkv_grad = weight_grads
    ff_rows = up_weight.shape[1] // features
    up_bias_grad = sums[6 : 6 + ff_rows].reshape(-1)
    qv_bias_grad = sums[6 + ff_rows :].reshape(-1)[: 2 * width].reshape(2, width)
    return (
        hidden_out[None],
        grad_input.astype(jnp.float32)[None],
        sums[3],
        sums[4],
        qkv_grad.reshape(-1, 3, width),
        qv_bias_grad,
        out_grad,
        sums[2],
        sums[0],
        sums[1],
        up_grad,
        up_bias_grad,
        down_grad,
        sums[5],
    )


def solution(mesh):
    rows = P("item", "seq", None)
    qkv = P(("item", "seq"), None, "mp")
    first = P(("item", "seq"), "mp")
    second = P("mp", ("item", "seq"))
    bias = P(None, "mp")
    return jax.shard_map(
        functools.partial(body, mesh.shape["item"], mesh.shape["seq"], mesh.shape["mp"]),
        mesh=mesh,
        in_specs=(
            rows,
            rows,
            P("item", None),
            P(),
            P(),
            qkv,
            bias,
            second,
            P(),
            P(),
            P(),
            first,
            P("mp"),
            second,
            P(),
        ),
        out_specs=(
            rows,
            rows,
            P(),
            P(),
            qkv,
            bias,
            second,
            P(),
            P(),
            P(),
            first,
            P("mp"),
            second,
            P(),
        ),
        check_vma=False,
    )
```

```python
import functools
import math

import jax
import jax.numpy as jnp
from jax import lax
from jax.experimental import pallas as pl
from jax.experimental.pallas import tpu as pltpu
from jax.sharding import PartitionSpec as P

HDIM = 64
SLOT = 1280
SEGS = 2
SUMM = 50
SUMM_ROWS = 64
TOKENS = 2560
PAIR = 2 * HDIM
PIECE = 32
SKEW = 2
MIB = 1 << 20
MESH = pl.DeviceIdType.MESH
MASKED = -1e30


eps = 1e-05

NN = (((1,), (0,)), ((), ()))
NT = (((1,), (1,)), ((), ()))


def mm(left, right, dims=NN):
    return lax.dot_general(left, right, dims, preferred_element_type=jnp.float32)


def norm_stats(values):
    center = jnp.mean(values, axis=-1, keepdims=True)
    centered = values - center
    inverse = lax.rsqrt(jnp.mean(centered * centered, axis=-1, keepdims=True) + eps)
    return centered * inverse, inverse


def norm_back(grad_out, normed, inverse, gain):
    scaled = grad_out * gain
    centered = scaled - jnp.mean(scaled, axis=-1, keepdims=True)
    return inverse * (centered - normed * jnp.mean(scaled * normed, axis=-1, keepdims=True))


def gelu_parts(values):
    c = math.sqrt(2 / math.pi)
    squared = values * values
    t = jnp.tanh(c * values * (1 + 0.044715 * squared))
    half = 0.5 * (1 + t)
    slope = half + 0.5 * values * (1 - t * t) * (c * (1 + 3 * 0.044715 * squared))
    return values * half, slope


def key_masks(facts_ref, block, rows, bq, nk):
    first = facts_ref[0] + block * bq
    limit = jnp.minimum(
        first + 1 + lax.broadcasted_iota(jnp.int32, (1, bq), 1), facts_ref[1]
    )
    own = lax.broadcasted_iota(jnp.int32, (nk, bq), 0) < limit
    earlier = lax.broadcasted_iota(jnp.int32, (SUMM_ROWS, bq), 0) < facts_ref[2]
    return own, earlier


def head_lanes(head):
    lane = lax.broadcasted_iota(jnp.int32, (1, PAIR), 1)
    return (lane >= head * HDIM) & (lane < (head + 1) * HDIM)


def attend_kernel(bq, causal, facts_ref, q_ref, k_ref, v_ref, ks_ref, vs_ref, o_ref, lse_ref):
    rows, seg = q_ref.shape[0], k_ref.shape[0]
    v_t = v_ref[...].T
    vs_t = vs_ref[...].T
    ks = ks_ref[...]
    low_half = lax.broadcasted_iota(jnp.int32, (PAIR, 1), 0) < HDIM
    for block in range(rows // bq):
        nk = (block + 1) * bq if causal else seg
        own, earlier = key_masks(facts_ref, block, rows, bq, nk)
        q = q_ref[block * bq : (block + 1) * bq, :] * jnp.bfloat16(HDIM**-0.5)
        mixed = []
        for head in range(2):
            qh = jnp.where(head_lanes(head), q, jnp.zeros_like(q))
            s = jnp.where(own, mm(k_ref[:nk, :], qh, NT), MASKED)
            s2 = jnp.where(earlier, mm(ks, qh, NT), MASKED)
            top = jnp.maximum(jnp.max(s, axis=0, keepdims=True), jnp.max(s2, axis=0, keepdims=True))
            p = jnp.exp(s - top)
            p2 = jnp.exp(s2 - top)
            total = jnp.sum(p, axis=0, keepdims=True) + jnp.sum(p2, axis=0, keepdims=True)
            out = mm(v_t[:, :nk], p.astype(jnp.bfloat16)) + mm(vs_t, p2.astype(jnp.bfloat16))
            mixed.append(out / total)
            lse_ref[0, head : head + 1, block * bq : (block + 1) * bq] = top + jnp.log(total)
        joined = jnp.where(low_half, mixed[0], mixed[1])
        o_ref[block * bq : (block + 1) * bq, :] = joined.T.astype(jnp.bfloat16)


def query_block(rows):
    return 256 if rows % 256 == 0 else math.gcd(rows, 160)


def attend(facts, q, k, v, ks, vs):
    rows, width = q.shape
    seg = k.shape[0]
    pairs = width // PAIR
    column = lambda n: pl.BlockSpec((n, PAIR), lambda i: (0, i))
    return pl.pallas_call(
        functools.partial(attend_kernel, query_block(rows), rows == seg),
        grid=(pairs,),
        in_specs=[pl.BlockSpec(memory_space=pltpu.SMEM)]
        + [column(n) for n in (rows, seg, seg, SUMM_ROWS, SUMM_ROWS)],
        out_specs=[column(rows), pl.BlockSpec((1, 2, rows), lambda i: (i, 0, 0))],
        out_shape=[
            jax.ShapeDtypeStruct((rows, width), jnp.bfloat16),
            jax.ShapeDtypeStruct((pairs, 2, rows), jnp.float32),
        ],
        compiler_params=pltpu.CompilerParams(vmem_limit_bytes=48 * MIB),
        cost_estimate=pl.CostEstimate(
            flops=4 * rows * seg * width, bytes_accessed=8 * rows * width, transcendentals=0
        ),
        name="attend",
    )(facts, q, k, v, ks, vs)


def keys_for(local, lengths, seq_count):
    rows, width = local.shape[-2:]
    pad = ((0, 0), (0, SUMM_ROWS - SUMM), (0, 0))
    if rows == SLOT:
        here = lengths[lax.axis_index("seq")]
        summary = jnp.pad(lax.dynamic_slice(local, (0, here, 0), (2, SUMM, width)), pad)
        moves = [(i, i + 1) for i in range(seq_count - 1)]
        return local, lax.ppermute(summary, "seq", moves)
    everything = lax.all_gather(local, "seq", axis=1, tiled=True)
    segment = lax.axis_index("seq") * rows // SLOT
    own = lax.dynamic_slice(everything, (0, segment * SLOT, 0), (2, SLOT, width))
    summary = lax.dynamic_slice(everything, (0, lengths[0], 0), (2, SUMM, width))
    return own, jnp.pad(summary, pad)


def keys_back(own, summary, rows, lengths, seq_count):
    width = own.shape[-1]
    summary = summary[:, :SUMM]
    if rows == SLOT:
        moves = [(i + 1, i) for i in range(seq_count - 1)]
        arrived = lax.ppermute(summary, "seq", moves)
        here = lengths[lax.axis_index("seq")]
        old = lax.dynamic_slice(own, (0, here, 0), (2, SUMM, width))
        new = (old.astype(jnp.float32) + arrived).astype(jnp.bfloat16)
        return lax.dynamic_update_slice(own, new, (0, here, 0))
    segment = lax.axis_index("seq") * rows // SLOT
    everything = jnp.zeros((2, TOKENS, width), jnp.float32)
    everything = lax.dynamic_update_slice(
        everything, own.astype(jnp.float32), (0, segment * SLOT, 0)
    )
    old = lax.dynamic_slice(everything, (0, lengths[0], 0), (2, SUMM, width))
    added = jnp.where(segment > 0, summary, 0.0)
    everything = lax.dynamic_update_slice(everything, old + added, (0, lengths[0], 0))
    return lax.psum_scatter(
        everything.astype(jnp.bfloat16), "seq", scatter_dimension=1, tiled=True
    )


class Line:
    def __init__(self, count, half, multiply, finish, out, part, moving, sems, late=False):
        self.count, self.half, self.multiply, self.finish = count, half, multiply, finish
        self.late = late
        self.out, self.part, self.moving = out, part, moving
        self.up_sent, self.up_got, self.down_sent, self.down_got, self.local = sems
        self.me = lax.axis_index("mp")
        self.pieces = half // PIECE
        self.per_group = part.shape[2] // PIECE
        self.steps = self.pieces + 2 * SKEW * (count - 1)

    @staticmethod
    def scratch(half, features):
        pieces = half // PIECE
        group = 160 if half % 160 == 0 else PIECE
        dma = lambda *shape: pltpu.SemaphoreType.DMA(shape)
        return [
            pltpu.VMEM((2, 2, group, features), jnp.float32),
            pltpu.VMEM((2 * half, features), jnp.bfloat16),
            dma(2, pieces),
            dma(2, pieces),
            dma(2, pieces),
            dma(2, pieces),
            dma(pieces),
        ]

    def place(self, flow):
        return self.count - 1 - self.me if flow == 0 else self.me

    def greet(self, barrier):
        me = self.me

        @pl.when(me > 0)
        def _():
            pl.semaphore_signal(barrier, inc=1, device_id={"mp": me - 1}, device_id_type=MESH)

        @pl.when(me < self.count - 1)
        def _():
            pl.semaphore_signal(barrier, inc=1, device_id={"mp": me + 1}, device_id_type=MESH)

    def meet(self, barrier, others=0):
        ends = (self.me == 0) | (self.me == self.count - 1)

        @pl.when(ends)
        def _():
            pl.semaphore_wait(barrier, 1 + others)

        @pl.when(jnp.logical_not(ends))
        def _():
            pl.semaphore_wait(barrier, 2 + others)

    def first(self):
        for flow in range(2):
            self.part[flow, 0] = self.multiply(flow, 0)

    def onward(self, flow, k):
        here = self.moving.at[pl.ds(flow * self.half + k * PIECE, PIECE)]
        return pltpu.make_async_remote_copy(
            src_ref=here,
            dst_ref=here,
            send_sem=self.up_sent.at[flow, k],
            recv_sem=self.up_got.at[flow, k],
            device_id={"mp": self.me - 1 if flow == 0 else self.me + 1},
            device_id_type=MESH,
        )

    def back(self, flow, k, owner):
        rows = self.out.at[pl.ds(flow * self.half + k * PIECE, PIECE)]
        return pltpu.make_async_remote_copy(
            src_ref=self.moving.at[pl.ds(flow * self.half + k * PIECE, PIECE)] if owner else rows,
            dst_ref=rows,
            send_sem=self.down_sent.at[flow, k],
            recv_sem=self.down_got.at[flow, k],
            device_id={"mp": self.me + 1 if flow == 0 else self.me - 1},
            device_id_type=MESH,
        )

    def keep(self, flow, k):
        return pltpu.make_async_copy(
            self.moving.at[pl.ds(flow * self.half + k * PIECE, PIECE)],
            self.out.at[pl.ds(flow * self.half + k * PIECE, PIECE)],
            self.local.at[k],
        )

    def step(self, t):
        last = self.count - 1
        for flow in range(2):
            place = self.place(flow)
            k = t - SKEW * place
            here = pl.ds(pl.multiple_of(flow * self.half + k * PIECE, PIECE), PIECE)
            busy = (k >= 0) & (k < self.pieces)

            def mine():
                slot = (k // self.per_group) % 2
                inner = pl.ds(pl.multiple_of((k % self.per_group) * PIECE, PIECE), PIECE)
                return self.part[flow, slot, inner, :]

            @pl.when(busy & (place == 0))
            def _():
                self.moving[here, :] = mine().astype(jnp.bfloat16)
                self.onward(flow, k).start()

            @pl.when(busy & (place > 0) & (place < last))
            def _():
                self.onward(flow, k).wait_recv()
                total = mine() + self.moving[here, :].astype(jnp.float32)
                self.moving[here, :] = total.astype(jnp.bfloat16)
                self.onward(flow, k).start()

            @pl.when(busy & (place == last))
            def _():
                self.onward(flow, k).wait_recv()
                total = mine() + self.moving[here, :].astype(jnp.float32)
                self.moving[here, :] = self.finish(flow, k, total).astype(jnp.bfloat16)
                self.back(flow, k, True).start()
                self.keep(flow, k).start()

        for flow in range(2):
            place = self.place(flow)
            j = t - SKEW * (2 * last - place)

            @pl.when((j >= 0) & (j < self.pieces) & (place < last))
            def _():
                self.back(flow, j, False).wait_recv()

                @pl.when(place > 0)
                def _():
                    self.back(flow, j, False).start()

        for flow in range(2 if self.multiply else 0):
            k = t - SKEW * self.place(flow)
            g = k // self.per_group + 1

            if self.late:

                @pl.when(k == -1)
                def _():
                    self.part[flow, 0] = self.multiply(flow, 0)

            @pl.when((k >= 0) & (k % self.per_group == 0) & (g < self.pieces // self.per_group))
            def _():
                self.part[flow, g % 2] = self.multiply(flow, g)

    def settle(self):
        def one(k, carry):
            for flow in range(2):
                place = self.place(flow)

                @pl.when(place < self.count - 1)
                def _():
                    self.onward(flow, k).wait_send()

                    @pl.when(place > 0)
                    def _():
                        self.back(flow, k, False).wait_send()

                @pl.when(place == self.count - 1)
                def _():
                    self.back(flow, k, True).wait_send()
                    self.keep(flow, k).wait()

            return carry

        lax.fori_loop(0, self.pieces, one, 0)


def group_product(lefts, right, dims, half, group):
    def multiply(flow, g):
        rows = pl.ds(pl.multiple_of(flow * half + g * group, 16), group)
        at, total = 0, None
        for left in lefts:
            depth = left.shape[1]
            cut = right[:, at : at + depth] if dims == NT else right[at : at + depth, :]
            product = mm(left[rows, :], cut, dims)
            total = product if total is None else total + product
            at += depth
        return total

    return multiply


def line_kernel(count, half, dims, n_left, n_extra, n_owned, n_acc, finish, sides, *refs):
    refs = list(refs)
    take = lambda n: [refs.pop(0) for _ in range(n)]
    lefts, (right,), extras = take(n_left), take(1), take(n_extra)
    side_in = [take(side.n_in) for side in sides]
    (out,), owned, accs = take(1), take(n_owned), take(1 if n_acc else 0)
    side_out = [take(side.n_out) for side in sides]
    part, moving, sems = *take(2), take(5)
    multiply = group_product(lefts, right, dims, half, part.shape[2])
    ending = lambda flow, k, total: finish(flow, k, total, extras, owned, accs)
    line = Line(count, half, multiply, ending, out, part, moving, sems)
    jobs = [
        side(ins, outs, take(len(side.scratch_shapes)), accs)
        for side, ins, outs in zip(sides, side_in, side_out)
    ]
    barrier = pltpu.get_barrier_semaphore()
    line.greet(barrier)
    for job in jobs:
        job.greet(barrier)
    if n_acc:
        accs[0][...] = jnp.zeros_like(accs[0])
    for job in jobs:
        job.first()
    line.first()
    line.meet(barrier, sum(job.others for job in jobs))

    def step(t, carry):
        line.step(t)
        for job in jobs:
            job.step(t)
        return carry

    lax.fori_loop(0, max([line.steps] + [job.steps for job in jobs]), step, 0)
    line.settle()
    for job in jobs:
        job.settle()


class Nothing:
    n_in = n_out = others = steps = 0
    operands, in_specs, out_shape, out_specs, scratch_shapes = (), (), (), (), ()

    def __call__(self, ins, outs, scratch, accs):
        return self

    def greet(self, barrier):
        pass

    def first(self):
        pass

    def step(self, t):
        pass

    def settle(self):
        pass


VMEM = pl.BlockSpec(memory_space=pltpu.VMEM)
ANY = pl.BlockSpec(memory_space=pl.ANY)
SMEM = pl.BlockSpec(memory_space=pltpu.SMEM)


def line_sum(number, count, lefts, right, dims, extras, n_owned, n_acc, finish, name, sides):
    rows = lefts[0].shape[0]
    features = right.shape[1 if dims == NN else 0]
    half = rows // 2
    acc = [jax.ShapeDtypeStruct((n_acc, 8, features), jnp.float32)] if n_acc else []
    return pl.pallas_call(
        functools.partial(
            line_kernel,
            count,
            half,
            dims,
            len(lefts),
            len(extras),
            n_owned,
            n_acc,
            finish,
            sides,
        ),
        in_specs=[VMEM] * (len(lefts) + 1 + len(extras)) + [s for side in sides for s in side.in_specs],
        out_specs=[ANY] + [VMEM] * (n_owned + len(acc)) + [s for side in sides for s in side.out_specs],
        out_shape=[jax.ShapeDtypeStruct((rows, features), jnp.bfloat16)]
        + [jax.ShapeDtypeStruct((half, features), jnp.float32)] * n_owned
        + acc
        + [s for side in sides for s in side.out_shape],
        scratch_shapes=Line.scratch(half, features) + [s for side in sides for s in side.scratch_shapes],
        compiler_params=pltpu.CompilerParams(
            collective_id=number, has_side_effects=True, vmem_limit_bytes=62 * MIB
        ),
        cost_estimate=pl.CostEstimate(
            flops=2 * rows * features * sum(left.shape[1] for left in lefts),
            bytes_accessed=4 * rows * features,
            transcendentals=0,
        ),
        name=name,
    )(*lefts, right, *extras, *[value for side in sides for value in side.operands])


def piece_rows(flow, k, half):
    return pl.ds(pl.multiple_of(flow * half + k * PIECE, PIECE), PIECE)


def fold(values):
    return jnp.sum(values.reshape(-1, 8, values.shape[-1]), axis=0)


def finish_input(flow, k, total, extras, owned, accs):
    hidden, grad, gain = extras
    (acc,) = accs
    half = grad.shape[0]
    normed, inverse = norm_stats(hidden[piece_rows(flow, k, half), :].astype(jnp.float32))
    acc[0] += fold(total * normed)
    acc[1] += fold(total)
    return grad[piece_rows(0, k, half), :] + norm_back(total, normed, inverse, gain[...])


def finish_out(flow, k, total, extras, owned, accs):
    residual, bias = extras
    half = residual.shape[0]
    return residual[piece_rows(0, k, half), :] + total + bias[...]


class AttendBack(Nothing):
    n_in, n_out = 8, 5

    def __init__(self, facts, q, k, v, ks, vs, do, lse):
        rows, width = q.shape
        seg = k.shape[0]
        self.operands = (facts, q, k, v, ks, vs, do, lse)
        self.in_specs = (SMEM,) + (VMEM,) * 7
        low = lambda n: jax.ShapeDtypeStruct((n, width), jnp.bfloat16)
        wide = lambda n: jax.ShapeDtypeStruct((n, width), jnp.float32)
        self.out_shape = (low(rows), low(seg), low(seg), wide(SUMM_ROWS), wide(SUMM_ROWS))
        self.out_specs = (VMEM,) * 5
        self.scratch_shapes = (
            pltpu.VMEM((seg, PAIR), jnp.float32),
            pltpu.VMEM((seg, PAIR), jnp.float32),
            pltpu.VMEM((PAIR, seg), jnp.bfloat16),
        )
        self.bq = query_block(rows)
        self.blocks = rows // self.bq
        self.pairs = width // PAIR
        self.steps = self.pairs * self.blocks
        self.causal = rows == seg

    def __call__(self, ins, outs, scratch, accs):
        self.ins, self.outs, self.scratch = ins, outs, scratch
        return self

    def step(self, t):
        pair = t // self.blocks
        for block in range(self.blocks):

            @pl.when((t < self.steps) & (t % self.blocks == block))
            def _():
                self.unit(pair, block)

    def unit(self, pair, block):
        facts, q_ref, k_ref, v_ref, ks_ref, vs_ref, do_ref, lse_ref = self.ins
        dq_ref, dk_ref, dv_ref, dks_ref, dvs_ref = self.outs
        dk_acc, dv_acc, k_t = self.scratch
        seg, bq = k_ref.shape[0], self.bq
        cols = pl.ds(pl.multiple_of(pair * PAIR, PAIR), PAIR)
        scale = jnp.bfloat16(HDIM**-0.5)
        low_half = lax.broadcasted_iota(jnp.int32, (PAIR, 1), 0) < HDIM
        if block == 0:
            k_t[...] = (k_ref[:, cols] * scale).T
            dk_acc[...] = jnp.zeros_like(dk_acc)
            dv_acc[...] = jnp.zeros_like(dv_acc)
            dks_ref[:, cols] = jnp.zeros((SUMM_ROWS, PAIR), jnp.float32)
            dvs_ref[:, cols] = jnp.zeros((SUMM_ROWS, PAIR), jnp.float32)
        ks, vs = ks_ref[:, cols], vs_ref[:, cols]
        ks_t = (ks * scale).T
        nk = (block + 1) * bq if self.causal else seg
        here = slice(block * bq, (block + 1) * bq)
        own, earlier = key_masks(facts, block, self.blocks * bq, bq, nk)
        q = q_ref[here, cols] * scale
        do = do_ref[here, cols]
        k, v = k_ref[:nk, cols], v_ref[:nk, cols]
        grads = []
        for head in range(2):
            qh = jnp.where(head_lanes(head), q, jnp.zeros_like(q))
            doh = jnp.where(head_lanes(head), do, jnp.zeros_like(do))
            lse = lse_ref[pair, head : head + 1, here]
            p = jnp.exp(jnp.where(own, mm(k, qh, NT), MASKED) - lse)
            p2 = jnp.exp(jnp.where(earlier, mm(ks, qh, NT), MASKED) - lse)
            dp = mm(v, doh, NT)
            dp2 = mm(vs, doh, NT)
            delta = jnp.sum(p * dp, axis=0, keepdims=True) + jnp.sum(p2 * dp2, axis=0, keepdims=True)
            ds = (p * (dp - delta)).astype(jnp.bfloat16)
            ds2 = (p2 * (dp2 - delta)).astype(jnp.bfloat16)
            dv_acc[:nk, :] += mm(p.astype(jnp.bfloat16), doh)
            dk_acc[:nk, :] += mm(ds, qh)
            dvs_ref[:, cols] += mm(p2.astype(jnp.bfloat16), doh)
            dks_ref[:, cols] += mm(ds2, qh)
            grads.append(mm(k_t[:, :nk], ds) + mm(ks_t, ds2))
        joined = jnp.where(low_half, grads[0], grads[1])
        dq_ref[here, cols] = joined.T.astype(jnp.bfloat16)
        if block == self.blocks - 1:
            dk_ref[:, cols] = dk_acc[...].astype(jnp.bfloat16)
            dv_ref[:, cols] = dv_acc[...].astype(jnp.bfloat16)


class Spread:
    others = 3
    block = 256
    lag = (2, 5, 8)
    across = (True, False, False, True)

    def __init__(self, lefts, columns, outs, left_now, scratch, start):
        self.lefts, self.outs, self.x_buf, self.start = lefts, outs, left_now, start
        self.table, self.phases, self.rights = [], {}, []
        at = 0
        for number, (left, right, result, place) in enumerate(columns):
            self.phases.setdefault(left, at)
            self.table.append((number, at, at + right.shape[1] // self.block, result, place))
            self.rights.append(right)
            at += right.shape[1] // self.block
        self.chunks = at
        self.steps = start + at + self.lag[2]
        (
            self.y_buf,
            self.s1,
            self.own,
            self.r1,
            self.s2x,
            self.s2y,
            self.top,
            self.low,
            self.r2x,
            self.r2y,
            self.s3,
            self.kept,
            self.r3,
            self.tile,
            self.x_sem,
            self.y_sem,
            self.s1_sem,
            self.r1_sem,
            self.s2x_sem,
            self.r2x_sem,
            self.s2y_sem,
            self.r2y_sem,
            self.s3y_sem,
            self.r3y_sem,
            self.s3x_sem,
            self.r3x_sem,
            self.out_sem,
        ) = scratch
        item, seq = lax.axis_index("item"), lax.axis_index("seq")
        self.core, self.x, self.y = item % 2, item // 2, seq
        self.to_core = {"item": item + 1 - 2 * self.core}
        self.to_x = {"item": item + 2 - 4 * self.x}
        self.to_y = {"seq": 1 - seq}

    @classmethod
    def scratch(cls, rows):
        block, half = cls.block, cls.block // 2
        low = lambda *shape: pltpu.VMEM(shape, jnp.bfloat16)
        wide = lambda *shape: pltpu.VMEM(shape, jnp.float32)
        return [
            low(2, rows, block),
            low(3, 2, block, 2 * block),
            wide(3, 2, block, 2 * block),
            low(4, 2, block, 2 * block),
            low(3, half, 2 * block),
            low(3, 2, half, block),
            wide(3, half, 2 * block),
            wide(3, 2, half, block),
            low(6, half, 2 * block),
            low(6, 2, half, block),
            low(3, 2, half, block),
            wide(3, 2, half, block),
            low(6, 2, half, block),
            wide(3, block, block),
        ] + [pltpu.SemaphoreType.DMA((n,)) for n in (1, 2, 3, 4, 3, 6, 3, 6, 3, 6, 3, 6, 3)]

    def greet(self, barrier):
        for to in (self.to_core, self.to_x, self.to_y):
            pl.semaphore_signal(barrier, inc=1, device_id=to, device_id_type=MESH)


    def left_copy(self, left):
        return pltpu.make_async_copy(self.lefts[left], self.x_buf, self.x_sem.at[0])

    def right_copy(self, m, act):
        for number, start, stop, _, _ in self.table:

            @pl.when((m >= start) & (m < stop))
            def _():
                cols = pl.ds(pl.multiple_of((m - start) * self.block, self.block), self.block)
                act(
                    pltpu.make_async_copy(
                        self.rights[number].at[:, cols], self.y_buf.at[m % 2], self.y_sem.at[m % 2]
                    )
                )

    def out_copy(self, m, act):
        for _, start, stop, result, place in self.table:

            @pl.when((m >= start) & (m < stop))
            def _():
                cols = pl.ds(
                    pl.multiple_of(place + (m - start) * self.block, self.block), self.block
                )
                out = self.outs[result]
                out = out.at[:, cols] if self.across[result] else out.at[cols, :]
                act(pltpu.make_async_copy(self.tile.at[m % 3], out, self.out_sem.at[m % 3]))

    def remote(self, src, dst, send, recv, to):
        return pltpu.make_async_remote_copy(
            src_ref=src, dst_ref=dst, send_sem=send, recv_sem=recv, device_id=to, device_id_type=MESH
        )

    def first_copy(self, m):
        return self.remote(
            self.s1.at[m % 3],
            self.r1.at[m % 4],
            self.s1_sem.at[m % 3],
            self.r1_sem.at[m % 4],
            self.to_core,
        )

    def second_copies(self, m):
        return (
            self.remote(
                self.s2x.at[m % 3],
                self.r2x.at[m % 6],
                self.s2x_sem.at[m % 3],
                self.r2x_sem.at[m % 6],
                self.to_x,
            ),
            self.remote(
                self.s2y.at[m % 3],
                self.r2y.at[m % 6],
                self.s2y_sem.at[m % 3],
                self.r2y_sem.at[m % 6],
                self.to_y,
            ),
        )

    def third_copies(self, m):
        return (
            self.remote(
                self.s3.at[m % 3, 0],
                self.r3.at[m % 6, 0],
                self.s3y_sem.at[m % 3],
                self.r3y_sem.at[m % 6],
                self.to_y,
            ),
            self.remote(
                self.s3.at[m % 3, 1],
                self.r3.at[m % 6, 1],
                self.s3x_sem.at[m % 3],
                self.r3x_sem.at[m % 6],
                self.to_x,
            ),
        )

    def step(self, t):
        @pl.when(t == self.start - 1)
        def _():
            self.left_copy(0).start()
            self.right_copy(0, lambda copy: copy.start())

        for stage, lag in ((self.fourth, 8), (self.third, 5), (self.second, 2), (self.multiply, 0)):
            m = t - self.start - lag

            @pl.when((m >= 0) & (m < self.chunks))
            def _():
                stage(m)

    def multiply(self, m):
        for left, start in self.phases.items():

            @pl.when(m == start)
            def _():
                if start > 0:
                    self.left_copy(left).start()
                self.left_copy(left).wait()

        @pl.when(m + 1 < self.chunks)
        def _():
            self.right_copy(m + 1, lambda copy: copy.start())

        self.right_copy(m, lambda copy: copy.wait())

        @pl.when(m >= 3)
        def _():
            self.first_copy(m - 3).wait_send()

        turned = self.y_buf[m % 2].T
        wide = 2 * self.block

        def product(x, core):
            cols = pl.ds(pl.multiple_of(x * 2 * wide + core * wide, wide), wide)
            return mm(turned, self.x_buf[:, cols])

        for x in range(2):
            self.s1[m % 3, x] = product(x, 1 - self.core).astype(jnp.bfloat16)
        self.first_copy(m).start()
        for x in range(2):
            self.own[m % 3, x] = product(x, self.core)

    def second(self, m):
        half = self.block // 2

        @pl.when(m >= 3)
        def _():
            for copy in self.second_copies(m - 3):
                copy.wait_send()

        self.first_copy(m).wait_recv()
        slot = m % 3
        here, there = self.x, 1 - self.x
        mine = pl.ds(pl.multiple_of(self.y * self.block, self.block), self.block)
        others = pl.ds(pl.multiple_of((1 - self.y) * self.block, self.block), self.block)
        added = lambda x, rows, cols: (
            self.own[slot, x, rows, cols] + self.r1[m % 4, x, rows, cols].astype(jnp.float32)
        )
        upper, lower, every = pl.ds(0, half), pl.ds(half, half), pl.ds(0, 2 * self.block)
        self.s2x[slot] = added(there, upper, every).astype(jnp.bfloat16)
        for x in range(2):
            self.s2y[slot, x] = added(x, lower, others).astype(jnp.bfloat16)
        for copy in self.second_copies(m):
            copy.start()
        self.top[slot] = added(here, upper, every)
        for x in range(2):
            self.low[slot, x] = added(x, lower, mine)

    def third(self, m):
        @pl.when(m >= 3)
        def _():
            for copy in self.third_copies(m - 3):
                copy.wait_send()

        for copy in self.second_copies(m):
            copy.wait_recv()
        slot, got = m % 3, m % 6
        mine = pl.ds(pl.multiple_of(self.y * self.block, self.block), self.block)
        others = pl.ds(pl.multiple_of((1 - self.y) * self.block, self.block), self.block)
        top = lambda cols: self.top[slot, :, cols] + self.r2x[got, :, cols].astype(jnp.float32)
        low = lambda x: self.low[slot, x] + self.r2y[got, x].astype(jnp.float32)
        self.s3[slot, 0] = top(others).astype(jnp.bfloat16)
        self.s3[slot, 1] = low(1 - self.x).astype(jnp.bfloat16)
        for copy in self.third_copies(m):
            copy.start()
        self.kept[slot, 0] = top(mine)
        self.kept[slot, 1] = low(self.x)

    def fourth(self, m):
        @pl.when(m >= 3)
        def _():
            self.out_copy(m - 3, lambda copy: copy.wait())

        for copy in self.third_copies(m):
            copy.wait_recv()
        slot, half = m % 3, self.block // 2
        total = self.kept[slot] + self.r3[m % 6].astype(jnp.float32)
        total = total.reshape(self.block, self.block)
        across = jnp.zeros((), jnp.bool_)
        for _, start, stop, result, _ in self.table:
            if self.across[result]:
                across = across | ((m >= start) & (m < stop))

        @pl.when(across)
        def _():
            self.tile[slot] = total.T

        @pl.when(jnp.logical_not(across))
        def _():
            self.tile[slot] = total

        self.out_copy(m, lambda copy: copy.start())

    def settle(self):
        for m in range(self.chunks - 3, self.chunks):
            self.first_copy(m).wait_send()
            for copy in self.second_copies(m) + self.third_copies(m):
                copy.wait_send()
            self.out_copy(jnp.int32(m), lambda copy: copy.wait())


class Gather:
    others = 3

    def __init__(self, shards, fulls, sems, ready):
        self.shards, self.fulls, self.ready = shards, fulls, ready
        self.sent, self.got, self.local = sems
        item, seq = lax.axis_index("item"), lax.axis_index("seq")
        self.core, self.x, self.y = item % 2, item // 2, seq
        self.to_core = {"item": item + 1 - 2 * self.core}
        self.to_x = {"item": item + 2 - 4 * self.x}
        self.to_y = {"seq": 1 - seq}

    @staticmethod
    def sems(count=2):
        dma = lambda *shape: pltpu.SemaphoreType.DMA(shape)
        return [dma(count, 9), dma(count, 9), dma(count)]

    def greet(self, barrier):
        for to in (self.to_core, self.to_x, self.to_y):
            pl.semaphore_signal(barrier, inc=1, device_id=to, device_id_type=MESH)

    def spot(self, w, x, core, y, part=None):
        size = self.shards[w].shape[w]
        at = pl.ds(pl.multiple_of(((2 * x + core) * 2 + y) * size, size), size)
        if w == 0:
            if part is not None:
                half = size // 2
                start = ((2 * x + core) * 2 + y) * size + part * half
                at = pl.ds(pl.multiple_of(start, half), half)
            return self.fulls[0].at[at, :]
        rows = self.fulls[1].shape[0]
        if part is not None:
            return self.fulls[1].at[pl.ds(part * (rows // 2), rows // 2), at]
        return self.fulls[1].at[:, at]

    def message(self, w, number, src, dst, to):
        return pltpu.make_async_remote_copy(
            src_ref=src,
            dst_ref=dst,
            send_sem=self.sent.at[w, number],
            recv_sem=self.got.at[w, number],
            device_id=to,
            device_id_type=MESH,
        )

    def messages(self, w):
        c, x, y = self.core, self.x, self.y
        own, spot = self.shards[w].at[...], functools.partial(self.spot, w)
        plan = (
            (own, spot(x, c, y), spot(x, 1 - c, y), self.to_core),
            (own, spot(x, c, y), spot(1 - x, c, y), self.to_x),
            (own, spot(x, c, y), spot(x, c, 1 - y), self.to_y),
            (None, spot(1 - x, c, y, 0), spot(1 - x, c, 1 - y, 0), self.to_y),
            (None, spot(x, c, 1 - y, 1), spot(1 - x, c, 1 - y, 1), self.to_x),
            (None, spot(1 - x, c, y), spot(1 - x, 1 - c, y), self.to_core),
            (None, spot(x, c, 1 - y), spot(x, 1 - c, 1 - y), self.to_core),
            (None, spot(1 - x, c, 1 - y, 0), spot(1 - x, 1 - c, 1 - y, 0), self.to_core),
            (None, spot(1 - x, c, 1 - y, 1), spot(1 - x, 1 - c, 1 - y, 1), self.to_core),
        )
        return [
            (
                self.message(w, number, out if src is None else src, out, to),
                self.message(w, number, landing, landing, to),
            )
            for number, (src, out, landing, to) in enumerate(plan)
        ]

    def send(self, w, numbers):
        messages = self.messages(w)
        for number in numbers:
            messages[number][0].start()

    def receive(self, w, numbers):
        messages = self.messages(w)
        for number in numbers:
            messages[number][1].wait_recv()

    def mine(self, w):
        return pltpu.make_async_copy(
            self.shards[w], self.spot(w, self.x, self.core, self.y), self.local.at[w]
        )

    def first(self):
        for w in range(len(self.shards)):
            self.mine(w).start()

    def begin(self):
        for w in range(2):
            self.send(w, (1, 2, 0))

    def step(self, t):
        for w, at in ((0, self.ready * 5 // 16), (1, self.ready * 9 // 16)):

            @pl.when(t == at)
            def _():
                self.receive(w, (1, 2))
                self.send(w, (3, 4, 5, 6))

        for w, at in ((0, self.ready * 12 // 16), (1, self.ready * 15 // 16)):

            @pl.when(t == at)
            def _():
                self.receive(w, (3, 4))
                self.send(w, (7, 8))

        @pl.when(t == self.ready)
        def _():
            for w in range(2):
                self.receive(w, (0, 5, 6, 7, 8))
                self.mine(w).wait()

    def settle(self):
        for w in range(len(self.shards)):
            for out, _ in self.messages(w):
                out.wait_send()


class Load:
    others = 0

    def __init__(self, shards, fulls, sems, ready):
        self.ready = ready
        self.copies = [
            pltpu.make_async_copy(shard, full, sems[2].at[w])
            for w, (shard, full) in enumerate(zip(shards, fulls))
        ]

    sems = Gather.sems

    def greet(self, barrier):
        pass

    def first(self):
        for copy in self.copies:
            copy.start()

    def begin(self):
        pass

    def step(self, t):
        @pl.when(t == self.ready)
        def _():
            for copy in self.copies:
                copy.wait()

    def settle(self):
        pass


class Attend:
    bq = 128

    def __init__(self, half, facts, q, k, v, earlier, attended, lse):
        self.half, self.facts, self.q, self.k, self.v = half, facts, q, k, v
        self.earlier, self.attended, self.lse = earlier, attended, lse
        self.pairs = q.shape[1] // PAIR
        self.blocks = half // self.bq

    def first(self):
        def one(pair, carry):
            for flow in range(2):
                self.unit(pair, flow * self.blocks)
            return carry

        lax.fori_loop(0, self.pairs, one, 0)

    def step(self, t):
        def both(pair, block):
            for flow in range(2):
                self.unit(pair, flow * self.blocks + block)

        @pl.when(t < 2)
        def _():
            each = self.pairs // 2

            def one(i, carry):
                both((t % 2) * each + i, 1)
                return carry

            lax.fori_loop(0, each, one, 0)

        for block in range(2, self.blocks):
            start = self.pairs * (block - 2) + 2

            @pl.when((t >= start) & (t < start + self.pairs))
            def _():
                both(t - start, block)

    def unit(self, pair, block):
        bq, nk = self.bq, (block + 1) * self.bq
        cols = pl.ds(pl.multiple_of(pair * PAIR, PAIR), PAIR)
        here = slice(block * bq, nk)
        query = block * bq + lax.broadcasted_iota(jnp.int32, (1, 2 * bq), 1) % bq
        limit = jnp.minimum(query + 1, self.facts[1])
        own = lax.broadcasted_iota(jnp.int32, (nk, 2 * bq), 0) < limit
        earlier = lax.broadcasted_iota(jnp.int32, (SUMM_ROWS, 2 * bq), 0) < self.facts[2]
        q = self.q[here, cols] * jnp.bfloat16(HDIM**-0.5)
        q = jnp.concatenate([jnp.where(head_lanes(h), q, jnp.zeros_like(q)) for h in range(2)])
        s = jnp.where(own, mm(self.k[:nk, cols], q, NT), MASKED)
        s2 = jnp.where(earlier, mm(self.earlier[0, :, cols], q, NT), MASKED)
        top = jnp.maximum(jnp.max(s, axis=0, keepdims=True), jnp.max(s2, axis=0, keepdims=True))
        p = jnp.exp(s - top)
        p2 = jnp.exp(s2 - top)
        total = jnp.sum(p, axis=0, keepdims=True) + jnp.sum(p2, axis=0, keepdims=True)
        out = mm(self.v[:nk, cols].T, p.astype(jnp.bfloat16))
        out = (out + mm(self.earlier[1, :, cols].T, p2.astype(jnp.bfloat16))) / total
        lse = top + jnp.log(total)
        for head in range(2):
            self.lse[pair, head : head + 1, here] = lse[:, head * bq : (head + 1) * bq]
        low_half = lax.broadcasted_iota(jnp.int32, (PAIR, 1), 0) < HDIM
        joined = jnp.where(low_half, out[:, :bq], out[:, bq:])
        self.attended[here, cols] = joined.T.astype(jnp.bfloat16)


def ffn_kernel(count, half, weights_job, n_attend, *refs):
    if n_attend == 1:
        ffn_body(count, half, weights_job, None, *refs)
    else:
        facts, q, k, v, earlier, *rest = refs
        inputs, outputs, scratch = rest[:9], rest[9:21], rest[21:]
        *outputs, attended, lse = outputs
        job = Attend(half, facts, q, k, v, earlier, attended, lse)
        ffn_body(count, half, weights_job, job, attended, *inputs, *outputs, *scratch)


def ffn_body(
    count,
    half,
    weights_job,
    attention,
    attended,
    out_w,
    out_bias,
    mid_gain,
    mid_shift,
    up_bias,
    hidden,
    cotangent,
    up_shard,
    down_shard,
    mid,
    act,
    grad_pre,
    residual_out,
    branch,
    grad_out,
    down_out,
    acc,
    acc_up,
    acc_down,
    part1,
    moving1,
    part2,
    moving2,
    rows_in,
    residual,
    up,
    down,
    mid_in,
    cot_in,
    act_out,
    pre_out,
    *sems,
):
    sems = list(sems)
    take = lambda n: [sems.pop(0) for _ in range(n)]
    sems1, sems2, weight_sems = take(5), take(5), take(3)
    in_sem, residual_sem, grad_sem, mid_sem, cot_sem, act_sem, pre_sem, down_sem = sems
    me = lax.axis_index("mp")
    group = part2.shape[2]
    blocks = 4
    block = up.shape[1] // blocks
    per_group = group // PIECE
    pieces = half // PIECE
    last = count - 1
    second = per_group + blocks + 2 * SKEW * (count - 1)
    weights = weights_job((up_shard, down_shard), (up, down), weight_sems, second - blocks - 1)
    piece = lambda k: pl.ds(pl.multiple_of(k * PIECE, PIECE), PIECE)
    owner = (me == 0) | (me == last)
    my_flow = jnp.where(me == 0, 0, 1)

    def piece_in(source, k, flow):
        return pltpu.make_async_copy(
            source.at[pl.ds(flow * half + k * PIECE, PIECE)], rows_in.at[piece(k)], in_sem.at[k]
        )

    def residual_copy(k):
        return pltpu.make_async_copy(
            residual.at[piece(k)], residual_out.at[piece(k)], residual_sem.at[k]
        )

    def grad_copy(k):
        return pltpu.make_async_copy(residual.at[piece(k)], grad_out.at[piece(k)], grad_sem.at[k])

    def finish_first(flow, k, total):
        piece_in(hidden, k, flow).wait()
        value = rows_in[piece(k), :].astype(jnp.float32) + total + out_bias[...]
        residual[piece(k), :] = value
        residual_copy(k).start()
        piece_in(cotangent, k, flow).start()
        return norm_stats(value)[0] * mid_gain[...] + mid_shift[...]

    def finish_second(flow, k, total):
        piece_in(cotangent, k, flow).wait()
        residual_copy(k).wait()
        normed, inverse = norm_stats(residual[piece(k), :])
        grad = rows_in[piece(k), :].astype(jnp.float32)
        grad = grad + norm_back(total, normed, inverse, mid_gain[...])
        residual[piece(k), :] = grad
        grad_copy(k).start()
        acc[0] += fold(total * normed)
        acc[1] += fold(total)
        acc[2] += fold(grad)
        return grad

    multiply = group_product([attended], out_w, NN, half, part1.shape[2])
    line1 = Line(count, half, multiply, finish_first, mid, part1, moving1, sems1)
    line2 = Line(count, half, None, finish_second, branch, part2, moving2, sems2)

    def group_rows(flow, g):
        return pl.ds(pl.multiple_of(flow * half + g * group, 16), group)

    def mid_fetch(flow, g, here):
        source = moving1.at[group_rows(flow, g)] if here else mid.at[group_rows(flow, g)]
        return pltpu.make_async_copy(source, mid_in.at[flow], mid_sem.at[flow])

    def cot_fetch(flow, g):
        return pltpu.make_async_copy(
            cotangent.at[group_rows(flow, g)], cot_in.at[flow], cot_sem.at[flow]
        )

    def act_copy(flow, g):
        return pltpu.make_async_copy(
            act_out.at[flow], act.at[group_rows(flow, g)], act_sem.at[flow]
        )

    def pre_copy(flow, g):
        return pltpu.make_async_copy(
            pre_out.at[flow], grad_pre.at[group_rows(flow, g)], pre_sem.at[flow]
        )

    def products(flow, g, number):
        @pl.when(number == 0)
        def _():
            mid_fetch(flow, g, False).wait()
            cot_fetch(flow, g).wait()
            acc_down[...] += fold(cot_in[flow].astype(jnp.float32))

            @pl.when(g > 0)
            def _():
                act_copy(flow, g - 1).wait()
                pre_copy(flow, g - 1).wait()

        cols = pl.ds(pl.multiple_of(number * block, block), block)
        value, slope = gelu_parts(mm(mid_in[flow], up[:, cols]) + up_bias[:, cols])
        act_out[flow, :, cols] = value.astype(jnp.bfloat16)
        pre = (slope * mm(cot_in[flow], down[cols, :], NT)).astype(jnp.bfloat16)
        pre_out[flow, :, cols] = pre
        acc_up[:, cols] += fold(pre.astype(jnp.float32))
        product = mm(pre, up[:, cols], NT)

        @pl.when(number == 0)
        def _():
            part2[flow, g % 2] = product

        @pl.when(number > 0)
        def _():
            part2[flow, g % 2] += product

        @pl.when(number == blocks - 1)
        def _():
            act_copy(flow, g).start()
            pre_copy(flow, g).start()

    barrier = pltpu.get_barrier_semaphore()
    line1.greet(barrier)
    weights.greet(barrier)
    acc[...] = jnp.zeros_like(acc)
    acc_up[...] = jnp.zeros_like(acc_up)
    acc_down[...] = jnp.zeros_like(acc_down)
    weights.first()

    @pl.when(owner)
    def _():
        def one(k, carry):
            piece_in(hidden, k, my_flow).start()
            return carry

        lax.fori_loop(0, pieces, one, 0)

    if attention is None:
        line1.first()
        line1.meet(barrier, weights.others)
        weights.begin()
    else:
        line1.meet(barrier, weights.others)
        weights.begin()
        attention.first()
        line1.first()

    def step(t, carry):
        if attention is not None:
            attention.step(t)
        line1.step(t)
        line2.step(t - second)
        weights.step(t)

        @pl.when(t == weights.ready + 1)
        def _():
            pltpu.make_async_copy(down, down_out, down_sem.at[0]).start()

        for flow in range(2):
            place = line1.place(flow)
            u = t - second - SKEW * place
            fetch = u + blocks + 1
            compute = u + blocks

            @pl.when((fetch >= 0) & (fetch % per_group == 0) & (fetch < pieces))
            def _():
                g = fetch // per_group
                cot_fetch(flow, g).start()

                @pl.when(place == last)
                def _():
                    mid_fetch(flow, g, True).start()

                @pl.when(place < last)
                def _():
                    mid_fetch(flow, g, False).start()

            @pl.when((compute >= 0) & (compute < pieces) & (compute % per_group < blocks))
            def _():
                products(flow, compute // per_group, compute % per_group)

        return carry

    lax.fori_loop(0, second + line2.steps, step, 0)
    line1.settle()
    line2.settle()
    weights.settle()
    pltpu.make_async_copy(down, down_out, down_sem.at[0]).wait()
    for flow in range(2):
        act_copy(flow, pieces // per_group - 1).wait()
        pre_copy(flow, pieces // per_group - 1).wait()

    @pl.when(owner)
    def _():
        def one(k, carry):
            grad_copy(k).wait()
            return carry

        lax.fori_loop(0, pieces, one, 0)


def ffn_sums(number, count, weights_job, attend_in, out_w, vectors, hidden, cotangent, up_w, down_w):
    rows, features = hidden.shape
    ff = up_w.shape[1]
    half = rows // 2
    pieces = half // PIECE
    low = lambda *shape: jax.ShapeDtypeStruct(shape, jnp.bfloat16)
    wide = lambda *shape: jax.ShapeDtypeStruct(shape, jnp.float32)
    attend_out = []
    if len(attend_in) > 1:
        width = attend_in[1].shape[1]
        attend_out = [low(rows, width), wide(width // PAIR, 2, rows)]
    first = Line.scratch(half, features)
    small = 64 if half % 64 == 0 else PIECE
    first[0] = pltpu.VMEM((2, 2, small, features), jnp.float32)
    second = Line.scratch(half, features)
    group = second[0].shape[2]
    dma = lambda n: pltpu.SemaphoreType.DMA((n,))
    return pl.pallas_call(
        functools.partial(ffn_kernel, count, half, weights_job, len(attend_in)),
        in_specs=[SMEM, VMEM, VMEM, VMEM, VMEM][-len(attend_in) :] + [VMEM] * 5 + [ANY] * 4,
        out_specs=[ANY] * 7 + [VMEM] * (3 + len(attend_out)),
        out_shape=[
            low(rows, features),
            low(rows, ff),
            low(rows, ff),
            wide(half, features),
            low(rows, features),
            wide(half, features),
            low(ff, features),
            wide(3, 8, features),
            wide(8, ff),
            wide(8, features),
        ]
        + attend_out,
        scratch_shapes=first[:2]
        + second[:2]
        + [
            pltpu.VMEM((half, features), jnp.bfloat16),
            pltpu.VMEM((half, features), jnp.float32),
            pltpu.VMEM((features, ff), jnp.bfloat16),
            pltpu.VMEM((ff, features), jnp.bfloat16),
            pltpu.VMEM((2, group, features), jnp.bfloat16),
            pltpu.VMEM((2, group, features), jnp.bfloat16),
            pltpu.VMEM((2, group, ff), jnp.bfloat16),
            pltpu.VMEM((2, group, ff), jnp.bfloat16),
        ]
        + first[2:]
        + second[2:]
        + Gather.sems()
        + [dma(pieces), dma(pieces), dma(pieces), dma(2), dma(2), dma(2), dma(2), dma(1)],
        compiler_params=pltpu.CompilerParams(
            collective_id=number, has_side_effects=True, vmem_limit_bytes=62 * MIB
        ),
        cost_estimate=pl.CostEstimate(
            flops=6 * rows * features * ff, bytes_accessed=30 * rows * features, transcendentals=0
        ),
        name="ffn_sums",
    )(*attend_in, out_w, *vectors, hidden, cotangent, up_w, down_w)


def start_kernel(
    facts,
    hidden,
    gain,
    shift,
    bias,
    shard,
    out_shard,
    q_ref,
    k_ref,
    v_ref,
    earlier,
    normed_out,
    weight_out,
    out_whole,
    normed,
    weight,
    out_weight,
    total,
    summary,
    *sems,
):
    gather = Gather((shard, out_shard), (weight, out_weight), sems[:3], 0)
    summary_sent, summary_got, out_sems = sems[3:]
    rows = hidden.shape[0]
    width = q_ref.shape[1]
    size = shard.shape[0]
    chunk = 128
    barrier = pltpu.get_barrier_semaphore()
    gather.greet(barrier)
    gather.first()
    pl.semaphore_wait(barrier, gather.others)
    gather.send(0, (1, 2, 0))

    def norm(i, carry):
        here = pl.ds(pl.multiple_of(i * chunk, chunk), chunk)
        value = norm_stats(hidden[here, :].astype(jnp.float32))[0]
        normed[here, :] = (value * gain[...] + shift[...]).astype(jnp.bfloat16)
        return carry

    lax.fori_loop(0, rows // chunk, norm, 0)
    keep = pltpu.make_async_copy(normed, normed_out, out_sems.at[0])
    keep.start()
    c, x, y = gather.core, gather.x, gather.y

    def add(places, first=False, last=False):
        starts = [
            pl.multiple_of(((2 * px + pc) * 2 + py) * size, size) for px, pc, py in places
        ]

        def rows_of(i, carry):
            here = pl.ds(pl.multiple_of(i * chunk, chunk), chunk)
            for j, out in enumerate((q_ref, k_ref, v_ref)):
                cols = slice(j * width, (j + 1) * width)
                value = None if first else total[here, cols]
                for start in starts:
                    at = pl.ds(start, size)
                    product = mm(normed[here, at], weight[at, cols])
                    value = product if value is None else value + product
                if not last:
                    total[here, cols] = value
                elif j == 1:
                    out[here, :] = value.astype(jnp.bfloat16)
                else:
                    out[here, :] = (value + bias[j // 2 : j // 2 + 1, :]).astype(jnp.bfloat16)
            return carry

        lax.fori_loop(0, rows // chunk, rows_of, 0)

    gather.mine(0).wait()
    gather.receive(0, (0,))
    add(((x, c, y), (x, 1 - c, y)), first=True)
    gather.receive(0, (1, 2))
    gather.send(0, (3, 4, 5, 6))
    gather.send(1, (1, 2, 0))
    add(((1 - x, c, y), (x, c, 1 - y)))
    gather.receive(0, (5, 6))
    add(((1 - x, 1 - c, y), (x, 1 - c, 1 - y)))
    gather.receive(0, (3, 4))
    gather.send(0, (7, 8))
    add(((1 - x, c, 1 - y),))
    gather.receive(1, (1, 2))
    gather.send(1, (3, 4, 5, 6))
    gather.receive(0, (7, 8))
    store = pltpu.make_async_copy(weight, weight_out, out_sems.at[1])
    store.start()
    add(((1 - x, 1 - c, 1 - y),), last=True)

    shape = (SUMM_ROWS, rows)
    chosen = lax.broadcasted_iota(jnp.int32, shape, 1) == (
        facts[1] - SUMM + lax.broadcasted_iota(jnp.int32, shape, 0)
    )
    chosen = jnp.where(chosen, 1.0, 0.0).astype(jnp.bfloat16)
    summary[0] = mm(chosen, k_ref[...]).astype(jnp.bfloat16)
    summary[1] = mm(chosen, v_ref[...]).astype(jnp.bfloat16)
    swap = pltpu.make_async_remote_copy(
        src_ref=summary,
        dst_ref=earlier,
        send_sem=summary_sent.at[0],
        recv_sem=summary_got.at[0],
        device_id=gather.to_y,
        device_id_type=MESH,
    )
    swap.start()
    gather.receive(1, (3, 4))
    gather.send(1, (7, 8))
    gather.receive(1, (0, 5, 6, 7, 8))
    gather.mine(1).wait()
    store_out = pltpu.make_async_copy(out_weight, out_whole, out_sems.at[2])
    store_out.start()
    gather.settle()
    keep.wait()
    store.wait()
    swap.wait()
    store_out.wait()


def start(number, facts, hidden, gain, shift, bias, shard, out_shard):
    rows, features = hidden.shape
    width = bias.shape[1]
    low = lambda *shape: jax.ShapeDtypeStruct(shape, jnp.bfloat16)
    dma = lambda n: pltpu.SemaphoreType.DMA((n,))
    return pl.pallas_call(
        start_kernel,
        in_specs=[SMEM] + [VMEM] * 4 + [ANY] * 2,
        out_specs=[VMEM] * 3 + [ANY] * 4,
        out_shape=[low(rows, width)] * 3
        + [low(2, SUMM_ROWS, width), low(rows, features), low(features, 3 * width)]
        + [low(width, features)],
        scratch_shapes=[
            pltpu.VMEM((rows, features), jnp.bfloat16),
            pltpu.VMEM((features, 3 * width), jnp.bfloat16),
            pltpu.VMEM((width, features), jnp.bfloat16),
            pltpu.VMEM((rows, 3 * width), jnp.float32),
            pltpu.VMEM((2, SUMM_ROWS, width), jnp.bfloat16),
        ]
        + Gather.sems()
        + [dma(1), dma(1), dma(3)],
        compiler_params=pltpu.CompilerParams(
            collective_id=number, has_side_effects=True, vmem_limit_bytes=60 * MIB
        ),
        cost_estimate=pl.CostEstimate(
            flops=6 * rows * features * width, bytes_accessed=16 * rows * features, transcendentals=0
        ),
        name="start",
    )(facts, hidden, gain, shift, bias, shard, out_shard)


class SmallSums(Nothing):
    n_in = n_out = 1

    def __init__(self, sizes, shared, start, values):
        self.stages = tuple(
            (axis, 1 << bit) for axis, size in sizes for bit in range(size.bit_length() - 1)
        )
        self.shared, self.start = shared, start
        self.others = len(self.stages)
        self.steps = start + self.others + 1
        self.operands = (values,)
        self.in_specs = self.out_specs = (VMEM,)
        self.out_shape = (jax.ShapeDtypeStruct(values.shape, jnp.float32),)
        buffers = pltpu.VMEM((self.others, *values.shape), jnp.float32)
        sems = pltpu.SemaphoreType.DMA((self.others,))
        self.scratch_shapes = (buffers, buffers, sems, sems)

    def __call__(self, ins, outs, scratch, accs):
        (self.own,), (self.out,), (self.acc,) = ins, outs, accs
        self.sent, self.got, self.send_sem, self.recv_sem = scratch
        return self

    def partner(self, axis, bit):
        index = lax.axis_index(axis)
        return {axis: index + bit - 2 * bit * ((index // bit) % 2)}

    def extra(self, row, start, grad):
        cols = slice(start, start + grad.shape[1])
        self.sent[0, row : row + 1, cols] = jnp.sum(
            grad[...].astype(jnp.float32), axis=0, keepdims=True
        )

    def greet(self, barrier):
        for axis, bit in self.stages:
            pl.semaphore_signal(
                barrier, inc=1, device_id=self.partner(axis, bit), device_id_type=MESH
            )

    def copy(self, number):
        return pltpu.make_async_remote_copy(
            src_ref=self.sent.at[number],
            dst_ref=self.got.at[number],
            send_sem=self.send_sem.at[number],
            recv_sem=self.recv_sem.at[number],
            device_id=self.partner(*self.stages[number]),
            device_id_type=MESH,
        )

    def first(self):
        self.sent[0] = self.own[...]

    def step(self, t):
        @pl.when(t == self.start)
        def _():
            for number in range(self.acc.shape[0]):
                self.sent[0, 3 + number : 4 + number, :] = jnp.sum(
                    self.acc[number], axis=0, keepdims=True
                )
            self.copy(0).start()

        row = lax.broadcasted_iota(jnp.int32, self.own.shape, 0)
        for number, (axis, _) in enumerate(self.stages):

            @pl.when(t == self.start + 1 + number)
            def _():
                self.copy(number).wait()
                total = self.sent[number] + self.got[number]
                if axis == "mp":
                    total = jnp.where(row < self.shared, total, self.sent[number])
                if number + 1 < len(self.stages):
                    self.sent[number + 1] = total
                    self.copy(number + 1).start()
                else:
                    self.out[...] = total


class Columns:
    def __init__(self, ref, start, width):
        self.ref, self.start, self.shape = ref, start, (ref.shape[0], width)

    def __getitem__(self, index):
        rows, cols = index
        start = pl.multiple_of(self.start + cols.start, PAIR)
        return self.ref[rows, pl.ds(start, cols.size)]


class Ring:
    depth = 4

    def __init__(self, source, buffer, sems, pieces, offset):
        self.source, self.buffer, self.sems = source, buffer, sems
        self.pieces, self.offset = pieces, offset

    @classmethod
    def scratch(cls, features, dtype):
        return [
            pltpu.VMEM((cls.depth, PIECE, features), dtype),
            pltpu.SemaphoreType.DMA((cls.depth,)),
        ]

    def copy(self, k):
        rows = pl.ds(self.offset + k * PIECE, PIECE)
        slot = k % self.depth
        return pltpu.make_async_copy(
            self.source.at[rows], self.buffer.at[slot], self.sems.at[slot]
        )

    def fill(self):
        for k in range(min(self.depth, self.pieces)):
            self.copy(k).start()

    def take(self, k):
        self.copy(k).wait()
        value = self.buffer[k % self.depth].astype(jnp.float32)

        @pl.when(k + self.depth < self.pieces)
        def _():
            self.copy(k + self.depth).start()

        return value


def back_kernel(
    count,
    half,
    sizes,
    facts,
    lse,
    earlier,
    down_bias,
    pre_gain,
    small_own,
    q_in,
    k_in,
    v_in,
    do_in,
    act,
    down_in,
    residual,
    hidden,
    grad_in,
    qkv_in,
    mid,
    cotangent,
    branch,
    normed,
    grad_pre,
    attended,
    hidden_out,
    input_grad,
    up_grad,
    down_grad,
    out_grad,
    qkv_grad,
    sums_out,
    part,
    moving1,
    moving2,
    down,
    qkv_w,
    dq,
    dk,
    dv,
    dk_acc,
    dv_acc,
    k_t,
    dks,
    dvs,
    swap_out,
    swap_in,
    act_in,
    acc,
    small_sent,
    small_got,
    *rest,
):
    rest = list(rest)
    take = lambda n: [rest.pop(0) for _ in range(n)]
    rings = take(6)
    sems1, sems2 = take(5), take(5)
    small_sems = take(2)
    load_sem, act_sem, swap_sent, swap_got = take(4)
    rows, width = 2 * half, dq.shape[1]
    pieces = half // PIECE
    me = lax.axis_index("mp")
    owner = (me == 0) | (me == count - 1)
    offset = jnp.where(me == 0, 0, half)
    residual_ring = Ring(residual, *rings[0:2], pieces, 0)
    grad_ring = Ring(grad_in, *rings[2:4], pieces, 0)
    hidden_ring = Ring(hidden, *rings[4:6], pieces, offset)
    group = part.shape[2]

    def act_copy(flow, g):
        return pltpu.make_async_copy(
            act.at[pl.ds(pl.multiple_of(flow * half + g * group, 16), group)],
            act_in.at[flow],
            act_sem.at[flow],
        )

    def multiply_down(flow, g):
        act_copy(flow, g).wait()
        product = mm(act_in[flow], down[...])

        @pl.when(g + 1 < half // group)
        def _():
            act_copy(flow, g + 1).start()

        return product

    def finish_first(flow, k, total):
        return residual_ring.take(k) + total + down_bias[...]

    def finish_second(flow, k, total):
        values, inverse = norm_stats(hidden_ring.take(k))
        acc[0] += fold(total * values)
        acc[1] += fold(total)
        return grad_ring.take(k) + norm_back(total, values, inverse, pre_gain[...])

    line1 = Line(count, half, multiply_down, finish_first, hidden_out, part, moving1, sems1)
    multiply_back = group_product([dq, dk, dv], qkv_w, NT, half, group)
    line2 = Line(
        count, half, multiply_back, finish_second, input_grad, part, moving2, sems2, late=True
    )
    heads = AttendBack.__new__(AttendBack)
    heads.bq = query_block(rows)
    heads.blocks = rows // heads.bq
    heads.pairs = width // PAIR
    heads.steps = heads.pairs * heads.blocks
    heads.causal = True
    views = [Columns(moving2, j * width, width) for j in range(4)]
    tables = [earlier.at[0], earlier.at[1]]
    heads.ins = (facts, *views[:3], *tables, views[3], lse)
    heads.outs = (dq, dk, dv, dks, dvs)
    heads.scratch = (dk_acc, dv_acc, k_t)
    second = heads.steps + 2
    columns = (
        (0, grad_pre, 0, 0),
        (1, act, 1, 0),
        (2, attended, 2, 0),
        (3, dq, 3, 0),
        (3, dk, 3, width),
        (3, dv, 3, 2 * width),
    )
    spread = Spread(
        (mid, cotangent, branch, normed),
        columns,
        (up_grad, down_grad, out_grad, qkv_grad),
        down.at[pl.ds(0, rows)],
        rest,
        heads.steps - 2,
    )
    small = SmallSums(sizes, 6, second + pieces + SKEW * (count - 1), small_own)
    small((small_own,), (sums_out,), (small_sent, small_got, *small_sems), (acc,))
    loads = [
        pltpu.make_async_copy(source, target, load_sem.at[number])
        for number, (source, target) in enumerate(
            [(down_in, down), (qkv_in, qkv_w)]
            + [
                (source, moving2.at[:, pl.ds(j * width, width)])
                for j, source in enumerate((q_in, k_in, v_in, do_in))
            ]
        )
    ]
    swap = pltpu.make_async_remote_copy(
        src_ref=swap_out,
        dst_ref=swap_in,
        send_sem=swap_sent.at[0],
        recv_sem=swap_got.at[0],
        device_id=spread.to_y,
        device_id_type=MESH,
    )

    barrier = pltpu.get_barrier_semaphore()
    line1.greet(barrier)
    spread.greet(barrier)
    small.greet(barrier)
    for flow in range(2):
        act_copy(flow, 0).start()
    for load in loads:
        load.start()

    @pl.when(owner)
    def _():
        for ring in (residual_ring, grad_ring, hidden_ring):
            ring.fill()

    acc[...] = jnp.zeros_like(acc)
    small.first()
    loads[0].wait()
    line1.first()
    line1.meet(barrier, spread.others + small.others)
    for load in loads[1:]:
        load.wait()

    def step(t, carry):
        line1.step(t)
        heads.step(t)

        @pl.when(t == heads.steps)
        def _():
            swap_out[0] = dks[...].astype(jnp.bfloat16)
            swap_out[1] = dvs[...].astype(jnp.bfloat16)
            swap.start()

        @pl.when(t == heads.steps + 1)
        def _():
            swap.wait()
            shape = (rows, SUMM_ROWS)
            chosen = lax.broadcasted_iota(jnp.int32, shape, 0) == (
                facts[1] - SUMM + lax.broadcasted_iota(jnp.int32, shape, 1)
            )
            chosen = jnp.where(chosen, 1.0, 0.0).astype(jnp.bfloat16)
            for number, grad in enumerate((dk, dv)):
                added = grad[...].astype(jnp.float32) + mm(chosen, swap_in[number])
                grad[...] = added.astype(jnp.bfloat16)
            for number, grad in enumerate((dq, dv)):
                small.extra(6 + down_in.shape[0] // down_in.shape[1], number * width, grad)

        line2.step(t - second)
        spread.step(t)
        small.step(t)
        return carry

    lax.fori_loop(0, max(second + line2.steps, spread.steps, small.steps), step, 0)
    line1.settle()
    line2.settle()
    spread.settle()


def back_sums(number, count, sizes, small_in, whole_in, vmem_in):
    rows, width = whole_in[0].shape
    features = whole_in[5].shape[1]
    ff = whole_in[5].shape[0]
    half = rows // 2
    low = lambda *shape: pltpu.VMEM(shape, jnp.bfloat16)
    wide = lambda *shape: pltpu.VMEM(shape, jnp.float32)
    dma = lambda *shape: pltpu.SemaphoreType.DMA(shape)
    lines = Line.scratch(half, features)
    group = lines[0].shape[2]
    stages = sum(size.bit_length() - 1 for _, size in sizes)
    block = Spread.block
    return pl.pallas_call(
        functools.partial(back_kernel, count, half, sizes),
        in_specs=[SMEM] + [VMEM] * 5 + [ANY] * len(whole_in),
        out_specs=[ANY] * 6 + [VMEM],
        out_shape=[
            jax.ShapeDtypeStruct((rows, features), jnp.bfloat16),
            jax.ShapeDtypeStruct((rows, features), jnp.bfloat16),
            jax.ShapeDtypeStruct((block, ff), jnp.float32),
            jax.ShapeDtypeStruct((ff, block), jnp.float32),
            jax.ShapeDtypeStruct((width, block), jnp.float32),
            jax.ShapeDtypeStruct((block, 3 * width), jnp.float32),
            jax.ShapeDtypeStruct(small_in.shape, jnp.float32),
        ],
        scratch_shapes=[
            lines[0],
            lines[1],
            lines[1],
            low(ff, features),
            low(features, 3 * width),
            low(rows, width),
            low(rows, width),
            low(rows, width),
            wide(rows, PAIR),
            wide(rows, PAIR),
            low(PAIR, rows),
            wide(SUMM_ROWS, width),
            wide(SUMM_ROWS, width),
            low(2, SUMM_ROWS, width),
            low(2, SUMM_ROWS, width),
            low(2, group, ff),
            wide(2, 8, features),
            wide(stages, *small_in.shape),
            wide(stages, *small_in.shape),
        ]
        + Ring.scratch(features, jnp.float32)
        + Ring.scratch(features, jnp.float32)
        + Ring.scratch(features, jnp.bfloat16)
        + lines[2:]
        + lines[2:]
        + [dma(stages), dma(stages), dma(6), dma(2), dma(1), dma(1)]
        + Spread.scratch(rows),
        compiler_params=pltpu.CompilerParams(
            collective_id=number, has_side_effects=True, vmem_limit_bytes=63 * MIB
        ),
        cost_estimate=pl.CostEstimate(
            flops=12 * rows * features * ff, bytes_accessed=60 * rows * features, transcendentals=0
        ),
        name="back_sums",
    )(*vmem_in, small_in, *whole_in)


def gradients_over(group, lefts, columns):
    over_rows = lambda left, right: mm(left, right, (((0,), (0,)), ((), ()))).astype(jnp.bfloat16)
    parts = [[] for _ in range(4)]
    for left, right, result, _ in columns:
        across = result in (0, 3)
        product = over_rows(lefts[left], right) if across else over_rows(right, lefts[left])
        parts[result].append(product)
    return [
        lax.psum_scatter(
            jnp.concatenate(part, axis=1),
            group,
            scatter_dimension=0 if result in (0, 3) else 1,
            tiled=True,
        ).astype(jnp.float32)
        for result, part in enumerate(parts)
    ]


def body(
    item_count,
    seq_count,
    mp_count,
    hidden_in,
    cotangent,
    seg_lengths,
    pre_gain,
    pre_shift,
    qkv_weight,
    qv_bias,
    out_weight,
    out_bias,
    mid_gain,
    mid_shift,
    up_weight,
    up_bias,
    down_weight,
    down_bias,
):
    group = ("item", "seq")
    width = qkv_weight.shape[2]
    gathered = lambda weight, axis: lax.all_gather(weight, group, axis=axis, tiled=True)
    hidden = hidden_in[0].astype(jnp.float32)
    lengths = seg_lengths[0]
    rows = hidden.shape[0]
    first_row = lax.axis_index("seq") * rows
    segment = first_row // SLOT
    facts = jnp.stack(
        [
            first_row % SLOT,
            lengths[segment] + SUMM,
            jnp.where(segment > 0, SUMM, 0),
        ]
    ).astype(jnp.int32)

    ours = (item_count, seq_count) == (4, 2) and rows == SLOT
    row = lambda vector: vector[None, :]
    shard = qkv_weight.reshape(-1, 3 * width)
    if ours:
        q, k, v, summary, normed, qkv_full, out_full = start(
            5, facts, hidden_in[0], row(pre_gain), row(pre_shift), qv_bias, shard, out_weight
        )
        attend_in = (facts, q, k, v, summary)
        tables = (k, v, summary[0], summary[1])
    else:
        qkv_full = gathered(shard, 0)
        out_full = gathered(out_weight, 1)
        normed = (norm_stats(hidden)[0] * pre_gain + pre_shift).astype(jnp.bfloat16)
        q = (mm(normed, qkv_full[:, :width]) + qv_bias[0]).astype(jnp.bfloat16)
        k = mm(normed, qkv_full[:, width : 2 * width]).astype(jnp.bfloat16)
        v = (mm(normed, qkv_full[:, 2 * width :]) + qv_bias[1]).astype(jnp.bfloat16)
        own, summary = keys_for(jnp.stack([k, v]), lengths, seq_count)
        tables = (own[0], own[1], summary[0], summary[1])
        attended, log_total = attend(facts, q, *tables)
        attend_in = (attended,)

    grad_down = cotangent[0]
    (
        mid_low,
        act_low,
        grad_pre,
        residual,
        grad_branch,
        grad_residual,
        down_full,
        mid_sums,
        up_sums,
        down_sums,
        *attend_out,
    ) = ffn_sums(
        1,
        mp_count,
        Gather if ours else Load,
        attend_in,
        out_full,
        (row(out_bias), row(mid_gain), row(mid_shift), row(up_bias)),
        hidden_in[0],
        grad_down,
        up_weight if ours else gathered(up_weight, 0),
        down_weight if ours else gathered(down_weight, 1),
    )
    if ours:
        attended, log_total = attend_out
    grad_attended = mm(grad_branch, out_full, NT).astype(jnp.bfloat16)
    total = lambda value: jnp.sum(value.astype(jnp.float32), axis=0)
    features = hidden.shape[1]
    sizes = [("item", item_count), ("seq", seq_count), ("mp", mp_count)]
    once = lambda value: jnp.where(lax.axis_index("mp") == 0, value, 0.0)
    small_in = lambda qv_sums: jnp.concatenate(
        [
            jnp.sum(mid_sums, axis=1),
            jnp.zeros((2, features), jnp.float32),
            row(once(total(down_sums))),
            total(up_sums).reshape(-1, features),
            jnp.pad(qv_sums, (0, -qv_sums.shape[0] % features)).reshape(-1, features),
        ]
    )
    if ours:
        hidden_out, grad_input, up_grad, down_grad, out_grad, qkv_grad, sums = back_sums(
            2,
            mp_count,
            sizes,
            small_in(jnp.zeros((2 * width,), jnp.float32)),
            (q, k, v, grad_attended, act_low, down_full, residual, hidden_in[0], grad_residual)
            + (qkv_full, mid_low, grad_down, grad_branch, normed, grad_pre, attended),
            (facts, log_total, summary, row(down_bias), row(pre_gain)),
        )
    else:
        hidden_out, dq, dk, dv, dks, dvs = line_sum(
            3,
            mp_count,
            [act_low],
            down_full,
            NN,
            [residual, row(down_bias)],
            0,
            0,
            finish_out,
            "down_sum",
            (AttendBack(facts, q, *tables, grad_attended, log_total),),
        )
        dk, dv = keys_back(jnp.stack([dk, dv]), jnp.stack([dks, dvs]), rows, lengths, seq_count)
        small = SmallSums(
            sizes,
            6,
            rows // 2 // PIECE + SKEW * (mp_count - 1),
            small_in(jnp.concatenate([total(dq), total(dv)])),
        )
        grad_input, _, sums = line_sum(
            4,
            mp_count,
            [dq, dk, dv],
            qkv_full,
            NT,
            [hidden_in[0], grad_residual, row(pre_gain)],
            0,
            2,
            finish_input,
            "input_sum",
            (small,),
        )
        lefts = (mid_low, grad_down, grad_branch, normed)
        columns = (
            (0, grad_pre, 0, 0),
            (1, act_low, 1, 0),
            (2, attended, 2, 0),
            (3, dq, 3, 0),
            (3, dk, 3, width),
            (3, dv, 3, 2 * width),
        )
        up_grad, down_grad, out_grad, qkv_grad = gradients_over(group, lefts, columns)
    ff_rows = up_weight.shape[1] // features
    up_bias_grad = sums[6 : 6 + ff_rows].reshape(-1)
    qv_bias_grad = sums[6 + ff_rows :].reshape(-1)[: 2 * width].reshape(2, width)
    return (
        hidden_out[None],
        grad_input.astype(jnp.float32)[None],
        sums[3],
        sums[4],
        qkv_grad.reshape(-1, 3, width),
        qv_bias_grad,
        out_grad,
        sums[2],
        sums[0],
        sums[1],
        up_grad,
        up_bias_grad,
        down_grad,
        sums[5],
    )


def solution(mesh):
    rows = P("item", "seq", None)
    qkv = P(("item", "seq"), None, "mp")
    first = P(("item", "seq"), "mp")
    second = P("mp", ("item", "seq"))
    bias = P(None, "mp")
    return jax.shard_map(
        functools.partial(body, mesh.shape["item"], mesh.shape["seq"], mesh.shape["mp"]),
        mesh=mesh,
        in_specs=(
            rows,
            rows,
            P("item", None),
            P(),
            P(),
            qkv,
            bias,
            second,
            P(),
            P(),
            P(),
            first,
            P("mp"),
            second,
            P(),
        ),
        out_specs=(
            rows,
            rows,
            P(),
            P(),
            qkv,
            bias,
            second,
            P(),
            P(),
            P(),
            first,
            P("mp"),
            second,
            P(),
        ),
        check_vma=False,
    )
```

```python
import functools
import math

import jax
import jax.numpy as jnp
from jax import lax
from jax.experimental import pallas as pl
from jax.experimental.pallas import tpu as pltpu
from jax.sharding import PartitionSpec as P

HDIM = 64
SLOT = 1280
SEGS = 2
SUMM = 50
SUMM_ROWS = 64
TOKENS = 2560
PAIR = 2 * HDIM
PIECE = 32
SKEW = 2
LEAD = 2
GATHER_STEPS = (7, 11, 13, 15)
MIB = 1 << 20
MESH = pl.DeviceIdType.MESH
MASKED = -1e30


eps = 1e-05

NN = (((1,), (0,)), ((), ()))
NT = (((1,), (1,)), ((), ()))


def mm(left, right, dims=NN):
    return lax.dot_general(left, right, dims, preferred_element_type=jnp.float32)


def norm_stats(values):
    center = jnp.mean(values, axis=-1, keepdims=True)
    centered = values - center
    inverse = lax.rsqrt(jnp.mean(centered * centered, axis=-1, keepdims=True) + eps)
    return centered * inverse, inverse


def norm_back(grad_out, normed, inverse, gain):
    scaled = grad_out * gain
    centered = scaled - jnp.mean(scaled, axis=-1, keepdims=True)
    return inverse * (centered - normed * jnp.mean(scaled * normed, axis=-1, keepdims=True))


def gelu_parts(values):
    c = math.sqrt(2 / math.pi)
    squared = values * values
    t = jnp.tanh(c * values * (1 + 0.044715 * squared))
    half = 0.5 * (1 + t)
    slope = half + 0.5 * values * (1 - t * t) * (c * (1 + 3 * 0.044715 * squared))
    return values * half, slope


def key_masks(facts_ref, block, rows, bq, nk):
    first = facts_ref[0] + block * bq
    limit = jnp.minimum(
        first + 1 + lax.broadcasted_iota(jnp.int32, (1, bq), 1), facts_ref[1]
    )
    own = lax.broadcasted_iota(jnp.int32, (nk, bq), 0) < limit
    earlier = lax.broadcasted_iota(jnp.int32, (SUMM_ROWS, bq), 0) < facts_ref[2]
    return own, earlier


class Facts:
    def __init__(self, lengths):
        segment = lax.axis_index("seq")
        self.values = (0, lengths[0, segment] + SUMM, jnp.where(segment > 0, SUMM, 0))

    def __getitem__(self, index):
        return self.values[index]


def head_lanes(head):
    lane = lax.broadcasted_iota(jnp.int32, (1, PAIR), 1)
    return (lane >= head * HDIM) & (lane < (head + 1) * HDIM)


def attend_kernel(bq, causal, facts_ref, q_ref, k_ref, v_ref, ks_ref, vs_ref, o_ref, lse_ref):
    rows, seg = q_ref.shape[0], k_ref.shape[0]
    v_t = v_ref[...].T
    vs_t = vs_ref[...].T
    ks = ks_ref[...]
    low_half = lax.broadcasted_iota(jnp.int32, (PAIR, 1), 0) < HDIM
    for block in range(rows // bq):
        nk = (block + 1) * bq if causal else seg
        own, earlier = key_masks(facts_ref, block, rows, bq, nk)
        q = q_ref[block * bq : (block + 1) * bq, :] * jnp.bfloat16(HDIM**-0.5)
        mixed = []
        for head in range(2):
            qh = jnp.where(head_lanes(head), q, jnp.zeros_like(q))
            s = jnp.where(own, mm(k_ref[:nk, :], qh, NT), MASKED)
            s2 = jnp.where(earlier, mm(ks, qh, NT), MASKED)
            top = jnp.maximum(jnp.max(s, axis=0, keepdims=True), jnp.max(s2, axis=0, keepdims=True))
            p = jnp.exp(s - top)
            p2 = jnp.exp(s2 - top)
            total = jnp.sum(p, axis=0, keepdims=True) + jnp.sum(p2, axis=0, keepdims=True)
            out = mm(v_t[:, :nk], p.astype(jnp.bfloat16)) + mm(vs_t, p2.astype(jnp.bfloat16))
            mixed.append(out / total)
            lse_ref[0, head : head + 1, block * bq : (block + 1) * bq] = top + jnp.log(total)
        joined = jnp.where(low_half, mixed[0], mixed[1])
        o_ref[block * bq : (block + 1) * bq, :] = joined.T.astype(jnp.bfloat16)


def query_block(rows):
    return 256 if rows % 256 == 0 else math.gcd(rows, 160)


def attend(facts, q, k, v, ks, vs):
    rows, width = q.shape
    seg = k.shape[0]
    pairs = width // PAIR
    column = lambda n: pl.BlockSpec((n, PAIR), lambda i: (0, i))
    return pl.pallas_call(
        functools.partial(attend_kernel, query_block(rows), rows == seg),
        grid=(pairs,),
        in_specs=[pl.BlockSpec(memory_space=pltpu.SMEM)]
        + [column(n) for n in (rows, seg, seg, SUMM_ROWS, SUMM_ROWS)],
        out_specs=[column(rows), pl.BlockSpec((1, 2, rows), lambda i: (i, 0, 0))],
        out_shape=[
            jax.ShapeDtypeStruct((rows, width), jnp.bfloat16),
            jax.ShapeDtypeStruct((pairs, 2, rows), jnp.float32),
        ],
        compiler_params=pltpu.CompilerParams(vmem_limit_bytes=48 * MIB),
        cost_estimate=pl.CostEstimate(
            flops=4 * rows * seg * width, bytes_accessed=8 * rows * width, transcendentals=0
        ),
        name="attend",
    )(facts, q, k, v, ks, vs)


def keys_for(local, lengths, seq_count):
    rows, width = local.shape[-2:]
    pad = ((0, 0), (0, SUMM_ROWS - SUMM), (0, 0))
    if rows == SLOT:
        here = lengths[lax.axis_index("seq")]
        summary = jnp.pad(lax.dynamic_slice(local, (0, here, 0), (2, SUMM, width)), pad)
        moves = [(i, i + 1) for i in range(seq_count - 1)]
        return local, lax.ppermute(summary, "seq", moves)
    everything = lax.all_gather(local, "seq", axis=1, tiled=True)
    segment = lax.axis_index("seq") * rows // SLOT
    own = lax.dynamic_slice(everything, (0, segment * SLOT, 0), (2, SLOT, width))
    summary = lax.dynamic_slice(everything, (0, lengths[0], 0), (2, SUMM, width))
    return own, jnp.pad(summary, pad)


def keys_back(own, summary, rows, lengths, seq_count):
    width = own.shape[-1]
    summary = summary[:, :SUMM]
    if rows == SLOT:
        moves = [(i + 1, i) for i in range(seq_count - 1)]
        arrived = lax.ppermute(summary, "seq", moves)
        here = lengths[lax.axis_index("seq")]
        old = lax.dynamic_slice(own, (0, here, 0), (2, SUMM, width))
        new = (old.astype(jnp.float32) + arrived).astype(jnp.bfloat16)
        return lax.dynamic_update_slice(own, new, (0, here, 0))
    segment = lax.axis_index("seq") * rows // SLOT
    everything = jnp.zeros((2, TOKENS, width), jnp.float32)
    everything = lax.dynamic_update_slice(
        everything, own.astype(jnp.float32), (0, segment * SLOT, 0)
    )
    old = lax.dynamic_slice(everything, (0, lengths[0], 0), (2, SUMM, width))
    added = jnp.where(segment > 0, summary, 0.0)
    everything = lax.dynamic_update_slice(everything, old + added, (0, lengths[0], 0))
    return lax.psum_scatter(
        everything.astype(jnp.bfloat16), "seq", scatter_dimension=1, tiled=True
    )


class Line:
    def __init__(self, count, half, multiply, finish, out, part, moving, sems, late=False):
        self.count, self.half, self.multiply, self.finish = count, half, multiply, finish
        self.late = late
        self.out, self.part, self.moving = out, part, moving
        self.up_sent, self.up_got, self.down_sent, self.down_got, self.local = sems
        self.me = lax.axis_index("mp")
        self.pieces = half // PIECE
        self.per_group = part.shape[2] // PIECE
        self.steps = self.pieces + 2 * SKEW * (count - 1)

    @staticmethod
    def scratch(half, features):
        pieces = half // PIECE
        group = 160 if half % 160 == 0 else PIECE
        dma = lambda *shape: pltpu.SemaphoreType.DMA(shape)
        return [
            pltpu.VMEM((2, 2, group, features), jnp.float32),
            pltpu.VMEM((2 * (half + LEAD * PIECE), features), jnp.bfloat16),
            dma(2, pieces),
            dma(2, pieces),
            dma(2, pieces),
            dma(2, pieces),
            dma(2, pieces),
        ]

    def place(self, flow):
        return self.count - 1 - self.me if flow == 0 else self.me

    def greet(self, barrier):
        me = self.me

        @pl.when(me > 0)
        def _():
            pl.semaphore_signal(barrier, inc=1, device_id={"mp": me - 1}, device_id_type=MESH)

        @pl.when(me < self.count - 1)
        def _():
            pl.semaphore_signal(barrier, inc=1, device_id={"mp": me + 1}, device_id_type=MESH)

    def meet(self, barrier, others=0):
        ends = (self.me == 0) | (self.me == self.count - 1)

        @pl.when(ends)
        def _():
            pl.semaphore_wait(barrier, 1 + others)

        @pl.when(jnp.logical_not(ends))
        def _():
            pl.semaphore_wait(barrier, 2 + others)

    def first(self):
        for flow in range(2):
            self.part[flow, 0] = self.multiply(flow, 0)

    def spot(self, flow, k):
        return flow * (self.half + LEAD * PIECE) + k * PIECE

    def spots(self, flow, k, size=PIECE):
        return pl.ds(pl.multiple_of(self.spot(flow, k), PIECE), size)

    def finished(self, flow, k, size):
        mine = self.place(flow) == self.count - 1
        return self.spots(flow, jnp.where(mine, k + LEAD, k), size)

    def onward(self, flow, k):
        here = self.moving.at[self.spots(flow, k + LEAD)]
        return pltpu.make_async_remote_copy(
            src_ref=here,
            dst_ref=here,
            send_sem=self.up_sent.at[flow, k],
            recv_sem=self.up_got.at[flow, k],
            device_id={"mp": self.me - 1 if flow == 0 else self.me + 1},
            device_id_type=MESH,
        )

    def back(self, flow, k, owner):
        here = self.moving.at[self.spots(flow, k)]
        return pltpu.make_async_remote_copy(
            src_ref=self.moving.at[self.spots(flow, k + LEAD)] if owner else here,
            dst_ref=here,
            send_sem=self.down_sent.at[flow, k],
            recv_sem=self.down_got.at[flow, k],
            device_id={"mp": self.me + 1 if flow == 0 else self.me - 1},
            device_id_type=MESH,
        )

    def keep(self, flow, k, owner):
        return pltpu.make_async_copy(
            self.moving.at[self.spots(flow, k + LEAD if owner else k)],
            self.out.at[pl.ds(flow * self.half + k * PIECE, PIECE)],
            self.local.at[flow, k],
        )

    def send_on(self, flow, k):
        @pl.when(k >= LEAD)
        def _():
            self.onward(flow, k - LEAD).wait_send()

        self.onward(flow, k).start()

    def step(self, t):
        last = self.count - 1
        for flow in range(2):
            place = self.place(flow)
            k = t - SKEW * place
            here = self.spots(flow, k + LEAD)
            busy = (k >= 0) & (k < self.pieces)

            def mine():
                slot = (k // self.per_group) % 2
                inner = pl.ds(pl.multiple_of((k % self.per_group) * PIECE, PIECE), PIECE)
                return self.part[flow, slot, inner, :]

            @pl.when(busy & (place == 0))
            def _():
                self.moving[here, :] = mine().astype(jnp.bfloat16)
                self.send_on(flow, k)

            @pl.when(busy & (place > 0) & (place < last))
            def _():
                self.onward(flow, k).wait_recv()
                total = mine() + self.moving[here, :].astype(jnp.float32)
                self.moving[here, :] = total.astype(jnp.bfloat16)
                self.send_on(flow, k)

            @pl.when(busy & (place == last))
            def _():
                self.onward(flow, k).wait_recv()
                total = mine() + self.moving[here, :].astype(jnp.float32)
                self.moving[here, :] = self.finish(flow, k, total).astype(jnp.bfloat16)
                self.back(flow, k, True).start()
                self.keep(flow, k, True).start()

        for flow in range(2):
            place = self.place(flow)
            j = t - SKEW * (2 * last - place)

            @pl.when((j >= 0) & (j < self.pieces) & (place < last))
            def _():
                self.back(flow, j, False).wait_recv()

                @pl.when(place > 0)
                def _():
                    self.back(flow, j, False).start()

                self.keep(flow, j, False).start()

        for flow in range(2 if self.multiply else 0):
            k = t - SKEW * self.place(flow)
            g = k // self.per_group + 1

            if self.late:

                @pl.when(k == -1)
                def _():
                    self.part[flow, 0] = self.multiply(flow, 0)

            @pl.when((k >= 0) & (k % self.per_group == 0) & (g < self.pieces // self.per_group))
            def _():
                self.part[flow, g % 2] = self.multiply(flow, g)

    def settle(self):
        last = self.count - 1

        def one(k, carry):
            for flow in range(2):
                place = self.place(flow)

                @pl.when((place < last) & (k >= self.pieces - LEAD))
                def _():
                    self.onward(flow, k).wait_send()

                @pl.when((place > 0) & (place < last))
                def _():
                    self.back(flow, k, False).wait_send()

                @pl.when(place < last)
                def _():
                    self.keep(flow, k, False).wait()

                @pl.when(place == last)
                def _():
                    self.back(flow, k, True).wait_send()
                    self.keep(flow, k, True).wait()

            return carry

        lax.fori_loop(0, self.pieces, one, 0)


def group_product(lefts, right, dims, half, group):
    def multiply(flow, g):
        rows = pl.ds(pl.multiple_of(flow * half + g * group, 16), group)
        at, total = 0, None
        for left in lefts:
            depth = left.shape[1]
            cut = right[:, at : at + depth] if dims == NT else right[at : at + depth, :]
            product = mm(left[rows, :], cut, dims)
            total = product if total is None else total + product
            at += depth
        return total

    return multiply


def line_kernel(count, half, dims, n_left, n_extra, n_owned, n_acc, finish, sides, *refs):
    refs = list(refs)
    take = lambda n: [refs.pop(0) for _ in range(n)]
    lefts, (right,), extras = take(n_left), take(1), take(n_extra)
    side_in = [take(side.n_in) for side in sides]
    (out,), owned, accs = take(1), take(n_owned), take(1 if n_acc else 0)
    side_out = [take(side.n_out) for side in sides]
    part, moving, sems = *take(2), take(5)
    multiply = group_product(lefts, right, dims, half, part.shape[2])
    ending = lambda flow, k, total: finish(flow, k, total, extras, owned, accs)
    line = Line(count, half, multiply, ending, out, part, moving, sems)
    jobs = [
        side(ins, outs, take(len(side.scratch_shapes)), accs)
        for side, ins, outs in zip(sides, side_in, side_out)
    ]
    barrier = pltpu.get_barrier_semaphore()
    line.greet(barrier)
    for job in jobs:
        job.greet(barrier)
    if n_acc:
        accs[0][...] = jnp.zeros_like(accs[0])
    for job in jobs:
        job.first()
    line.first()
    line.meet(barrier, sum(job.others for job in jobs))

    def step(t, carry):
        line.step(t)
        for job in jobs:
            job.step(t)
        return carry

    lax.fori_loop(0, max([line.steps] + [job.steps for job in jobs]), step, 0)
    line.settle()
    for job in jobs:
        job.settle()


class Nothing:
    n_in = n_out = others = steps = 0
    operands, in_specs, out_shape, out_specs, scratch_shapes = (), (), (), (), ()

    def __call__(self, ins, outs, scratch, accs):
        return self

    def greet(self, barrier):
        pass

    def first(self):
        pass

    def step(self, t):
        pass

    def settle(self):
        pass


VMEM = pl.BlockSpec(memory_space=pltpu.VMEM)
ANY = pl.BlockSpec(memory_space=pl.ANY)
SMEM = pl.BlockSpec(memory_space=pltpu.SMEM)


def line_sum(number, count, lefts, right, dims, extras, n_owned, n_acc, finish, name, sides):
    rows = lefts[0].shape[0]
    features = right.shape[1 if dims == NN else 0]
    half = rows // 2
    acc = [jax.ShapeDtypeStruct((n_acc, 8, features), jnp.float32)] if n_acc else []
    return pl.pallas_call(
        functools.partial(
            line_kernel,
            count,
            half,
            dims,
            len(lefts),
            len(extras),
            n_owned,
            n_acc,
            finish,
            sides,
        ),
        in_specs=[VMEM] * (len(lefts) + 1 + len(extras)) + [s for side in sides for s in side.in_specs],
        out_specs=[ANY] + [VMEM] * (n_owned + len(acc)) + [s for side in sides for s in side.out_specs],
        out_shape=[jax.ShapeDtypeStruct((rows, features), jnp.bfloat16)]
        + [jax.ShapeDtypeStruct((half, features), jnp.float32)] * n_owned
        + acc
        + [s for side in sides for s in side.out_shape],
        scratch_shapes=Line.scratch(half, features) + [s for side in sides for s in side.scratch_shapes],
        compiler_params=pltpu.CompilerParams(
            collective_id=number, has_side_effects=True, vmem_limit_bytes=62 * MIB
        ),
        cost_estimate=pl.CostEstimate(
            flops=2 * rows * features * sum(left.shape[1] for left in lefts),
            bytes_accessed=4 * rows * features,
            transcendentals=0,
        ),
        name=name,
    )(*lefts, right, *extras, *[value for side in sides for value in side.operands])


def piece_rows(flow, k, half):
    return pl.ds(pl.multiple_of(flow * half + k * PIECE, PIECE), PIECE)


def fold(values):
    return jnp.sum(values.reshape(-1, 8, values.shape[-1]), axis=0)


def finish_input(flow, k, total, extras, owned, accs):
    hidden, grad, gain = extras
    (acc,) = accs
    half = grad.shape[0]
    normed, inverse = norm_stats(hidden[piece_rows(flow, k, half), :].astype(jnp.float32))
    acc[0] += fold(total * normed)
    acc[1] += fold(total)
    return grad[piece_rows(0, k, half), :] + norm_back(total, normed, inverse, gain[...])


def finish_out(flow, k, total, extras, owned, accs):
    residual, bias = extras
    half = residual.shape[0]
    return residual[piece_rows(0, k, half), :] + total + bias[...]


class AttendBack(Nothing):
    n_in, n_out = 8, 5

    def __init__(self, facts, q, k, v, ks, vs, do, lse):
        rows, width = q.shape
        seg = k.shape[0]
        self.operands = (facts, q, k, v, ks, vs, do, lse)
        self.in_specs = (SMEM,) + (VMEM,) * 7
        low = lambda n: jax.ShapeDtypeStruct((n, width), jnp.bfloat16)
        wide = lambda n: jax.ShapeDtypeStruct((n, width), jnp.float32)
        self.out_shape = (low(rows), low(seg), low(seg), wide(SUMM_ROWS), wide(SUMM_ROWS))
        self.out_specs = (VMEM,) * 5
        self.scratch_shapes = (
            pltpu.VMEM((seg, PAIR), jnp.float32),
            pltpu.VMEM((seg, PAIR), jnp.float32),
            pltpu.VMEM((PAIR, seg), jnp.bfloat16),
        )
        self.bq = query_block(rows)
        self.blocks = rows // self.bq
        self.pairs = width // PAIR
        self.steps = self.pairs * self.blocks
        self.causal = rows == seg

    def __call__(self, ins, outs, scratch, accs):
        self.ins, self.outs, self.scratch = ins, outs, scratch
        return self

    def step(self, t):
        pair = t // self.blocks
        for block in range(self.blocks):

            @pl.when((t >= 0) & (t < self.steps) & (t % self.blocks == block))
            def _():
                self.unit(pair, block)

    def unit(self, pair, block):
        facts, q_ref, k_ref, v_ref, ks_ref, vs_ref, do_ref, lse_ref = self.ins
        dq_ref, dk_ref, dv_ref, dks_ref, dvs_ref = self.outs
        dk_acc, dv_acc, k_t = self.scratch
        seg, bq = k_ref.shape[0], self.bq
        cols = pl.ds(pl.multiple_of(pair * PAIR, PAIR), PAIR)
        scale = jnp.bfloat16(HDIM**-0.5)
        low_half = lax.broadcasted_iota(jnp.int32, (PAIR, 1), 0) < HDIM
        if block == 0:
            k_t[...] = (k_ref[:, cols] * scale).T
            dk_acc[...] = jnp.zeros_like(dk_acc)
            dv_acc[...] = jnp.zeros_like(dv_acc)
            dks_ref[:, cols] = jnp.zeros((SUMM_ROWS, PAIR), jnp.float32)
            dvs_ref[:, cols] = jnp.zeros((SUMM_ROWS, PAIR), jnp.float32)
        ks, vs = ks_ref[:, cols], vs_ref[:, cols]
        ks_t = (ks * scale).T
        nk = (block + 1) * bq if self.causal else seg
        here = slice(block * bq, (block + 1) * bq)
        own, earlier = key_masks(facts, block, self.blocks * bq, bq, nk)
        q = q_ref[here, cols] * scale
        do = do_ref[here, cols]
        k, v = k_ref[:nk, cols], v_ref[:nk, cols]
        grads = []
        for head in range(2):
            qh = jnp.where(head_lanes(head), q, jnp.zeros_like(q))
            doh = jnp.where(head_lanes(head), do, jnp.zeros_like(do))
            lse = lse_ref[pair, head : head + 1, here]
            p = jnp.exp(jnp.where(own, mm(k, qh, NT), MASKED) - lse)
            p2 = jnp.exp(jnp.where(earlier, mm(ks, qh, NT), MASKED) - lse)
            dp = mm(v, doh, NT)
            dp2 = mm(vs, doh, NT)
            delta = jnp.sum(p * dp, axis=0, keepdims=True) + jnp.sum(p2 * dp2, axis=0, keepdims=True)
            ds = (p * (dp - delta)).astype(jnp.bfloat16)
            ds2 = (p2 * (dp2 - delta)).astype(jnp.bfloat16)
            dv_acc[:nk, :] += mm(p.astype(jnp.bfloat16), doh)
            dk_acc[:nk, :] += mm(ds, qh)
            dvs_ref[:, cols] += mm(p2.astype(jnp.bfloat16), doh)
            dks_ref[:, cols] += mm(ds2, qh)
            grads.append(mm(k_t[:, :nk], ds) + mm(ks_t, ds2))
        joined = jnp.where(low_half, grads[0], grads[1])
        dq_ref[here, cols] = joined.T.astype(jnp.bfloat16)
        if block == self.blocks - 1:
            dk_ref[:, cols] = dk_acc[...].astype(jnp.bfloat16)
            dv_ref[:, cols] = dv_acc[...].astype(jnp.bfloat16)


class Spread:
    others = 3
    block = 256
    lag = (2, 5, 8)
    across = (True, False, False, True)

    def __init__(self, lefts, columns, outs, left_now, scratch, start):
        self.lefts, self.outs, self.x_buf, self.start = lefts, outs, left_now, start
        self.table, self.phases, self.rights = [], {}, []
        at = 0
        for number, (left, right, result, place) in enumerate(columns):
            self.phases.setdefault(left, at)
            self.table.append((number, at, at + right.shape[1] // self.block, result, place))
            self.rights.append(right)
            at += right.shape[1] // self.block
        self.chunks = at
        self.steps = start + at + self.lag[2]
        (
            self.y_buf,
            self.s1,
            self.own,
            self.r1,
            self.s2x,
            self.s2y,
            self.top,
            self.low,
            self.r2x,
            self.r2y,
            self.s3,
            self.kept,
            self.r3,
            self.tile,
            self.x_sem,
            self.y_sem,
            self.s1_sem,
            self.r1_sem,
            self.s2x_sem,
            self.r2x_sem,
            self.s2y_sem,
            self.r2y_sem,
            self.s3y_sem,
            self.r3y_sem,
            self.s3x_sem,
            self.r3x_sem,
            self.out_sem,
        ) = scratch
        item, seq = lax.axis_index("item"), lax.axis_index("seq")
        self.core, self.x, self.y = item % 2, item // 2, seq
        self.to_core = {"item": item + 1 - 2 * self.core}
        self.to_x = {"item": item + 2 - 4 * self.x}
        self.to_y = {"seq": 1 - seq}

    @classmethod
    def scratch(cls, rows):
        block, half = cls.block, cls.block // 2
        low = lambda *shape: pltpu.VMEM(shape, jnp.bfloat16)
        wide = lambda *shape: pltpu.VMEM(shape, jnp.float32)
        return [
            low(2, rows, block),
            low(3, 2, block, 2 * block),
            wide(3, 2, block, 2 * block),
            low(4, 2, block, 2 * block),
            low(3, half, 2 * block),
            low(3, 2, half, block),
            wide(3, half, 2 * block),
            wide(3, 2, half, block),
            low(6, half, 2 * block),
            low(6, 2, half, block),
            low(3, 2, half, block),
            wide(3, 2, half, block),
            low(6, 2, half, block),
            wide(3, block, block),
        ] + [pltpu.SemaphoreType.DMA((n,)) for n in (1, 2, 3, 4, 3, 6, 3, 6, 3, 6, 3, 6, 3)]

    def greet(self, barrier):
        for to in (self.to_core, self.to_x, self.to_y):
            pl.semaphore_signal(barrier, inc=1, device_id=to, device_id_type=MESH)


    def left_copy(self, left):
        return pltpu.make_async_copy(self.lefts[left], self.x_buf, self.x_sem.at[0])

    def right_copy(self, m, act):
        for number, start, stop, _, _ in self.table:

            @pl.when((m >= start) & (m < stop))
            def _():
                cols = pl.ds(pl.multiple_of((m - start) * self.block, self.block), self.block)
                act(
                    pltpu.make_async_copy(
                        self.rights[number].at[:, cols], self.y_buf.at[m % 2], self.y_sem.at[m % 2]
                    )
                )

    def out_copy(self, m, act):
        for _, start, stop, result, place in self.table:

            @pl.when((m >= start) & (m < stop))
            def _():
                cols = pl.ds(
                    pl.multiple_of(place + (m - start) * self.block, self.block), self.block
                )
                out = self.outs[result]
                out = out.at[:, cols] if self.across[result] else out.at[cols, :]
                act(pltpu.make_async_copy(self.tile.at[m % 3], out, self.out_sem.at[m % 3]))

    def remote(self, src, dst, send, recv, to):
        return pltpu.make_async_remote_copy(
            src_ref=src, dst_ref=dst, send_sem=send, recv_sem=recv, device_id=to, device_id_type=MESH
        )

    def first_copy(self, m):
        return self.remote(
            self.s1.at[m % 3],
            self.r1.at[m % 4],
            self.s1_sem.at[m % 3],
            self.r1_sem.at[m % 4],
            self.to_core,
        )

    def second_copies(self, m):
        return (
            self.remote(
                self.s2x.at[m % 3],
                self.r2x.at[m % 6],
                self.s2x_sem.at[m % 3],
                self.r2x_sem.at[m % 6],
                self.to_x,
            ),
            self.remote(
                self.s2y.at[m % 3],
                self.r2y.at[m % 6],
                self.s2y_sem.at[m % 3],
                self.r2y_sem.at[m % 6],
                self.to_y,
            ),
        )

    def third_copies(self, m):
        return (
            self.remote(
                self.s3.at[m % 3, 0],
                self.r3.at[m % 6, 0],
                self.s3y_sem.at[m % 3],
                self.r3y_sem.at[m % 6],
                self.to_y,
            ),
            self.remote(
                self.s3.at[m % 3, 1],
                self.r3.at[m % 6, 1],
                self.s3x_sem.at[m % 3],
                self.r3x_sem.at[m % 6],
                self.to_x,
            ),
        )

    def step(self, t):
        @pl.when(t == self.start - 1)
        def _():
            self.left_copy(0).start()
            self.right_copy(0, lambda copy: copy.start())

        for stage, lag in ((self.fourth, 8), (self.third, 5), (self.second, 2), (self.multiply, 0)):
            m = t - self.start - lag

            @pl.when((m >= 0) & (m < self.chunks))
            def _():
                stage(m)

    def multiply(self, m):
        for left, start in self.phases.items():

            @pl.when(m == start)
            def _():
                if start > 0:
                    self.left_copy(left).start()
                self.left_copy(left).wait()

        @pl.when(m + 1 < self.chunks)
        def _():
            self.right_copy(m + 1, lambda copy: copy.start())

        self.right_copy(m, lambda copy: copy.wait())

        @pl.when(m >= 3)
        def _():
            self.first_copy(m - 3).wait_send()

        turned = self.y_buf[m % 2].T
        wide = 2 * self.block

        def product(x, core):
            cols = pl.ds(pl.multiple_of(x * 2 * wide + core * wide, wide), wide)
            return mm(turned, self.x_buf[:, cols])

        for x in range(2):
            self.s1[m % 3, x] = product(x, 1 - self.core).astype(jnp.bfloat16)
        self.first_copy(m).start()
        for x in range(2):
            self.own[m % 3, x] = product(x, self.core)

    def second(self, m):
        half = self.block // 2

        @pl.when(m >= 3)
        def _():
            for copy in self.second_copies(m - 3):
                copy.wait_send()

        self.first_copy(m).wait_recv()
        slot = m % 3
        here, there = self.x, 1 - self.x
        mine = pl.ds(pl.multiple_of(self.y * self.block, self.block), self.block)
        others = pl.ds(pl.multiple_of((1 - self.y) * self.block, self.block), self.block)
        added = lambda x, rows, cols: (
            self.own[slot, x, rows, cols] + self.r1[m % 4, x, rows, cols].astype(jnp.float32)
        )
        upper, lower, every = pl.ds(0, half), pl.ds(half, half), pl.ds(0, 2 * self.block)
        self.s2x[slot] = added(there, upper, every).astype(jnp.bfloat16)
        for x in range(2):
            self.s2y[slot, x] = added(x, lower, others).astype(jnp.bfloat16)
        for copy in self.second_copies(m):
            copy.start()
        self.top[slot] = added(here, upper, every)
        for x in range(2):
            self.low[slot, x] = added(x, lower, mine)

    def third(self, m):
        @pl.when(m >= 3)
        def _():
            for copy in self.third_copies(m - 3):
                copy.wait_send()

        for copy in self.second_copies(m):
            copy.wait_recv()
        slot, got = m % 3, m % 6
        mine = pl.ds(pl.multiple_of(self.y * self.block, self.block), self.block)
        others = pl.ds(pl.multiple_of((1 - self.y) * self.block, self.block), self.block)
        top = lambda cols: self.top[slot, :, cols] + self.r2x[got, :, cols].astype(jnp.float32)
        low = lambda x: self.low[slot, x] + self.r2y[got, x].astype(jnp.float32)
        self.s3[slot, 0] = top(others).astype(jnp.bfloat16)
        self.s3[slot, 1] = low(1 - self.x).astype(jnp.bfloat16)
        for copy in self.third_copies(m):
            copy.start()
        self.kept[slot, 0] = top(mine)
        self.kept[slot, 1] = low(self.x)

    def fourth(self, m):
        @pl.when(m >= 3)
        def _():
            self.out_copy(m - 3, lambda copy: copy.wait())

        for copy in self.third_copies(m):
            copy.wait_recv()
        slot, half = m % 3, self.block // 2
        total = self.kept[slot] + self.r3[m % 6].astype(jnp.float32)
        total = total.reshape(self.block, self.block)
        across = jnp.zeros((), jnp.bool_)
        for _, start, stop, result, _ in self.table:
            if self.across[result]:
                across = across | ((m >= start) & (m < stop))

        @pl.when(across)
        def _():
            self.tile[slot] = total.T

        @pl.when(jnp.logical_not(across))
        def _():
            self.tile[slot] = total

        self.out_copy(m, lambda copy: copy.start())

    def settle(self):
        for m in range(self.chunks - 3, self.chunks):
            self.first_copy(m).wait_send()
            for copy in self.second_copies(m) + self.third_copies(m):
                copy.wait_send()
            self.out_copy(jnp.int32(m), lambda copy: copy.wait())


class Gather:
    others = 3

    def __init__(self, shards, fulls, sems, ready):
        self.shards, self.fulls, self.ready = shards, fulls, ready
        self.sent, self.got, self.local = sems
        item, seq = lax.axis_index("item"), lax.axis_index("seq")
        self.core, self.x, self.y = item % 2, item // 2, seq
        self.to_core = {"item": item + 1 - 2 * self.core}
        self.to_x = {"item": item + 2 - 4 * self.x}
        self.to_y = {"seq": 1 - seq}

    @staticmethod
    def sems(count=2):
        dma = lambda *shape: pltpu.SemaphoreType.DMA(shape)
        return [dma(count, 9), dma(count, 9), dma(count)]

    def greet(self, barrier):
        for to in (self.to_core, self.to_x, self.to_y):
            pl.semaphore_signal(barrier, inc=1, device_id=to, device_id_type=MESH)

    def spot(self, w, x, core, y, part=None):
        size = self.shards[w].shape[w]
        at = pl.ds(pl.multiple_of(((2 * x + core) * 2 + y) * size, size), size)
        if w == 0:
            if part is not None:
                half = size // 2
                start = ((2 * x + core) * 2 + y) * size + part * half
                at = pl.ds(pl.multiple_of(start, half), half)
            return self.fulls[0].at[at, :]
        rows = self.fulls[1].shape[0]
        if part is not None:
            return self.fulls[1].at[pl.ds(part * (rows // 2), rows // 2), at]
        return self.fulls[1].at[:, at]

    def message(self, w, number, src, dst, to):
        return pltpu.make_async_remote_copy(
            src_ref=src,
            dst_ref=dst,
            send_sem=self.sent.at[w, number],
            recv_sem=self.got.at[w, number],
            device_id=to,
            device_id_type=MESH,
        )

    def plan(self, w):
        c, x, y = self.core, self.x, self.y
        own, spot = self.shards[w].at[...], functools.partial(self.spot, w)
        return (
            (own, spot(x, c, y), spot(x, 1 - c, y), self.to_core),
            (own, spot(x, c, y), spot(1 - x, c, y), self.to_x),
            (own, spot(x, c, y), spot(x, c, 1 - y), self.to_y),
            (None, spot(1 - x, c, y, 0), spot(1 - x, c, 1 - y, 0), self.to_y),
            (None, spot(x, c, 1 - y, 1), spot(1 - x, c, 1 - y, 1), self.to_x),
            (None, spot(1 - x, c, y), spot(1 - x, 1 - c, y), self.to_core),
            (None, spot(x, c, 1 - y), spot(x, 1 - c, 1 - y), self.to_core),
            (None, spot(1 - x, c, 1 - y, 0), spot(1 - x, 1 - c, 1 - y, 0), self.to_core),
            (None, spot(1 - x, c, 1 - y, 1), spot(1 - x, 1 - c, 1 - y, 1), self.to_core),
        )
    def send(self, w, numbers):
        plan = self.plan(w)
        for number in numbers:
            src, out, _, to = plan[number]
            self.message(w, number, out if src is None else src, out, to).start()

    def receive(self, w, numbers):
        plan = self.plan(w)
        for number in numbers:
            _, _, landing, to = plan[number]
            self.message(w, number, landing, landing, to).wait_recv()

    def mine(self, w):
        return pltpu.make_async_copy(
            self.shards[w], self.spot(w, self.x, self.core, self.y), self.local.at[w]
        )

    def first(self):
        for w in range(len(self.shards)):
            self.mine(w).start()

    def begin(self):
        for w in range(2):
            self.send(w, (1, 2, 0))

    def step(self, t):
        for w, at in ((0, GATHER_STEPS[0]), (1, GATHER_STEPS[1])):

            @pl.when(t == at)
            def _():
                self.receive(w, (1, 2))
                self.send(w, (3, 4, 5, 6))

        for w, at in ((0, GATHER_STEPS[2]), (1, GATHER_STEPS[3])):

            @pl.when(t == at)
            def _():
                self.receive(w, (3, 4))
                self.send(w, (7, 8))

        @pl.when(t == self.ready)
        def _():
            for w in range(2):
                self.receive(w, (0, 5, 6, 7, 8))
                self.mine(w).wait()

    def settle(self):
        for w in range(len(self.shards)):
            for number, (src, out, _, to) in enumerate(self.plan(w)):
                self.message(w, number, out if src is None else src, out, to).wait_send()


class Load:
    others = 0

    def __init__(self, shards, fulls, sems, ready):
        self.ready = ready
        self.copies = [
            pltpu.make_async_copy(shard, full, sems[2].at[w])
            for w, (shard, full) in enumerate(zip(shards, fulls))
        ]

    sems = Gather.sems

    def greet(self, barrier):
        pass

    def first(self):
        for copy in self.copies:
            copy.start()

    def begin(self):
        pass

    def step(self, t):
        @pl.when(t == self.ready)
        def _():
            for copy in self.copies:
                copy.wait()

    def settle(self):
        pass


class Attend:
    bq = 128

    def __init__(self, half, facts, q, k, v, earlier, attended, lse):
        self.half, self.facts, self.q, self.k, self.v = half, facts, q, k, v
        self.earlier, self.attended, self.lse = earlier, attended, lse
        self.pairs = q.shape[1] // PAIR
        self.blocks = half // self.bq

    def first(self):
        def one(pair, carry):
            for flow in range(2):
                self.unit(pair, flow * self.blocks)
            return carry

        lax.fori_loop(0, self.pairs, one, 0)

    def step(self, t):
        def both(pair, block):
            for flow in range(2):
                self.unit(pair, flow * self.blocks + block)

        @pl.when((t >= 0) & (t < 2))
        def _():
            each = self.pairs // 2

            def one(i, carry):
                both((t % 2) * each + i, 1)
                return carry

            lax.fori_loop(0, each, one, 0)

        for block in range(2, self.blocks):
            start = self.pairs * (block - 2) + 2

            @pl.when((t >= start) & (t < start + self.pairs))
            def _():
                both(t - start, block)

    def unit(self, pair, block):
        bq, nk = self.bq, (block + 1) * self.bq
        cols = pl.ds(pl.multiple_of(pair * PAIR, PAIR), PAIR)
        here = slice(block * bq, nk)
        query = block * bq + lax.broadcasted_iota(jnp.int32, (1, 2 * bq), 1) % bq
        limit = jnp.minimum(query + 1, self.facts[1])
        own = lax.broadcasted_iota(jnp.int32, (nk, 2 * bq), 0) < limit
        earlier = lax.broadcasted_iota(jnp.int32, (SUMM_ROWS, 2 * bq), 0) < self.facts[2]
        q = self.q[here, cols] * jnp.bfloat16(HDIM**-0.5)
        q = jnp.concatenate([jnp.where(head_lanes(h), q, jnp.zeros_like(q)) for h in range(2)])
        s = jnp.where(own, mm(self.k[:nk, cols], q, NT), MASKED)
        s2 = jnp.where(earlier, mm(self.earlier[0, :, cols], q, NT), MASKED)
        top = jnp.maximum(jnp.max(s, axis=0, keepdims=True), jnp.max(s2, axis=0, keepdims=True))
        p = jnp.exp(s - top)
        p2 = jnp.exp(s2 - top)
        total = jnp.sum(p, axis=0, keepdims=True) + jnp.sum(p2, axis=0, keepdims=True)
        out = mm(self.v[:nk, cols].T, p.astype(jnp.bfloat16))
        out = (out + mm(self.earlier[1, :, cols].T, p2.astype(jnp.bfloat16))) / total
        lse = top + jnp.log(total)
        for head in range(2):
            self.lse[pair, head : head + 1, here] = lse[:, head * bq : (head + 1) * bq]
        low_half = lax.broadcasted_iota(jnp.int32, (PAIR, 1), 0) < HDIM
        joined = jnp.where(low_half, out[:, :bq], out[:, bq:])
        self.attended[here, cols] = joined.T.astype(jnp.bfloat16)


def ffn_kernel(count, half, weights_job, n_attend, *refs):
    if n_attend == 1:
        ffn_body(count, half, weights_job, None, *refs)
    else:
        lengths, earlier, *rest = refs
        sources, rest = rest[:3], rest[3:]
        inputs, outputs, scratch = rest[:9], rest[9:22], rest[22:]
        *outputs, attended, lse = outputs
        *scratch, q, k, v, sems = scratch
        job = Attend(half, Facts(lengths), q, k, v, earlier, attended, lse)
        job.loads = [
            pltpu.make_async_copy(source, target, sems.at[number])
            for number, (source, target) in enumerate(zip(sources, (q, k, v)))
        ]
        for load in job.loads:
            load.start()
        ffn_body(count, half, weights_job, job, attended, *inputs, *outputs, *scratch)


def ffn_body(
    count,
    half,
    weights_job,
    attention,
    attended,
    out_w,
    out_bias,
    mid_gain,
    mid_shift,
    up_bias,
    hidden,
    cotangent,
    up_shard,
    down_shard,
    mid,
    act,
    grad_pre,
    residual_out,
    branch,
    grad_out,
    down_out,
    acc,
    acc_up,
    acc_down,
    grad_attended,
    part1,
    moving1,
    part2,
    moving2,
    rows_in,
    residual,
    up,
    down,
    cot_in,
    act_out,
    pre_out,
    attended_out,
    *sems,
):
    sems = list(sems)
    take = lambda n: [sems.pop(0) for _ in range(n)]
    sems1, sems2, weight_sems = take(5), take(5), take(3)
    in_sem, residual_sem, grad_sem, cot_sem, act_sem, pre_sem, down_sem = sems[:7]
    (attended_sem,) = sems[7:]
    me = lax.axis_index("mp")
    group = part2.shape[2]
    blocks = 4
    block = up.shape[1] // blocks
    per_group = group // PIECE
    pieces = half // PIECE
    last = count - 1
    second = per_group + blocks + 2 * SKEW * (count - 1)
    weights = weights_job((up_shard, down_shard), (up, down), weight_sems, second - blocks - 1)
    piece = lambda k: pl.ds(pl.multiple_of(k * PIECE, PIECE), PIECE)
    owner = (me == 0) | (me == last)
    my_flow = jnp.where(me == 0, 0, 1)

    def piece_in(source, k, flow):
        return pltpu.make_async_copy(
            source.at[pl.ds(flow * half + k * PIECE, PIECE)], rows_in.at[piece(k)], in_sem.at[k]
        )

    def residual_copy(k):
        return pltpu.make_async_copy(
            residual.at[piece(k)], residual_out.at[piece(k)], residual_sem.at[k]
        )

    def grad_copy(k):
        return pltpu.make_async_copy(residual.at[piece(k)], grad_out.at[piece(k)], grad_sem.at[k])

    def finish_first(flow, k, total):
        piece_in(hidden, k, flow).wait()
        value = rows_in[piece(k), :].astype(jnp.float32) + total + out_bias[...]
        residual[piece(k), :] = value
        residual_copy(k).start()
        piece_in(cotangent, k, flow).start()
        return norm_stats(value)[0] * mid_gain[...] + mid_shift[...]

    def finish_second(flow, k, total):
        piece_in(cotangent, k, flow).wait()
        residual_copy(k).wait()
        normed, inverse = norm_stats(residual[piece(k), :])
        grad = rows_in[piece(k), :].astype(jnp.float32)
        grad = grad + norm_back(total, normed, inverse, mid_gain[...])
        residual[piece(k), :] = grad
        grad_copy(k).start()
        acc[0] += fold(total * normed)
        acc[1] += fold(total)
        acc[2] += fold(grad)
        return grad

    multiply = group_product([attended], out_w, NN, half, part1.shape[2])
    line1 = Line(count, half, multiply, finish_first, mid, part1, moving1, sems1)
    line2 = Line(count, half, None, finish_second, branch, part2, moving2, sems2)

    def group_rows(flow, g):
        return pl.ds(pl.multiple_of(flow * half + g * group, 16), group)

    def cot_fetch(flow, g):
        return pltpu.make_async_copy(
            cotangent.at[group_rows(flow, g)], cot_in.at[flow], cot_sem.at[flow]
        )

    def act_copy(flow, g):
        return pltpu.make_async_copy(
            act_out.at[flow], act.at[group_rows(flow, g)], act_sem.at[flow]
        )

    def pre_copy(flow, g):
        return pltpu.make_async_copy(
            pre_out.at[flow], grad_pre.at[group_rows(flow, g)], pre_sem.at[flow]
        )

    def products(flow, g, number):
        @pl.when(number == 0)
        def _():
            cot_fetch(flow, g).wait()
            acc_down[...] += fold(cot_in[flow].astype(jnp.float32))

            @pl.when(g > 0)
            def _():
                act_copy(flow, g - 1).wait()
                pre_copy(flow, g - 1).wait()

        cols = pl.ds(pl.multiple_of(number * block, block), block)
        value, slope = gelu_parts(mm(moving1[line1.finished(flow, g * per_group, group), :], up[:, cols]) + up_bias[:, cols])
        act_out[flow, :, cols] = value.astype(jnp.bfloat16)
        pre = (slope * mm(cot_in[flow], down[cols, :], NT)).astype(jnp.bfloat16)
        pre_out[flow, :, cols] = pre
        acc_up[:, cols] += fold(pre.astype(jnp.float32))
        product = mm(pre, up[:, cols], NT)

        @pl.when(number == 0)
        def _():
            part2[flow, g % 2] = product

        @pl.when(number > 0)
        def _():
            part2[flow, g % 2] += product

        @pl.when(number == blocks - 1)
        def _():
            act_copy(flow, g).start()
            pre_copy(flow, g).start()

    def attended_copy(flow, g):
        return pltpu.make_async_copy(
            attended_out.at[flow], grad_attended.at[group_rows(flow, g)], attended_sem.at[flow]
        )

    def through_out(flow, g):
        @pl.when(g > 0)
        def _():
            attended_copy(flow, g - 1).wait()

        attended_out[flow] = mm(moving2[line2.finished(flow, g * per_group, group), :], out_w[...], NT).astype(jnp.bfloat16)
        attended_copy(flow, g).start()

    barrier = pltpu.get_barrier_semaphore()
    line1.greet(barrier)
    weights.greet(barrier)
    acc[...] = jnp.zeros_like(acc)
    acc_up[...] = jnp.zeros_like(acc_up)
    acc_down[...] = jnp.zeros_like(acc_down)
    weights.first()

    @pl.when(owner)
    def _():
        def one(k, carry):
            piece_in(hidden, k, my_flow).start()
            return carry

        lax.fori_loop(0, pieces, one, 0)

    if attention is None:
        line1.first()
        line1.meet(barrier, weights.others)
        weights.begin()
    else:
        line1.meet(barrier, weights.others)
        weights.begin()
        for load in attention.loads:
            load.wait()
        attention.first()
        line1.first()

    def step(t, carry):
        if attention is not None:
            attention.step(t)
        line1.step(t)
        line2.step(t - second)
        weights.step(t)

        @pl.when(t == weights.ready + 1)
        def _():
            pltpu.make_async_copy(down, down_out, down_sem.at[0]).start()

        for flow in range(2):
            place = line1.place(flow)
            u = t - second - SKEW * place
            fetch = u + blocks + 1
            compute = u + blocks

            @pl.when((fetch >= 0) & (fetch % per_group == 0) & (fetch < pieces))
            def _():
                cot_fetch(flow, fetch // per_group).start()

            @pl.when((compute >= 0) & (compute < pieces) & (compute % per_group < blocks))
            def _():
                products(flow, compute // per_group, compute % per_group)

            here = t - second - SKEW * (2 * last - place)

            @pl.when((here >= 0) & (here < pieces) & (here % per_group == per_group - 1))
            def _():
                through_out(flow, here // per_group)

        return carry

    lax.fori_loop(0, second + line2.steps, step, 0)
    line1.settle()
    line2.settle()
    weights.settle()
    pltpu.make_async_copy(down, down_out, down_sem.at[0]).wait()
    for flow in range(2):
        act_copy(flow, pieces // per_group - 1).wait()
        pre_copy(flow, pieces // per_group - 1).wait()
        attended_copy(flow, pieces // per_group - 1).wait()

    @pl.when(owner)
    def _():
        def one(k, carry):
            grad_copy(k).wait()
            return carry

        lax.fori_loop(0, pieces, one, 0)


def ffn_sums(number, count, weights_job, attend_in, out_w, vectors, hidden, cotangent, up_w, down_w):
    rows, features = hidden.shape
    ff = up_w.shape[1]
    half = rows // 2
    pieces = half // PIECE
    low = lambda *shape: jax.ShapeDtypeStruct(shape, jnp.bfloat16)
    wide = lambda *shape: jax.ShapeDtypeStruct(shape, jnp.float32)
    attend_out, attend_scratch = [], []
    if len(attend_in) > 1:
        width = attend_in[2].shape[1]
        attend_scratch = [pltpu.VMEM((rows, width), jnp.bfloat16)] * 3
        attend_scratch += [pltpu.SemaphoreType.DMA((3,))]
        attend_out = [low(rows, width), wide(width // PAIR, 2, rows)]
    first = Line.scratch(half, features)
    small = 64 if half % 64 == 0 else PIECE
    first[0] = pltpu.VMEM((2, 2, small, features), jnp.float32)
    second = Line.scratch(half, features)
    group = second[0].shape[2]
    dma = lambda n: pltpu.SemaphoreType.DMA((n,))
    return pl.pallas_call(
        functools.partial(ffn_kernel, count, half, weights_job, len(attend_in)),
        in_specs=([SMEM, VMEM] + [ANY] * 3 if len(attend_in) > 1 else [VMEM]) + [VMEM] * 5 + [ANY] * 4,
        out_specs=[ANY] * 7 + [VMEM] * 3 + [ANY] + [VMEM] * len(attend_out),
        out_shape=[
            low(rows, features),
            low(rows, ff),
            low(rows, ff),
            wide(half, features),
            low(rows, features),
            wide(half, features),
            low(ff, features),
            wide(3, 8, features),
            wide(8, ff),
            wide(8, features),
            low(rows, out_w.shape[0]),
        ]
        + attend_out,
        scratch_shapes=first[:2]
        + second[:2]
        + [
            pltpu.VMEM((half, features), jnp.bfloat16),
            pltpu.VMEM((half, features), jnp.float32),
            pltpu.VMEM((features, ff), jnp.bfloat16),
            pltpu.VMEM((ff, features), jnp.bfloat16),
            pltpu.VMEM((2, group, features), jnp.bfloat16),
            pltpu.VMEM((2, group, ff), jnp.bfloat16),
            pltpu.VMEM((2, group, ff), jnp.bfloat16),
            pltpu.VMEM((2, group, out_w.shape[0]), jnp.bfloat16),
        ]
        + first[2:]
        + second[2:]
        + Gather.sems()
        + [dma(pieces), dma(pieces), dma(pieces), dma(2), dma(2), dma(2), dma(1)]
        + [dma(2)]
        + attend_scratch,
        compiler_params=pltpu.CompilerParams(
            collective_id=number, has_side_effects=True, vmem_limit_bytes=62 * MIB
        ),
        cost_estimate=pl.CostEstimate(
            flops=6 * rows * features * ff, bytes_accessed=30 * rows * features, transcendentals=0
        ),
        name="ffn_sums",
    )(*attend_in, out_w, *vectors, hidden, cotangent, up_w, down_w)


def start_kernel(
    lengths,
    gain,
    shift,
    bias,
    hidden_in,
    shard,
    out_shard,
    q_ref,
    k_ref,
    v_ref,
    earlier,
    normed_out,
    weight_out,
    out_whole,
    normed,
    weight,
    out_weight,
    total,
    summary,
    hidden,
    *sems,
):
    facts = Facts(lengths)
    gather = Gather((shard, out_shard), (weight, out_weight), sems[:3], 0)
    summary_sent, summary_got, out_sems = sems[3:]
    rows = hidden.shape[0]
    width = q_ref.shape[1]
    size = shard.shape[0]
    chunk = 128
    barrier = pltpu.get_barrier_semaphore()
    gather.greet(barrier)
    load = pltpu.make_async_copy(hidden_in, hidden, out_sems.at[3])
    load.start()
    gather.first()
    pl.semaphore_wait(barrier, gather.others)
    gather.send(0, (1, 2, 0))

    def norm(i, carry):
        here = pl.ds(pl.multiple_of(i * chunk, chunk), chunk)
        value = norm_stats(hidden[here, :].astype(jnp.float32))[0]
        normed[here, :] = (value * gain[...] + shift[...]).astype(jnp.bfloat16)
        return carry

    load.wait()
    lax.fori_loop(0, rows // chunk, norm, 0)
    keep = pltpu.make_async_copy(normed, normed_out, out_sems.at[0])
    keep.start()
    c, x, y = gather.core, gather.x, gather.y

    def add(places, first=False, last=False):
        starts = [
            pl.multiple_of(((2 * px + pc) * 2 + py) * size, size) for px, pc, py in places
        ]

        def rows_of(i, carry):
            here = pl.ds(pl.multiple_of(i * chunk, chunk), chunk)
            for j, out in enumerate((q_ref, k_ref, v_ref)):
                cols = slice(j * width, (j + 1) * width)
                value = None if first else total[here, cols]
                for start in starts:
                    at = pl.ds(start, size)
                    product = mm(normed[here, at], weight[at, cols])
                    value = product if value is None else value + product
                if not last:
                    total[here, cols] = value
                elif j == 1:
                    out[here, :] = value.astype(jnp.bfloat16)
                else:
                    out[here, :] = (value + bias[j // 2 : j // 2 + 1, :]).astype(jnp.bfloat16)
            return carry

        lax.fori_loop(0, rows // chunk, rows_of, 0)

    gather.mine(0).wait()
    gather.receive(0, (0,))
    add(((x, c, y), (x, 1 - c, y)), first=True)
    gather.receive(0, (1, 2))
    gather.send(0, (3, 4, 5, 6))
    gather.send(1, (1, 2, 0))
    add(((1 - x, c, y), (x, c, 1 - y)))
    gather.receive(0, (5, 6))
    add(((1 - x, 1 - c, y), (x, 1 - c, 1 - y)))
    gather.receive(0, (3, 4))
    gather.send(0, (7, 8))
    add(((1 - x, c, 1 - y),))
    gather.receive(1, (1, 2))
    gather.send(1, (3, 4, 5, 6))
    gather.receive(0, (7, 8))
    store = pltpu.make_async_copy(weight, weight_out, out_sems.at[1])
    store.start()
    add(((1 - x, 1 - c, 1 - y),), last=True)

    shape = (SUMM_ROWS, rows)
    chosen = lax.broadcasted_iota(jnp.int32, shape, 1) == (
        facts[1] - SUMM + lax.broadcasted_iota(jnp.int32, shape, 0)
    )
    chosen = jnp.where(chosen, 1.0, 0.0).astype(jnp.bfloat16)
    summary[0] = mm(chosen, k_ref[...]).astype(jnp.bfloat16)
    summary[1] = mm(chosen, v_ref[...]).astype(jnp.bfloat16)
    swap = pltpu.make_async_remote_copy(
        src_ref=summary,
        dst_ref=earlier,
        send_sem=summary_sent.at[0],
        recv_sem=summary_got.at[0],
        device_id=gather.to_y,
        device_id_type=MESH,
    )
    swap.start()
    gather.receive(1, (3, 4))
    gather.send(1, (7, 8))
    gather.receive(1, (0, 5, 6, 7, 8))
    gather.mine(1).wait()
    store_out = pltpu.make_async_copy(out_weight, out_whole, out_sems.at[2])
    store_out.start()
    gather.settle()
    keep.wait()
    store.wait()
    swap.wait()
    store_out.wait()


def start(number, lengths, hidden, gain, shift, bias, shard, out_shard):
    rows, features = hidden.shape
    width = bias.shape[1]
    low = lambda *shape: jax.ShapeDtypeStruct(shape, jnp.bfloat16)
    dma = lambda n: pltpu.SemaphoreType.DMA((n,))
    return pl.pallas_call(
        start_kernel,
        in_specs=[SMEM] + [VMEM] * 3 + [ANY] * 3,
        out_specs=[VMEM] * 3 + [ANY] * 4,
        out_shape=[low(rows, width)] * 3
        + [low(2, SUMM_ROWS, width), low(rows, features), low(features, 3 * width)]
        + [low(width, features)],
        scratch_shapes=[
            pltpu.VMEM((rows, features), jnp.bfloat16),
            pltpu.VMEM((features, 3 * width), jnp.bfloat16),
            pltpu.VMEM((width, features), jnp.bfloat16),
            pltpu.VMEM((rows, 3 * width), jnp.float32),
            pltpu.VMEM((2, SUMM_ROWS, width), jnp.bfloat16),
            pltpu.VMEM((rows, features), jnp.bfloat16),
        ]
        + Gather.sems()
        + [dma(1), dma(1), dma(4)],
        compiler_params=pltpu.CompilerParams(
            collective_id=number, has_side_effects=True, vmem_limit_bytes=60 * MIB
        ),
        cost_estimate=pl.CostEstimate(
            flops=6 * rows * features * width, bytes_accessed=16 * rows * features, transcendentals=0
        ),
        name="start",
    )(lengths, gain, shift, bias, hidden, shard, out_shard)


class SmallSums(Nothing):
    n_in = n_out = 1

    def __init__(self, sizes, shared, start, values):
        self.stages = tuple(
            (axis, 1 << bit) for axis, size in sizes for bit in range(size.bit_length() - 1)
        )
        self.shared, self.start = shared, start
        self.others = len(self.stages)
        self.steps = start + self.others + 1
        self.operands = (values,)
        self.in_specs = self.out_specs = (VMEM,)
        self.out_shape = (jax.ShapeDtypeStruct(values.shape, jnp.float32),)
        buffers = pltpu.VMEM((self.others, *values.shape), jnp.float32)
        sems = pltpu.SemaphoreType.DMA((self.others,))
        self.scratch_shapes = (buffers, buffers, sems, sems)

    def __call__(self, ins, outs, scratch, accs):
        (self.own,), (self.out,), (self.acc,) = ins, outs, accs
        self.sent, self.got, self.send_sem, self.recv_sem = scratch
        return self

    def partner(self, axis, bit):
        index = lax.axis_index(axis)
        return {axis: index + bit - 2 * bit * ((index // bit) % 2)}

    def extra(self, row, start, grad):
        cols = slice(start, start + grad.shape[1])
        self.sent[0, row : row + 1, cols] = jnp.sum(
            grad[...].astype(jnp.float32), axis=0, keepdims=True
        )

    def greet(self, barrier):
        for axis, bit in self.stages:
            pl.semaphore_signal(
                barrier, inc=1, device_id=self.partner(axis, bit), device_id_type=MESH
            )

    def copy(self, number):
        return pltpu.make_async_remote_copy(
            src_ref=self.sent.at[number],
            dst_ref=self.got.at[number],
            send_sem=self.send_sem.at[number],
            recv_sem=self.recv_sem.at[number],
            device_id=self.partner(*self.stages[number]),
            device_id_type=MESH,
        )

    def first(self):
        self.sent[0] = self.own[...]

    def step(self, t):
        @pl.when(t == self.start)
        def _():
            for number in range(self.acc.shape[0]):
                self.sent[0, 3 + number : 4 + number, :] = jnp.sum(
                    self.acc[number], axis=0, keepdims=True
                )
            self.copy(0).start()

        row = lax.broadcasted_iota(jnp.int32, self.out.shape, 0)
        for number, (axis, _) in enumerate(self.stages):

            @pl.when(t == self.start + 1 + number)
            def _():
                self.copy(number).wait()
                total = self.sent[number] + self.got[number]
                if axis == "mp":
                    total = jnp.where(row < self.shared, total, self.sent[number])
                if number + 1 < len(self.stages):
                    self.sent[number + 1] = total
                    self.copy(number + 1).start()
                else:
                    self.out[...] = total


class Columns:
    def __init__(self, ref, start, width):
        self.ref, self.start, self.shape = ref, start, (ref.shape[0], width)

    def __getitem__(self, index):
        rows, cols = index
        start = pl.multiple_of(self.start + cols.start, PAIR)
        return self.ref[rows, pl.ds(start, cols.size)]


class Ring:
    depth = 2

    def __init__(self, source, buffer, sems, pieces, offset):
        self.source, self.buffer, self.sems = source, buffer, sems
        self.pieces, self.offset = pieces, offset

    @classmethod
    def scratch(cls, features, dtype):
        return [
            pltpu.VMEM((cls.depth, PIECE, features), dtype),
            pltpu.SemaphoreType.DMA((cls.depth,)),
        ]

    def copy(self, k):
        rows = pl.ds(self.offset + k * PIECE, PIECE)
        slot = k % self.depth
        return pltpu.make_async_copy(
            self.source.at[rows], self.buffer.at[slot], self.sems.at[slot]
        )

    def fill(self):
        for k in range(min(self.depth, self.pieces)):
            self.copy(k).start()

    def take(self, k):
        self.copy(k).wait()
        value = self.buffer[k % self.depth].astype(jnp.float32)

        @pl.when(k + self.depth < self.pieces)
        def _():
            self.copy(k + self.depth).start()

        return value


def back_kernel(
    count,
    half,
    sizes,
    lengths,
    lse,
    earlier,
    down_bias,
    pre_gain,
    mid_sums,
    up_sums,
    down_sums,
    q_in,
    k_in,
    v_in,
    do_in,
    act,
    down_in,
    residual,
    hidden,
    grad_in,
    qkv_in,
    mid,
    cotangent,
    branch,
    normed,
    grad_pre,
    attended,
    hidden_out,
    input_grad,
    up_grad,
    down_grad,
    out_grad,
    qkv_grad,
    sums_out,
    part,
    moving1,
    moving2,
    down,
    qkv_w,
    dq,
    dk,
    dv,
    dk_acc,
    dv_acc,
    k_t,
    dks,
    dvs,
    swap_out,
    swap_in,
    act_in,
    acc,
    small_sent,
    small_got,
    *rest,
):
    rest = list(rest)
    facts = Facts(lengths)
    take = lambda n: [rest.pop(0) for _ in range(n)]
    rings = take(6)
    sems1, sems2 = take(5), take(5)
    small_sems = take(2)
    load_sem, act_sem, swap_sent, swap_got = take(4)
    rows, width = 2 * half, dq.shape[1]
    pieces = half // PIECE
    me = lax.axis_index("mp")
    owner = (me == 0) | (me == count - 1)
    offset = jnp.where(me == 0, 0, half)
    residual_ring = Ring(residual, *rings[0:2], pieces, 0)
    grad_ring = Ring(grad_in, *rings[2:4], pieces, 0)
    hidden_ring = Ring(hidden, *rings[4:6], pieces, offset)
    group = part.shape[2]

    def act_copy(flow, g):
        return pltpu.make_async_copy(
            act.at[pl.ds(pl.multiple_of(flow * half + g * group, 16), group)],
            act_in.at[flow],
            act_sem.at[flow],
        )

    def multiply_down(flow, g):
        act_copy(flow, g).wait()
        product = mm(act_in[flow], down[...])

        @pl.when(g + 1 < half // group)
        def _():
            act_copy(flow, g + 1).start()

        return product

    def finish_first(flow, k, total):
        return residual_ring.take(k) + total + down_bias[...]

    def finish_second(flow, k, total):
        values, inverse = norm_stats(hidden_ring.take(k))
        acc[0] += fold(total * values)
        acc[1] += fold(total)
        return grad_ring.take(k) + norm_back(total, values, inverse, pre_gain[...])

    line1 = Line(count, half, multiply_down, finish_first, hidden_out, part, moving1, sems1)
    multiply_back = group_product([dq, dk, dv], qkv_w, NT, half, group)
    line2 = Line(
        count, half, multiply_back, finish_second, input_grad, part, moving2, sems2, late=True
    )
    heads = AttendBack.__new__(AttendBack)
    heads.bq = query_block(rows)
    heads.blocks = rows // heads.bq
    heads.pairs = width // PAIR
    heads.steps = heads.pairs * heads.blocks
    heads.causal = True
    first = moving2.at[pl.ds(0, rows)]
    views = [Columns(first, j * width, width) for j in range(4)]
    tables = [earlier.at[0], earlier.at[1]]
    heads.ins = (facts, *views[:3], *tables, views[3], lse)
    heads.outs = (dq, dk, dv, dks, dvs)
    heads.scratch = (dk_acc, dv_acc, k_t)
    second = heads.steps + 2
    columns = (
        (0, grad_pre, 0, 0),
        (1, act, 1, 0),
        (2, attended, 2, 0),
        (3, dq, 3, 0),
        (3, dk, 3, width),
        (3, dv, 3, 2 * width),
    )
    spread = Spread(
        (mid, cotangent, branch, normed),
        columns,
        (up_grad, down_grad, out_grad, qkv_grad),
        down.at[pl.ds(0, rows)],
        rest,
        heads.steps - 2,
    )
    small = SmallSums(sizes, 6, second + pieces + SKEW * (count - 1), sums_out)
    small((None,), (sums_out,), (small_sent, small_got, *small_sems), (acc,))
    column_sums = lambda values: jnp.sum(values, axis=0, keepdims=True)
    features = down_in.shape[1]
    ff_rows = down_in.shape[0] // features
    loads = [
        pltpu.make_async_copy(source, target, load_sem.at[number])
        for number, (source, target) in enumerate(
            [(down_in, down), (qkv_in, qkv_w)]
            + [
                (source, first.at[:, pl.ds(j * width, width)])
                for j, source in enumerate((q_in, k_in, v_in, do_in))
            ]
        )
    ]
    swap = pltpu.make_async_remote_copy(
        src_ref=swap_out,
        dst_ref=swap_in,
        send_sem=swap_sent.at[0],
        recv_sem=swap_got.at[0],
        device_id=spread.to_y,
        device_id_type=MESH,
    )

    barrier = pltpu.get_barrier_semaphore()
    line1.greet(barrier)
    spread.greet(barrier)
    small.greet(barrier)
    for flow in range(2):
        act_copy(flow, 0).start()
    for load in loads:
        load.start()

    @pl.when(owner)
    def _():
        for ring in (residual_ring, grad_ring, hidden_ring):
            ring.fill()

    acc[...] = jnp.zeros_like(acc)
    small_sent[0] = jnp.zeros_like(small_sent[0])
    for number in range(3):
        small_sent[0, number : number + 1, :] = mid_sums[number : number + 1, :]
    small_sent[0, 5:6, :] = jnp.where(me == 0, column_sums(down_sums[...]), 0.0)
    for number in range(ff_rows):
        cols = slice(number * features, (number + 1) * features)
        small_sent[0, 6 + number : 7 + number, :] = column_sums(up_sums[:, cols])
    loads[0].wait()
    line1.first()
    line1.meet(barrier, spread.others + small.others)
    for load in loads[2:]:
        load.wait()

    def step(t, carry):
        line1.step(t)
        heads.step(t)

        @pl.when(t == heads.steps)
        def _():
            swap_out[0] = dks[...].astype(jnp.bfloat16)
            swap_out[1] = dvs[...].astype(jnp.bfloat16)
            swap.start()

        @pl.when(t == heads.steps + 1)
        def _():
            swap.wait()
            loads[1].wait()
            shape = (rows, SUMM_ROWS)
            chosen = lax.broadcasted_iota(jnp.int32, shape, 0) == (
                facts[1] - SUMM + lax.broadcasted_iota(jnp.int32, shape, 1)
            )
            chosen = jnp.where(chosen, 1.0, 0.0).astype(jnp.bfloat16)
            for number, grad in enumerate((dk, dv)):
                added = grad[...].astype(jnp.float32) + mm(chosen, swap_in[number])
                grad[...] = added.astype(jnp.bfloat16)
            for number, grad in enumerate((dq, dv)):
                small.extra(6 + ff_rows, number * width, grad)

        line2.step(t - second)
        spread.step(t)
        small.step(t)
        return carry

    lax.fori_loop(0, max(second + line2.steps, spread.steps, small.steps), step, 0)
    line1.settle()
    line2.settle()
    spread.settle()


def back_sums(number, count, sizes, whole_in, vmem_in):
    rows, width = whole_in[0].shape
    features = whole_in[5].shape[1]
    ff = whole_in[5].shape[0]
    half = rows // 2
    low = lambda *shape: pltpu.VMEM(shape, jnp.bfloat16)
    wide = lambda *shape: pltpu.VMEM(shape, jnp.float32)
    dma = lambda *shape: pltpu.SemaphoreType.DMA(shape)
    lines = Line.scratch(half, features)
    group = lines[0].shape[2]
    stages = sum(size.bit_length() - 1 for _, size in sizes)
    block = Spread.block
    sums_shape = (6 + ff // features + -(-2 * width // features), features)
    return pl.pallas_call(
        functools.partial(back_kernel, count, half, sizes),
        in_specs=[SMEM] + [VMEM] * 7 + [ANY] * len(whole_in),
        out_specs=[ANY] * 6 + [VMEM],
        out_shape=[
            jax.ShapeDtypeStruct((rows, features), jnp.bfloat16),
            jax.ShapeDtypeStruct((rows, features), jnp.bfloat16),
            jax.ShapeDtypeStruct((block, ff), jnp.float32),
            jax.ShapeDtypeStruct((ff, block), jnp.float32),
            jax.ShapeDtypeStruct((width, block), jnp.float32),
            jax.ShapeDtypeStruct((block, 3 * width), jnp.float32),
            jax.ShapeDtypeStruct(sums_shape, jnp.float32),
        ],
        scratch_shapes=[
            lines[0],
            lines[1],
            lines[1],
            low(ff, features),
            low(features, 3 * width),
            low(rows, width),
            low(rows, width),
            low(rows, width),
            wide(rows, PAIR),
            wide(rows, PAIR),
            low(PAIR, rows),
            wide(SUMM_ROWS, width),
            wide(SUMM_ROWS, width),
            low(2, SUMM_ROWS, width),
            low(2, SUMM_ROWS, width),
            low(2, group, ff),
            wide(2, 8, features),
            wide(stages, *sums_shape),
            wide(stages, *sums_shape),
        ]
        + Ring.scratch(features, jnp.float32)
        + Ring.scratch(features, jnp.float32)
        + Ring.scratch(features, jnp.bfloat16)
        + lines[2:]
        + lines[2:]
        + [dma(stages), dma(stages), dma(6), dma(2), dma(1), dma(1)]
        + Spread.scratch(rows),
        compiler_params=pltpu.CompilerParams(
            collective_id=number, has_side_effects=True, vmem_limit_bytes=63 * MIB
        ),
        cost_estimate=pl.CostEstimate(
            flops=12 * rows * features * ff, bytes_accessed=60 * rows * features, transcendentals=0
        ),
        name="back_sums",
    )(*vmem_in, *whole_in)


def gradients_over(group, lefts, columns):
    over_rows = lambda left, right: mm(left, right, (((0,), (0,)), ((), ()))).astype(jnp.bfloat16)
    parts = [[] for _ in range(4)]
    for left, right, result, _ in columns:
        across = result in (0, 3)
        product = over_rows(lefts[left], right) if across else over_rows(right, lefts[left])
        parts[result].append(product)
    return [
        lax.psum_scatter(
            jnp.concatenate(part, axis=1),
            group,
            scatter_dimension=0 if result in (0, 3) else 1,
            tiled=True,
        ).astype(jnp.float32)
        for result, part in enumerate(parts)
    ]


def body(
    item_count,
    seq_count,
    mp_count,
    hidden_in,
    cotangent,
    seg_lengths,
    pre_gain,
    pre_shift,
    qkv_weight,
    qv_bias,
    out_weight,
    out_bias,
    mid_gain,
    mid_shift,
    up_weight,
    up_bias,
    down_weight,
    down_bias,
):
    group = ("item", "seq")
    width = qkv_weight.shape[2]
    gathered = lambda weight, axis: lax.all_gather(weight, group, axis=axis, tiled=True)
    hidden = hidden_in[0].astype(jnp.float32)
    lengths = seg_lengths[0]
    rows = hidden.shape[0]
    first_row = lax.axis_index("seq") * rows
    segment = first_row // SLOT
    facts = jnp.stack(
        [
            first_row % SLOT,
            lengths[segment] + SUMM,
            jnp.where(segment > 0, SUMM, 0),
        ]
    ).astype(jnp.int32)

    ours = (item_count, seq_count) == (4, 2) and rows == SLOT
    row = lambda vector: vector[None, :]
    shard = qkv_weight.reshape(-1, 3 * width)
    if ours:
        q, k, v, summary, normed, qkv_full, out_full = start(
            5, seg_lengths, hidden_in[0], row(pre_gain), row(pre_shift), qv_bias, shard, out_weight
        )
        attend_in = (seg_lengths, summary, q, k, v)
        tables = (k, v, summary[0], summary[1])
    else:
        qkv_full = gathered(shard, 0)
        out_full = gathered(out_weight, 1)
        normed = (norm_stats(hidden)[0] * pre_gain + pre_shift).astype(jnp.bfloat16)
        q = (mm(normed, qkv_full[:, :width]) + qv_bias[0]).astype(jnp.bfloat16)
        k = mm(normed, qkv_full[:, width : 2 * width]).astype(jnp.bfloat16)
        v = (mm(normed, qkv_full[:, 2 * width :]) + qv_bias[1]).astype(jnp.bfloat16)
        own, summary = keys_for(jnp.stack([k, v]), lengths, seq_count)
        tables = (own[0], own[1], summary[0], summary[1])
        attended, log_total = attend(facts, q, *tables)
        attend_in = (attended,)

    grad_down = cotangent[0]
    (
        mid_low,
        act_low,
        grad_pre,
        residual,
        grad_branch,
        grad_residual,
        down_full,
        mid_sums,
        up_sums,
        down_sums,
        grad_attended,
        *attend_out,
    ) = ffn_sums(
        1,
        mp_count,
        Gather if ours else Load,
        attend_in,
        out_full,
        (row(out_bias), row(mid_gain), row(mid_shift), row(up_bias)),
        hidden_in[0],
        grad_down,
        up_weight if ours else gathered(up_weight, 0),
        down_weight if ours else gathered(down_weight, 1),
    )
    if ours:
        attended, log_total = attend_out
    total = lambda value: jnp.sum(value.astype(jnp.float32), axis=0)
    features = hidden.shape[1]
    sizes = [("item", item_count), ("seq", seq_count), ("mp", mp_count)]
    once = lambda value: jnp.where(lax.axis_index("mp") == 0, value, 0.0)
    small_in = lambda qv_sums: jnp.concatenate(
        [
            jnp.sum(mid_sums, axis=1),
            jnp.zeros((2, features), jnp.float32),
            row(once(total(down_sums))),
            total(up_sums).reshape(-1, features),
            jnp.pad(qv_sums, (0, -qv_sums.shape[0] % features)).reshape(-1, features),
        ]
    )
    if ours:
        hidden_out, grad_input, up_grad, down_grad, out_grad, qkv_grad, sums = back_sums(
            2,
            mp_count,
            sizes,
            (q, k, v, grad_attended, act_low, down_full, residual, hidden_in[0], grad_residual)
            + (qkv_full, mid_low, grad_down, grad_branch, normed, grad_pre, attended),
            (seg_lengths, log_total, summary, row(down_bias), row(pre_gain))
            + (jnp.sum(mid_sums, axis=1), up_sums, down_sums),
        )
    else:
        hidden_out, dq, dk, dv, dks, dvs = line_sum(
            3,
            mp_count,
            [act_low],
            down_full,
            NN,
            [residual, row(down_bias)],
            0,
            0,
            finish_out,
            "down_sum",
            (AttendBack(facts, q, *tables, grad_attended, log_total),),
        )
        dk, dv = keys_back(jnp.stack([dk, dv]), jnp.stack([dks, dvs]), rows, lengths, seq_count)
        small = SmallSums(
            sizes,
            6,
            rows // 2 // PIECE + SKEW * (mp_count - 1),
            small_in(jnp.concatenate([total(dq), total(dv)])),
        )
        grad_input, _, sums = line_sum(
            4,
            mp_count,
            [dq, dk, dv],
            qkv_full,
            NT,
            [hidden_in[0], grad_residual, row(pre_gain)],
            0,
            2,
            finish_input,
            "input_sum",
            (small,),
        )
        lefts = (mid_low, grad_down, grad_branch, normed)
        columns = (
            (0, grad_pre, 0, 0),
            (1, act_low, 1, 0),
            (2, attended, 2, 0),
            (3, dq, 3, 0),
            (3, dk, 3, width),
            (3, dv, 3, 2 * width),
        )
        up_grad, down_grad, out_grad, qkv_grad = gradients_over(group, lefts, columns)
    ff_rows = up_weight.shape[1] // features
    up_bias_grad = sums[6 : 6 + ff_rows].reshape(-1)
    qv_bias_grad = sums[6 + ff_rows :].reshape(-1)[: 2 * width].reshape(2, width)
    return (
        hidden_out[None],
        grad_input.astype(jnp.float32)[None],
        sums[3],
        sums[4],
        qkv_grad.reshape(-1, 3, width),
        qv_bias_grad,
        out_grad,
        sums[2],
        sums[0],
        sums[1],
        up_grad,
        up_bias_grad,
        down_grad,
        sums[5],
    )


def solution(mesh):
    rows = P("item", "seq", None)
    qkv = P(("item", "seq"), None, "mp")
    first = P(("item", "seq"), "mp")
    second = P("mp", ("item", "seq"))
    bias = P(None, "mp")
    return jax.shard_map(
        functools.partial(body, mesh.shape["item"], mesh.shape["seq"], mesh.shape["mp"]),
        mesh=mesh,
        in_specs=(
            rows,
            rows,
            P("item", None),
            P(),
            P(),
            qkv,
            bias,
            second,
            P(),
            P(),
            P(),
            first,
            P("mp"),
            second,
            P(),
        ),
        out_specs=(
            rows,
            rows,
            P(),
            P(),
            qkv,
            bias,
            second,
            P(),
            P(),
            P(),
            first,
            P("mp"),
            second,
            P(),
        ),
        check_vma=False,
    )
```

```python
import functools
import math

import jax
import jax.numpy as jnp
from jax import lax
from jax.experimental import pallas as pl
from jax.experimental.pallas import tpu as pltpu
from jax.sharding import PartitionSpec as P

HDIM = 64
SLOT = 1280
SEGS = 2
SUMM = 50
SUMM_ROWS = 64
TOKENS = 2560
PAIR = 2 * HDIM
PIECE = 32
SKEW = 2
LEAD = 2
GATHER_STEPS = (10, 11, 14, 15)
MIB = 1 << 20
MESH = pl.DeviceIdType.MESH
MASKED = -1e30


eps = 1e-05

NN = (((1,), (0,)), ((), ()))
NT = (((1,), (1,)), ((), ()))


def mm(left, right, dims=NN):
    return lax.dot_general(left, right, dims, preferred_element_type=jnp.float32)


def norm_stats(values):
    center = jnp.mean(values, axis=-1, keepdims=True)
    centered = values - center
    inverse = lax.rsqrt(jnp.mean(centered * centered, axis=-1, keepdims=True) + eps)
    return centered * inverse, inverse


def norm_back(grad_out, normed, inverse, gain):
    scaled = grad_out * gain
    centered = scaled - jnp.mean(scaled, axis=-1, keepdims=True)
    return inverse * (centered - normed * jnp.mean(scaled * normed, axis=-1, keepdims=True))


def gelu_parts(values):
    c = math.sqrt(2 / math.pi)
    squared = values * values
    t = jnp.tanh(c * values * (1 + 0.044715 * squared))
    half = 0.5 * (1 + t)
    slope = half + 0.5 * values * (1 - t * t) * (c * (1 + 3 * 0.044715 * squared))
    return values * half, slope


def key_masks(facts_ref, block, rows, bq, nk):
    first = facts_ref[0] + block * bq
    limit = jnp.minimum(
        first + 1 + lax.broadcasted_iota(jnp.int32, (1, bq), 1), facts_ref[1]
    )
    own = lax.broadcasted_iota(jnp.int32, (nk, bq), 0) < limit
    earlier = lax.broadcasted_iota(jnp.int32, (SUMM_ROWS, bq), 0) < facts_ref[2]
    return own, earlier


class Facts:
    def __init__(self, lengths):
        segment = lax.axis_index("seq")
        self.values = (0, lengths[0, segment] + SUMM, jnp.where(segment > 0, SUMM, 0))

    def __getitem__(self, index):
        return self.values[index]


def head_lanes(head):
    lane = lax.broadcasted_iota(jnp.int32, (1, PAIR), 1)
    return (lane >= head * HDIM) & (lane < (head + 1) * HDIM)


def attend_kernel(bq, causal, facts_ref, q_ref, k_ref, v_ref, ks_ref, vs_ref, o_ref, lse_ref):
    rows, seg = q_ref.shape[0], k_ref.shape[0]
    v_t = v_ref[...].T
    vs_t = vs_ref[...].T
    ks = ks_ref[...]
    low_half = lax.broadcasted_iota(jnp.int32, (PAIR, 1), 0) < HDIM
    for block in range(rows // bq):
        nk = (block + 1) * bq if causal else seg
        own, earlier = key_masks(facts_ref, block, rows, bq, nk)
        q = q_ref[block * bq : (block + 1) * bq, :] * jnp.bfloat16(HDIM**-0.5)
        mixed = []
        for head in range(2):
            qh = jnp.where(head_lanes(head), q, jnp.zeros_like(q))
            s = jnp.where(own, mm(k_ref[:nk, :], qh, NT), MASKED)
            s2 = jnp.where(earlier, mm(ks, qh, NT), MASKED)
            top = jnp.maximum(jnp.max(s, axis=0, keepdims=True), jnp.max(s2, axis=0, keepdims=True))
            p = jnp.exp(s - top)
            p2 = jnp.exp(s2 - top)
            total = jnp.sum(p, axis=0, keepdims=True) + jnp.sum(p2, axis=0, keepdims=True)
            out = mm(v_t[:, :nk], p.astype(jnp.bfloat16)) + mm(vs_t, p2.astype(jnp.bfloat16))
            mixed.append(out / total)
            lse_ref[0, head : head + 1, block * bq : (block + 1) * bq] = top + jnp.log(total)
        joined = jnp.where(low_half, mixed[0], mixed[1])
        o_ref[block * bq : (block + 1) * bq, :] = joined.T.astype(jnp.bfloat16)


def query_block(rows):
    return 256 if rows % 256 == 0 else math.gcd(rows, 160)


def attend(facts, q, k, v, ks, vs):
    rows, width = q.shape
    seg = k.shape[0]
    pairs = width // PAIR
    column = lambda n: pl.BlockSpec((n, PAIR), lambda i: (0, i))
    return pl.pallas_call(
        functools.partial(attend_kernel, query_block(rows), rows == seg),
        grid=(pairs,),
        in_specs=[pl.BlockSpec(memory_space=pltpu.SMEM)]
        + [column(n) for n in (rows, seg, seg, SUMM_ROWS, SUMM_ROWS)],
        out_specs=[column(rows), pl.BlockSpec((1, 2, rows), lambda i: (i, 0, 0))],
        out_shape=[
            jax.ShapeDtypeStruct((rows, width), jnp.bfloat16),
            jax.ShapeDtypeStruct((pairs, 2, rows), jnp.float32),
        ],
        compiler_params=pltpu.CompilerParams(vmem_limit_bytes=48 * MIB),
        cost_estimate=pl.CostEstimate(
            flops=4 * rows * seg * width, bytes_accessed=8 * rows * width, transcendentals=0
        ),
        name="attend",
    )(facts, q, k, v, ks, vs)


def keys_for(local, lengths, seq_count):
    rows, width = local.shape[-2:]
    pad = ((0, 0), (0, SUMM_ROWS - SUMM), (0, 0))
    if rows == SLOT:
        here = lengths[lax.axis_index("seq")]
        summary = jnp.pad(lax.dynamic_slice(local, (0, here, 0), (2, SUMM, width)), pad)
        moves = [(i, i + 1) for i in range(seq_count - 1)]
        return local, lax.ppermute(summary, "seq", moves)
    everything = lax.all_gather(local, "seq", axis=1, tiled=True)
    segment = lax.axis_index("seq") * rows // SLOT
    own = lax.dynamic_slice(everything, (0, segment * SLOT, 0), (2, SLOT, width))
    summary = lax.dynamic_slice(everything, (0, lengths[0], 0), (2, SUMM, width))
    return own, jnp.pad(summary, pad)


def keys_back(own, summary, rows, lengths, seq_count):
    width = own.shape[-1]
    summary = summary[:, :SUMM]
    if rows == SLOT:
        moves = [(i + 1, i) for i in range(seq_count - 1)]
        arrived = lax.ppermute(summary, "seq", moves)
        here = lengths[lax.axis_index("seq")]
        old = lax.dynamic_slice(own, (0, here, 0), (2, SUMM, width))
        new = (old.astype(jnp.float32) + arrived).astype(jnp.bfloat16)
        return lax.dynamic_update_slice(own, new, (0, here, 0))
    segment = lax.axis_index("seq") * rows // SLOT
    everything = jnp.zeros((2, TOKENS, width), jnp.float32)
    everything = lax.dynamic_update_slice(
        everything, own.astype(jnp.float32), (0, segment * SLOT, 0)
    )
    old = lax.dynamic_slice(everything, (0, lengths[0], 0), (2, SUMM, width))
    added = jnp.where(segment > 0, summary, 0.0)
    everything = lax.dynamic_update_slice(everything, old + added, (0, lengths[0], 0))
    return lax.psum_scatter(
        everything.astype(jnp.bfloat16), "seq", scatter_dimension=1, tiled=True
    )


class Line:
    def __init__(self, count, half, multiply, finish, out, part, moving, sems, late=False, wide=None):
        self.count, self.half, self.multiply, self.finish = count, half, multiply, finish
        self.late, self.wide = late, wide
        self.out, self.part, self.moving = out, part, moving
        self.up_sent, self.up_got, self.down_sent, self.down_got, self.local = sems
        self.me = lax.axis_index("mp")
        self.pieces = half // PIECE
        self.per_group = part.shape[2] // PIECE
        self.steps = self.pieces + 2 * SKEW * (count - 1)

    @staticmethod
    def scratch(half, features):
        pieces = half // PIECE
        group = 160 if half % 160 == 0 else PIECE
        dma = lambda *shape: pltpu.SemaphoreType.DMA(shape)
        return [
            pltpu.VMEM((2, 2, group, features), jnp.float32),
            pltpu.VMEM((2 * (half + LEAD * PIECE), features), jnp.bfloat16),
            dma(2, pieces),
            dma(2, pieces),
            dma(2, pieces),
            dma(2, pieces),
            dma(2, pieces),
        ]

    def place(self, flow):
        return self.count - 1 - self.me if flow == 0 else self.me

    def greet(self, barrier):
        me = self.me

        @pl.when(me > 0)
        def _():
            pl.semaphore_signal(barrier, inc=1, device_id={"mp": me - 1}, device_id_type=MESH)

        @pl.when(me < self.count - 1)
        def _():
            pl.semaphore_signal(barrier, inc=1, device_id={"mp": me + 1}, device_id_type=MESH)

    def meet(self, barrier, others=0):
        ends = (self.me == 0) | (self.me == self.count - 1)

        @pl.when(ends)
        def _():
            pl.semaphore_wait(barrier, 1 + others)

        @pl.when(jnp.logical_not(ends))
        def _():
            pl.semaphore_wait(barrier, 2 + others)

    def first(self):
        for flow in range(2):
            self.part[flow, 0] = self.multiply(flow, 0)

    def spot(self, flow, k):
        return flow * (self.half + LEAD * PIECE) + k * PIECE

    def spots(self, flow, k, size=PIECE):
        return pl.ds(pl.multiple_of(self.spot(flow, k), PIECE), size)

    def finished(self, flow, k, size):
        mine = self.place(flow) == self.count - 1
        return self.spots(flow, jnp.where(mine, k + LEAD, k), size)

    def onward(self, flow, k):
        here = self.moving.at[self.spots(flow, k + LEAD)]
        return pltpu.make_async_remote_copy(
            src_ref=here,
            dst_ref=here,
            send_sem=self.up_sent.at[flow, k],
            recv_sem=self.up_got.at[flow, k],
            device_id={"mp": self.me - 1 if flow == 0 else self.me + 1},
            device_id_type=MESH,
        )

    def back(self, flow, k, owner):
        here = self.moving.at[self.spots(flow, k)]
        return pltpu.make_async_remote_copy(
            src_ref=self.moving.at[self.spots(flow, k + LEAD)] if owner else here,
            dst_ref=here,
            send_sem=self.down_sent.at[flow, k],
            recv_sem=self.down_got.at[flow, k],
            device_id={"mp": self.me + 1 if flow == 0 else self.me - 1},
            device_id_type=MESH,
        )

    def keep(self, flow, k, owner):
        spots = self.moving.at[self.spots(flow, k + LEAD if owner else k)]
        return pltpu.make_async_copy(
            spots if self.wide is None else self.wide.at[flow],
            self.out.at[pl.ds(flow * self.half + k * PIECE, PIECE)],
            self.local.at[flow, k],
        )

    def store(self, flow, k, owner):
        if self.wide is not None:

            @pl.when(k >= 1)
            def _():
                self.keep(flow, k - 1, owner).wait()

            spots = self.spots(flow, k + LEAD if owner else k)
            self.wide[flow] = self.moving[spots, :].astype(jnp.float32)
        self.keep(flow, k, owner).start()

    def send_on(self, flow, k):
        @pl.when(k >= LEAD)
        def _():
            self.onward(flow, k - LEAD).wait_send()

        self.onward(flow, k).start()

    def step(self, t):
        last = self.count - 1
        for flow in range(2):
            place = self.place(flow)
            k = t - SKEW * place
            here = self.spots(flow, k + LEAD)
            busy = (k >= 0) & (k < self.pieces)

            def mine():
                slot = (k // self.per_group) % 2
                inner = pl.ds(pl.multiple_of((k % self.per_group) * PIECE, PIECE), PIECE)
                return self.part[flow, slot, inner, :]

            @pl.when(busy & (place == 0))
            def _():
                self.moving[here, :] = mine().astype(jnp.bfloat16)
                self.send_on(flow, k)

            @pl.when(busy & (place > 0) & (place < last))
            def _():
                self.onward(flow, k).wait_recv()
                total = mine() + self.moving[here, :].astype(jnp.float32)
                self.moving[here, :] = total.astype(jnp.bfloat16)
                self.send_on(flow, k)

            @pl.when(busy & (place == last))
            def _():
                self.onward(flow, k).wait_recv()
                total = mine() + self.moving[here, :].astype(jnp.float32)
                self.moving[here, :] = self.finish(flow, k, total).astype(jnp.bfloat16)
                self.back(flow, k, True).start()
                self.store(flow, k, True)

        for flow in range(2):
            place = self.place(flow)
            j = t - SKEW * (2 * last - place)

            @pl.when((j >= 0) & (j < self.pieces) & (place < last))
            def _():
                self.back(flow, j, False).wait_recv()

                @pl.when(place > 0)
                def _():
                    self.back(flow, j, False).start()

                self.store(flow, j, False)

        for flow in range(2 if self.multiply else 0):
            k = t - SKEW * self.place(flow)
            g = k // self.per_group + 1

            if self.late:

                @pl.when(k == -1)
                def _():
                    self.part[flow, 0] = self.multiply(flow, 0)

            @pl.when((k >= 0) & (k % self.per_group == 0) & (g < self.pieces // self.per_group))
            def _():
                self.part[flow, g % 2] = self.multiply(flow, g)

    def settle(self):
        last = self.count - 1

        def one(k, carry):
            for flow in range(2):
                place = self.place(flow)

                @pl.when((place < last) & (k >= self.pieces - LEAD))
                def _():
                    self.onward(flow, k).wait_send()

                @pl.when((place > 0) & (place < last))
                def _():
                    self.back(flow, k, False).wait_send()

                @pl.when(place == last)
                def _():
                    self.back(flow, k, True).wait_send()

                @pl.when((k == self.pieces - 1) | (self.wide is None))
                def _():
                    self.keep(flow, k, False).wait()

            return carry

        lax.fori_loop(0, self.pieces, one, 0)


def group_product(lefts, right, dims, half, group):
    def multiply(flow, g):
        rows = pl.ds(pl.multiple_of(flow * half + g * group, 16), group)
        at, total = 0, None
        for left in lefts:
            depth = left.shape[1]
            cut = right[:, at : at + depth] if dims == NT else right[at : at + depth, :]
            product = mm(left[rows, :], cut, dims)
            total = product if total is None else total + product
            at += depth
        return total

    return multiply


def line_kernel(count, half, dims, n_left, n_extra, n_owned, n_acc, finish, sides, *refs):
    refs = list(refs)
    take = lambda n: [refs.pop(0) for _ in range(n)]
    lefts, (right,), extras = take(n_left), take(1), take(n_extra)
    side_in = [take(side.n_in) for side in sides]
    (out,), owned, accs = take(1), take(n_owned), take(1 if n_acc else 0)
    side_out = [take(side.n_out) for side in sides]
    part, moving, sems = *take(2), take(5)
    multiply = group_product(lefts, right, dims, half, part.shape[2])
    ending = lambda flow, k, total: finish(flow, k, total, extras, owned, accs)
    line = Line(count, half, multiply, ending, out, part, moving, sems)
    jobs = [
        side(ins, outs, take(len(side.scratch_shapes)), accs)
        for side, ins, outs in zip(sides, side_in, side_out)
    ]
    barrier = pltpu.get_barrier_semaphore()
    line.greet(barrier)
    for job in jobs:
        job.greet(barrier)
    if n_acc:
        accs[0][...] = jnp.zeros_like(accs[0])
    for job in jobs:
        job.first()
    line.first()
    line.meet(barrier, sum(job.others for job in jobs))

    def step(t, carry):
        line.step(t)
        for job in jobs:
            job.step(t)
        return carry

    lax.fori_loop(0, max([line.steps] + [job.steps for job in jobs]), step, 0)
    line.settle()
    for job in jobs:
        job.settle()


class Nothing:
    n_in = n_out = others = steps = 0
    operands, in_specs, out_shape, out_specs, scratch_shapes = (), (), (), (), ()

    def __call__(self, ins, outs, scratch, accs):
        return self

    def greet(self, barrier):
        pass

    def first(self):
        pass

    def step(self, t):
        pass

    def settle(self):
        pass


VMEM = pl.BlockSpec(memory_space=pltpu.VMEM)
ANY = pl.BlockSpec(memory_space=pl.ANY)
SMEM = pl.BlockSpec(memory_space=pltpu.SMEM)


def line_sum(number, count, lefts, right, dims, extras, n_owned, n_acc, finish, name, sides):
    rows = lefts[0].shape[0]
    features = right.shape[1 if dims == NN else 0]
    half = rows // 2
    acc = [jax.ShapeDtypeStruct((n_acc, 8, features), jnp.float32)] if n_acc else []
    return pl.pallas_call(
        functools.partial(
            line_kernel,
            count,
            half,
            dims,
            len(lefts),
            len(extras),
            n_owned,
            n_acc,
            finish,
            sides,
        ),
        in_specs=[VMEM] * (len(lefts) + 1 + len(extras)) + [s for side in sides for s in side.in_specs],
        out_specs=[ANY] + [VMEM] * (n_owned + len(acc)) + [s for side in sides for s in side.out_specs],
        out_shape=[jax.ShapeDtypeStruct((rows, features), jnp.bfloat16)]
        + [jax.ShapeDtypeStruct((half, features), jnp.float32)] * n_owned
        + acc
        + [s for side in sides for s in side.out_shape],
        scratch_shapes=Line.scratch(half, features) + [s for side in sides for s in side.scratch_shapes],
        compiler_params=pltpu.CompilerParams(
            collective_id=number, has_side_effects=True, vmem_limit_bytes=62 * MIB
        ),
        cost_estimate=pl.CostEstimate(
            flops=2 * rows * features * sum(left.shape[1] for left in lefts),
            bytes_accessed=4 * rows * features,
            transcendentals=0,
        ),
        name=name,
    )(*lefts, right, *extras, *[value for side in sides for value in side.operands])


def piece_rows(flow, k, half):
    return pl.ds(pl.multiple_of(flow * half + k * PIECE, PIECE), PIECE)


def fold(values):
    return jnp.sum(values.reshape(-1, 8, values.shape[-1]), axis=0)


def finish_input(flow, k, total, extras, owned, accs):
    hidden, grad, gain = extras
    (acc,) = accs
    half = grad.shape[0]
    normed, inverse = norm_stats(hidden[piece_rows(flow, k, half), :].astype(jnp.float32))
    acc[0] += fold(total * normed)
    acc[1] += fold(total)
    return grad[piece_rows(0, k, half), :] + norm_back(total, normed, inverse, gain[...])


def finish_out(flow, k, total, extras, owned, accs):
    residual, bias = extras
    half = residual.shape[0]
    return residual[piece_rows(0, k, half), :] + total + bias[...]


class AttendBack(Nothing):
    n_in, n_out = 8, 5

    def __init__(self, facts, q, k, v, ks, vs, do, lse):
        rows, width = q.shape
        seg = k.shape[0]
        self.operands = (facts, q, k, v, ks, vs, do, lse)
        self.in_specs = (SMEM,) + (VMEM,) * 7
        low = lambda n: jax.ShapeDtypeStruct((n, width), jnp.bfloat16)
        wide = lambda n: jax.ShapeDtypeStruct((n, width), jnp.float32)
        self.out_shape = (low(rows), low(seg), low(seg), wide(SUMM_ROWS), wide(SUMM_ROWS))
        self.out_specs = (VMEM,) * 5
        self.scratch_shapes = (
            pltpu.VMEM((seg, PAIR), jnp.float32),
            pltpu.VMEM((seg, PAIR), jnp.float32),
            pltpu.VMEM((PAIR, seg), jnp.bfloat16),
        )
        self.bq = query_block(rows)
        self.blocks = rows // self.bq
        self.pairs = width // PAIR
        self.steps = self.pairs * self.blocks
        self.causal = rows == seg

    def __call__(self, ins, outs, scratch, accs):
        self.ins, self.outs, self.scratch = ins, outs, scratch
        return self

    def step(self, t):
        pair = t // self.blocks
        for block in range(self.blocks):

            @pl.when((t >= 0) & (t < self.steps) & (t % self.blocks == block))
            def _():
                self.unit(pair, block)

    def unit(self, pair, block):
        facts, q_ref, k_ref, v_ref, ks_ref, vs_ref, do_ref, lse_ref = self.ins
        dq_ref, dk_ref, dv_ref, dks_ref, dvs_ref = self.outs
        dk_acc, dv_acc, k_t = self.scratch
        seg, bq = k_ref.shape[0], self.bq
        cols = pl.ds(pl.multiple_of(pair * PAIR, PAIR), PAIR)
        scale = jnp.bfloat16(HDIM**-0.5)
        low_half = lax.broadcasted_iota(jnp.int32, (PAIR, 1), 0) < HDIM
        if block == 0:
            k_t[...] = (k_ref[:, cols] * scale).T
            dk_acc[...] = jnp.zeros_like(dk_acc)
            dv_acc[...] = jnp.zeros_like(dv_acc)
            dks_ref[:, cols] = jnp.zeros((SUMM_ROWS, PAIR), jnp.float32)
            dvs_ref[:, cols] = jnp.zeros((SUMM_ROWS, PAIR), jnp.float32)
        ks, vs = ks_ref[:, cols], vs_ref[:, cols]
        ks_t = (ks * scale).T
        nk = (block + 1) * bq if self.causal else seg
        here = slice(block * bq, (block + 1) * bq)
        own, earlier = key_masks(facts, block, self.blocks * bq, bq, nk)
        q = q_ref[here, cols] * scale
        do = do_ref[here, cols]
        k, v = k_ref[:nk, cols], v_ref[:nk, cols]
        grads = []
        for head in range(2):
            qh = jnp.where(head_lanes(head), q, jnp.zeros_like(q))
            doh = jnp.where(head_lanes(head), do, jnp.zeros_like(do))
            lse = lse_ref[pair, head : head + 1, here]
            p = jnp.exp(jnp.where(own, mm(k, qh, NT), MASKED) - lse)
            p2 = jnp.exp(jnp.where(earlier, mm(ks, qh, NT), MASKED) - lse)
            dp = mm(v, doh, NT)
            dp2 = mm(vs, doh, NT)
            delta = jnp.sum(p * dp, axis=0, keepdims=True) + jnp.sum(p2 * dp2, axis=0, keepdims=True)
            ds = (p * (dp - delta)).astype(jnp.bfloat16)
            ds2 = (p2 * (dp2 - delta)).astype(jnp.bfloat16)
            dv_acc[:nk, :] += mm(p.astype(jnp.bfloat16), doh)
            dk_acc[:nk, :] += mm(ds, qh)
            dvs_ref[:, cols] += mm(p2.astype(jnp.bfloat16), doh)
            dks_ref[:, cols] += mm(ds2, qh)
            grads.append(mm(k_t[:, :nk], ds) + mm(ks_t, ds2))
        joined = jnp.where(low_half, grads[0], grads[1])
        dq_ref[here, cols] = joined.T.astype(jnp.bfloat16)
        if block == self.blocks - 1:
            dk_ref[:, cols] = dk_acc[...].astype(jnp.bfloat16)
            dv_ref[:, cols] = dv_acc[...].astype(jnp.bfloat16)


class Spread:
    others = 3
    block = 256
    lag = (2, 5, 8)
    across = (True, False, False, True)

    def __init__(self, lefts, columns, outs, left_now, scratch, start):
        self.lefts, self.outs, self.x_buf, self.start = lefts, outs, left_now, start
        self.table, self.phases, self.rights = [], {}, []
        at = 0
        for number, (left, right, result, place) in enumerate(columns):
            self.phases.setdefault(left, at)
            self.table.append((number, at, at + right.shape[1] // self.block, result, place))
            self.rights.append(right)
            at += right.shape[1] // self.block
        self.chunks = at
        self.steps = start + at + self.lag[2]
        (
            self.y_buf,
            self.s1,
            self.own,
            self.r1,
            self.s2x,
            self.s2y,
            self.top,
            self.low,
            self.r2x,
            self.r2y,
            self.s3,
            self.kept,
            self.r3,
            self.tile,
            self.x_sem,
            self.y_sem,
            self.s1_sem,
            self.r1_sem,
            self.s2x_sem,
            self.r2x_sem,
            self.s2y_sem,
            self.r2y_sem,
            self.s3y_sem,
            self.r3y_sem,
            self.s3x_sem,
            self.r3x_sem,
            self.out_sem,
        ) = scratch
        item, seq = lax.axis_index("item"), lax.axis_index("seq")
        self.core, self.x, self.y = item % 2, item // 2, seq
        self.to_core = {"item": item + 1 - 2 * self.core}
        self.to_x = {"item": item + 2 - 4 * self.x}
        self.to_y = {"seq": 1 - seq}

    @classmethod
    def scratch(cls, rows):
        block, half = cls.block, cls.block // 2
        low = lambda *shape: pltpu.VMEM(shape, jnp.bfloat16)
        wide = lambda *shape: pltpu.VMEM(shape, jnp.float32)
        return [
            low(2, rows, block),
            low(2, 2, block, 2 * block),
            wide(3, 2, block, 2 * block),
            low(4, 2, block, 2 * block),
            low(3, half, 2 * block),
            low(3, 2, half, block),
            wide(3, half, 2 * block),
            wide(3, 2, half, block),
            low(6, half, 2 * block),
            low(6, 2, half, block),
            low(3, 2, half, block),
            wide(3, 2, half, block),
            low(6, 2, half, block),
            wide(3, block, block),
        ] + [pltpu.SemaphoreType.DMA((n,)) for n in (1, 2, 2, 4, 3, 6, 3, 6, 3, 6, 3, 6, 3)]

    def greet(self, barrier):
        for to in (self.to_core, self.to_x, self.to_y):
            pl.semaphore_signal(barrier, inc=1, device_id=to, device_id_type=MESH)


    def left_copy(self, left):
        return pltpu.make_async_copy(self.lefts[left], self.x_buf, self.x_sem.at[0])

    def right_copy(self, m, act):
        for number, start, stop, _, _ in self.table:

            @pl.when((m >= start) & (m < stop))
            def _():
                cols = pl.ds(pl.multiple_of((m - start) * self.block, self.block), self.block)
                act(
                    pltpu.make_async_copy(
                        self.rights[number].at[:, cols], self.y_buf.at[m % 2], self.y_sem.at[m % 2]
                    )
                )

    def out_copy(self, m, act):
        for _, start, stop, result, place in self.table:

            @pl.when((m >= start) & (m < stop))
            def _():
                cols = pl.ds(
                    pl.multiple_of(place + (m - start) * self.block, self.block), self.block
                )
                out = self.outs[result]
                out = out.at[:, cols] if self.across[result] else out.at[cols, :]
                act(pltpu.make_async_copy(self.tile.at[m % 3], out, self.out_sem.at[m % 3]))

    def remote(self, src, dst, send, recv, to):
        return pltpu.make_async_remote_copy(
            src_ref=src, dst_ref=dst, send_sem=send, recv_sem=recv, device_id=to, device_id_type=MESH
        )

    def first_copy(self, m):
        return self.remote(
            self.s1.at[m % 2],
            self.r1.at[m % 4],
            self.s1_sem.at[m % 2],
            self.r1_sem.at[m % 4],
            self.to_core,
        )

    def second_copies(self, m):
        return (
            self.remote(
                self.s2x.at[m % 3],
                self.r2x.at[m % 6],
                self.s2x_sem.at[m % 3],
                self.r2x_sem.at[m % 6],
                self.to_x,
            ),
            self.remote(
                self.s2y.at[m % 3],
                self.r2y.at[m % 6],
                self.s2y_sem.at[m % 3],
                self.r2y_sem.at[m % 6],
                self.to_y,
            ),
        )

    def third_copies(self, m):
        return (
            self.remote(
                self.s3.at[m % 3, 0],
                self.r3.at[m % 6, 0],
                self.s3y_sem.at[m % 3],
                self.r3y_sem.at[m % 6],
                self.to_y,
            ),
            self.remote(
                self.s3.at[m % 3, 1],
                self.r3.at[m % 6, 1],
                self.s3x_sem.at[m % 3],
                self.r3x_sem.at[m % 6],
                self.to_x,
            ),
        )

    def step(self, t):
        @pl.when(t == self.start - 1)
        def _():
            self.left_copy(0).start()
            self.right_copy(0, lambda copy: copy.start())

        for stage, lag in ((self.fourth, 8), (self.third, 5), (self.second, 2), (self.multiply, 0)):
            m = t - self.start - lag

            @pl.when((m >= 0) & (m < self.chunks))
            def _():
                stage(m)

    def multiply(self, m):
        for left, start in self.phases.items():

            @pl.when(m == start)
            def _():
                if start > 0:
                    self.left_copy(left).start()
                self.left_copy(left).wait()

        @pl.when(m + 1 < self.chunks)
        def _():
            self.right_copy(m + 1, lambda copy: copy.start())

        self.right_copy(m, lambda copy: copy.wait())

        @pl.when(m >= 2)
        def _():
            self.first_copy(m - 2).wait_send()

        turned = self.y_buf[m % 2].T
        wide = 2 * self.block

        def product(x, core):
            cols = pl.ds(pl.multiple_of(x * 2 * wide + core * wide, wide), wide)
            return mm(turned, self.x_buf[:, cols])

        for x in range(2):
            self.s1[m % 2, x] = product(x, 1 - self.core).astype(jnp.bfloat16)
        self.first_copy(m).start()
        for x in range(2):
            self.own[m % 3, x] = product(x, self.core)

    def second(self, m):
        half = self.block // 2

        @pl.when(m >= 3)
        def _():
            for copy in self.second_copies(m - 3):
                copy.wait_send()

        self.first_copy(m).wait_recv()
        slot = m % 3
        here, there = self.x, 1 - self.x
        mine = pl.ds(pl.multiple_of(self.y * self.block, self.block), self.block)
        others = pl.ds(pl.multiple_of((1 - self.y) * self.block, self.block), self.block)
        added = lambda x, rows, cols: (
            self.own[slot, x, rows, cols] + self.r1[m % 4, x, rows, cols].astype(jnp.float32)
        )
        upper, lower, every = pl.ds(0, half), pl.ds(half, half), pl.ds(0, 2 * self.block)
        self.s2x[slot] = added(there, upper, every).astype(jnp.bfloat16)
        for x in range(2):
            self.s2y[slot, x] = added(x, lower, others).astype(jnp.bfloat16)
        for copy in self.second_copies(m):
            copy.start()
        self.top[slot] = added(here, upper, every)
        for x in range(2):
            self.low[slot, x] = added(x, lower, mine)

    def third(self, m):
        @pl.when(m >= 3)
        def _():
            for copy in self.third_copies(m - 3):
                copy.wait_send()

        for copy in self.second_copies(m):
            copy.wait_recv()
        slot, got = m % 3, m % 6
        mine = pl.ds(pl.multiple_of(self.y * self.block, self.block), self.block)
        others = pl.ds(pl.multiple_of((1 - self.y) * self.block, self.block), self.block)
        top = lambda cols: self.top[slot, :, cols] + self.r2x[got, :, cols].astype(jnp.float32)
        low = lambda x: self.low[slot, x] + self.r2y[got, x].astype(jnp.float32)
        self.s3[slot, 0] = top(others).astype(jnp.bfloat16)
        self.s3[slot, 1] = low(1 - self.x).astype(jnp.bfloat16)
        for copy in self.third_copies(m):
            copy.start()
        self.kept[slot, 0] = top(mine)
        self.kept[slot, 1] = low(self.x)

    def fourth(self, m):
        @pl.when(m >= 3)
        def _():
            self.out_copy(m - 3, lambda copy: copy.wait())

        for copy in self.third_copies(m):
            copy.wait_recv()
        slot, half = m % 3, self.block // 2
        total = self.kept[slot] + self.r3[m % 6].astype(jnp.float32)
        total = total.reshape(self.block, self.block)
        across = jnp.zeros((), jnp.bool_)
        for _, start, stop, result, _ in self.table:
            if self.across[result]:
                across = across | ((m >= start) & (m < stop))

        @pl.when(across)
        def _():
            self.tile[slot] = total.T

        @pl.when(jnp.logical_not(across))
        def _():
            self.tile[slot] = total

        self.out_copy(m, lambda copy: copy.start())

    def settle(self):
        for m in range(self.chunks - 3, self.chunks):
            if m >= self.chunks - 2:
                self.first_copy(m).wait_send()
            for copy in self.second_copies(m) + self.third_copies(m):
                copy.wait_send()
            self.out_copy(jnp.int32(m), lambda copy: copy.wait())


class Gather:
    others = 3

    def __init__(self, shards, fulls, sems, ready):
        self.shards, self.fulls, self.ready = shards, fulls, ready
        self.sent, self.got, self.local = sems
        item, seq = lax.axis_index("item"), lax.axis_index("seq")
        self.core, self.x, self.y = item % 2, item // 2, seq
        self.to_core = {"item": item + 1 - 2 * self.core}
        self.to_x = {"item": item + 2 - 4 * self.x}
        self.to_y = {"seq": 1 - seq}

    @staticmethod
    def sems(count=2):
        dma = lambda *shape: pltpu.SemaphoreType.DMA(shape)
        return [dma(count, 9), dma(count, 9), dma(count)]

    def greet(self, barrier):
        for to in (self.to_core, self.to_x, self.to_y):
            pl.semaphore_signal(barrier, inc=1, device_id=to, device_id_type=MESH)

    def spot(self, w, x, core, y, part=None):
        size = self.shards[w].shape[w]
        at = pl.ds(pl.multiple_of(((2 * x + core) * 2 + y) * size, size), size)
        if w == 0:
            if part is not None:
                half = size // 2
                start = ((2 * x + core) * 2 + y) * size + part * half
                at = pl.ds(pl.multiple_of(start, half), half)
            return self.fulls[0].at[at, :]
        rows = self.fulls[1].shape[0]
        if part is not None:
            return self.fulls[1].at[pl.ds(part * (rows // 2), rows // 2), at]
        return self.fulls[1].at[:, at]

    def message(self, w, number, src, dst, to):
        return pltpu.make_async_remote_copy(
            src_ref=src,
            dst_ref=dst,
            send_sem=self.sent.at[w, number],
            recv_sem=self.got.at[w, number],
            device_id=to,
            device_id_type=MESH,
        )

    def plan(self, w):
        c, x, y = self.core, self.x, self.y
        own, spot = self.shards[w].at[...], functools.partial(self.spot, w)
        return (
            (own, spot(x, c, y), spot(x, 1 - c, y), self.to_core),
            (own, spot(x, c, y), spot(1 - x, c, y), self.to_x),
            (own, spot(x, c, y), spot(x, c, 1 - y), self.to_y),
            (None, spot(1 - x, c, y, 0), spot(1 - x, c, 1 - y, 0), self.to_y),
            (None, spot(x, c, 1 - y, 1), spot(1 - x, c, 1 - y, 1), self.to_x),
            (None, spot(1 - x, c, y), spot(1 - x, 1 - c, y), self.to_core),
            (None, spot(x, c, 1 - y), spot(x, 1 - c, 1 - y), self.to_core),
            (None, spot(1 - x, c, 1 - y, 0), spot(1 - x, 1 - c, 1 - y, 0), self.to_core),
            (None, spot(1 - x, c, 1 - y, 1), spot(1 - x, 1 - c, 1 - y, 1), self.to_core),
        )
    def send(self, w, numbers):
        plan = self.plan(w)
        for number in numbers:
            src, out, _, to = plan[number]
            self.message(w, number, out if src is None else src, out, to).start()

    def receive(self, w, numbers):
        plan = self.plan(w)
        for number in numbers:
            _, _, landing, to = plan[number]
            self.message(w, number, landing, landing, to).wait_recv()

    def mine(self, w):
        return pltpu.make_async_copy(
            self.shards[w], self.spot(w, self.x, self.core, self.y), self.local.at[w]
        )

    def first(self):
        for w in range(len(self.shards)):
            self.mine(w).start()

    def begin(self):
        for w in range(2):
            self.send(w, (1, 2, 0))

    def step(self, t):
        for w, at in ((0, GATHER_STEPS[0]), (1, GATHER_STEPS[1])):

            @pl.when(t == at)
            def _():
                self.receive(w, (1, 2))
                self.send(w, (3, 4, 5, 6))

        for w, at in ((0, GATHER_STEPS[2]), (1, GATHER_STEPS[3])):

            @pl.when(t == at)
            def _():
                self.receive(w, (3, 4))
                self.send(w, (7, 8))

        @pl.when(t == self.ready)
        def _():
            for w in range(2):
                self.receive(w, (0, 5, 6, 7, 8))
                self.mine(w).wait()

    def settle(self):
        for w in range(len(self.shards)):
            for number, (src, out, _, to) in enumerate(self.plan(w)):
                self.message(w, number, out if src is None else src, out, to).wait_send()


class Load:
    others = 0

    def __init__(self, shards, fulls, sems, ready):
        self.ready = ready
        self.copies = [
            pltpu.make_async_copy(shard, full, sems[2].at[w])
            for w, (shard, full) in enumerate(zip(shards, fulls))
        ]

    sems = Gather.sems

    def greet(self, barrier):
        pass

    def first(self):
        for copy in self.copies:
            copy.start()

    def begin(self):
        pass

    def step(self, t):
        @pl.when(t == self.ready)
        def _():
            for copy in self.copies:
                copy.wait()

    def settle(self):
        pass


class Attend:
    bq = 128

    def __init__(self, half, facts, q, k, v, earlier, attended, lse):
        self.half, self.facts, self.q, self.k, self.v = half, facts, q, k, v
        self.earlier, self.attended, self.lse = earlier, attended, lse
        self.pairs = q.shape[1] // PAIR
        self.blocks = half // self.bq

    def first(self):
        def one(pair, carry):
            for flow in range(2):
                self.unit(pair, flow * self.blocks)
            return carry

        lax.fori_loop(0, self.pairs, one, 0)

    def step(self, t):
        def both(pair, block):
            for flow in range(2):
                self.unit(pair, flow * self.blocks + block)

        @pl.when((t >= 0) & (t < 2))
        def _():
            each = self.pairs // 2

            def one(i, carry):
                both((t % 2) * each + i, 1)
                return carry

            lax.fori_loop(0, each, one, 0)

        for block in range(2, self.blocks):
            start = self.pairs * (block - 2) + 2

            @pl.when((t >= start) & (t < start + self.pairs))
            def _():
                both(t - start, block)

    def unit(self, pair, block):
        bq, nk = self.bq, (block + 1) * self.bq
        cols = pl.ds(pl.multiple_of(pair * PAIR, PAIR), PAIR)
        here = slice(block * bq, nk)
        query = block * bq + lax.broadcasted_iota(jnp.int32, (1, 2 * bq), 1) % bq
        limit = jnp.minimum(query + 1, self.facts[1])
        own = lax.broadcasted_iota(jnp.int32, (nk, 2 * bq), 0) < limit
        earlier = lax.broadcasted_iota(jnp.int32, (SUMM_ROWS, 2 * bq), 0) < self.facts[2]
        q = self.q[here, cols] * jnp.bfloat16(HDIM**-0.5)
        q = jnp.concatenate([jnp.where(head_lanes(h), q, jnp.zeros_like(q)) for h in range(2)])
        s = jnp.where(own, mm(self.k[:nk, cols], q, NT), MASKED)
        s2 = jnp.where(earlier, mm(self.earlier[0, :, cols], q, NT), MASKED)
        top = jnp.maximum(jnp.max(s, axis=0, keepdims=True), jnp.max(s2, axis=0, keepdims=True))
        p = jnp.exp(s - top)
        p2 = jnp.exp(s2 - top)
        total = jnp.sum(p, axis=0, keepdims=True) + jnp.sum(p2, axis=0, keepdims=True)
        out = mm(self.v[:nk, cols].T, p.astype(jnp.bfloat16))
        out = (out + mm(self.earlier[1, :, cols].T, p2.astype(jnp.bfloat16))) / total
        lse = top + jnp.log(total)
        for head in range(2):
            self.lse[pair, head : head + 1, here] = lse[:, head * bq : (head + 1) * bq]
        low_half = lax.broadcasted_iota(jnp.int32, (PAIR, 1), 0) < HDIM
        joined = jnp.where(low_half, out[:, :bq], out[:, bq:])
        self.attended[here, cols] = joined.T.astype(jnp.bfloat16)


def ffn_kernel(count, half, weights_job, n_attend, *refs):
    if n_attend == 1:
        ffn_body(count, half, weights_job, None, *refs)
    else:
        lengths, earlier, *rest = refs
        sources, rest = rest[:3], rest[3:]
        inputs, outputs, scratch = rest[:9], rest[9:22], rest[22:]
        *outputs, attended, lse = outputs
        *scratch, q, k, v, sems = scratch
        job = Attend(half, Facts(lengths), q, k, v, earlier, attended, lse)
        job.loads = [
            pltpu.make_async_copy(source, target, sems.at[number])
            for number, (source, target) in enumerate(zip(sources, (q, k, v)))
        ]
        for load in job.loads:
            load.start()
        ffn_body(count, half, weights_job, job, attended, *inputs, *outputs, *scratch)


def ffn_body(
    count,
    half,
    weights_job,
    attention,
    attended,
    out_w,
    out_bias,
    mid_gain,
    mid_shift,
    up_bias,
    hidden,
    cotangent,
    up_shard,
    down_shard,
    mid,
    act,
    grad_pre,
    residual_out,
    branch,
    grad_out,
    down_out,
    acc,
    acc_up,
    acc_down,
    grad_attended,
    part1,
    moving1,
    part2,
    moving2,
    rows_in,
    residual,
    up,
    down,
    cot_in,
    act_out,
    pre_out,
    attended_out,
    *sems,
):
    sems = list(sems)
    take = lambda n: [sems.pop(0) for _ in range(n)]
    sems1, sems2, weight_sems = take(5), take(5), take(3)
    in_sem, residual_sem, grad_sem, cot_sem, act_sem, pre_sem, down_sem = sems[:7]
    (attended_sem,) = sems[7:]
    me = lax.axis_index("mp")
    group = part2.shape[2]
    blocks = 4
    block = up.shape[1] // blocks
    per_group = group // PIECE
    pieces = half // PIECE
    last = count - 1
    second = per_group + blocks + 2 * SKEW * (count - 1)
    weights = weights_job((up_shard, down_shard), (up, down), weight_sems, second - blocks - 1)
    piece = lambda k: pl.ds(pl.multiple_of(k * PIECE, PIECE), PIECE)
    owner = (me == 0) | (me == last)
    my_flow = jnp.where(me == 0, 0, 1)

    def piece_in(source, k, flow):
        return pltpu.make_async_copy(
            source.at[pl.ds(flow * half + k * PIECE, PIECE)], rows_in.at[piece(k)], in_sem.at[k]
        )

    def residual_copy(k):
        return pltpu.make_async_copy(
            residual.at[piece(k)], residual_out.at[piece(k)], residual_sem.at[k]
        )

    def grad_copy(k):
        return pltpu.make_async_copy(residual.at[piece(k)], grad_out.at[piece(k)], grad_sem.at[k])

    def finish_first(flow, k, total):
        piece_in(hidden, k, flow).wait()
        value = rows_in[piece(k), :].astype(jnp.float32) + total + out_bias[...]
        residual[piece(k), :] = value
        residual_copy(k).start()
        piece_in(cotangent, k, flow).start()
        return norm_stats(value)[0] * mid_gain[...] + mid_shift[...]

    def finish_second(flow, k, total):
        piece_in(cotangent, k, flow).wait()
        residual_copy(k).wait()
        normed, inverse = norm_stats(residual[piece(k), :])
        grad = rows_in[piece(k), :].astype(jnp.float32)
        grad = grad + norm_back(total, normed, inverse, mid_gain[...])
        residual[piece(k), :] = grad
        grad_copy(k).start()
        acc[0] += fold(total * normed)
        acc[1] += fold(total)
        acc[2] += fold(grad)
        return grad

    multiply = group_product([attended], out_w, NN, half, part1.shape[2])
    line1 = Line(count, half, multiply, finish_first, mid, part1, moving1, sems1)
    line2 = Line(count, half, None, finish_second, branch, part2, moving2, sems2)

    def group_rows(flow, g):
        return pl.ds(pl.multiple_of(flow * half + g * group, 16), group)

    def cot_fetch(flow, g):
        return pltpu.make_async_copy(
            cotangent.at[group_rows(flow, g)], cot_in.at[flow], cot_sem.at[flow]
        )

    def act_copy(flow, g):
        return pltpu.make_async_copy(
            act_out.at[flow], act.at[group_rows(flow, g)], act_sem.at[flow]
        )

    def pre_copy(flow, g):
        return pltpu.make_async_copy(
            pre_out.at[flow], grad_pre.at[group_rows(flow, g)], pre_sem.at[flow]
        )

    def products(flow, g, number):
        @pl.when(number == 0)
        def _():
            cot_fetch(flow, g).wait()
            acc_down[...] += fold(cot_in[flow].astype(jnp.float32))

            @pl.when(g > 0)
            def _():
                act_copy(flow, g - 1).wait()
                pre_copy(flow, g - 1).wait()

        cols = pl.ds(pl.multiple_of(number * block, block), block)
        value, slope = gelu_parts(mm(moving1[line1.finished(flow, g * per_group, group), :], up[:, cols]) + up_bias[:, cols])
        act_out[flow, :, cols] = value.astype(jnp.bfloat16)
        pre = (slope * mm(cot_in[flow], down[cols, :], NT)).astype(jnp.bfloat16)
        pre_out[flow, :, cols] = pre
        acc_up[:, cols] += fold(pre.astype(jnp.float32))
        product = mm(pre, up[:, cols], NT)

        @pl.when(number == 0)
        def _():
            part2[flow, g % 2] = product

        @pl.when(number > 0)
        def _():
            part2[flow, g % 2] += product

        @pl.when(number == blocks - 1)
        def _():
            act_copy(flow, g).start()
            pre_copy(flow, g).start()

    def attended_copy(flow, g):
        return pltpu.make_async_copy(
            attended_out.at[flow], grad_attended.at[group_rows(flow, g)], attended_sem.at[flow]
        )

    def through_out(flow, g):
        @pl.when(g > 0)
        def _():
            attended_copy(flow, g - 1).wait()

        attended_out[flow] = mm(moving2[line2.finished(flow, g * per_group, group), :], out_w[...], NT).astype(jnp.bfloat16)
        attended_copy(flow, g).start()

    barrier = pltpu.get_barrier_semaphore()
    line1.greet(barrier)
    weights.greet(barrier)
    acc[...] = jnp.zeros_like(acc)
    acc_up[...] = jnp.zeros_like(acc_up)
    acc_down[...] = jnp.zeros_like(acc_down)
    weights.first()

    @pl.when(owner)
    def _():
        def one(k, carry):
            piece_in(hidden, k, my_flow).start()
            return carry

        lax.fori_loop(0, pieces, one, 0)

    if attention is None:
        line1.first()
        line1.meet(barrier, weights.others)
        weights.begin()
    else:
        for load in attention.loads:
            load.wait()
        attention.first()
        line1.first()
        line1.meet(barrier, weights.others)
        weights.begin()

    def step(t, carry):
        if attention is not None:
            attention.step(t)
        line1.step(t)
        line2.step(t - second)
        weights.step(t)

        @pl.when(t == weights.ready + 1)
        def _():
            pltpu.make_async_copy(down, down_out, down_sem.at[0]).start()

        for flow in range(2):
            place = line1.place(flow)
            u = t - second - SKEW * place
            fetch = u + blocks + 1
            compute = u + blocks

            @pl.when((fetch >= 0) & (fetch % per_group == 0) & (fetch < pieces))
            def _():
                cot_fetch(flow, fetch // per_group).start()

            @pl.when((compute >= 0) & (compute < pieces) & (compute % per_group < blocks))
            def _():
                products(flow, compute // per_group, compute % per_group)

            here = t - second - SKEW * (2 * last - place)

            @pl.when((here >= 0) & (here < pieces) & (here % per_group == per_group - 1))
            def _():
                through_out(flow, here // per_group)

        return carry

    lax.fori_loop(0, second + line2.steps, step, 0)
    line1.settle()
    line2.settle()
    weights.settle()
    pltpu.make_async_copy(down, down_out, down_sem.at[0]).wait()
    for flow in range(2):
        act_copy(flow, pieces // per_group - 1).wait()
        pre_copy(flow, pieces // per_group - 1).wait()
        attended_copy(flow, pieces // per_group - 1).wait()

    @pl.when(owner)
    def _():
        def one(k, carry):
            grad_copy(k).wait()
            return carry

        lax.fori_loop(0, pieces, one, 0)


def ffn_sums(number, count, weights_job, attend_in, out_w, vectors, hidden, cotangent, up_w, down_w):
    rows, features = hidden.shape
    ff = up_w.shape[1]
    half = rows // 2
    pieces = half // PIECE
    low = lambda *shape: jax.ShapeDtypeStruct(shape, jnp.bfloat16)
    wide = lambda *shape: jax.ShapeDtypeStruct(shape, jnp.float32)
    attend_out, attend_scratch = [], []
    if len(attend_in) > 1:
        width = attend_in[2].shape[1]
        attend_scratch = [pltpu.VMEM((rows, width), jnp.bfloat16)] * 3
        attend_scratch += [pltpu.SemaphoreType.DMA((3,))]
        attend_out = [low(rows, width), wide(width // PAIR, 2, rows)]
    first = Line.scratch(half, features)
    small = 64 if half % 64 == 0 else PIECE
    first[0] = pltpu.VMEM((2, 2, small, features), jnp.float32)
    second = Line.scratch(half, features)
    group = second[0].shape[2]
    dma = lambda n: pltpu.SemaphoreType.DMA((n,))
    return pl.pallas_call(
        functools.partial(ffn_kernel, count, half, weights_job, len(attend_in)),
        in_specs=([SMEM, VMEM] + [ANY] * 3 if len(attend_in) > 1 else [VMEM]) + [VMEM] * 5 + [ANY] * 4,
        out_specs=[ANY] * 7 + [VMEM] * 3 + [ANY] + [VMEM] * len(attend_out),
        out_shape=[
            low(rows, features),
            low(rows, ff),
            low(rows, ff),
            wide(half, features),
            low(rows, features),
            wide(half, features),
            low(ff, features),
            wide(3, 8, features),
            wide(8, ff),
            wide(8, features),
            low(rows, out_w.shape[0]),
        ]
        + attend_out,
        scratch_shapes=first[:2]
        + second[:2]
        + [
            pltpu.VMEM((half, features), jnp.bfloat16),
            pltpu.VMEM((half, features), jnp.float32),
            pltpu.VMEM((features, ff), jnp.bfloat16),
            pltpu.VMEM((ff, features), jnp.bfloat16),
            pltpu.VMEM((2, group, features), jnp.bfloat16),
            pltpu.VMEM((2, group, ff), jnp.bfloat16),
            pltpu.VMEM((2, group, ff), jnp.bfloat16),
            pltpu.VMEM((2, group, out_w.shape[0]), jnp.bfloat16),
        ]
        + first[2:]
        + second[2:]
        + Gather.sems()
        + [dma(pieces), dma(pieces), dma(pieces), dma(2), dma(2), dma(2), dma(1)]
        + [dma(2)]
        + attend_scratch,
        compiler_params=pltpu.CompilerParams(
            collective_id=number, has_side_effects=True, vmem_limit_bytes=62 * MIB
        ),
        cost_estimate=pl.CostEstimate(
            flops=6 * rows * features * ff, bytes_accessed=30 * rows * features, transcendentals=0
        ),
        name="ffn_sums",
    )(*attend_in, out_w, *vectors, hidden, cotangent, up_w, down_w)


def start_kernel(
    lengths,
    gain,
    shift,
    bias,
    hidden_in,
    shard,
    out_shard,
    q_ref,
    k_ref,
    v_ref,
    earlier,
    normed_out,
    weight_out,
    out_whole,
    normed,
    weight,
    out_weight,
    total,
    summary,
    hidden,
    *sems,
):
    facts = Facts(lengths)
    gather = Gather((shard, out_shard), (weight, out_weight), sems[:3], 0)
    summary_sent, summary_got, out_sems = sems[3:]
    rows = hidden.shape[0]
    width = q_ref.shape[1]
    size = shard.shape[0]
    chunk = 128
    barrier = pltpu.get_barrier_semaphore()
    gather.greet(barrier)
    load = pltpu.make_async_copy(hidden_in, hidden, out_sems.at[3])
    load.start()
    gather.first()
    pl.semaphore_wait(barrier, gather.others)
    gather.send(0, (1, 2, 0))

    def norm(i, carry):
        here = pl.ds(pl.multiple_of(i * chunk, chunk), chunk)
        value = norm_stats(hidden[here, :].astype(jnp.float32))[0]
        normed[here, :] = (value * gain[...] + shift[...]).astype(jnp.bfloat16)
        return carry

    load.wait()
    lax.fori_loop(0, rows // chunk, norm, 0)
    keep = pltpu.make_async_copy(normed, normed_out, out_sems.at[0])
    keep.start()
    c, x, y = gather.core, gather.x, gather.y

    def add(places, first=False, last=False):
        starts = [
            pl.multiple_of(((2 * px + pc) * 2 + py) * size, size) for px, pc, py in places
        ]

        def rows_of(i, carry):
            here = pl.ds(pl.multiple_of(i * chunk, chunk), chunk)
            for j, out in enumerate((q_ref, k_ref, v_ref)):
                cols = slice(j * width, (j + 1) * width)
                value = None if first else total[here, cols]
                for start in starts:
                    at = pl.ds(start, size)
                    product = mm(normed[here, at], weight[at, cols])
                    value = product if value is None else value + product
                if not last:
                    total[here, cols] = value
                elif j == 1:
                    out[here, :] = value.astype(jnp.bfloat16)
                else:
                    out[here, :] = (value + bias[j // 2 : j // 2 + 1, :]).astype(jnp.bfloat16)
            return carry

        lax.fori_loop(0, rows // chunk, rows_of, 0)

    gather.mine(0).wait()
    gather.receive(0, (0,))
    add(((x, c, y), (x, 1 - c, y)), first=True)
    gather.receive(0, (1, 2))
    gather.send(0, (3, 4, 5, 6))
    gather.send(1, (1, 2, 0))
    add(((1 - x, c, y), (x, c, 1 - y)))
    gather.receive(0, (5, 6))
    add(((1 - x, 1 - c, y), (x, 1 - c, 1 - y)))
    gather.receive(0, (3, 4))
    gather.send(0, (7, 8))
    add(((1 - x, c, 1 - y),))
    gather.receive(1, (1, 2))
    gather.send(1, (3, 4, 5, 6))
    gather.receive(0, (7, 8))
    store = pltpu.make_async_copy(weight, weight_out, out_sems.at[1])
    store.start()
    add(((1 - x, 1 - c, 1 - y),), last=True)

    shape = (SUMM_ROWS, rows)
    chosen = lax.broadcasted_iota(jnp.int32, shape, 1) == (
        facts[1] - SUMM + lax.broadcasted_iota(jnp.int32, shape, 0)
    )
    chosen = jnp.where(chosen, 1.0, 0.0).astype(jnp.bfloat16)
    summary[0] = mm(chosen, k_ref[...]).astype(jnp.bfloat16)
    summary[1] = mm(chosen, v_ref[...]).astype(jnp.bfloat16)
    swap = pltpu.make_async_remote_copy(
        src_ref=summary,
        dst_ref=earlier,
        send_sem=summary_sent.at[0],
        recv_sem=summary_got.at[0],
        device_id=gather.to_y,
        device_id_type=MESH,
    )
    swap.start()
    gather.receive(1, (3, 4))
    gather.send(1, (7, 8))
    gather.receive(1, (0, 5, 6, 7, 8))
    gather.mine(1).wait()
    store_out = pltpu.make_async_copy(out_weight, out_whole, out_sems.at[2])
    store_out.start()
    gather.settle()
    keep.wait()
    store.wait()
    swap.wait()
    store_out.wait()


def start(number, lengths, hidden, gain, shift, bias, shard, out_shard):
    rows, features = hidden.shape
    width = bias.shape[1]
    low = lambda *shape: jax.ShapeDtypeStruct(shape, jnp.bfloat16)
    dma = lambda n: pltpu.SemaphoreType.DMA((n,))
    return pl.pallas_call(
        start_kernel,
        in_specs=[SMEM] + [VMEM] * 3 + [ANY] * 3,
        out_specs=[VMEM] * 3 + [ANY] * 4,
        out_shape=[low(rows, width)] * 3
        + [low(2, SUMM_ROWS, width), low(rows, features), low(features, 3 * width)]
        + [low(width, features)],
        scratch_shapes=[
            pltpu.VMEM((rows, features), jnp.bfloat16),
            pltpu.VMEM((features, 3 * width), jnp.bfloat16),
            pltpu.VMEM((width, features), jnp.bfloat16),
            pltpu.VMEM((rows, 3 * width), jnp.float32),
            pltpu.VMEM((2, SUMM_ROWS, width), jnp.bfloat16),
            pltpu.VMEM((rows, features), jnp.bfloat16),
        ]
        + Gather.sems()
        + [dma(1), dma(1), dma(4)],
        compiler_params=pltpu.CompilerParams(
            collective_id=number, has_side_effects=True, vmem_limit_bytes=60 * MIB
        ),
        cost_estimate=pl.CostEstimate(
            flops=6 * rows * features * width, bytes_accessed=16 * rows * features, transcendentals=0
        ),
        name="start",
    )(lengths, gain, shift, bias, hidden, shard, out_shard)


class SmallSums(Nothing):
    n_in = n_out = 1

    def __init__(self, sizes, shared, start, values):
        self.stages = tuple(
            (axis, 1 << bit) for axis, size in sizes for bit in range(size.bit_length() - 1)
        )
        self.shared, self.start = shared, start
        self.others = len(self.stages)
        self.steps = start + self.others + 1
        self.operands = (values,)
        self.in_specs = self.out_specs = (VMEM,)
        self.out_shape = (jax.ShapeDtypeStruct(values.shape, jnp.float32),)
        buffers = pltpu.VMEM((self.others, *values.shape), jnp.float32)
        sems = pltpu.SemaphoreType.DMA((self.others,))
        self.scratch_shapes = (buffers, buffers, sems, sems)

    def __call__(self, ins, outs, scratch, accs):
        (self.own,), (self.out,), (self.acc,) = ins, outs, accs
        self.sent, self.got, self.send_sem, self.recv_sem = scratch
        return self

    def partner(self, axis, bit):
        index = lax.axis_index(axis)
        return {axis: index + bit - 2 * bit * ((index // bit) % 2)}

    def extra(self, row, start, grad):
        cols = slice(start, start + grad.shape[1])
        self.sent[0, row : row + 1, cols] = jnp.sum(
            grad[...].astype(jnp.float32), axis=0, keepdims=True
        )

    def greet(self, barrier):
        for axis, bit in self.stages:
            pl.semaphore_signal(
                barrier, inc=1, device_id=self.partner(axis, bit), device_id_type=MESH
            )

    def copy(self, number):
        return pltpu.make_async_remote_copy(
            src_ref=self.sent.at[number],
            dst_ref=self.got.at[number],
            send_sem=self.send_sem.at[number],
            recv_sem=self.recv_sem.at[number],
            device_id=self.partner(*self.stages[number]),
            device_id_type=MESH,
        )

    def first(self):
        self.sent[0] = self.own[...]

    def step(self, t):
        @pl.when(t == self.start)
        def _():
            for number in range(self.acc.shape[0]):
                self.sent[0, 3 + number : 4 + number, :] = jnp.sum(
                    self.acc[number], axis=0, keepdims=True
                )
            self.copy(0).start()

        row = lax.broadcasted_iota(jnp.int32, self.out.shape, 0)
        for number, (axis, _) in enumerate(self.stages):

            @pl.when(t == self.start + 1 + number)
            def _():
                self.copy(number).wait()
                total = self.sent[number] + self.got[number]
                if axis == "mp":
                    total = jnp.where(row < self.shared, total, self.sent[number])
                if number + 1 < len(self.stages):
                    self.sent[number + 1] = total
                    self.copy(number + 1).start()
                else:
                    self.out[...] = total


class Columns:
    def __init__(self, ref, start, width):
        self.ref, self.start, self.shape = ref, start, (ref.shape[0], width)

    def __getitem__(self, index):
        rows, cols = index
        start = pl.multiple_of(self.start + cols.start, PAIR)
        return self.ref[rows, pl.ds(start, cols.size)]


class Ring:
    depth = 2

    def __init__(self, source, buffer, sems, pieces, offset):
        self.source, self.buffer, self.sems = source, buffer, sems
        self.pieces, self.offset = pieces, offset

    @classmethod
    def scratch(cls, features, dtype):
        return [
            pltpu.VMEM((cls.depth, PIECE, features), dtype),
            pltpu.SemaphoreType.DMA((cls.depth,)),
        ]

    def copy(self, k):
        rows = pl.ds(self.offset + k * PIECE, PIECE)
        slot = k % self.depth
        return pltpu.make_async_copy(
            self.source.at[rows], self.buffer.at[slot], self.sems.at[slot]
        )

    def fill(self):
        for k in range(min(self.depth, self.pieces)):
            self.copy(k).start()

    def take(self, k):
        self.copy(k).wait()
        value = self.buffer[k % self.depth].astype(jnp.float32)

        @pl.when(k + self.depth < self.pieces)
        def _():
            self.copy(k + self.depth).start()

        return value


def back_kernel(
    count,
    half,
    sizes,
    lengths,
    lse,
    earlier,
    down_bias,
    pre_gain,
    mid_sums,
    up_sums,
    down_sums,
    q_in,
    k_in,
    v_in,
    do_in,
    act,
    down_in,
    residual,
    hidden,
    grad_in,
    qkv_in,
    mid,
    cotangent,
    branch,
    normed,
    grad_pre,
    attended,
    hidden_out,
    input_grad,
    up_grad,
    down_grad,
    out_grad,
    qkv_grad,
    sums_out,
    part,
    moving1,
    moving2,
    down,
    qkv_w,
    dq,
    dk,
    dv,
    dk_acc,
    dv_acc,
    k_t,
    dks,
    dvs,
    swap_out,
    swap_in,
    act_in,
    acc,
    small_sent,
    small_got,
    wide_out,
    *rest,
):
    rest = list(rest)
    facts = Facts(lengths)
    take = lambda n: [rest.pop(0) for _ in range(n)]
    rings = take(6)
    sems1, sems2 = take(5), take(5)
    small_sems = take(2)
    load_sem, act_sem, swap_sent, swap_got = take(4)
    rows, width = 2 * half, dq.shape[1]
    pieces = half // PIECE
    me = lax.axis_index("mp")
    owner = (me == 0) | (me == count - 1)
    offset = jnp.where(me == 0, 0, half)
    residual_ring = Ring(residual, *rings[0:2], pieces, 0)
    grad_ring = Ring(grad_in, *rings[2:4], pieces, 0)
    hidden_ring = Ring(hidden, *rings[4:6], pieces, offset)
    group = part.shape[2]

    def act_copy(flow, g):
        return pltpu.make_async_copy(
            act.at[pl.ds(pl.multiple_of(flow * half + g * group, 16), group)],
            act_in.at[flow],
            act_sem.at[flow],
        )

    def multiply_down(flow, g):
        act_copy(flow, g).wait()
        product = mm(act_in[flow], down[...])

        @pl.when(g + 1 < half // group)
        def _():
            act_copy(flow, g + 1).start()

        return product

    def finish_first(flow, k, total):
        return residual_ring.take(k) + total + down_bias[...]

    def finish_second(flow, k, total):
        values, inverse = norm_stats(hidden_ring.take(k))
        acc[0] += fold(total * values)
        acc[1] += fold(total)
        return grad_ring.take(k) + norm_back(total, values, inverse, pre_gain[...])

    line1 = Line(count, half, multiply_down, finish_first, hidden_out, part, moving1, sems1)
    multiply_back = group_product([dq, dk, dv], qkv_w, NT, half, group)
    line2 = Line(
        count, half, multiply_back, finish_second, input_grad, part, moving2, sems2, late=True, wide=wide_out
    )
    heads = AttendBack.__new__(AttendBack)
    heads.bq = query_block(rows)
    heads.blocks = rows // heads.bq
    heads.pairs = width // PAIR
    heads.steps = heads.pairs * heads.blocks
    heads.causal = True
    first = moving2.at[pl.ds(0, rows)]
    views = [Columns(first, j * width, width) for j in range(4)]
    tables = [earlier.at[0], earlier.at[1]]
    heads.ins = (facts, *views[:3], *tables, views[3], lse)
    heads.outs = (dq, dk, dv, dks, dvs)
    heads.scratch = (dk_acc, dv_acc, k_t)
    second = heads.steps + 2
    columns = (
        (0, grad_pre, 0, 0),
        (1, act, 1, 0),
        (2, attended, 2, 0),
        (3, dq, 3, 0),
        (3, dk, 3, width),
        (3, dv, 3, 2 * width),
    )
    spread = Spread(
        (mid, cotangent, branch, normed),
        columns,
        (up_grad, down_grad, out_grad, qkv_grad),
        down.at[pl.ds(0, rows)],
        rest,
        heads.steps - 2,
    )
    small = SmallSums(sizes, 6, second + pieces + SKEW * (count - 1), sums_out)
    small((None,), (sums_out,), (small_sent, small_got, *small_sems), (acc,))
    column_sums = lambda values: jnp.sum(values, axis=0, keepdims=True)
    features = down_in.shape[1]
    ff_rows = down_in.shape[0] // features
    loads = [
        pltpu.make_async_copy(source, target, load_sem.at[number])
        for number, (source, target) in enumerate(
            [(down_in, down), (qkv_in, qkv_w)]
            + [
                (source, first.at[:, pl.ds(j * width, width)])
                for j, source in enumerate((q_in, k_in, v_in, do_in))
            ]
        )
    ]
    swap = pltpu.make_async_remote_copy(
        src_ref=swap_out,
        dst_ref=swap_in,
        send_sem=swap_sent.at[0],
        recv_sem=swap_got.at[0],
        device_id=spread.to_y,
        device_id_type=MESH,
    )

    barrier = pltpu.get_barrier_semaphore()
    line1.greet(barrier)
    spread.greet(barrier)
    small.greet(barrier)
    for flow in range(2):
        act_copy(flow, 0).start()
    for load in loads:
        load.start()

    @pl.when(owner)
    def _():
        for ring in (residual_ring, grad_ring, hidden_ring):
            ring.fill()

    acc[...] = jnp.zeros_like(acc)
    small_sent[0] = jnp.zeros_like(small_sent[0])
    for number in range(3):
        small_sent[0, number : number + 1, :] = mid_sums[number : number + 1, :]
    small_sent[0, 5:6, :] = jnp.where(me == 0, column_sums(down_sums[...]), 0.0)
    for number in range(ff_rows):
        cols = slice(number * features, (number + 1) * features)
        small_sent[0, 6 + number : 7 + number, :] = column_sums(up_sums[:, cols])
    loads[0].wait()
    line1.first()
    line1.meet(barrier, spread.others + small.others)
    for load in loads[2:]:
        load.wait()

    def step(t, carry):
        line1.step(t)
        heads.step(t)

        @pl.when(t == heads.steps)
        def _():
            swap_out[0] = dks[...].astype(jnp.bfloat16)
            swap_out[1] = dvs[...].astype(jnp.bfloat16)
            swap.start()

        @pl.when(t == heads.steps + 1)
        def _():
            swap.wait()
            loads[1].wait()
            shape = (rows, SUMM_ROWS)
            chosen = lax.broadcasted_iota(jnp.int32, shape, 0) == (
                facts[1] - SUMM + lax.broadcasted_iota(jnp.int32, shape, 1)
            )
            chosen = jnp.where(chosen, 1.0, 0.0).astype(jnp.bfloat16)
            for number, grad in enumerate((dk, dv)):
                added = grad[...].astype(jnp.float32) + mm(chosen, swap_in[number])
                grad[...] = added.astype(jnp.bfloat16)
            for number, grad in enumerate((dq, dv)):
                small.extra(6 + ff_rows, number * width, grad)

        line2.step(t - second)
        spread.step(t)
        small.step(t)
        return carry

    lax.fori_loop(0, max(second + line2.steps, spread.steps, small.steps), step, 0)
    line1.settle()
    line2.settle()
    spread.settle()


def back_sums(number, count, sizes, whole_in, vmem_in):
    rows, width = whole_in[0].shape
    features = whole_in[5].shape[1]
    ff = whole_in[5].shape[0]
    half = rows // 2
    low = lambda *shape: pltpu.VMEM(shape, jnp.bfloat16)
    wide = lambda *shape: pltpu.VMEM(shape, jnp.float32)
    dma = lambda *shape: pltpu.SemaphoreType.DMA(shape)
    lines = Line.scratch(half, features)
    group = lines[0].shape[2]
    stages = sum(size.bit_length() - 1 for _, size in sizes)
    block = Spread.block
    sums_shape = (6 + ff // features + -(-2 * width // features), features)
    return pl.pallas_call(
        functools.partial(back_kernel, count, half, sizes),
        in_specs=[SMEM] + [VMEM] * 7 + [ANY] * len(whole_in),
        out_specs=[ANY] * 6 + [VMEM],
        out_shape=[
            jax.ShapeDtypeStruct((rows, features), jnp.bfloat16),
            jax.ShapeDtypeStruct((rows, features), jnp.float32),
            jax.ShapeDtypeStruct((block, ff), jnp.float32),
            jax.ShapeDtypeStruct((ff, block), jnp.float32),
            jax.ShapeDtypeStruct((width, block), jnp.float32),
            jax.ShapeDtypeStruct((block, 3 * width), jnp.float32),
            jax.ShapeDtypeStruct(sums_shape, jnp.float32),
        ],
        scratch_shapes=[
            lines[0],
            lines[1],
            lines[1],
            low(ff, features),
            low(features, 3 * width),
            low(rows, width),
            low(rows, width),
            low(rows, width),
            wide(rows, PAIR),
            wide(rows, PAIR),
            low(PAIR, rows),
            wide(SUMM_ROWS, width),
            wide(SUMM_ROWS, width),
            low(2, SUMM_ROWS, width),
            low(2, SUMM_ROWS, width),
            low(2, group, ff),
            wide(2, 8, features),
            wide(stages, *sums_shape),
            wide(stages, *sums_shape),
            wide(2, PIECE, features),
        ]
        + Ring.scratch(features, jnp.float32)
        + Ring.scratch(features, jnp.float32)
        + Ring.scratch(features, jnp.bfloat16)
        + lines[2:]
        + lines[2:]
        + [dma(stages), dma(stages), dma(6), dma(2), dma(1), dma(1)]
        + Spread.scratch(rows),
        compiler_params=pltpu.CompilerParams(
            collective_id=number, has_side_effects=True, vmem_limit_bytes=63 * MIB
        ),
        cost_estimate=pl.CostEstimate(
            flops=12 * rows * features * ff, bytes_accessed=60 * rows * features, transcendentals=0
        ),
        name="back_sums",
    )(*vmem_in, *whole_in)


def gradients_over(group, lefts, columns):
    over_rows = lambda left, right: mm(left, right, (((0,), (0,)), ((), ()))).astype(jnp.bfloat16)
    parts = [[] for _ in range(4)]
    for left, right, result, _ in columns:
        across = result in (0, 3)
        product = over_rows(lefts[left], right) if across else over_rows(right, lefts[left])
        parts[result].append(product)
    return [
        lax.psum_scatter(
            jnp.concatenate(part, axis=1),
            group,
            scatter_dimension=0 if result in (0, 3) else 1,
            tiled=True,
        ).astype(jnp.float32)
        for result, part in enumerate(parts)
    ]


def body(
    item_count,
    seq_count,
    mp_count,
    hidden_in,
    cotangent,
    seg_lengths,
    pre_gain,
    pre_shift,
    qkv_weight,
    qv_bias,
    out_weight,
    out_bias,
    mid_gain,
    mid_shift,
    up_weight,
    up_bias,
    down_weight,
    down_bias,
):
    group = ("item", "seq")
    width = qkv_weight.shape[2]
    gathered = lambda weight, axis: lax.all_gather(weight, group, axis=axis, tiled=True)
    hidden = hidden_in[0].astype(jnp.float32)
    lengths = seg_lengths[0]
    rows = hidden.shape[0]
    first_row = lax.axis_index("seq") * rows
    segment = first_row // SLOT
    facts = jnp.stack(
        [
            first_row % SLOT,
            lengths[segment] + SUMM,
            jnp.where(segment > 0, SUMM, 0),
        ]
    ).astype(jnp.int32)

    ours = (item_count, seq_count) == (4, 2) and rows == SLOT
    row = lambda vector: vector[None, :]
    shard = qkv_weight.reshape(-1, 3 * width)
    if ours:
        q, k, v, summary, normed, qkv_full, out_full = start(
            5, seg_lengths, hidden_in[0], row(pre_gain), row(pre_shift), qv_bias, shard, out_weight
        )
        attend_in = (seg_lengths, summary, q, k, v)
        tables = (k, v, summary[0], summary[1])
    else:
        qkv_full = gathered(shard, 0)
        out_full = gathered(out_weight, 1)
        normed = (norm_stats(hidden)[0] * pre_gain + pre_shift).astype(jnp.bfloat16)
        q = (mm(normed, qkv_full[:, :width]) + qv_bias[0]).astype(jnp.bfloat16)
        k = mm(normed, qkv_full[:, width : 2 * width]).astype(jnp.bfloat16)
        v = (mm(normed, qkv_full[:, 2 * width :]) + qv_bias[1]).astype(jnp.bfloat16)
        own, summary = keys_for(jnp.stack([k, v]), lengths, seq_count)
        tables = (own[0], own[1], summary[0], summary[1])
        attended, log_total = attend(facts, q, *tables)
        attend_in = (attended,)

    grad_down = cotangent[0]
    (
        mid_low,
        act_low,
        grad_pre,
        residual,
        grad_branch,
        grad_residual,
        down_full,
        mid_sums,
        up_sums,
        down_sums,
        grad_attended,
        *attend_out,
    ) = ffn_sums(
        1,
        mp_count,
        Gather if ours else Load,
        attend_in,
        out_full,
        (row(out_bias), row(mid_gain), row(mid_shift), row(up_bias)),
        hidden_in[0],
        grad_down,
        up_weight if ours else gathered(up_weight, 0),
        down_weight if ours else gathered(down_weight, 1),
    )
    if ours:
        attended, log_total = attend_out
    total = lambda value: jnp.sum(value.astype(jnp.float32), axis=0)
    features = hidden.shape[1]
    sizes = [("item", item_count), ("seq", seq_count), ("mp", mp_count)]
    once = lambda value: jnp.where(lax.axis_index("mp") == 0, value, 0.0)
    small_in = lambda qv_sums: jnp.concatenate(
        [
            jnp.sum(mid_sums, axis=1),
            jnp.zeros((2, features), jnp.float32),
            row(once(total(down_sums))),
            total(up_sums).reshape(-1, features),
            jnp.pad(qv_sums, (0, -qv_sums.shape[0] % features)).reshape(-1, features),
        ]
    )
    if ours:
        hidden_out, grad_input, up_grad, down_grad, out_grad, qkv_grad, sums = back_sums(
            2,
            mp_count,
            sizes,
            (q, k, v, grad_attended, act_low, down_full, residual, hidden_in[0], grad_residual)
            + (qkv_full, mid_low, grad_down, grad_branch, normed, grad_pre, attended),
            (seg_lengths, log_total, summary, row(down_bias), row(pre_gain))
            + (jnp.sum(mid_sums, axis=1), up_sums, down_sums),
        )
    else:
        hidden_out, dq, dk, dv, dks, dvs = line_sum(
            3,
            mp_count,
            [act_low],
            down_full,
            NN,
            [residual, row(down_bias)],
            0,
            0,
            finish_out,
            "down_sum",
            (AttendBack(facts, q, *tables, grad_attended, log_total),),
        )
        dk, dv = keys_back(jnp.stack([dk, dv]), jnp.stack([dks, dvs]), rows, lengths, seq_count)
        small = SmallSums(
            sizes,
            6,
            rows // 2 // PIECE + SKEW * (mp_count - 1),
            small_in(jnp.concatenate([total(dq), total(dv)])),
        )
        grad_input, _, sums = line_sum(
            4,
            mp_count,
            [dq, dk, dv],
            qkv_full,
            NT,
            [hidden_in[0], grad_residual, row(pre_gain)],
            0,
            2,
            finish_input,
            "input_sum",
            (small,),
        )
        lefts = (mid_low, grad_down, grad_branch, normed)
        columns = (
            (0, grad_pre, 0, 0),
            (1, act_low, 1, 0),
            (2, attended, 2, 0),
            (3, dq, 3, 0),
            (3, dk, 3, width),
            (3, dv, 3, 2 * width),
        )
        up_grad, down_grad, out_grad, qkv_grad = gradients_over(group, lefts, columns)
    ff_rows = up_weight.shape[1] // features
    up_bias_grad = sums[6 : 6 + ff_rows].reshape(-1)
    qv_bias_grad = sums[6 + ff_rows :].reshape(-1)[: 2 * width].reshape(2, width)
    return (
        hidden_out[None],
        grad_input.astype(jnp.float32)[None],
        sums[3],
        sums[4],
        qkv_grad.reshape(-1, 3, width),
        qv_bias_grad,
        out_grad,
        sums[2],
        sums[0],
        sums[1],
        up_grad,
        up_bias_grad,
        down_grad,
        sums[5],
    )


def solution(mesh):
    rows = P("item", "seq", None)
    qkv = P(("item", "seq"), None, "mp")
    first = P(("item", "seq"), "mp")
    second = P("mp", ("item", "seq"))
    bias = P(None, "mp")
    return jax.shard_map(
        functools.partial(body, mesh.shape["item"], mesh.shape["seq"], mesh.shape["mp"]),
        mesh=mesh,
        in_specs=(
            rows,
            rows,
            P("item", None),
            P(),
            P(),
            qkv,
            bias,
            second,
            P(),
            P(),
            P(),
            first,
            P("mp"),
            second,
            P(),
        ),
        out_specs=(
            rows,
            rows,
            P(),
            P(),
            qkv,
            bias,
            second,
            P(),
            P(),
            P(),
            first,
            P("mp"),
            second,
            P(),
        ),
        check_vma=False,
    )
```

```python
import functools
import math

import jax
import jax.numpy as jnp
from jax import lax
from jax.experimental import pallas as pl
from jax.experimental.pallas import tpu as pltpu
from jax.sharding import PartitionSpec as P

HDIM = 64
SLOT = 1280
SEGS = 2
SUMM = 50
SUMM_ROWS = 64
TOKENS = 2560
PAIR = 2 * HDIM
PIECE = 32
SKEW = 2
LEAD = 2
GATHER_STEPS = (7, 11, 13, 15)
MIB = 1 << 20
MESH = pl.DeviceIdType.MESH
MASKED = -1e30


eps = 1e-05

NN = (((1,), (0,)), ((), ()))
NT = (((1,), (1,)), ((), ()))


def mm(left, right, dims=NN):
    return lax.dot_general(left, right, dims, preferred_element_type=jnp.float32)


def norm_stats(values):
    center = jnp.mean(values, axis=-1, keepdims=True)
    centered = values - center
    inverse = lax.rsqrt(jnp.mean(centered * centered, axis=-1, keepdims=True) + eps)
    return centered * inverse, inverse


def norm_back(grad_out, normed, inverse, gain):
    scaled = grad_out * gain
    centered = scaled - jnp.mean(scaled, axis=-1, keepdims=True)
    return inverse * (centered - normed * jnp.mean(scaled * normed, axis=-1, keepdims=True))


def gelu_parts(values):
    c = math.sqrt(2 / math.pi)
    squared = values * values
    t = jnp.tanh(c * values * (1 + 0.044715 * squared))
    half = 0.5 * (1 + t)
    slope = half + 0.5 * values * (1 - t * t) * (c * (1 + 3 * 0.044715 * squared))
    return values * half, slope


def key_masks(facts_ref, block, rows, bq, nk):
    first = facts_ref[0] + block * bq
    limit = jnp.minimum(
        first + 1 + lax.broadcasted_iota(jnp.int32, (1, bq), 1), facts_ref[1]
    )
    own = lax.broadcasted_iota(jnp.int32, (nk, bq), 0) < limit
    earlier = lax.broadcasted_iota(jnp.int32, (SUMM_ROWS, bq), 0) < facts_ref[2]
    return own, earlier


class Facts:
    def __init__(self, lengths):
        segment = lax.axis_index("seq")
        self.values = (0, lengths[0, segment] + SUMM, jnp.where(segment > 0, SUMM, 0))

    def __getitem__(self, index):
        return self.values[index]


def head_lanes(head):
    lane = lax.broadcasted_iota(jnp.int32, (1, PAIR), 1)
    return (lane >= head * HDIM) & (lane < (head + 1) * HDIM)


def attend_kernel(bq, causal, facts_ref, q_ref, k_ref, v_ref, ks_ref, vs_ref, o_ref, lse_ref):
    rows, seg = q_ref.shape[0], k_ref.shape[0]
    v_t = v_ref[...].T
    vs_t = vs_ref[...].T
    ks = ks_ref[...]
    low_half = lax.broadcasted_iota(jnp.int32, (PAIR, 1), 0) < HDIM
    for block in range(rows // bq):
        nk = (block + 1) * bq if causal else seg
        own, earlier = key_masks(facts_ref, block, rows, bq, nk)
        q = q_ref[block * bq : (block + 1) * bq, :] * jnp.bfloat16(HDIM**-0.5)
        mixed = []
        for head in range(2):
            qh = jnp.where(head_lanes(head), q, jnp.zeros_like(q))
            s = jnp.where(own, mm(k_ref[:nk, :], qh, NT), MASKED)
            s2 = jnp.where(earlier, mm(ks, qh, NT), MASKED)
            top = jnp.maximum(jnp.max(s, axis=0, keepdims=True), jnp.max(s2, axis=0, keepdims=True))
            p = jnp.exp(s - top)
            p2 = jnp.exp(s2 - top)
            total = jnp.sum(p, axis=0, keepdims=True) + jnp.sum(p2, axis=0, keepdims=True)
            out = mm(v_t[:, :nk], p.astype(jnp.bfloat16)) + mm(vs_t, p2.astype(jnp.bfloat16))
            mixed.append(out / total)
            lse_ref[0, head : head + 1, block * bq : (block + 1) * bq] = top + jnp.log(total)
        joined = jnp.where(low_half, mixed[0], mixed[1])
        o_ref[block * bq : (block + 1) * bq, :] = joined.T.astype(jnp.bfloat16)


def query_block(rows):
    return 256 if rows % 256 == 0 else math.gcd(rows, 160)


def attend(facts, q, k, v, ks, vs):
    rows, width = q.shape
    seg = k.shape[0]
    pairs = width // PAIR
    column = lambda n: pl.BlockSpec((n, PAIR), lambda i: (0, i))
    return pl.pallas_call(
        functools.partial(attend_kernel, query_block(rows), rows == seg),
        grid=(pairs,),
        in_specs=[pl.BlockSpec(memory_space=pltpu.SMEM)]
        + [column(n) for n in (rows, seg, seg, SUMM_ROWS, SUMM_ROWS)],
        out_specs=[column(rows), pl.BlockSpec((1, 2, rows), lambda i: (i, 0, 0))],
        out_shape=[
            jax.ShapeDtypeStruct((rows, width), jnp.bfloat16),
            jax.ShapeDtypeStruct((pairs, 2, rows), jnp.float32),
        ],
        compiler_params=pltpu.CompilerParams(vmem_limit_bytes=48 * MIB),
        cost_estimate=pl.CostEstimate(
            flops=4 * rows * seg * width, bytes_accessed=8 * rows * width, transcendentals=0
        ),
        name="attend",
    )(facts, q, k, v, ks, vs)


def keys_for(local, lengths, seq_count):
    rows, width = local.shape[-2:]
    pad = ((0, 0), (0, SUMM_ROWS - SUMM), (0, 0))
    if rows == SLOT:
        here = lengths[lax.axis_index("seq")]
        summary = jnp.pad(lax.dynamic_slice(local, (0, here, 0), (2, SUMM, width)), pad)
        moves = [(i, i + 1) for i in range(seq_count - 1)]
        return local, lax.ppermute(summary, "seq", moves)
    everything = lax.all_gather(local, "seq", axis=1, tiled=True)
    segment = lax.axis_index("seq") * rows // SLOT
    own = lax.dynamic_slice(everything, (0, segment * SLOT, 0), (2, SLOT, width))
    summary = lax.dynamic_slice(everything, (0, lengths[0], 0), (2, SUMM, width))
    return own, jnp.pad(summary, pad)


def keys_back(own, summary, rows, lengths, seq_count):
    width = own.shape[-1]
    summary = summary[:, :SUMM]
    if rows == SLOT:
        moves = [(i + 1, i) for i in range(seq_count - 1)]
        arrived = lax.ppermute(summary, "seq", moves)
        here = lengths[lax.axis_index("seq")]
        old = lax.dynamic_slice(own, (0, here, 0), (2, SUMM, width))
        new = (old.astype(jnp.float32) + arrived).astype(jnp.bfloat16)
        return lax.dynamic_update_slice(own, new, (0, here, 0))
    segment = lax.axis_index("seq") * rows // SLOT
    everything = jnp.zeros((2, TOKENS, width), jnp.float32)
    everything = lax.dynamic_update_slice(
        everything, own.astype(jnp.float32), (0, segment * SLOT, 0)
    )
    old = lax.dynamic_slice(everything, (0, lengths[0], 0), (2, SUMM, width))
    added = jnp.where(segment > 0, summary, 0.0)
    everything = lax.dynamic_update_slice(everything, old + added, (0, lengths[0], 0))
    return lax.psum_scatter(
        everything.astype(jnp.bfloat16), "seq", scatter_dimension=1, tiled=True
    )


class Line:
    def __init__(self, count, half, multiply, finish, out, part, moving, sems, late=False):
        self.count, self.half, self.multiply, self.finish = count, half, multiply, finish
        self.late = late
        self.out, self.part, self.moving = out, part, moving
        self.up_sent, self.up_got, self.down_sent, self.down_got, self.local = sems
        self.me = lax.axis_index("mp")
        self.pieces = half // PIECE
        self.per_group = part.shape[2] // PIECE
        self.steps = self.pieces + 2 * SKEW * (count - 1)

    @staticmethod
    def scratch(half, features):
        pieces = half // PIECE
        group = 160 if half % 160 == 0 else PIECE
        dma = lambda *shape: pltpu.SemaphoreType.DMA(shape)
        return [
            pltpu.VMEM((2, 2, group, features), jnp.float32),
            pltpu.VMEM((2 * (half + LEAD * PIECE), features), jnp.bfloat16),
            dma(2, pieces),
            dma(2, pieces),
            dma(2, pieces),
            dma(2, pieces),
            dma(2, pieces),
        ]

    def place(self, flow):
        return self.count - 1 - self.me if flow == 0 else self.me

    def greet(self, barrier):
        me = self.me

        @pl.when(me > 0)
        def _():
            pl.semaphore_signal(barrier, inc=1, device_id={"mp": me - 1}, device_id_type=MESH)

        @pl.when(me < self.count - 1)
        def _():
            pl.semaphore_signal(barrier, inc=1, device_id={"mp": me + 1}, device_id_type=MESH)

    def meet(self, barrier, others=0):
        ends = (self.me == 0) | (self.me == self.count - 1)

        @pl.when(ends)
        def _():
            pl.semaphore_wait(barrier, 1 + others)

        @pl.when(jnp.logical_not(ends))
        def _():
            pl.semaphore_wait(barrier, 2 + others)

    def first(self):
        for flow in range(2):
            self.part[flow, 0] = self.multiply(flow, 0)

    def spot(self, flow, k):
        return flow * (self.half + LEAD * PIECE) + k * PIECE

    def spots(self, flow, k, size=PIECE):
        return pl.ds(pl.multiple_of(self.spot(flow, k), PIECE), size)

    def finished(self, flow, k, size):
        mine = self.place(flow) == self.count - 1
        return self.spots(flow, jnp.where(mine, k + LEAD, k), size)

    def onward(self, flow, k):
        here = self.moving.at[self.spots(flow, k + LEAD)]
        return pltpu.make_async_remote_copy(
            src_ref=here,
            dst_ref=here,
            send_sem=self.up_sent.at[flow, k],
            recv_sem=self.up_got.at[flow, k],
            device_id={"mp": self.me - 1 if flow == 0 else self.me + 1},
            device_id_type=MESH,
        )

    def back(self, flow, k, owner):
        here = self.moving.at[self.spots(flow, k)]
        return pltpu.make_async_remote_copy(
            src_ref=self.moving.at[self.spots(flow, k + LEAD)] if owner else here,
            dst_ref=here,
            send_sem=self.down_sent.at[flow, k],
            recv_sem=self.down_got.at[flow, k],
            device_id={"mp": self.me + 1 if flow == 0 else self.me - 1},
            device_id_type=MESH,
        )

    def keep(self, flow, k, owner):
        return pltpu.make_async_copy(
            self.moving.at[self.spots(flow, k + LEAD if owner else k)],
            self.out.at[pl.ds(flow * self.half + k * PIECE, PIECE)],
            self.local.at[flow, k],
        )

    def send_on(self, flow, k):
        @pl.when(k >= LEAD)
        def _():
            self.onward(flow, k - LEAD).wait_send()

        self.onward(flow, k).start()

    def step(self, t):
        last = self.count - 1
        for flow in range(2):
            place = self.place(flow)
            k = t - SKEW * place
            here = self.spots(flow, k + LEAD)
            busy = (k >= 0) & (k < self.pieces)

            def mine():
                slot = (k // self.per_group) % 2
                inner = pl.ds(pl.multiple_of((k % self.per_group) * PIECE, PIECE), PIECE)
                return self.part[flow, slot, inner, :]

            @pl.when(busy & (place == 0))
            def _():
                self.moving[here, :] = mine().astype(jnp.bfloat16)
                self.send_on(flow, k)

            @pl.when(busy & (place > 0) & (place < last))
            def _():
                self.onward(flow, k).wait_recv()
                total = mine() + self.moving[here, :].astype(jnp.float32)
                self.moving[here, :] = total.astype(jnp.bfloat16)
                self.send_on(flow, k)

            @pl.when(busy & (place == last))
            def _():
                self.onward(flow, k).wait_recv()
                total = mine() + self.moving[here, :].astype(jnp.float32)
                self.moving[here, :] = self.finish(flow, k, total).astype(jnp.bfloat16)
                self.back(flow, k, True).start()
                self.keep(flow, k, True).start()

        for flow in range(2):
            place = self.place(flow)
            j = t - SKEW * (2 * last - place)

            @pl.when((j >= 0) & (j < self.pieces) & (place < last))
            def _():
                self.back(flow, j, False).wait_recv()

                @pl.when(place > 0)
                def _():
                    self.back(flow, j, False).start()

                self.keep(flow, j, False).start()

        for flow in range(2 if self.multiply else 0):
            k = t - SKEW * self.place(flow)
            g = k // self.per_group + 1

            if self.late:

                @pl.when(k == -1)
                def _():
                    self.part[flow, 0] = self.multiply(flow, 0)

            @pl.when((k >= 0) & (k % self.per_group == 0) & (g < self.pieces // self.per_group))
            def _():
                self.part[flow, g % 2] = self.multiply(flow, g)

    def settle(self):
        last = self.count - 1

        def one(k, carry):
            for flow in range(2):
                place = self.place(flow)

                @pl.when((place < last) & (k >= self.pieces - LEAD))
                def _():
                    self.onward(flow, k).wait_send()

                @pl.when((place > 0) & (place < last))
                def _():
                    self.back(flow, k, False).wait_send()

                @pl.when(place < last)
                def _():
                    self.keep(flow, k, False).wait()

                @pl.when(place == last)
                def _():
                    self.back(flow, k, True).wait_send()
                    self.keep(flow, k, True).wait()

            return carry

        lax.fori_loop(0, self.pieces, one, 0)


def group_product(lefts, right, dims, half, group):
    def multiply(flow, g):
        rows = pl.ds(pl.multiple_of(flow * half + g * group, 16), group)
        at, total = 0, None
        for left in lefts:
            depth = left.shape[1]
            cut = right[:, at : at + depth] if dims == NT else right[at : at + depth, :]
            product = mm(left[rows, :], cut, dims)
            total = product if total is None else total + product
            at += depth
        return total

    return multiply


def line_kernel(count, half, dims, n_left, n_extra, n_owned, n_acc, finish, sides, *refs):
    refs = list(refs)
    take = lambda n: [refs.pop(0) for _ in range(n)]
    lefts, (right,), extras = take(n_left), take(1), take(n_extra)
    side_in = [take(side.n_in) for side in sides]
    (out,), owned, accs = take(1), take(n_owned), take(1 if n_acc else 0)
    side_out = [take(side.n_out) for side in sides]
    part, moving, sems = *take(2), take(5)
    multiply = group_product(lefts, right, dims, half, part.shape[2])
    ending = lambda flow, k, total: finish(flow, k, total, extras, owned, accs)
    line = Line(count, half, multiply, ending, out, part, moving, sems)
    jobs = [
        side(ins, outs, take(len(side.scratch_shapes)), accs)
        for side, ins, outs in zip(sides, side_in, side_out)
    ]
    barrier = pltpu.get_barrier_semaphore()
    line.greet(barrier)
    for job in jobs:
        job.greet(barrier)
    if n_acc:
        accs[0][...] = jnp.zeros_like(accs[0])
    for job in jobs:
        job.first()
    line.first()
    line.meet(barrier, sum(job.others for job in jobs))

    def step(t, carry):
        line.step(t)
        for job in jobs:
            job.step(t)
        return carry

    lax.fori_loop(0, max([line.steps] + [job.steps for job in jobs]), step, 0)
    line.settle()
    for job in jobs:
        job.settle()


class Nothing:
    n_in = n_out = others = steps = 0
    operands, in_specs, out_shape, out_specs, scratch_shapes = (), (), (), (), ()

    def __call__(self, ins, outs, scratch, accs):
        return self

    def greet(self, barrier):
        pass

    def first(self):
        pass

    def step(self, t):
        pass

    def settle(self):
        pass


VMEM = pl.BlockSpec(memory_space=pltpu.VMEM)
ANY = pl.BlockSpec(memory_space=pl.ANY)
SMEM = pl.BlockSpec(memory_space=pltpu.SMEM)


def line_sum(number, count, lefts, right, dims, extras, n_owned, n_acc, finish, name, sides):
    rows = lefts[0].shape[0]
    features = right.shape[1 if dims == NN else 0]
    half = rows // 2
    acc = [jax.ShapeDtypeStruct((n_acc, 8, features), jnp.float32)] if n_acc else []
    return pl.pallas_call(
        functools.partial(
            line_kernel,
            count,
            half,
            dims,
            len(lefts),
            len(extras),
            n_owned,
            n_acc,
            finish,
            sides,
        ),
        in_specs=[VMEM] * (len(lefts) + 1 + len(extras)) + [s for side in sides for s in side.in_specs],
        out_specs=[ANY] + [VMEM] * (n_owned + len(acc)) + [s for side in sides for s in side.out_specs],
        out_shape=[jax.ShapeDtypeStruct((rows, features), jnp.bfloat16)]
        + [jax.ShapeDtypeStruct((half, features), jnp.float32)] * n_owned
        + acc
        + [s for side in sides for s in side.out_shape],
        scratch_shapes=Line.scratch(half, features) + [s for side in sides for s in side.scratch_shapes],
        compiler_params=pltpu.CompilerParams(
            collective_id=number, has_side_effects=True, vmem_limit_bytes=62 * MIB
        ),
        cost_estimate=pl.CostEstimate(
            flops=2 * rows * features * sum(left.shape[1] for left in lefts),
            bytes_accessed=4 * rows * features,
            transcendentals=0,
        ),
        name=name,
    )(*lefts, right, *extras, *[value for side in sides for value in side.operands])


def piece_rows(flow, k, half):
    return pl.ds(pl.multiple_of(flow * half + k * PIECE, PIECE), PIECE)


def fold(values):
    return jnp.sum(values.reshape(-1, 8, values.shape[-1]), axis=0)


def finish_input(flow, k, total, extras, owned, accs):
    hidden, grad, gain = extras
    (acc,) = accs
    half = grad.shape[0]
    normed, inverse = norm_stats(hidden[piece_rows(flow, k, half), :].astype(jnp.float32))
    acc[0] += fold(total * normed)
    acc[1] += fold(total)
    return grad[piece_rows(0, k, half), :] + norm_back(total, normed, inverse, gain[...])


def finish_out(flow, k, total, extras, owned, accs):
    residual, bias = extras
    half = residual.shape[0]
    return residual[piece_rows(0, k, half), :] + total + bias[...]


class AttendBack(Nothing):
    n_in, n_out = 8, 5

    def __init__(self, facts, q, k, v, ks, vs, do, lse):
        rows, width = q.shape
        seg = k.shape[0]
        self.operands = (facts, q, k, v, ks, vs, do, lse)
        self.in_specs = (SMEM,) + (VMEM,) * 7
        low = lambda n: jax.ShapeDtypeStruct((n, width), jnp.bfloat16)
        wide = lambda n: jax.ShapeDtypeStruct((n, width), jnp.float32)
        self.out_shape = (low(rows), low(seg), low(seg), wide(SUMM_ROWS), wide(SUMM_ROWS))
        self.out_specs = (VMEM,) * 5
        self.scratch_shapes = (
            pltpu.VMEM((seg, PAIR), jnp.float32),
            pltpu.VMEM((seg, PAIR), jnp.float32),
            pltpu.VMEM((PAIR, seg), jnp.bfloat16),
        )
        self.bq = query_block(rows)
        self.blocks = rows // self.bq
        self.pairs = width // PAIR
        self.steps = self.pairs * self.blocks
        self.causal = rows == seg

    def __call__(self, ins, outs, scratch, accs):
        self.ins, self.outs, self.scratch = ins, outs, scratch
        return self

    def step(self, t):
        pair = t // self.blocks
        for block in range(self.blocks):

            @pl.when((t >= 0) & (t < self.steps) & (t % self.blocks == block))
            def _():
                self.unit(pair, block)

    def unit(self, pair, block):
        facts, q_ref, k_ref, v_ref, ks_ref, vs_ref, do_ref, lse_ref = self.ins
        dq_ref, dk_ref, dv_ref, dks_ref, dvs_ref = self.outs
        dk_acc, dv_acc, k_t = self.scratch
        seg, bq = k_ref.shape[0], self.bq
        cols = pl.ds(pl.multiple_of(pair * PAIR, PAIR), PAIR)
        scale = jnp.bfloat16(HDIM**-0.5)
        low_half = lax.broadcasted_iota(jnp.int32, (PAIR, 1), 0) < HDIM
        if block == 0:
            k_t[...] = (k_ref[:, cols] * scale).T
            dk_acc[...] = jnp.zeros_like(dk_acc)
            dv_acc[...] = jnp.zeros_like(dv_acc)
            dks_ref[:, cols] = jnp.zeros((SUMM_ROWS, PAIR), jnp.float32)
            dvs_ref[:, cols] = jnp.zeros((SUMM_ROWS, PAIR), jnp.float32)
        ks, vs = ks_ref[:, cols], vs_ref[:, cols]
        ks_t = (ks * scale).T
        nk = (block + 1) * bq if self.causal else seg
        here = slice(block * bq, (block + 1) * bq)
        own, earlier = key_masks(facts, block, self.blocks * bq, bq, nk)
        q = q_ref[here, cols] * scale
        do = do_ref[here, cols]
        k, v = k_ref[:nk, cols], v_ref[:nk, cols]
        grads = []
        for head in range(2):
            qh = jnp.where(head_lanes(head), q, jnp.zeros_like(q))
            doh = jnp.where(head_lanes(head), do, jnp.zeros_like(do))
            lse = lse_ref[pair, head : head + 1, here]
            p = jnp.exp(jnp.where(own, mm(k, qh, NT), MASKED) - lse)
            p2 = jnp.exp(jnp.where(earlier, mm(ks, qh, NT), MASKED) - lse)
            dp = mm(v, doh, NT)
            dp2 = mm(vs, doh, NT)
            delta = jnp.sum(p * dp, axis=0, keepdims=True) + jnp.sum(p2 * dp2, axis=0, keepdims=True)
            ds = (p * (dp - delta)).astype(jnp.bfloat16)
            ds2 = (p2 * (dp2 - delta)).astype(jnp.bfloat16)
            dv_acc[:nk, :] += mm(p.astype(jnp.bfloat16), doh)
            dk_acc[:nk, :] += mm(ds, qh)
            dvs_ref[:, cols] += mm(p2.astype(jnp.bfloat16), doh)
            dks_ref[:, cols] += mm(ds2, qh)
            grads.append(mm(k_t[:, :nk], ds) + mm(ks_t, ds2))
        joined = jnp.where(low_half, grads[0], grads[1])
        dq_ref[here, cols] = joined.T.astype(jnp.bfloat16)
        if block == self.blocks - 1:
            dk_ref[:, cols] = dk_acc[...].astype(jnp.bfloat16)
            dv_ref[:, cols] = dv_acc[...].astype(jnp.bfloat16)


class Spread:
    others = 3
    block = 256
    lag = (2, 5, 8)
    across = (True, False, False, True)

    def __init__(self, lefts, columns, outs, left_now, scratch, start):
        self.lefts, self.outs, self.x_buf, self.start = lefts, outs, left_now, start
        self.table, self.phases, self.rights = [], {}, []
        at = 0
        for number, (left, right, result, place) in enumerate(columns):
            self.phases.setdefault(left, at)
            self.table.append((number, at, at + right.shape[1] // self.block, result, place))
            self.rights.append(right)
            at += right.shape[1] // self.block
        self.chunks = at
        self.steps = start + at + self.lag[2]
        (
            self.y_buf,
            self.s1,
            self.own,
            self.r1,
            self.s2x,
            self.s2y,
            self.top,
            self.low,
            self.r2x,
            self.r2y,
            self.s3,
            self.kept,
            self.r3,
            self.tile,
            self.x_sem,
            self.y_sem,
            self.s1_sem,
            self.r1_sem,
            self.s2x_sem,
            self.r2x_sem,
            self.s2y_sem,
            self.r2y_sem,
            self.s3y_sem,
            self.r3y_sem,
            self.s3x_sem,
            self.r3x_sem,
            self.out_sem,
        ) = scratch
        item, seq = lax.axis_index("item"), lax.axis_index("seq")
        self.core, self.x, self.y = item % 2, item // 2, seq
        self.to_core = {"item": item + 1 - 2 * self.core}
        self.to_x = {"item": item + 2 - 4 * self.x}
        self.to_y = {"seq": 1 - seq}

    @classmethod
    def scratch(cls, rows):
        block, half = cls.block, cls.block // 2
        low = lambda *shape: pltpu.VMEM(shape, jnp.bfloat16)
        wide = lambda *shape: pltpu.VMEM(shape, jnp.float32)
        return [
            low(2, rows, block),
            low(3, 2, block, 2 * block),
            wide(3, 2, block, 2 * block),
            low(4, 2, block, 2 * block),
            low(3, half, 2 * block),
            low(3, 2, half, block),
            wide(3, half, 2 * block),
            wide(3, 2, half, block),
            low(6, half, 2 * block),
            low(6, 2, half, block),
            low(3, 2, half, block),
            wide(3, 2, half, block),
            low(6, 2, half, block),
            wide(3, block, block),
        ] + [pltpu.SemaphoreType.DMA((n,)) for n in (1, 2, 3, 4, 3, 6, 3, 6, 3, 6, 3, 6, 3)]

    def greet(self, barrier):
        for to in (self.to_core, self.to_x, self.to_y):
            pl.semaphore_signal(barrier, inc=1, device_id=to, device_id_type=MESH)


    def left_copy(self, left):
        return pltpu.make_async_copy(self.lefts[left], self.x_buf, self.x_sem.at[0])

    def right_copy(self, m, act):
        for number, start, stop, _, _ in self.table:

            @pl.when((m >= start) & (m < stop))
            def _():
                cols = pl.ds(pl.multiple_of((m - start) * self.block, self.block), self.block)
                act(
                    pltpu.make_async_copy(
                        self.rights[number].at[:, cols], self.y_buf.at[m % 2], self.y_sem.at[m % 2]
                    )
                )

    def out_copy(self, m, act):
        for _, start, stop, result, place in self.table:

            @pl.when((m >= start) & (m < stop))
            def _():
                cols = pl.ds(
                    pl.multiple_of(place + (m - start) * self.block, self.block), self.block
                )
                out = self.outs[result]
                out = out.at[:, cols] if self.across[result] else out.at[cols, :]
                act(pltpu.make_async_copy(self.tile.at[m % 3], out, self.out_sem.at[m % 3]))

    def remote(self, src, dst, send, recv, to):
        return pltpu.make_async_remote_copy(
            src_ref=src, dst_ref=dst, send_sem=send, recv_sem=recv, device_id=to, device_id_type=MESH
        )

    def first_copy(self, m):
        return self.remote(
            self.s1.at[m % 3],
            self.r1.at[m % 4],
            self.s1_sem.at[m % 3],
            self.r1_sem.at[m % 4],
            self.to_core,
        )

    def second_copies(self, m):
        return (
            self.remote(
                self.s2x.at[m % 3],
                self.r2x.at[m % 6],
                self.s2x_sem.at[m % 3],
                self.r2x_sem.at[m % 6],
                self.to_x,
            ),
            self.remote(
                self.s2y.at[m % 3],
                self.r2y.at[m % 6],
                self.s2y_sem.at[m % 3],
                self.r2y_sem.at[m % 6],
                self.to_y,
            ),
        )

    def third_copies(self, m):
        return (
            self.remote(
                self.s3.at[m % 3, 0],
                self.r3.at[m % 6, 0],
                self.s3y_sem.at[m % 3],
                self.r3y_sem.at[m % 6],
                self.to_y,
            ),
            self.remote(
                self.s3.at[m % 3, 1],
                self.r3.at[m % 6, 1],
                self.s3x_sem.at[m % 3],
                self.r3x_sem.at[m % 6],
                self.to_x,
            ),
        )

    def step(self, t):
        @pl.when(t == self.start - 1)
        def _():
            self.left_copy(0).start()
            self.right_copy(0, lambda copy: copy.start())

        for stage, lag in ((self.fourth, 8), (self.third, 5), (self.second, 2), (self.multiply, 0)):
            m = t - self.start - lag

            @pl.when((m >= 0) & (m < self.chunks))
            def _():
                stage(m)

    def multiply(self, m):
        for left, start in self.phases.items():

            @pl.when(m == start)
            def _():
                if start > 0:
                    self.left_copy(left).start()
                self.left_copy(left).wait()

        @pl.when(m + 1 < self.chunks)
        def _():
            self.right_copy(m + 1, lambda copy: copy.start())

        self.right_copy(m, lambda copy: copy.wait())

        @pl.when(m >= 3)
        def _():
            self.first_copy(m - 3).wait_send()

        turned = self.y_buf[m % 2].T
        wide = 2 * self.block

        def product(x, core):
            cols = pl.ds(pl.multiple_of(x * 2 * wide + core * wide, wide), wide)
            return mm(turned, self.x_buf[:, cols])

        for x in range(2):
            self.s1[m % 3, x] = product(x, 1 - self.core).astype(jnp.bfloat16)
        self.first_copy(m).start()
        for x in range(2):
            self.own[m % 3, x] = product(x, self.core)

    def second(self, m):
        half = self.block // 2

        @pl.when(m >= 3)
        def _():
            for copy in self.second_copies(m - 3):
                copy.wait_send()

        self.first_copy(m).wait_recv()
        slot = m % 3
        here, there = self.x, 1 - self.x
        mine = pl.ds(pl.multiple_of(self.y * self.block, self.block), self.block)
        others = pl.ds(pl.multiple_of((1 - self.y) * self.block, self.block), self.block)
        added = lambda x, rows, cols: (
            self.own[slot, x, rows, cols] + self.r1[m % 4, x, rows, cols].astype(jnp.float32)
        )
        upper, lower, every = pl.ds(0, half), pl.ds(half, half), pl.ds(0, 2 * self.block)
        self.s2x[slot] = added(there, upper, every).astype(jnp.bfloat16)
        for x in range(2):
            self.s2y[slot, x] = added(x, lower, others).astype(jnp.bfloat16)
        for copy in self.second_copies(m):
            copy.start()
        self.top[slot] = added(here, upper, every)
        for x in range(2):
            self.low[slot, x] = added(x, lower, mine)

    def third(self, m):
        @pl.when(m >= 3)
        def _():
            for copy in self.third_copies(m - 3):
                copy.wait_send()

        for copy in self.second_copies(m):
            copy.wait_recv()
        slot, got = m % 3, m % 6
        mine = pl.ds(pl.multiple_of(self.y * self.block, self.block), self.block)
        others = pl.ds(pl.multiple_of((1 - self.y) * self.block, self.block), self.block)
        top = lambda cols: self.top[slot, :, cols] + self.r2x[got, :, cols].astype(jnp.float32)
        low = lambda x: self.low[slot, x] + self.r2y[got, x].astype(jnp.float32)
        self.s3[slot, 0] = top(others).astype(jnp.bfloat16)
        self.s3[slot, 1] = low(1 - self.x).astype(jnp.bfloat16)
        for copy in self.third_copies(m):
            copy.start()
        self.kept[slot, 0] = top(mine)
        self.kept[slot, 1] = low(self.x)

    def fourth(self, m):
        @pl.when(m >= 3)
        def _():
            self.out_copy(m - 3, lambda copy: copy.wait())

        for copy in self.third_copies(m):
            copy.wait_recv()
        slot, half = m % 3, self.block // 2
        total = self.kept[slot] + self.r3[m % 6].astype(jnp.float32)
        total = total.reshape(self.block, self.block)
        across = jnp.zeros((), jnp.bool_)
        for _, start, stop, result, _ in self.table:
            if self.across[result]:
                across = across | ((m >= start) & (m < stop))

        @pl.when(across)
        def _():
            self.tile[slot] = total.T

        @pl.when(jnp.logical_not(across))
        def _():
            self.tile[slot] = total

        self.out_copy(m, lambda copy: copy.start())

    def settle(self):
        for m in range(self.chunks - 3, self.chunks):
            self.first_copy(m).wait_send()
            for copy in self.second_copies(m) + self.third_copies(m):
                copy.wait_send()
            self.out_copy(jnp.int32(m), lambda copy: copy.wait())


class Gather:
    others = 3

    def __init__(self, shards, fulls, sems, ready):
        self.shards, self.fulls, self.ready = shards, fulls, ready
        self.sent, self.got, self.local = sems
        item, seq = lax.axis_index("item"), lax.axis_index("seq")
        self.core, self.x, self.y = item % 2, item // 2, seq
        self.to_core = {"item": item + 1 - 2 * self.core}
        self.to_x = {"item": item + 2 - 4 * self.x}
        self.to_y = {"seq": 1 - seq}

    @staticmethod
    def sems(count=2):
        dma = lambda *shape: pltpu.SemaphoreType.DMA(shape)
        return [dma(count, 9), dma(count, 9), dma(count)]

    def greet(self, barrier):
        for to in (self.to_core, self.to_x, self.to_y):
            pl.semaphore_signal(barrier, inc=1, device_id=to, device_id_type=MESH)

    def spot(self, w, x, core, y, part=None):
        size = self.shards[w].shape[w]
        at = pl.ds(pl.multiple_of(((2 * x + core) * 2 + y) * size, size), size)
        if w == 0:
            if part is not None:
                half = size // 2
                start = ((2 * x + core) * 2 + y) * size + part * half
                at = pl.ds(pl.multiple_of(start, half), half)
            return self.fulls[0].at[at, :]
        rows = self.fulls[1].shape[0]
        if part is not None:
            return self.fulls[1].at[pl.ds(part * (rows // 2), rows // 2), at]
        return self.fulls[1].at[:, at]

    def message(self, w, number, src, dst, to):
        return pltpu.make_async_remote_copy(
            src_ref=src,
            dst_ref=dst,
            send_sem=self.sent.at[w, number],
            recv_sem=self.got.at[w, number],
            device_id=to,
            device_id_type=MESH,
        )

    def plan(self, w):
        c, x, y = self.core, self.x, self.y
        own, spot = self.shards[w].at[...], functools.partial(self.spot, w)
        return (
            (own, spot(x, c, y), spot(x, 1 - c, y), self.to_core),
            (own, spot(x, c, y), spot(1 - x, c, y), self.to_x),
            (own, spot(x, c, y), spot(x, c, 1 - y), self.to_y),
            (None, spot(1 - x, c, y, 0), spot(1 - x, c, 1 - y, 0), self.to_y),
            (None, spot(x, c, 1 - y, 1), spot(1 - x, c, 1 - y, 1), self.to_x),
            (None, spot(1 - x, c, y), spot(1 - x, 1 - c, y), self.to_core),
            (None, spot(x, c, 1 - y), spot(x, 1 - c, 1 - y), self.to_core),
            (None, spot(1 - x, c, 1 - y, 0), spot(1 - x, 1 - c, 1 - y, 0), self.to_core),
            (None, spot(1 - x, c, 1 - y, 1), spot(1 - x, 1 - c, 1 - y, 1), self.to_core),
        )
    def send(self, w, numbers):
        plan = self.plan(w)
        for number in numbers:
            src, out, _, to = plan[number]
            self.message(w, number, out if src is None else src, out, to).start()

    def receive(self, w, numbers):
        plan = self.plan(w)
        for number in numbers:
            _, _, landing, to = plan[number]
            self.message(w, number, landing, landing, to).wait_recv()

    def mine(self, w):
        return pltpu.make_async_copy(
            self.shards[w], self.spot(w, self.x, self.core, self.y), self.local.at[w]
        )

    def first(self):
        for w in range(len(self.shards)):
            self.mine(w).start()

    def begin(self):
        for w in range(2):
            self.send(w, (1, 2, 0))

    def step(self, t):
        for w, at in ((0, GATHER_STEPS[0]), (1, GATHER_STEPS[1])):

            @pl.when(t == at)
            def _():
                self.receive(w, (1, 2))
                self.send(w, (3, 4, 5, 6))

        for w, at in ((0, GATHER_STEPS[2]), (1, GATHER_STEPS[3])):

            @pl.when(t == at)
            def _():
                self.receive(w, (3, 4))
                self.send(w, (7, 8))

        @pl.when(t == self.ready)
        def _():
            for w in range(2):
                self.receive(w, (0, 5, 6, 7, 8))
                self.mine(w).wait()

    def settle(self):
        for w in range(len(self.shards)):
            for number, (src, out, _, to) in enumerate(self.plan(w)):
                self.message(w, number, out if src is None else src, out, to).wait_send()


class Load:
    others = 0

    def __init__(self, shards, fulls, sems, ready):
        self.ready = ready
        self.copies = [
            pltpu.make_async_copy(shard, full, sems[2].at[w])
            for w, (shard, full) in enumerate(zip(shards, fulls))
        ]

    sems = Gather.sems

    def greet(self, barrier):
        pass

    def first(self):
        for copy in self.copies:
            copy.start()

    def begin(self):
        pass

    def step(self, t):
        @pl.when(t == self.ready)
        def _():
            for copy in self.copies:
                copy.wait()

    def settle(self):
        pass


class Attend:
    bq = 128

    def __init__(self, half, facts, q, k, v, earlier, attended, lse):
        self.half, self.facts, self.q, self.k, self.v = half, facts, q, k, v
        self.earlier, self.attended, self.lse = earlier, attended, lse
        self.pairs = q.shape[1] // PAIR
        self.blocks = half // self.bq

    def first(self):
        def one(pair, carry):
            for flow in range(2):
                self.unit(pair, flow * self.blocks)
            return carry

        lax.fori_loop(0, self.pairs, one, 0)

    def step(self, t):
        def both(pair, block):
            for flow in range(2):
                self.unit(pair, flow * self.blocks + block)

        @pl.when((t >= 0) & (t < 2))
        def _():
            each = self.pairs // 2

            def one(i, carry):
                both((t % 2) * each + i, 1)
                return carry

            lax.fori_loop(0, each, one, 0)

        for block in range(2, self.blocks):
            start = self.pairs * (block - 2) + 2

            @pl.when((t >= start) & (t < start + self.pairs))
            def _():
                both(t - start, block)

    def unit(self, pair, block):
        bq, nk = self.bq, (block + 1) * self.bq
        cols = pl.ds(pl.multiple_of(pair * PAIR, PAIR), PAIR)
        here = slice(block * bq, nk)
        query = block * bq + lax.broadcasted_iota(jnp.int32, (1, 2 * bq), 1) % bq
        limit = jnp.minimum(query + 1, self.facts[1])
        own = lax.broadcasted_iota(jnp.int32, (nk, 2 * bq), 0) < limit
        earlier = lax.broadcasted_iota(jnp.int32, (SUMM_ROWS, 2 * bq), 0) < self.facts[2]
        q = self.q[here, cols] * jnp.bfloat16(HDIM**-0.5)
        q = jnp.concatenate([jnp.where(head_lanes(h), q, jnp.zeros_like(q)) for h in range(2)])
        s = jnp.where(own, mm(self.k[:nk, cols], q, NT), MASKED)
        s2 = jnp.where(earlier, mm(self.earlier[0, :, cols], q, NT), MASKED)
        top = jnp.maximum(jnp.max(s, axis=0, keepdims=True), jnp.max(s2, axis=0, keepdims=True))
        p = jnp.exp(s - top)
        p2 = jnp.exp(s2 - top)
        total = jnp.sum(p, axis=0, keepdims=True) + jnp.sum(p2, axis=0, keepdims=True)
        out = mm(self.v[:nk, cols].T, p.astype(jnp.bfloat16))
        out = (out + mm(self.earlier[1, :, cols].T, p2.astype(jnp.bfloat16))) / total
        lse = top + jnp.log(total)
        for head in range(2):
            self.lse[pair, head : head + 1, here] = lse[:, head * bq : (head + 1) * bq]
        low_half = lax.broadcasted_iota(jnp.int32, (PAIR, 1), 0) < HDIM
        joined = jnp.where(low_half, out[:, :bq], out[:, bq:])
        self.attended[here, cols] = joined.T.astype(jnp.bfloat16)


def ffn_kernel(count, half, weights_job, n_attend, *refs):
    if n_attend == 1:
        ffn_body(count, half, weights_job, None, *refs)
    else:
        lengths, earlier, *rest = refs
        sources, rest = rest[:3], rest[3:]
        inputs, outputs, scratch = rest[:9], rest[9:22], rest[22:]
        *outputs, attended, lse = outputs
        *scratch, q, k, v, sems = scratch
        job = Attend(half, Facts(lengths), q, k, v, earlier, attended, lse)
        job.loads = [
            pltpu.make_async_copy(source, target, sems.at[number])
            for number, (source, target) in enumerate(zip(sources, (q, k, v)))
        ]
        for load in job.loads:
            load.start()
        ffn_body(count, half, weights_job, job, attended, *inputs, *outputs, *scratch)


def ffn_body(
    count,
    half,
    weights_job,
    attention,
    attended,
    out_w,
    out_bias,
    mid_gain,
    mid_shift,
    up_bias,
    hidden,
    cotangent,
    up_shard,
    down_shard,
    mid,
    act,
    grad_pre,
    residual_out,
    branch,
    grad_out,
    down_out,
    acc,
    acc_up,
    acc_down,
    grad_attended,
    part1,
    moving1,
    part2,
    moving2,
    rows_in,
    residual,
    up,
    down,
    cot_in,
    act_out,
    pre_out,
    attended_out,
    *sems,
):
    sems = list(sems)
    take = lambda n: [sems.pop(0) for _ in range(n)]
    sems1, sems2, weight_sems = take(5), take(5), take(3)
    in_sem, residual_sem, grad_sem, cot_sem, act_sem, pre_sem, down_sem = sems[:7]
    (attended_sem,) = sems[7:]
    me = lax.axis_index("mp")
    group = part2.shape[2]
    blocks = 4
    block = up.shape[1] // blocks
    per_group = group // PIECE
    pieces = half // PIECE
    last = count - 1
    second = per_group + blocks + 2 * SKEW * (count - 1)
    weights = weights_job((up_shard, down_shard), (up, down), weight_sems, second - blocks - 1)
    piece = lambda k: pl.ds(pl.multiple_of(k * PIECE, PIECE), PIECE)
    owner = (me == 0) | (me == last)
    my_flow = jnp.where(me == 0, 0, 1)

    def piece_in(source, k, flow):
        return pltpu.make_async_copy(
            source.at[pl.ds(flow * half + k * PIECE, PIECE)], rows_in.at[piece(k)], in_sem.at[k]
        )

    def residual_copy(k):
        return pltpu.make_async_copy(
            residual.at[piece(k)], residual_out.at[piece(k)], residual_sem.at[k]
        )

    def grad_copy(k):
        return pltpu.make_async_copy(residual.at[piece(k)], grad_out.at[piece(k)], grad_sem.at[k])

    def finish_first(flow, k, total):
        piece_in(hidden, k, flow).wait()
        value = rows_in[piece(k), :].astype(jnp.float32) + total + out_bias[...]
        residual[piece(k), :] = value
        residual_copy(k).start()
        piece_in(cotangent, k, flow).start()
        return norm_stats(value)[0] * mid_gain[...] + mid_shift[...]

    def finish_second(flow, k, total):
        piece_in(cotangent, k, flow).wait()
        residual_copy(k).wait()
        normed, inverse = norm_stats(residual[piece(k), :])
        grad = rows_in[piece(k), :].astype(jnp.float32)
        grad = grad + norm_back(total, normed, inverse, mid_gain[...])
        residual[piece(k), :] = grad
        grad_copy(k).start()
        acc[0] += fold(total * normed)
        acc[1] += fold(total)
        acc[2] += fold(grad)
        return grad

    multiply = group_product([attended], out_w, NN, half, part1.shape[2])
    line1 = Line(count, half, multiply, finish_first, mid, part1, moving1, sems1)
    line2 = Line(count, half, None, finish_second, branch, part2, moving2, sems2)

    def group_rows(flow, g):
        return pl.ds(pl.multiple_of(flow * half + g * group, 16), group)

    def cot_fetch(flow, g):
        return pltpu.make_async_copy(
            cotangent.at[group_rows(flow, g)], cot_in.at[flow], cot_sem.at[flow]
        )

    def act_copy(flow, g):
        return pltpu.make_async_copy(
            act_out.at[flow], act.at[group_rows(flow, g)], act_sem.at[flow]
        )

    def pre_copy(flow, g):
        return pltpu.make_async_copy(
            pre_out.at[flow], grad_pre.at[group_rows(flow, g)], pre_sem.at[flow]
        )

    def products(flow, g, number):
        @pl.when(number == 0)
        def _():
            cot_fetch(flow, g).wait()
            acc_down[...] += fold(cot_in[flow].astype(jnp.float32))

            @pl.when(g > 0)
            def _():
                act_copy(flow, g - 1).wait()
                pre_copy(flow, g - 1).wait()

        cols = pl.ds(pl.multiple_of(number * block, block), block)
        value, slope = gelu_parts(mm(moving1[line1.finished(flow, g * per_group, group), :], up[:, cols]) + up_bias[:, cols])
        act_out[flow, :, cols] = value.astype(jnp.bfloat16)
        pre = (slope * mm(cot_in[flow], down[cols, :], NT)).astype(jnp.bfloat16)
        pre_out[flow, :, cols] = pre
        acc_up[:, cols] += fold(pre.astype(jnp.float32))
        product = mm(pre, up[:, cols], NT)

        @pl.when(number == 0)
        def _():
            part2[flow, g % 2] = product

        @pl.when(number > 0)
        def _():
            part2[flow, g % 2] += product

        @pl.when(number == blocks - 1)
        def _():
            act_copy(flow, g).start()
            pre_copy(flow, g).start()

    def attended_copy(flow, g):
        return pltpu.make_async_copy(
            attended_out.at[flow], grad_attended.at[group_rows(flow, g)], attended_sem.at[flow]
        )

    def through_out(flow, g):
        @pl.when(g > 0)
        def _():
            attended_copy(flow, g - 1).wait()

        attended_out[flow] = mm(moving2[line2.finished(flow, g * per_group, group), :], out_w[...], NT).astype(jnp.bfloat16)
        attended_copy(flow, g).start()

    barrier = pltpu.get_barrier_semaphore()
    line1.greet(barrier)
    weights.greet(barrier)
    acc[...] = jnp.zeros_like(acc)
    acc_up[...] = jnp.zeros_like(acc_up)
    acc_down[...] = jnp.zeros_like(acc_down)
    weights.first()

    @pl.when(owner)
    def _():
        def one(k, carry):
            piece_in(hidden, k, my_flow).start()
            return carry

        lax.fori_loop(0, pieces, one, 0)

    if attention is None:
        line1.first()
        line1.meet(barrier, weights.others)
        weights.begin()
    else:
        line1.meet(barrier, weights.others)
        weights.begin()
        for load in attention.loads:
            load.wait()
        attention.first()
        line1.first()

    def step(t, carry):
        if attention is not None:
            attention.step(t)
        line1.step(t)
        line2.step(t - second)
        weights.step(t)

        @pl.when(t == weights.ready + 1)
        def _():
            pltpu.make_async_copy(down, down_out, down_sem.at[0]).start()

        for flow in range(2):
            place = line1.place(flow)
            u = t - second - SKEW * place
            fetch = u + blocks + 1
            compute = u + blocks

            @pl.when((fetch >= 0) & (fetch % per_group == 0) & (fetch < pieces))
            def _():
                cot_fetch(flow, fetch // per_group).start()

            @pl.when((compute >= 0) & (compute < pieces) & (compute % per_group < blocks))
            def _():
                products(flow, compute // per_group, compute % per_group)

            here = t - second - SKEW * (2 * last - place)

            @pl.when((here >= 0) & (here < pieces) & (here % per_group == per_group - 1))
            def _():
                through_out(flow, here // per_group)

        return carry

    lax.fori_loop(0, second + line2.steps, step, 0)
    line1.settle()
    line2.settle()
    weights.settle()
    pltpu.make_async_copy(down, down_out, down_sem.at[0]).wait()
    for flow in range(2):
        act_copy(flow, pieces // per_group - 1).wait()
        pre_copy(flow, pieces // per_group - 1).wait()
        attended_copy(flow, pieces // per_group - 1).wait()

    @pl.when(owner)
    def _():
        def one(k, carry):
            grad_copy(k).wait()
            return carry

        lax.fori_loop(0, pieces, one, 0)


def ffn_sums(number, count, weights_job, attend_in, out_w, vectors, hidden, cotangent, up_w, down_w):
    rows, features = hidden.shape
    ff = up_w.shape[1]
    half = rows // 2
    pieces = half // PIECE
    low = lambda *shape: jax.ShapeDtypeStruct(shape, jnp.bfloat16)
    wide = lambda *shape: jax.ShapeDtypeStruct(shape, jnp.float32)
    attend_out, attend_scratch = [], []
    if len(attend_in) > 1:
        width = attend_in[2].shape[1]
        attend_scratch = [pltpu.VMEM((rows, width), jnp.bfloat16)] * 3
        attend_scratch += [pltpu.SemaphoreType.DMA((3,))]
        attend_out = [low(rows, width), wide(width // PAIR, 2, rows)]
    first = Line.scratch(half, features)
    small = 64 if half % 64 == 0 else PIECE
    first[0] = pltpu.VMEM((2, 2, small, features), jnp.float32)
    second = Line.scratch(half, features)
    group = second[0].shape[2]
    dma = lambda n: pltpu.SemaphoreType.DMA((n,))
    return pl.pallas_call(
        functools.partial(ffn_kernel, count, half, weights_job, len(attend_in)),
        in_specs=([SMEM, VMEM] + [ANY] * 3 if len(attend_in) > 1 else [VMEM]) + [VMEM] * 5 + [ANY] * 4,
        out_specs=[ANY] * 7 + [VMEM] * 3 + [ANY] + [VMEM] * len(attend_out),
        out_shape=[
            low(rows, features),
            low(rows, ff),
            low(rows, ff),
            wide(half, features),
            low(rows, features),
            wide(half, features),
            low(ff, features),
            wide(3, 8, features),
            wide(8, ff),
            wide(8, features),
            low(rows, out_w.shape[0]),
        ]
        + attend_out,
        scratch_shapes=first[:2]
        + second[:2]
        + [
            pltpu.VMEM((half, features), jnp.bfloat16),
            pltpu.VMEM((half, features), jnp.float32),
            pltpu.VMEM((features, ff), jnp.bfloat16),
            pltpu.VMEM((ff, features), jnp.bfloat16),
            pltpu.VMEM((2, group, features), jnp.bfloat16),
            pltpu.VMEM((2, group, ff), jnp.bfloat16),
            pltpu.VMEM((2, group, ff), jnp.bfloat16),
            pltpu.VMEM((2, group, out_w.shape[0]), jnp.bfloat16),
        ]
        + first[2:]
        + second[2:]
        + Gather.sems()
        + [dma(pieces), dma(pieces), dma(pieces), dma(2), dma(2), dma(2), dma(1)]
        + [dma(2)]
        + attend_scratch,
        compiler_params=pltpu.CompilerParams(
            collective_id=number, has_side_effects=True, vmem_limit_bytes=62 * MIB
        ),
        cost_estimate=pl.CostEstimate(
            flops=6 * rows * features * ff, bytes_accessed=30 * rows * features, transcendentals=0
        ),
        name="ffn_sums",
    )(*attend_in, out_w, *vectors, hidden, cotangent, up_w, down_w)


def start_kernel(
    lengths,
    gain,
    shift,
    bias,
    hidden_in,
    shard,
    out_shard,
    q_out,
    k_out,
    v_out,
    earlier,
    normed_out,
    weight_out,
    out_whole,
    normed,
    weight,
    out_weight,
    total,
    summary,
    hidden,
    q_ref,
    k_ref,
    v_ref,
    *sems,
):
    facts = Facts(lengths)
    gather = Gather((shard, out_shard), (weight, out_weight), sems[:3], 0)
    summary_sent, summary_got, out_sems = sems[3:]
    rows = hidden.shape[0]
    width = q_ref.shape[1]
    size = shard.shape[0]
    chunk = 128
    barrier = pltpu.get_barrier_semaphore()
    gather.greet(barrier)
    load = pltpu.make_async_copy(hidden_in, hidden, out_sems.at[3])
    load.start()
    gather.first()
    pl.semaphore_wait(barrier, gather.others)
    gather.send(0, (1, 2, 0))

    def norm(i, carry):
        here = pl.ds(pl.multiple_of(i * chunk, chunk), chunk)
        value = norm_stats(hidden[here, :].astype(jnp.float32))[0]
        normed[here, :] = (value * gain[...] + shift[...]).astype(jnp.bfloat16)
        return carry

    load.wait()
    lax.fori_loop(0, rows // chunk, norm, 0)
    keep = pltpu.make_async_copy(normed, normed_out, out_sems.at[0])
    keep.start()
    c, x, y = gather.core, gather.x, gather.y

    def add(places, first=False, last=False):
        starts = [
            pl.multiple_of(((2 * px + pc) * 2 + py) * size, size) for px, pc, py in places
        ]

        def rows_of(i, carry):
            here = pl.ds(pl.multiple_of(i * chunk, chunk), chunk)
            for j, out in enumerate((q_ref, k_ref, v_ref)):
                cols = slice(j * width, (j + 1) * width)
                value = None if first else total[here, cols]
                for start in starts:
                    at = pl.ds(start, size)
                    product = mm(normed[here, at], weight[at, cols])
                    value = product if value is None else value + product
                if not last:
                    total[here, cols] = value
                elif j == 1:
                    out[here, :] = value.astype(jnp.bfloat16)
                else:
                    out[here, :] = (value + bias[j // 2 : j // 2 + 1, :]).astype(jnp.bfloat16)
            return carry

        lax.fori_loop(0, rows // chunk, rows_of, 0)

    gather.mine(0).wait()
    gather.receive(0, (0,))
    add(((x, c, y), (x, 1 - c, y)), first=True)
    gather.receive(0, (1, 2))
    gather.send(0, (3, 4, 5, 6))
    gather.send(1, (1, 2, 0))
    add(((1 - x, c, y), (x, c, 1 - y)))
    gather.receive(0, (5, 6))
    add(((1 - x, 1 - c, y), (x, 1 - c, 1 - y)))
    gather.receive(0, (3, 4))
    gather.send(0, (7, 8))
    add(((1 - x, c, 1 - y),))
    gather.receive(1, (1, 2))
    gather.send(1, (3, 4, 5, 6))
    gather.receive(0, (7, 8))
    store = pltpu.make_async_copy(weight, weight_out, out_sems.at[1])
    store.start()
    add(((1 - x, 1 - c, 1 - y),), last=True)
    results = [
        pltpu.make_async_copy(source, target, out_sems.at[4 + number])
        for number, (source, target) in enumerate(
            ((q_ref, q_out), (k_ref, k_out), (v_ref, v_out))
        )
    ]
    for result in results:
        result.start()

    shape = (SUMM_ROWS, rows)
    chosen = lax.broadcasted_iota(jnp.int32, shape, 1) == (
        facts[1] - SUMM + lax.broadcasted_iota(jnp.int32, shape, 0)
    )
    chosen = jnp.where(chosen, 1.0, 0.0).astype(jnp.bfloat16)
    summary[0] = mm(chosen, k_ref[...]).astype(jnp.bfloat16)
    summary[1] = mm(chosen, v_ref[...]).astype(jnp.bfloat16)
    swap = pltpu.make_async_remote_copy(
        src_ref=summary,
        dst_ref=earlier,
        send_sem=summary_sent.at[0],
        recv_sem=summary_got.at[0],
        device_id=gather.to_y,
        device_id_type=MESH,
    )
    swap.start()
    gather.receive(1, (3, 4))
    gather.send(1, (7, 8))
    gather.receive(1, (0, 5, 6, 7, 8))
    gather.mine(1).wait()
    store_out = pltpu.make_async_copy(out_weight, out_whole, out_sems.at[2])
    store_out.start()
    gather.settle()
    keep.wait()
    store.wait()
    swap.wait()
    store_out.wait()
    for result in results:
        result.wait()


def start(number, lengths, hidden, gain, shift, bias, shard, out_shard):
    rows, features = hidden.shape
    width = bias.shape[1]
    low = lambda *shape: jax.ShapeDtypeStruct(shape, jnp.bfloat16)
    dma = lambda n: pltpu.SemaphoreType.DMA((n,))
    return pl.pallas_call(
        start_kernel,
        in_specs=[SMEM] + [VMEM] * 3 + [ANY] * 3,
        out_specs=[ANY] * 7,
        out_shape=[low(rows, width)] * 3
        + [low(2, SUMM_ROWS, width), low(rows, features), low(features, 3 * width)]
        + [low(width, features)],
        scratch_shapes=[
            pltpu.VMEM((rows, features), jnp.bfloat16),
            pltpu.VMEM((features, 3 * width), jnp.bfloat16),
            pltpu.VMEM((width, features), jnp.bfloat16),
            pltpu.VMEM((rows, 3 * width), jnp.float32),
            pltpu.VMEM((2, SUMM_ROWS, width), jnp.bfloat16),
            pltpu.VMEM((rows, features), jnp.bfloat16),
        ]
        + [pltpu.VMEM((rows, width), jnp.bfloat16)] * 3
        + Gather.sems()
        + [dma(1), dma(1), dma(7)],
        compiler_params=pltpu.CompilerParams(
            collective_id=number, has_side_effects=True, vmem_limit_bytes=60 * MIB
        ),
        cost_estimate=pl.CostEstimate(
            flops=6 * rows * features * width, bytes_accessed=16 * rows * features, transcendentals=0
        ),
        name="start",
    )(lengths, gain, shift, bias, hidden, shard, out_shard)


class SmallSums(Nothing):
    n_in = n_out = 1

    def __init__(self, sizes, shared, start, values):
        self.stages = tuple(
            (axis, 1 << bit) for axis, size in sizes for bit in range(size.bit_length() - 1)
        )
        self.shared, self.start = shared, start
        self.others = len(self.stages)
        self.steps = start + self.others + 1
        self.operands = (values,)
        self.in_specs = self.out_specs = (VMEM,)
        self.out_shape = (jax.ShapeDtypeStruct(values.shape, jnp.float32),)
        buffers = pltpu.VMEM((self.others, *values.shape), jnp.float32)
        sems = pltpu.SemaphoreType.DMA((self.others,))
        self.scratch_shapes = (buffers, buffers, sems, sems)

    def __call__(self, ins, outs, scratch, accs):
        (self.own,), (self.out,), (self.acc,) = ins, outs, accs
        self.sent, self.got, self.send_sem, self.recv_sem = scratch
        return self

    def partner(self, axis, bit):
        index = lax.axis_index(axis)
        return {axis: index + bit - 2 * bit * ((index // bit) % 2)}

    def extra(self, row, start, grad):
        cols = slice(start, start + grad.shape[1])
        self.sent[0, row : row + 1, cols] = jnp.sum(
            grad[...].astype(jnp.float32), axis=0, keepdims=True
        )

    def greet(self, barrier):
        for axis, bit in self.stages:
            pl.semaphore_signal(
                barrier, inc=1, device_id=self.partner(axis, bit), device_id_type=MESH
            )

    def copy(self, number):
        return pltpu.make_async_remote_copy(
            src_ref=self.sent.at[number],
            dst_ref=self.got.at[number],
            send_sem=self.send_sem.at[number],
            recv_sem=self.recv_sem.at[number],
            device_id=self.partner(*self.stages[number]),
            device_id_type=MESH,
        )

    def first(self):
        self.sent[0] = self.own[...]

    def step(self, t):
        @pl.when(t == self.start)
        def _():
            for number in range(self.acc.shape[0]):
                self.sent[0, 3 + number : 4 + number, :] = jnp.sum(
                    self.acc[number], axis=0, keepdims=True
                )
            self.copy(0).start()

        row = lax.broadcasted_iota(jnp.int32, self.out.shape, 0)
        for number, (axis, _) in enumerate(self.stages):

            @pl.when(t == self.start + 1 + number)
            def _():
                self.copy(number).wait()
                total = self.sent[number] + self.got[number]
                if axis == "mp":
                    total = jnp.where(row < self.shared, total, self.sent[number])
                if number + 1 < len(self.stages):
                    self.sent[number + 1] = total
                    self.copy(number + 1).start()
                else:
                    self.out[...] = total


class Columns:
    def __init__(self, ref, start, width):
        self.ref, self.start, self.shape = ref, start, (ref.shape[0], width)

    def __getitem__(self, index):
        rows, cols = index
        start = pl.multiple_of(self.start + cols.start, PAIR)
        return self.ref[rows, pl.ds(start, cols.size)]


class Ring:
    depth = 2

    def __init__(self, source, buffer, sems, pieces, offset):
        self.source, self.buffer, self.sems = source, buffer, sems
        self.pieces, self.offset = pieces, offset

    @classmethod
    def scratch(cls, features, dtype):
        return [
            pltpu.VMEM((cls.depth, PIECE, features), dtype),
            pltpu.SemaphoreType.DMA((cls.depth,)),
        ]

    def copy(self, k):
        rows = pl.ds(self.offset + k * PIECE, PIECE)
        slot = k % self.depth
        return pltpu.make_async_copy(
            self.source.at[rows], self.buffer.at[slot], self.sems.at[slot]
        )

    def fill(self):
        for k in range(min(self.depth, self.pieces)):
            self.copy(k).start()

    def take(self, k):
        self.copy(k).wait()
        value = self.buffer[k % self.depth].astype(jnp.float32)

        @pl.when(k + self.depth < self.pieces)
        def _():
            self.copy(k + self.depth).start()

        return value


def back_kernel(
    count,
    half,
    sizes,
    lengths,
    lse,
    earlier,
    down_bias,
    pre_gain,
    mid_sums,
    up_sums,
    down_sums,
    q_in,
    k_in,
    v_in,
    do_in,
    act,
    down_in,
    residual,
    hidden,
    grad_in,
    qkv_in,
    mid,
    cotangent,
    branch,
    normed,
    grad_pre,
    attended,
    hidden_out,
    input_grad,
    up_grad,
    down_grad,
    out_grad,
    qkv_grad,
    sums_out,
    part,
    moving1,
    moving2,
    down,
    qkv_w,
    dq,
    dk,
    dv,
    dk_acc,
    dv_acc,
    k_t,
    dks,
    dvs,
    swap_out,
    swap_in,
    act_in,
    acc,
    small_sent,
    small_got,
    *rest,
):
    rest = list(rest)
    facts = Facts(lengths)
    take = lambda n: [rest.pop(0) for _ in range(n)]
    rings = take(6)
    sems1, sems2 = take(5), take(5)
    small_sems = take(2)
    load_sem, act_sem, swap_sent, swap_got = take(4)
    rows, width = 2 * half, dq.shape[1]
    pieces = half // PIECE
    me = lax.axis_index("mp")
    owner = (me == 0) | (me == count - 1)
    offset = jnp.where(me == 0, 0, half)
    residual_ring = Ring(residual, *rings[0:2], pieces, 0)
    grad_ring = Ring(grad_in, *rings[2:4], pieces, 0)
    hidden_ring = Ring(hidden, *rings[4:6], pieces, offset)
    group = part.shape[2]

    def act_copy(flow, g):
        return pltpu.make_async_copy(
            act.at[pl.ds(pl.multiple_of(flow * half + g * group, 16), group)],
            act_in.at[flow],
            act_sem.at[flow],
        )

    def multiply_down(flow, g):
        act_copy(flow, g).wait()
        product = mm(act_in[flow], down[...])

        @pl.when(g + 1 < half // group)
        def _():
            act_copy(flow, g + 1).start()

        return product

    def finish_first(flow, k, total):
        return residual_ring.take(k) + total + down_bias[...]

    def finish_second(flow, k, total):
        values, inverse = norm_stats(hidden_ring.take(k))
        acc[0] += fold(total * values)
        acc[1] += fold(total)
        return grad_ring.take(k) + norm_back(total, values, inverse, pre_gain[...])

    line1 = Line(count, half, multiply_down, finish_first, hidden_out, part, moving1, sems1)
    multiply_back = group_product([dq, dk, dv], qkv_w, NT, half, group)
    line2 = Line(
        count, half, multiply_back, finish_second, input_grad, part, moving2, sems2, late=True
    )
    heads = AttendBack.__new__(AttendBack)
    heads.bq = query_block(rows)
    heads.blocks = rows // heads.bq
    heads.pairs = width // PAIR
    heads.steps = heads.pairs * heads.blocks
    heads.causal = True
    first = moving2.at[pl.ds(0, rows)]
    views = [Columns(first, j * width, width) for j in range(4)]
    tables = [earlier.at[0], earlier.at[1]]
    heads.ins = (facts, *views[:3], *tables, views[3], lse)
    heads.outs = (dq, dk, dv, dks, dvs)
    heads.scratch = (dk_acc, dv_acc, k_t)
    second = heads.steps + 2
    columns = (
        (0, grad_pre, 0, 0),
        (1, act, 1, 0),
        (2, attended, 2, 0),
        (3, dq, 3, 0),
        (3, dk, 3, width),
        (3, dv, 3, 2 * width),
    )
    spread = Spread(
        (mid, cotangent, branch, normed),
        columns,
        (up_grad, down_grad, out_grad, qkv_grad),
        down.at[pl.ds(0, rows)],
        rest,
        heads.steps - 2,
    )
    small = SmallSums(sizes, 6, second + pieces + SKEW * (count - 1), sums_out)
    small((None,), (sums_out,), (small_sent, small_got, *small_sems), (acc,))
    column_sums = lambda values: jnp.sum(values, axis=0, keepdims=True)
    features = down_in.shape[1]
    ff_rows = down_in.shape[0] // features
    loads = [
        pltpu.make_async_copy(source, target, load_sem.at[number])
        for number, (source, target) in enumerate(
            [(down_in, down), (qkv_in, qkv_w)]
            + [
                (source, first.at[:, pl.ds(j * width, width)])
                for j, source in enumerate((q_in, k_in, v_in, do_in))
            ]
        )
    ]
    swap = pltpu.make_async_remote_copy(
        src_ref=swap_out,
        dst_ref=swap_in,
        send_sem=swap_sent.at[0],
        recv_sem=swap_got.at[0],
        device_id=spread.to_y,
        device_id_type=MESH,
    )

    barrier = pltpu.get_barrier_semaphore()
    line1.greet(barrier)
    spread.greet(barrier)
    small.greet(barrier)
    for flow in range(2):
        act_copy(flow, 0).start()
    for load in loads:
        load.start()

    @pl.when(owner)
    def _():
        for ring in (residual_ring, grad_ring, hidden_ring):
            ring.fill()

    acc[...] = jnp.zeros_like(acc)
    small_sent[0] = jnp.zeros_like(small_sent[0])
    for number in range(3):
        small_sent[0, number : number + 1, :] = mid_sums[number : number + 1, :]
    small_sent[0, 5:6, :] = jnp.where(me == 0, column_sums(down_sums[...]), 0.0)
    for number in range(ff_rows):
        cols = slice(number * features, (number + 1) * features)
        small_sent[0, 6 + number : 7 + number, :] = column_sums(up_sums[:, cols])
    loads[0].wait()
    line1.first()
    line1.meet(barrier, spread.others + small.others)
    for load in loads[2:]:
        load.wait()

    def step(t, carry):
        line1.step(t)
        heads.step(t)

        @pl.when(t == heads.steps)
        def _():
            swap_out[0] = dks[...].astype(jnp.bfloat16)
            swap_out[1] = dvs[...].astype(jnp.bfloat16)
            swap.start()

        @pl.when(t == heads.steps + 1)
        def _():
            swap.wait()
            loads[1].wait()
            shape = (rows, SUMM_ROWS)
            chosen = lax.broadcasted_iota(jnp.int32, shape, 0) == (
                facts[1] - SUMM + lax.broadcasted_iota(jnp.int32, shape, 1)
            )
            chosen = jnp.where(chosen, 1.0, 0.0).astype(jnp.bfloat16)
            for number, grad in enumerate((dk, dv)):
                added = grad[...].astype(jnp.float32) + mm(chosen, swap_in[number])
                grad[...] = added.astype(jnp.bfloat16)
            for number, grad in enumerate((dq, dv)):
                small.extra(6 + ff_rows, number * width, grad)

        line2.step(t - second)
        spread.step(t)
        small.step(t)
        return carry

    lax.fori_loop(0, max(second + line2.steps, spread.steps, small.steps), step, 0)
    line1.settle()
    line2.settle()
    spread.settle()


def back_sums(number, count, sizes, whole_in, vmem_in):
    rows, width = whole_in[0].shape
    features = whole_in[5].shape[1]
    ff = whole_in[5].shape[0]
    half = rows // 2
    low = lambda *shape: pltpu.VMEM(shape, jnp.bfloat16)
    wide = lambda *shape: pltpu.VMEM(shape, jnp.float32)
    dma = lambda *shape: pltpu.SemaphoreType.DMA(shape)
    lines = Line.scratch(half, features)
    group = lines[0].shape[2]
    stages = sum(size.bit_length() - 1 for _, size in sizes)
    block = Spread.block
    sums_shape = (6 + ff // features + -(-2 * width // features), features)
    return pl.pallas_call(
        functools.partial(back_kernel, count, half, sizes),
        in_specs=[SMEM] + [VMEM] * 7 + [ANY] * len(whole_in),
        out_specs=[ANY] * 6 + [VMEM],
        out_shape=[
            jax.ShapeDtypeStruct((rows, features), jnp.bfloat16),
            jax.ShapeDtypeStruct((rows, features), jnp.bfloat16),
            jax.ShapeDtypeStruct((block, ff), jnp.float32),
            jax.ShapeDtypeStruct((ff, block), jnp.float32),
            jax.ShapeDtypeStruct((width, block), jnp.float32),
            jax.ShapeDtypeStruct((block, 3 * width), jnp.float32),
            jax.ShapeDtypeStruct(sums_shape, jnp.float32),
        ],
        scratch_shapes=[
            lines[0],
            lines[1],
            lines[1],
            low(ff, features),
            low(features, 3 * width),
            low(rows, width),
            low(rows, width),
            low(rows, width),
            wide(rows, PAIR),
            wide(rows, PAIR),
            low(PAIR, rows),
            wide(SUMM_ROWS, width),
            wide(SUMM_ROWS, width),
            low(2, SUMM_ROWS, width),
            low(2, SUMM_ROWS, width),
            low(2, group, ff),
            wide(2, 8, features),
            wide(stages, *sums_shape),
            wide(stages, *sums_shape),
        ]
        + Ring.scratch(features, jnp.float32)
        + Ring.scratch(features, jnp.float32)
        + Ring.scratch(features, jnp.bfloat16)
        + lines[2:]
        + lines[2:]
        + [dma(stages), dma(stages), dma(6), dma(2), dma(1), dma(1)]
        + Spread.scratch(rows),
        compiler_params=pltpu.CompilerParams(
            collective_id=number, has_side_effects=True, vmem_limit_bytes=63 * MIB
        ),
        cost_estimate=pl.CostEstimate(
            flops=12 * rows * features * ff, bytes_accessed=60 * rows * features, transcendentals=0
        ),
        name="back_sums",
    )(*vmem_in, *whole_in)


def gradients_over(group, lefts, columns):
    over_rows = lambda left, right: mm(left, right, (((0,), (0,)), ((), ()))).astype(jnp.bfloat16)
    parts = [[] for _ in range(4)]
    for left, right, result, _ in columns:
        across = result in (0, 3)
        product = over_rows(lefts[left], right) if across else over_rows(right, lefts[left])
        parts[result].append(product)
    return [
        lax.psum_scatter(
            jnp.concatenate(part, axis=1),
            group,
            scatter_dimension=0 if result in (0, 3) else 1,
            tiled=True,
        ).astype(jnp.float32)
        for result, part in enumerate(parts)
    ]


def body(
    item_count,
    seq_count,
    mp_count,
    hidden_in,
    cotangent,
    seg_lengths,
    pre_gain,
    pre_shift,
    qkv_weight,
    qv_bias,
    out_weight,
    out_bias,
    mid_gain,
    mid_shift,
    up_weight,
    up_bias,
    down_weight,
    down_bias,
):
    group = ("item", "seq")
    width = qkv_weight.shape[2]
    gathered = lambda weight, axis: lax.all_gather(weight, group, axis=axis, tiled=True)
    hidden = hidden_in[0].astype(jnp.float32)
    lengths = seg_lengths[0]
    rows = hidden.shape[0]
    first_row = lax.axis_index("seq") * rows
    segment = first_row // SLOT
    facts = jnp.stack(
        [
            first_row % SLOT,
            lengths[segment] + SUMM,
            jnp.where(segment > 0, SUMM, 0),
        ]
    ).astype(jnp.int32)

    ours = (item_count, seq_count) == (4, 2) and rows == SLOT
    row = lambda vector: vector[None, :]
    shard = qkv_weight.reshape(-1, 3 * width)
    if ours:
        q, k, v, summary, normed, qkv_full, out_full = start(
            5, seg_lengths, hidden_in[0], row(pre_gain), row(pre_shift), qv_bias, shard, out_weight
        )
        attend_in = (seg_lengths, summary, q, k, v)
        tables = (k, v, summary[0], summary[1])
    else:
        qkv_full = gathered(shard, 0)
        out_full = gathered(out_weight, 1)
        normed = (norm_stats(hidden)[0] * pre_gain + pre_shift).astype(jnp.bfloat16)
        q = (mm(normed, qkv_full[:, :width]) + qv_bias[0]).astype(jnp.bfloat16)
        k = mm(normed, qkv_full[:, width : 2 * width]).astype(jnp.bfloat16)
        v = (mm(normed, qkv_full[:, 2 * width :]) + qv_bias[1]).astype(jnp.bfloat16)
        own, summary = keys_for(jnp.stack([k, v]), lengths, seq_count)
        tables = (own[0], own[1], summary[0], summary[1])
        attended, log_total = attend(facts, q, *tables)
        attend_in = (attended,)

    grad_down = cotangent[0]
    (
        mid_low,
        act_low,
        grad_pre,
        residual,
        grad_branch,
        grad_residual,
        down_full,
        mid_sums,
        up_sums,
        down_sums,
        grad_attended,
        *attend_out,
    ) = ffn_sums(
        1,
        mp_count,
        Gather if ours else Load,
        attend_in,
        out_full,
        (row(out_bias), row(mid_gain), row(mid_shift), row(up_bias)),
        hidden_in[0],
        grad_down,
        up_weight if ours else gathered(up_weight, 0),
        down_weight if ours else gathered(down_weight, 1),
    )
    if ours:
        attended, log_total = attend_out
    total = lambda value: jnp.sum(value.astype(jnp.float32), axis=0)
    features = hidden.shape[1]
    sizes = [("item", item_count), ("seq", seq_count), ("mp", mp_count)]
    once = lambda value: jnp.where(lax.axis_index("mp") == 0, value, 0.0)
    small_in = lambda qv_sums: jnp.concatenate(
        [
            jnp.sum(mid_sums, axis=1),
            jnp.zeros((2, features), jnp.float32),
            row(once(total(down_sums))),
            total(up_sums).reshape(-1, features),
            jnp.pad(qv_sums, (0, -qv_sums.shape[0] % features)).reshape(-1, features),
        ]
    )
    if ours:
        hidden_out, grad_input, up_grad, down_grad, out_grad, qkv_grad, sums = back_sums(
            2,
            mp_count,
            sizes,
            (q, k, v, grad_attended, act_low, down_full, residual, hidden_in[0], grad_residual)
            + (qkv_full, mid_low, grad_down, grad_branch, normed, grad_pre, attended),
            (seg_lengths, log_total, summary, row(down_bias), row(pre_gain))
            + (jnp.sum(mid_sums, axis=1), up_sums, down_sums),
        )
    else:
        hidden_out, dq, dk, dv, dks, dvs = line_sum(
            3,
            mp_count,
            [act_low],
            down_full,
            NN,
            [residual, row(down_bias)],
            0,
            0,
            finish_out,
            "down_sum",
            (AttendBack(facts, q, *tables, grad_attended, log_total),),
        )
        dk, dv = keys_back(jnp.stack([dk, dv]), jnp.stack([dks, dvs]), rows, lengths, seq_count)
        small = SmallSums(
            sizes,
            6,
            rows // 2 // PIECE + SKEW * (mp_count - 1),
            small_in(jnp.concatenate([total(dq), total(dv)])),
        )
        grad_input, _, sums = line_sum(
            4,
            mp_count,
            [dq, dk, dv],
            qkv_full,
            NT,
            [hidden_in[0], grad_residual, row(pre_gain)],
            0,
            2,
            finish_input,
            "input_sum",
            (small,),
        )
        lefts = (mid_low, grad_down, grad_branch, normed)
        columns = (
            (0, grad_pre, 0, 0),
            (1, act_low, 1, 0),
            (2, attended, 2, 0),
            (3, dq, 3, 0),
            (3, dk, 3, width),
            (3, dv, 3, 2 * width),
        )
        up_grad, down_grad, out_grad, qkv_grad = gradients_over(group, lefts, columns)
    ff_rows = up_weight.shape[1] // features
    up_bias_grad = sums[6 : 6 + ff_rows].reshape(-1)
    qv_bias_grad = sums[6 + ff_rows :].reshape(-1)[: 2 * width].reshape(2, width)
    return (
        hidden_out[None],
        grad_input.astype(jnp.float32)[None],
        sums[3],
        sums[4],
        qkv_grad.reshape(-1, 3, width),
        qv_bias_grad,
        out_grad,
        sums[2],
        sums[0],
        sums[1],
        up_grad,
        up_bias_grad,
        down_grad,
        sums[5],
    )


def solution(mesh):
    rows = P("item", "seq", None)
    qkv = P(("item", "seq"), None, "mp")
    first = P(("item", "seq"), "mp")
    second = P("mp", ("item", "seq"))
    bias = P(None, "mp")
    return jax.shard_map(
        functools.partial(body, mesh.shape["item"], mesh.shape["seq"], mesh.shape["mp"]),
        mesh=mesh,
        in_specs=(
            rows,
            rows,
            P("item", None),
            P(),
            P(),
            qkv,
            bias,
            second,
            P(),
            P(),
            P(),
            first,
            P("mp"),
            second,
            P(),
        ),
        out_specs=(
            rows,
            rows,
            P(),
            P(),
            qkv,
            bias,
            second,
            P(),
            P(),
            P(),
            first,
            P("mp"),
            second,
            P(),
        ),
        check_vma=False,
    )
```
